32 devices in a mesh: section: 2 (over x), dp: 8 (over z, y), mp: 2 (over core).
Axes of the slice: x: 2, y: 2, z: 4, core: 2. Of those that a mesh axis runs over, the one named last changes fastest.
Arguments:
- act_in: bfloat16 [2, 9408, 1024], P('section', ('dp', 'mp')), may hold values from -6 to 6
- packing: int32 [8, 2, 1176], P('dp'), may hold values from 0 to 195, as said below
- enc_weights: float32 [1024, 2, 6400], P(('section', 'dp'), 'mp'), as said below
- enc_first: float32 [1024, 2, 6400], P(('section', 'dp'), 'mp'), may hold values from -56 to 56
- enc_second: float32 [1024, 2, 6400], P(('section', 'dp'), 'mp'), may hold values from 1000 to 4000
- dec_weights: float32 [512, 2, 3072], P(('section', 'dp'), 'mp'), as said below
- dec_first: float32 [512, 2, 3072], P(('section', 'dp'), 'mp'), may hold values from -56 to 56
- dec_second: float32 [512, 2, 3072], P(('section', 'dp'), 'mp'), may hold values from 1000 to 4000
- enc_norms: float32 [4, 1024], P(None, ('section', 'dp')), as said below
- enc_norm_first: float32 [4, 1024], P(None, ('section', 'dp')), may hold values from -112 to 112
- enc_norm_second: float32 [4, 1024], P(None, ('section', 'dp')), may hold values from 2000 to 32000
- dec_norms: float32 [4, 512], P(None, ('section', 'dp')), as said below
- dec_norm_first: float32 [4, 512], P(None, ('section', 'dp')), may hold values from -112 to 112
- dec_norm_second: float32 [4, 512], P(None, ('section', 'dp')), may hold values from 2000 to 32000
- mask_token: float32 [512], replicated, may hold values from -6 to 6
- dec_position: float32 [196, 512], replicated, may hold values from -6 to 6
- learning_rate: float32 [2], replicated, may hold values from 0.5 to 10, as said below
- step_count: int32 [1], replicated, may hold values from 2 to 5
Outputs:
- act_out: float32 [2, 9408, 1024], P('section', ('dp', 'mp'))
- new_enc_weights: float32 [1024, 2, 6400], P(('section', 'dp'), 'mp')
- new_dec_weights: float32 [512, 2, 3072], P(('section', 'dp'), 'mp')
- new_enc_norms: float32 [4, 1024], P(None, ('section', 'dp'))
- new_dec_norms: float32 [4, 512], P(None, ('section', 'dp'))
- enc_grads: float32 [1024, 2, 6400], P(('section', 'dp'), 'mp')
- dec_grads: float32 [512, 2, 3072], P(('section', 'dp'), 'mp')
- enc_norm_grads: float32 [4, 1024], P(None, ('section', 'dp'))
- dec_norm_grads: float32 [4, 512], P(None, ('section', 'dp'))
- grad_norm: float32 [1], replicated
The draws below stay inside these ranges and needn't reach their ends.
Inputs may be any that keep to these rules, and one draw needn't show every extreme that they name: For each index of dp, packing[., 0, :] holds image slots 0 to 11 in order, each a contiguous run of 24 to 73 rows, then 12 on every remaining (padding) row; at least one padding row exists. packing[., 1, :] holds distinct patches within an image and 0 on padding rows. Some image has exactly 73 visible patches and some exactly 24. `enc_weights`: normal entries within six standard deviations, each column group scaled by its own factor. `dec_weights`: normal entries within six standard deviations, each column group scaled by its own factor. `enc_norms`: gains between 0.5 and 1.5, biases within 1.2 of zero. `dec_norms`: gains between 0.5 and 1.5, biases within 1.2 of zero. learning_rate[0] lies between 0.5 and 2, learning_rate[1] between 5 and 10.
All inputs are finite; a program needn't handle non-finite values.
Results may differ from the reference program's by a relative error of at most 0.014.
Values may be sent and summed in bfloat16 or wider, within the bound.
A program may use at most 320 MiB of HBM per device.

```python
import math
import jax
import jax.numpy as jnp
from jax import lax

D = 1024
FF = 4096
HEADS = 16
DD = 512
FFD = 2048
GRID = 196
IMG = 12
CAP = 1176
ENC_COLS = 6400
DEC_COLS = 3072
PARAMS = 16259072
N_SECTION = 2
N_DP = 8
N_MP = 2


def column_scales(feature_width, hidden_units, tail_columns, keys_counted):
    part_width = feature_width // N_MP
    part_hidden = hidden_units // N_MP
    drawn = feature_width ** (-0.5)
    pieces = [jnp.full((3 * part_width,), drawn, jnp.float32), jnp.full((part_width,), math.sqrt(keys_counted) * drawn, jnp.float32), jnp.full((part_hidden,), drawn, jnp.float32), jnp.full((part_hidden,), hidden_units ** (-0.5), jnp.float32), jnp.full((tail_columns,), drawn, jnp.float32)]
    return jnp.concatenate(pieces)


def draw_enc_weights(key, part):
    scales = column_scales(D, FF, DD // N_MP, GRID / 4.0)
    noise = jax.random.normal(jax.random.fold_in(key, 11), (D, N_MP, scales.shape[0]), jnp.float32)
    return jnp.clip(noise, -6.0, 6.0) * scales


def draw_dec_weights(key, part):
    scales = column_scales(DD, FFD, 0, GRID * 1.0)
    noise = jax.random.normal(jax.random.fold_in(key, 23), (DD, N_MP, scales.shape[0]), jnp.float32)
    return jnp.clip(noise, -6.0, 6.0) * scales


def gain_block(key, feature_width):
    gain_key, shift_key = jax.random.split(key)
    gains = jax.random.uniform(gain_key, (2, feature_width), jnp.float32, 0.5, 1.5)
    shifts = 0.3 * jnp.clip(jax.random.normal(shift_key, (2, feature_width), jnp.float32), -4.0, 4.0)
    return jnp.stack([gains[0], shifts[0], gains[1], shifts[1]])


def draw_enc_norms(key, part):
    return gain_block(jax.random.fold_in(key, 37), D)


def draw_dec_norms(key, part):
    return gain_block(jax.random.fold_in(key, 41), DD)


def draw_learning_rate(key, part):
    key = jax.random.fold_in(key, 67)
    unit = jax.random.uniform(key, (2,), jnp.float32)
    lowest = jnp.array([0.5, 5.0], jnp.float32)
    widths = jnp.array([1.5, 5.0], jnp.float32)
    return lowest + unit * widths


def draw_packing(key, part):
    count_key, order_key = jax.random.split(jax.random.fold_in(key, 53))
    low_count = GRID // 8
    high_count = GRID * 3 // 8
    counts = jax.random.randint(count_key, (N_DP, IMG), low_count, high_count + 1)
    counts = counts.at[0, 0].set(high_count)
    counts = counts.at[0, IMG - 1].set(low_count)
    ends = jnp.cumsum(counts, axis=1)
    starts = ends - counts
    row_index = jnp.arange(CAP)
    slot_ids = jnp.sum((row_index[None, None, :] >= ends[:, :, None]).astype(jnp.int32), axis=1)
    order_keys = jax.random.split(order_key, N_DP * IMG)
    orders = jax.vmap(lambda single_key: jax.random.permutation(single_key, GRID))(order_keys).reshape(N_DP, IMG, GRID)
    leading = orders[0, 0]
    where_last = jnp.argmax((leading == GRID - 1).astype(jnp.int32))
    orders = orders.at[0, 0].set(jnp.roll(leading, -where_last))
    bounded = jnp.minimum(slot_ids, IMG - 1)
    offsets = row_index[None, :] - jnp.take_along_axis(starts, bounded, axis=1)
    offsets = jnp.clip(offsets, 0, GRID - 1)
    patch_ids = jnp.take_along_axis(orders.reshape(N_DP, IMG * GRID), bounded * GRID + offsets, axis=1)
    patch_ids = jnp.where(slot_ids < IMG, patch_ids, 0)
    return jnp.stack([slot_ids, patch_ids], axis=1).astype(jnp.int32)


def levels(key, shape, shards, low, largest):
    level, own = 1.0, jax.random.fold_in(key, 6)
    for axis_at, blocks in shards:
        draws = jnp.exp(jax.random.uniform(jax.random.fold_in(own, axis_at), (blocks,), jnp.float32, low / len(shards), largest / len(shards)))
        level = level * jnp.repeat(draws, shape[axis_at] // blocks).reshape([-1 if axis == axis_at else 1 for axis in range(len(shape))])
    return level


def scatter_about(key, dims, scale, limit, cuts=(), kind=jnp.bfloat16):
    drawn = scale * jax.random.normal(key, dims, jnp.float32)
    if cuts:
        drawn = drawn * levels(key, dims, cuts, -0.22, 0.18)
    return jnp.clip(drawn, -limit, limit).astype(kind)


def setup_inputs(seed: int = 0) -> dict:
    key_of = jax.random.split(jax.random.key(seed), 19)
    act_in = scatter_about(key_of[0], (N_SECTION, N_DP * CAP, D), 1.0, 6.0, ((0, 2), (1, 16)))
    packing = draw_packing(jax.random.fold_in(key_of[18], 71), 0)
    enc_weights = draw_enc_weights(jax.random.fold_in(key_of[18], 71), 0)
    enc_first = scatter_about(key_of[3], (D, N_MP, ENC_COLS), 9.0, 56.0, ((0, 16), (1, 2)), jnp.float32)
    enc_second = jnp.clip(jnp.exp(math.log(4000.0) - 1.3862944 * jax.random.uniform(key_of[4], (D, N_MP, ENC_COLS), jnp.float32) ** levels(key_of[4], (D, N_MP, ENC_COLS), ((0, 16), (1, 2)), -0.2, 0.2)), 1000.0, 4000.0)
    dec_weights = draw_dec_weights(jax.random.fold_in(key_of[18], 71), 0)
    dec_first = scatter_about(key_of[6], (DD, N_MP, DEC_COLS), 9.0, 56.0, ((0, 16), (1, 2)), jnp.float32)
    dec_second = jnp.clip(jnp.exp(math.log(4000.0) - 1.3862944 * jax.random.uniform(key_of[7], (DD, N_MP, DEC_COLS), jnp.float32) ** levels(key_of[7], (DD, N_MP, DEC_COLS), ((0, 16), (1, 2)), -0.2, 0.2)), 1000.0, 4000.0)
    enc_norms = draw_enc_norms(jax.random.fold_in(key_of[18], 71), 0)
    enc_norm_first = scatter_about(key_of[9], (4, D), 18.0, 112.0, ((1, 16),), jnp.float32)
    enc_norm_second = jnp.clip(jnp.exp(math.log(32000.0) - 2.7725887 * jax.random.uniform(key_of[10], (4, D), jnp.float32) ** levels(key_of[10], (4, D), ((1, 16),), -0.2, 0.2)), 2000.0, 32000.0)
    dec_norms = draw_dec_norms(jax.random.fold_in(key_of[18], 71), 0)
    dec_norm_first = scatter_about(key_of[12], (4, DD), 18.0, 112.0, ((1, 16),), jnp.float32)
    dec_norm_second = jnp.clip(jnp.exp(math.log(32000.0) - 2.7725887 * jax.random.uniform(key_of[13], (4, DD), jnp.float32) ** levels(key_of[13], (4, DD), ((1, 16),), -0.2, 0.2)), 2000.0, 32000.0)
    mask_token = scatter_about(key_of[14], (DD,), 1.0, 6.0, (), jnp.float32)
    dec_position = scatter_about(key_of[15], (GRID, DD), 1.0, 6.0, (), jnp.float32)
    learning_rate = draw_learning_rate(jax.random.fold_in(key_of[18], 71), 0)
    step_count = jax.random.randint(key_of[17], (1,), 2, 6).astype(jnp.int32)
    return dict(act_in=act_in, packing=packing, enc_weights=enc_weights, enc_first=enc_first, enc_second=enc_second, dec_weights=dec_weights, dec_first=dec_first, dec_second=dec_second, enc_norms=enc_norms, enc_norm_first=enc_norm_first, enc_norm_second=enc_norm_second, dec_norms=dec_norms, dec_norm_first=dec_norm_first, dec_norm_second=dec_norm_second, mask_token=mask_token, dec_position=dec_position, learning_rate=learning_rate, step_count=step_count)


PRECISE = lax.Precision.HIGHEST
NORM_EPS = 1e-06
BETA_FIRST = 0.9
BETA_SECOND = 0.999
ADAM_EPS = 1e-08
WEIGHT_DECAY = 0.05
MASKED = -1e+30

@jax.custom_vjp
def low(v):
    return lax.optimization_barrier(v.astype(jnp.bfloat16)).astype(jnp.float32)

@jax.custom_vjp
def low_back(v):
    return v

def low_keep(v):
    return (low(v), None)

def low_pass(kept, grad):
    return (grad,)

def back_keep(v):
    return (v, None)

def back_low(kept, grad):
    return (low(grad),)
low.defvjp(low_keep, low_pass)
low_back.defvjp(back_keep, back_low)

def product(left_side, right_side):
    return jnp.dot(left_side, right_side, precision=PRECISE)

def normed(tokens, gain_row, shift_row):
    average = lax.optimization_barrier(jnp.mean(tokens, axis=-1, keepdims=True))
    centred = tokens - average
    spread = lax.optimization_barrier(jnp.mean(centred * centred, axis=-1, keepdims=True))
    return centred * lax.rsqrt(spread + NORM_EPS) * gain_row + shift_row

def attention(queries, key_rows, values, allowed):
    groups, length, feature_width = queries.shape
    head_size = feature_width // HEADS
    shaped = [tensor.reshape(groups, length, HEADS, head_size) for tensor in (queries, key_rows, values)]
    scores = jnp.einsum('glhs,gmhs->ghlm', shaped[0], shaped[1], precision=PRECISE) * head_size ** (-0.5)
    scores = jnp.where(allowed[:, None], low_back(scores), MASKED)
    shares = low(jax.nn.softmax(scores, axis=-1))
    mixture = jnp.einsum('ghlm,gmhs->glhs', shares, shaped[2], precision=PRECISE)
    return mixture.reshape(groups, length, feature_width)

def unpack(pack, feature_width, hidden_units):
    part_width = feature_width // N_MP
    part_hidden = hidden_units // N_MP

    def take(begin_at, column_count):
        return pack[:, :, begin_at:begin_at + column_count].reshape(pack.shape[0], N_MP * column_count)
    tail_begin = 4 * part_width + 2 * part_hidden
    return (take(0, part_width), take(part_width, part_width), take(2 * part_width, part_width), take(3 * part_width, part_width), take(4 * part_width, part_hidden), take(4 * part_width + part_hidden, part_hidden), take(tail_begin, pack.shape[2] - tail_begin))

def block(stream, matrices, gain_rows, groups, allowed):
    query_weight, key_weight, value_weight, out_weight, up_weight, down_weight = matrices
    total_rows = stream.shape[0]
    length = total_rows // groups
    first_normed = low(normed(stream, gain_rows[0], gain_rows[1]))
    queries = low_back(low(product(first_normed, query_weight)))
    key_rows = low_back(low(product(first_normed, key_weight)))
    values = low_back(low(product(first_normed, value_weight)))
    mixture = attention(queries.reshape(groups, length, -1), key_rows.reshape(groups, length, -1), values.reshape(groups, length, -1), allowed).reshape(total_rows, -1)
    mixture = low_back(low(mixture))
    after_mix = stream + low_back(product(mixture, out_weight.T))
    second_normed = low(normed(after_mix, gain_rows[2], gain_rows[3]))
    pre_act = low_back(product(second_normed, up_weight))
    hidden = low(jax.nn.gelu(pre_act, approximate=False))
    return after_mix + low_back(product(hidden, down_weight.T))

def update(weight, first_moment, second_moment, gradient, factor, step_rate, fix_first, fix_second, decay_rate):
    clipped = gradient * factor
    new_first = BETA_FIRST * first_moment + (1.0 - BETA_FIRST) * clipped
    new_second = BETA_SECOND * second_moment + (1.0 - BETA_SECOND) * clipped * clipped
    stepped = new_first / fix_first / (jnp.sqrt(new_second / fix_second) + ADAM_EPS)
    return weight - step_rate * (stepped + decay_rate * weight)

def reference(act_in, packing, enc_weights, enc_first, enc_second, dec_weights, dec_first, dec_second, enc_norms, enc_norm_first, enc_norm_second, dec_norms, dec_norm_first, dec_norm_second, mask_token, dec_position, learning_rate, step_count):
    stream_in = act_in[0].astype(jnp.float32).reshape(N_DP, CAP, D)
    cotangent = act_in[1].astype(jnp.float32).reshape(N_DP, IMG * GRID, DD)
    token_row = mask_token.astype(jnp.float32)
    position_rows = jnp.tile(dec_position.astype(jnp.float32), (IMG, 1))
    grid_allowed = jnp.ones((1, 1, 1), dtype=jnp.bool_)

    def forward(enc_pack, dec_pack, enc_gain_rows, dec_gain_rows, stream_all):
        enc_parts = unpack(low(enc_pack), D, FF)
        dec_parts = unpack(low(dec_pack), DD, FFD)
        enc_gains = low(enc_gain_rows)
        dec_gains = low(dec_gain_rows)

        def one_device(carry_value, item_pair):
            stream, packed = item_pair
            slot_ids = packed[0]
            patch_ids = packed[1]
            allowed = (slot_ids[:, None] == slot_ids[None, :])[None]
            encoded = block(stream, enc_parts[:6], enc_gains, 1, allowed)
            projected = low_back(low(product(low(encoded), enc_parts[6])))
            target = jnp.where(slot_ids < IMG, slot_ids * GRID + patch_ids, IMG * GRID).astype(jnp.int32)
            grid_rows = jnp.zeros((IMG * GRID, DD), jnp.float32).at[target].set(projected, mode='drop')
            seen_mask = jnp.zeros((IMG * GRID,), jnp.float32).at[target].set(1.0, mode='drop')
            dec_stream = jnp.where(seen_mask[:, None] > 0, grid_rows, token_row[None, :]) + position_rows
            return (carry_value, block(dec_stream, dec_parts[:6], dec_gains, IMG, grid_allowed))
        return lax.scan(jax.checkpoint(one_device), jnp.zeros((), jnp.float32), (stream_all, packing))[1]
    decoded, pull_back = jax.vjp(forward, enc_weights, dec_weights, enc_norms, dec_norms, stream_in)
    grad_enc, grad_dec, grad_enc_norms, grad_dec_norms, grad_input = pull_back(cotangent)
    square_total = jnp.sum(grad_enc * grad_enc) + jnp.sum(grad_dec * grad_dec) + jnp.sum(grad_enc_norms * grad_enc_norms) + jnp.sum(grad_dec_norms * grad_dec_norms)
    grad_norm = jnp.sqrt(square_total)
    factor = jnp.minimum(1.0, math.sqrt(PARAMS) / (grad_norm + 1e-06))
    step_value = step_count[0].astype(jnp.float32)
    fix_first = 1.0 - jnp.power(BETA_FIRST, step_value)
    fix_second = 1.0 - jnp.power(BETA_SECOND, step_value)
    step_rate = learning_rate[0]
    norm_rate = learning_rate[1]
    enc_new = update(enc_weights, enc_first, enc_second, grad_enc, factor, step_rate, fix_first, fix_second, WEIGHT_DECAY)
    dec_new = update(dec_weights, dec_first, dec_second, grad_dec, factor, step_rate, fix_first, fix_second, WEIGHT_DECAY)
    enc_norm_new = update(enc_norms, enc_norm_first, enc_norm_second, grad_enc_norms, factor, norm_rate, fix_first, fix_second, 0.0)
    dec_norm_new = update(dec_norms, dec_norm_first, dec_norm_second, grad_dec_norms, factor, norm_rate, fix_first, fix_second, 0.0)
    act_out = jnp.stack([grad_input.reshape(N_DP * CAP, D), decoded.reshape(N_DP * CAP, D)])
    return (act_out, enc_new, dec_new, enc_norm_new, dec_norm_new, grad_enc * factor, grad_dec * factor, grad_enc_norms * factor, grad_dec_norms * factor, grad_norm.reshape(1))
```

```python
import functools
import itertools
import math

import jax
import jax.numpy as jnp
from jax import lax
from jax.experimental import pallas as pl
from jax.experimental.pallas import tpu as pltpu
from jax.sharding import PartitionSpec as P

FF = 4096
FFD = 2048
GRID = 196
IMG = 12
PARAMS = 16259072

BETA_FIRST = 0.9
BETA_SECOND = 0.999
ADAM_EPS = 1e-08
WEIGHT_DECAY = 0.05
ROW_BLOCK = 240
GATHER_ORDERS = ("hlxy", "hlyx", "hlxy", "hlyx", "yxhl")
SCATTER_ORDERS = ("xylh", "yxlh", "xylh", "yxlh", "lhxy")

MESH_ID = pl.DeviceIdType.MESH
EVERY = slice(None)
BOTH = -1
DIMS = "xhly"


class Place:
    def __init__(self):
        s, depth, core = lax.axis_index("section"), lax.axis_index("dp"), lax.axis_index("mp")
        y, low, high = depth % 2, (depth // 2) % 2, depth // 4
        self.at = {"x": s, "h": high, "l": low, "y": y}
        self.s, self.core = s, core
        self.device = {
            "x": (1 - s, depth, core),
            "h": (s, depth + 4 - 8 * high, core),
            "l": (s, depth + 2 - 4 * low, core),
            "y": (s, depth + 1 - 2 * y, core),
        }

    def greet(self):
        barrier = pltpu.get_barrier_semaphore()
        for name in DIMS:
            pl.semaphore_signal(
                barrier, inc=1, device_id=self.device[name], device_id_type=MESH_ID
            )
        pl.semaphore_wait(barrier, len(DIMS))


def run(condition, action):
    if condition is None:
        action()
    else:
        pl.when(condition)(action)


def gather_kernel(chunks, n_in, n_out, ahead, *refs):
    ins, outs = refs[:n_in], refs[n_in : n_in + n_out]
    send, recv, local = refs[n_in + n_out :]
    here = Place()
    count = len(chunks)

    def region(chunk, gathered, sender):
        at = [
            EVERY if d in gathered else 1 - here.at[d] if d == sender else here.at[d] for d in DIMS
        ]
        return outs[chunk[1]].at[(*at, EVERY, pl.ds(chunk[3], chunk[4]))]

    def own(i):
        chunk = chunks[i]
        return pltpu.make_async_copy(
            ins[chunk[0]].at[:, pl.ds(chunk[2], chunk[4])], region(chunk, "", None), local.at[i]
        )

    def copy(i, stage, incoming):
        chunk = chunks[i]
        order = chunk[5]
        axis = order[stage]
        block = region(chunk, order[:stage], axis if incoming else None)
        source = block
        if stage == 0 and not incoming:
            source = ins[chunk[0]].at[:, pl.ds(chunk[2], chunk[4])]
        return pltpu.make_async_remote_copy(
            src_ref=source,
            dst_ref=block,
            send_sem=send.at[i, stage],
            recv_sem=recv.at[i, stage],
            device_id=here.device[axis],
            device_id_type=MESH_ID,
        )

    def roles(i, stage):
        order, owner = chunks[i][5], chunks[i][6]
        if owner == BOTH:
            return None, None
        if order[stage] == "x":
            return here.s != owner, here.s == owner
        if "x" in order[:stage]:
            return here.s == owner, here.s == owner
        return None, None

    def begin(i, stage):
        run(roles(i, stage)[0], lambda: copy(i, stage, False).start())

    def arrive(i, stage):
        run(roles(i, stage)[1], lambda: copy(i, stage, True).wait_recv())
        if stage == 0:
            own(i).wait()

    here.greet()
    for i in range(count):
        own(i).start()
    for i in range(min(ahead, count)):
        begin(i, 0)
    for step in range(count + 2):
        for stage in range(3):
            i = step - stage
            if not 0 <= i < count:
                continue
            arrive(i, stage)
            begin(i, stage + 1)
            if stage == 0 and i + ahead < count:
                begin(i + ahead, 0)
    for i in range(count):
        arrive(i, 3)
    for i in range(count):
        for stage in range(4):
            run(
                roles(i, stage)[0],
                lambda i=i, stage=stage: copy(i, stage, False).wait_send(),
            )


def gather_weights(shards, outputs, chunks, collective_id, ahead=4):
    count = len(chunks)
    call = pl.pallas_call(
        functools.partial(gather_kernel, chunks, len(shards), len(outputs), ahead),
        out_shape=[
            jax.ShapeDtypeStruct((2, 2, 2, 2, rows, width), dtype) for rows, width, dtype in outputs
        ],
        in_specs=[pl.BlockSpec(memory_space=pltpu.VMEM)] * len(shards),
        out_specs=[pl.BlockSpec(memory_space=pl.ANY)] * len(outputs),
        scratch_shapes=[
            pltpu.SemaphoreType.DMA((count, 4)),
            pltpu.SemaphoreType.DMA((count, 4)),
            pltpu.SemaphoreType.DMA((count,)),
        ],
        compiler_params=pltpu.CompilerParams(
            collective_id=collective_id, has_side_effects=True, vmem_limit_bytes=40 * 2**20
        ),
    )
    results = call(*shards)
    return [
        r.reshape(16 * rows, width) for r, (rows, width, _) in zip(results, outputs, strict=True)
    ]


def spread(total, pieces, unit=128):
    units = total // unit
    widths = [units // pieces + (1 if k < units % pieces else 0) for k in range(pieces)]
    return [w * unit for w in widths if w]


def chunk_list(widths, pieces, owner, orders):
    chunks = []
    column = turn = 0
    for index, (width, count) in enumerate(zip(widths, pieces, strict=True)):
        begin = 0
        for piece in spread(width, count):
            chunks.append((index, begin, column, piece, orders[turn % len(orders)], owner))
            begin += piece
            column += piece
            turn += 1
    return chunks


def left_after(order, stage):
    return [d for d in DIMS if d not in order[: stage + 1]]


def scatter_buffers(order, owner):
    shapes = [(2,) * 3]
    for stage in range(4):
        if order[stage] == "x" and owner != BOTH:
            continue
        shapes.append((2,) * (3 - stage))
    return shapes


def scatter_kernel(chunks, n_in, n_out, ahead, lag, *refs):
    ins, outs = refs[:n_in], refs[n_in : n_in + n_out]
    rest = refs[n_in + n_out :]
    send, recv, local = rest[:3]
    here = Place()
    s = here.s
    count = len(chunks)
    own, got = [], []
    position = 3
    for chunk in chunks:
        order, owner = chunk[5], chunk[6]
        own.append(rest[position])
        position += 1
        mine = []
        for stage in range(4):
            if order[stage] == "x" and owner != BOTH:
                mine.append(None)
                continue
            mine.append(rest[position])
            position += 1
        got.append(mine)

    def source(i, axis, keep):
        chunk = chunks[i]
        at = [
            (here.at[d] if keep else 1 - here.at[d]) if d == axis else EVERY for d in DIMS
        ]
        return ins[chunk[0]].at[(*at, EVERY, pl.ds(chunk[2], chunk[4]))]

    def load(i):
        return pltpu.make_async_copy(source(i, chunks[i][5][0], True), own[i], local.at[i])

    def spot(i, stage, flip):
        order = chunks[i][5]
        at = []
        for d in DIMS:
            if d == order[0]:
                continue
            if d in order[:stage]:
                at.append(here.at[d])
            elif d == order[stage]:
                at.append(1 - here.at[d] if flip else here.at[d])
            else:
                at.append(EVERY)
        return tuple(at)

    def copy(i, stage, incoming):
        order = chunks[i][5]
        axis = order[stage]
        moved = got[i][stage] is None
        src = source(i, axis, False) if stage == 0 else own[i].at[spot(i, stage, True)]
        if not moved:
            there = mine = got[i][stage]
        elif stage == 0:
            there = mine = own[i]
        else:
            there, mine = own[i].at[spot(i, stage, True)], own[i].at[spot(i, stage, False)]
        return pltpu.make_async_remote_copy(
            src_ref=mine if incoming else src,
            dst_ref=mine if incoming else there,
            send_sem=send.at[i, stage],
            recv_sem=recv.at[i, stage],
            device_id=here.device[axis],
            device_id_type=MESH_ID,
        )

    def roles(i, stage):
        order, owner = chunks[i][5], chunks[i][6]
        if owner == BOTH:
            return None, None
        if order[stage] == "x":
            return s == owner, s != owner
        if "x" in order[:stage]:
            return None, None
        return s == owner, s == owner

    def begin(i, stage):
        run(roles(i, stage)[0], lambda: copy(i, stage, False).start())

    def arrive(i, stage):
        chunk, a, r = chunks[i], own[i], got[i][stage]
        order, owner = chunk[5], chunk[6]
        run(roles(i, stage)[1], lambda: copy(i, stage, True).wait_recv())
        if stage == 0:
            run(None if owner == BOTH else s == owner, lambda: load(i).wait())
        out = outs[chunk[1]].at[:, pl.ds(chunk[3], chunk[4])]
        place = spot(i, stage, False)
        if stage == 3:
            result = a[place].astype(jnp.float32)
            if r is not None:
                result = result + r[...].astype(jnp.float32)
            out[...] = result
            return
        if r is None:
            return

        def add():
            free = [k for k, p in enumerate(place) if p is EVERY]
            for combo in itertools.product(range(2), repeat=len(free)):
                at = list(place)
                for k, c in zip(free, combo):
                    at[k] = c
                at = tuple(at)
                a[at] = (a[at].astype(jnp.float32) + r[combo].astype(jnp.float32)).astype(a.dtype)

        run(roles(i, stage)[1], add)

    here.greet()
    for i in range(count):
        run(
            None if chunks[i][6] == BOTH else s == chunks[i][6],
            lambda i=i: load(i).start(),
        )
    for i in range(min(ahead, count)):
        begin(i, 0)
    for step in range(count + 3 * lag):
        for stage in range(3, -1, -1):
            i = step - stage * lag
            if not 0 <= i < count:
                continue
            arrive(i, stage)
            if stage < 3:
                begin(i, stage + 1)
            if stage == 0 and i + ahead < count:
                begin(i + ahead, 0)
    for i in range(count):
        for stage in range(4):
            run(
                roles(i, stage)[0],
                lambda i=i, stage=stage: copy(i, stage, False).wait_send(),
            )


def scatter_grads(parts, outputs, chunks, collective_id, ahead=4, lag=1):
    count = len(chunks)
    views = [p.reshape(2, 2, 2, 2, p.shape[0] // 16, p.shape[1]) for p in parts]
    buffers = []
    for chunk in chunks:
        view = views[chunk[0]]
        for lead in scatter_buffers(chunk[5], chunk[6]):
            buffers.append(pltpu.VMEM((*lead, view.shape[4], chunk[4]), view.dtype))
    call = pl.pallas_call(
        functools.partial(scatter_kernel, chunks, len(parts), len(outputs), ahead, lag),
        out_shape=[jax.ShapeDtypeStruct((rows, width), jnp.float32) for rows, width in outputs],
        in_specs=[pl.BlockSpec(memory_space=pl.ANY)] * len(parts),
        out_specs=[pl.BlockSpec(memory_space=pltpu.VMEM)] * len(outputs),
        scratch_shapes=[
            pltpu.SemaphoreType.DMA((count, 4)),
            pltpu.SemaphoreType.DMA((count, 4)),
            pltpu.SemaphoreType.DMA((count,)),
            *buffers,
        ],
        compiler_params=pltpu.CompilerParams(
            collective_id=collective_id, has_side_effects=True, vmem_limit_bytes=56 * 2**20
        ),
    )
    return call(*views)


HEADS = 16
NORM_EPS = 1e-06
MASKED = -1e30
LOW = jnp.bfloat16
WIDE = jnp.float32


def mm(left, right, left_dim=1, right_dim=0):
    return lax.dot_general(
        left, right, (((left_dim,), (right_dim,)), ((), ())), preferred_element_type=WIDE
    )


def centre(tokens):
    average = jnp.mean(tokens, axis=-1, keepdims=True)
    centred = tokens - average
    spread_ = jnp.mean(centred * centred, axis=-1, keepdims=True)
    scale = lax.rsqrt(spread_ + NORM_EPS)
    return centred * scale, scale


def centre_back(unit, scale, gain, grad):
    pulled = grad * gain
    first = jnp.mean(pulled, axis=-1, keepdims=True)
    second = jnp.mean(pulled * unit, axis=-1, keepdims=True)
    return scale * (pulled - first - unit * second)


def gelu_pair(z):
    cdf = 0.5 * (1.0 + lax.erf(z * math.sqrt(0.5)))
    return z * cdf, cdf + z * (jnp.exp(-0.5 * z * z) * (1.0 / math.sqrt(2.0 * math.pi)))


def decoder_kernel(
    grid_cells,
    length,
    target_row,
    target_column,
    visible,
    mask,
    position,
    gains,
    qkv_t,
    qkv_w,
    out_t,
    out_w,
    up_w,
    down_w,
    cotangent,
    decoded,
    grad_visible,
    grad_qkv,
    grad_out,
    grad_up,
    grad_down,
    grad_gains,
    qkv_rows,
    shares,
    mixture,
    hidden,
    slope,
    grad_rows,
):
    image = pl.program_id(0)
    rows, width = decoded.shape[1], decoded.shape[2]
    head = width // HEADS
    units = hidden.shape[1]
    scaling = head ** (-0.5)

    @pl.when(image == 0)
    def _():
        for ref in (grad_visible, grad_qkv, grad_out, grad_up, grad_down, grad_gains):
            ref[...] = jnp.zeros_like(ref)

    packed = target_row.shape[1]
    cell = lax.broadcasted_iota(jnp.int32, (rows, packed), 0)
    wanted = jnp.where(cell < length, cell + image * length, -7)
    chosen = (target_row[...] == wanted).astype(WIDE)
    seen = jnp.max(chosen, axis=1, keepdims=True)
    placed = mm(chosen.astype(LOW), visible[...])
    stream = jnp.where(seen > 0.0, placed, mask[...]) + position[...]

    unit_one, scale_one = centre(stream)
    first = (unit_one * gains[0:1] + gains[1:2]).astype(LOW)
    qkv_rows[...] = mm(qkv_t[...], first, 1, 1).astype(LOW)

    key_index = lax.broadcasted_iota(jnp.int32, (rows, rows), 0)

    def attend(h, carry):
        begin = pl.multiple_of(h * head, head)
        q = qkv_rows[pl.ds(begin, head), :]
        k = qkv_rows[pl.ds(pl.multiple_of(width + begin, head), head), :]
        v = qkv_rows[pl.ds(pl.multiple_of(2 * width + begin, head), head), :]
        scores = mm(k, q, 0, 0) * scaling
        scores = jnp.where(key_index < length, scores, MASKED)
        weights = jnp.exp(scores - jnp.max(scores, axis=0, keepdims=True))
        share = weights * (1.0 / jnp.sum(weights, axis=0, keepdims=True))
        shares[h] = share
        mixture[pl.ds(begin, head), :] = mm(v, share.astype(LOW)).astype(LOW)
        return carry

    lax.fori_loop(0, HEADS, attend, 0, unroll=4)
    mixed = mixture[...]
    after = stream + mm(jnp.transpose(mixed), out_w[...], 1, 1)
    unit_two, scale_two = centre(after)
    second = (unit_two * gains[2:3] + gains[3:4]).astype(LOW)
    piece = 256
    result = after
    for c in range(0, units, piece):
        z = mm(second, up_w[:, c : c + piece])
        h, g = gelu_pair(z)
        hidden[:, c : c + piece] = h.astype(LOW)
        slope[:, c : c + piece] = g
    decoded[0] = after + mm(hidden[...], down_w[...], 1, 1)

    grad_low = cotangent[0]
    grad_result = grad_low.astype(WIDE)
    turned = jnp.transpose(grad_low)
    second_turned = jnp.transpose(second)
    for c in range(0, units, piece):
        cut = slice(c, c + piece)
        grad_down[:, cut] += mm(turned, hidden[:, cut])
        grad_z = (mm(grad_low, down_w[:, cut]) * slope[:, cut]).astype(LOW)
        hidden[:, cut] = grad_z
        grad_up[:, cut] += mm(second_turned, grad_z)
    grad_second = mm(hidden[...], up_w[...], 1, 1)
    grad_after = grad_result + centre_back(unit_two, scale_two, gains[2:3], grad_second)
    grad_gains[2:3] += jnp.sum(grad_second * unit_two, axis=0, keepdims=True)
    grad_gains[3:4] += jnp.sum(grad_second, axis=0, keepdims=True)

    after_low = grad_after.astype(LOW)
    grad_out[...] += mm(mixed, after_low)
    grad_rows[...] = mm(out_t[...], after_low, 1, 1).astype(LOW)

    def attend_back(h, carry):
        begin = pl.multiple_of(h * head, head)
        key_at = pl.multiple_of(width + begin, head)
        value_at = pl.multiple_of(2 * width + begin, head)
        q = qkv_rows[pl.ds(begin, head), :]
        k = qkv_rows[pl.ds(key_at, head), :]
        v = qkv_rows[pl.ds(value_at, head), :]
        grad_mixture = grad_rows[pl.ds(begin, head), :]
        share = shares[h]
        grad_share = mm(v, grad_mixture, 0, 0)
        grad_value = mm(grad_mixture, share.astype(LOW), 1, 1)
        inner = jnp.sum(share * grad_share, axis=0, keepdims=True)
        grad_score = (share * (grad_share - inner)).astype(LOW)
        grad_query = mm(k, grad_score) * scaling
        grad_key = mm(q, grad_score, 1, 1) * scaling
        qkv_rows[pl.ds(begin, head), :] = grad_query.astype(LOW)
        qkv_rows[pl.ds(key_at, head), :] = grad_key.astype(LOW)
        qkv_rows[pl.ds(value_at, head), :] = grad_value.astype(LOW)
        return carry

    lax.fori_loop(0, HEADS, attend_back, 0, unroll=4)
    grads = qkv_rows[...]
    grad_qkv[...] += mm(grads, first)
    grad_first = jnp.transpose(mm(qkv_w[...], grads))
    grad_stream = grad_after + centre_back(unit_one, scale_one, gains[0:1], grad_first)
    grad_gains[0:1] += jnp.sum(grad_first * unit_one, axis=0, keepdims=True)
    grad_gains[1:2] += jnp.sum(grad_first, axis=0, keepdims=True)

    cell_lane = lax.broadcasted_iota(jnp.int32, (packed, rows), 1)
    wanted_lane = jnp.where(cell_lane < length, cell_lane + image * length, -7)
    chosen_back = (target_column[...] == wanted_lane).astype(WIDE).astype(LOW)
    grad_visible[...] += mm(chosen_back, grad_stream.astype(LOW))


def decoder_step(
    visible, target, mask, position, gains, qkv_w, out_w, up_w, down_w, cotangent, images
):
    length, width = position.shape
    rows = -(-length // 16) * 16
    packed = -(-visible.shape[0] // 128) * 128
    spare = packed - visible.shape[0]
    units = up_w.shape[1]
    visible = jnp.pad(visible, ((0, spare), (0, 0)))
    target = jnp.pad(target, (0, spare), constant_values=-1)
    longer = ((0, 0), (0, rows - length), (0, 0))
    cotangent = jnp.pad(cotangent.reshape(images, length, width), longer)
    position = jnp.pad(position, ((0, rows - length), (0, 0)))

    def fixed(shape):
        return pl.BlockSpec(shape, lambda i: (0,) * len(shape), pipeline_mode=pl.Buffered(1))

    per_image = pl.BlockSpec((1, rows, width), lambda i: (i, 0, 0))
    grads = [
        ((packed, width), WIDE),
        ((3 * width, width), WIDE),
        ((width, width), WIDE),
        ((width, units), WIDE),
        ((width, units), WIDE),
        ((8, width), WIDE),
    ]
    results = pl.pallas_call(
        functools.partial(decoder_kernel, images * length, length),
        grid=(images,),
        out_shape=[jax.ShapeDtypeStruct((images, rows, width), WIDE)]
        + [jax.ShapeDtypeStruct(s, d) for s, d in grads],
        in_specs=[
            fixed((1, packed)),
            fixed((packed, 1)),
            fixed((packed, width)),
            fixed((1, width)),
            fixed((rows, width)),
            fixed((4, width)),
            fixed((3 * width, width)),
            fixed((width, 3 * width)),
            fixed((width, width)),
            fixed((width, width)),
            fixed((width, units)),
            fixed((width, units)),
            per_image,
        ],
        out_specs=[per_image] + [fixed(s) for s, _ in grads],
        scratch_shapes=[
            pltpu.VMEM((3 * width, rows), LOW),
            pltpu.VMEM((HEADS, rows, rows), WIDE),
            pltpu.VMEM((width, rows), LOW),
            pltpu.VMEM((rows, units), LOW),
            pltpu.VMEM((rows, units), WIDE),
            pltpu.VMEM((width, rows), LOW),
        ],
        compiler_params=pltpu.CompilerParams(
            dimension_semantics=("arbitrary",), vmem_limit_bytes=60 * 2**20
        ),
    )(
        target[None, :],
        target[:, None],
        visible,
        mask[None, :],
        position,
        gains,
        qkv_w.T,
        qkv_w,
        out_w.T,
        out_w,
        up_w,
        down_w,
        cotangent,
    )
    decoded, grad_visible, grad_qkv, grad_out, grad_up, grad_down, grad_gains = results
    return (
        decoded[:, :length].reshape(images * length, width),
        grad_visible[: packed - spare],
        grad_qkv,
        grad_out,
        grad_up,
        grad_down,
        grad_gains[:4],
    )


TILE = 256
GROUP = 4


def fixed(shape):
    return pl.BlockSpec(shape, lambda i: (0,) * len(shape), pipeline_mode=pl.Buffered(1))


def down_rows(rows, width):
    return pl.BlockSpec((rows, width), lambda i: (i, 0))


def params(megabytes=60):
    return pltpu.CompilerParams(
        dimension_semantics=("arbitrary",), vmem_limit_bytes=megabytes * 2**20
    )


def attend_kernel(
    head, bounds, stream, slots_row, slots_column, gains, qkv_w, out_w, first, turned, mixture, log_sum, partial
):
    rows, width = stream.shape
    part, lanes = mixture.shape
    tiles = lanes // TILE
    scaling = head ** (-0.5)
    unit, _ = centre(stream[...].astype(WIDE))
    first[...] = (unit * gains[0:1] + gains[1:2]).astype(LOW)
    turned[:, rows:] = jnp.zeros((3 * part, lanes - rows), LOW)
    for c in range(0, 3 * part, TILE):
        weight = jnp.transpose(qkv_w[:, c : c + TILE])
        turned[c : c + TILE, :rows] = mm(weight, first[...], 1, 1).astype(LOW)

    def at(which, h, tile):
        return (
            pl.ds(pl.multiple_of(which * part + h * head, head), head),
            pl.ds(pl.multiple_of(tile * TILE, TILE), TILE),
        )

    def step(n, carry):
        group, i = n // tiles, n % tiles
        heads = [group * GROUP + g for g in range(GROUP)]
        lane_i = pl.ds(pl.multiple_of(i * TILE, TILE), TILE)
        queries = [turned[at(0, h, i)] for h in heads]
        slot_i = slots_row[:, lane_i]

        def inner(j, state):
            same = slots_column[pl.ds(pl.multiple_of(j * TILE, TILE), TILE), :] == slot_i
            result = []
            for g, h in enumerate(heads):
                high, total, mixed = state[g]
                scores = mm(turned[at(1, h, j)], queries[g], 0, 0) * scaling
                scores = jnp.where(same, scores, MASKED)
                higher = jnp.maximum(high, jnp.max(scores, axis=0, keepdims=True))
                weights = jnp.exp(scores - higher)
                fix = jnp.exp(high - higher)
                total = total * fix + jnp.sum(weights, axis=0, keepdims=True)
                mixed = mixed * fix + mm(turned[at(2, h, j)], weights.astype(LOW))
                result.append((higher, total, mixed))
            return tuple(result)

        begin = (
            jnp.full((1, TILE), MASKED, WIDE),
            jnp.zeros((1, TILE), WIDE),
            jnp.zeros((head, TILE), WIDE),
        )
        state = lax.fori_loop(bounds[i, 0], bounds[i, 1], inner, (begin,) * GROUP)
        for g, h in enumerate(heads):
            high, total, mixed = state[g]
            mixture[at(0, h, i)] = (mixed / total).astype(LOW)
            log_sum[pl.ds(h, 1), lane_i] = high + jnp.log(total)
        return carry

    lax.fori_loop(0, part // head // GROUP * tiles, step, 0)
    mixed = jnp.transpose(mixture[...])[:rows]
    for c in range(0, width, TILE):
        partial[:, c : c + TILE] = mm(mixed, out_w[c : c + TILE, :], 1, 1).astype(LOW)


def encoder_attend(stream, slots, bounds, gains, qkv_w, out_w, head):
    rows, width = stream.shape
    lanes = slots.shape[0]
    part = out_w.shape[1]
    return pl.pallas_call(
        functools.partial(attend_kernel, head),
        in_specs=[pl.BlockSpec(memory_space=pltpu.SMEM)]
        + [pl.BlockSpec(memory_space=pltpu.VMEM)] * 6,
        out_specs=[pl.BlockSpec(memory_space=pltpu.VMEM)] * 5,
        out_shape=[
            jax.ShapeDtypeStruct((rows, width), LOW),
            jax.ShapeDtypeStruct((3 * part, lanes), LOW),
            jax.ShapeDtypeStruct((part, lanes), LOW),
            jax.ShapeDtypeStruct((part // head, lanes), WIDE),
            jax.ShapeDtypeStruct((rows, width), LOW),
        ],
        compiler_params=pltpu.CompilerParams(vmem_limit_bytes=60 * 2**20),
    )(bounds, stream, slots[None, :], slots[:, None], gains, qkv_w, out_w)


def attend_back_kernel(
    head,
    bounds,
    slots_row,
    slots_column,
    first,
    turned,
    mixture,
    log_sum,
    grad_low,
    qkv_w,
    out_w,
    grad_qkv_w,
    grad_out_w,
    partial,
    grad_mixture,
    grad_turned,
    inner_sum,
    key_sum,
    value_sum,
):
    rows, width = grad_low.shape
    part, lanes = mixture.shape
    tiles = lanes // TILE
    scaling = head ** (-0.5)
    grad_mixture[:, rows:] = jnp.zeros((part, lanes - rows), LOW)
    for c in range(0, width, TILE):
        grad_out_w[c : c + TILE, :] = jnp.transpose(
            mm(mixture[:, :rows], grad_low[:, c : c + TILE]).astype(LOW)
        )
    for c in range(0, part, TILE):
        weight = jnp.transpose(out_w[:, c : c + TILE])
        grad_mixture[c : c + TILE, :rows] = mm(weight, grad_low[...], 1, 1).astype(LOW)
    for h in range(part // head):
        cut = slice(h * head, (h + 1) * head)
        inner_sum[h : h + 1, :] = jnp.sum(
            grad_mixture[cut, :].astype(WIDE) * mixture[cut, :].astype(WIDE), axis=0, keepdims=True
        )

    def at(which, h, tile):
        return (
            pl.ds(pl.multiple_of(which * part + h * head, head), head),
            pl.ds(pl.multiple_of(tile * TILE, TILE), TILE),
        )

    def over_group(group, carry):
        heads = [group * GROUP + g for g in range(GROUP)]
        key_sum[...] = jnp.zeros_like(key_sum)
        value_sum[...] = jnp.zeros_like(value_sum)

        def over_queries(i, carry):
            lane_i = pl.ds(pl.multiple_of(i * TILE, TILE), TILE)
            slot_i = slots_row[:, lane_i]
            queries = [turned[at(0, h, i)] for h in heads]
            grads = [grad_mixture[at(0, h, i)] for h in heads]
            logs = [log_sum[pl.ds(h, 1), lane_i] for h in heads]
            sums = [inner_sum[pl.ds(h, 1), lane_i] for h in heads]

            def inner(j, state):
                lane_j = pl.ds(pl.multiple_of(j * TILE, TILE), TILE)
                same = slots_column[lane_j, :] == slot_i
                result = []
                for g, h in enumerate(heads):
                    cut = slice(g * head, (g + 1) * head)
                    keys, values = turned[at(1, h, j)], turned[at(2, h, j)]
                    scores = jnp.where(same, mm(keys, queries[g], 0, 0) * scaling, MASKED)
                    share = jnp.exp(scores - logs[g])
                    grad_share = mm(values, grads[g], 0, 0)
                    grad_score = (share * (grad_share - sums[g])).astype(LOW)
                    value_sum[cut, lane_j] += mm(grads[g], share.astype(LOW), 1, 1)
                    key_sum[cut, lane_j] += mm(queries[g], grad_score, 1, 1)
                    result.append(state[g] + mm(keys, grad_score))
                return tuple(result)

            begin = (jnp.zeros((head, TILE), WIDE),) * GROUP
            state = lax.fori_loop(bounds[i, 0], bounds[i, 1], inner, begin)
            for g, h in enumerate(heads):
                grad_turned[at(0, h, i)] = (state[g] * scaling).astype(LOW)
            return carry

        lax.fori_loop(0, tiles, over_queries, 0)
        size = GROUP * head
        key_at = pl.ds(pl.multiple_of(part + group * size, size), size)
        value_at = pl.ds(pl.multiple_of(2 * part + group * size, size), size)
        grad_turned[key_at, :] = (key_sum[...] * scaling).astype(LOW)
        grad_turned[value_at, :] = value_sum[...].astype(LOW)
        return carry

    lax.fori_loop(0, part // head // GROUP, over_group, 0)
    for c in range(0, 3 * part, TILE):
        grad_qkv_w[:, c : c + TILE] = jnp.transpose(
            mm(grad_turned[c : c + TILE, :rows], first[...]).astype(LOW)
        )
    for c in range(0, width, TILE):
        partial[:, c : c + TILE] = jnp.transpose(
            mm(qkv_w[c : c + TILE, :], grad_turned[:, :rows]).astype(LOW)
        )


def encoder_attend_back(
    slots, bounds, first, turned, mixture, log_sum, grad_low, qkv_w, out_w, head
):
    rows, width = first.shape
    part, lanes = mixture.shape
    return pl.pallas_call(
        functools.partial(attend_back_kernel, head),
        in_specs=[pl.BlockSpec(memory_space=pltpu.SMEM)]
        + [pl.BlockSpec(memory_space=pltpu.VMEM)] * 9,
        out_specs=[pl.BlockSpec(memory_space=pltpu.VMEM)] * 3,
        out_shape=[
            jax.ShapeDtypeStruct((width, 3 * part), LOW),
            jax.ShapeDtypeStruct((width, part), LOW),
            jax.ShapeDtypeStruct((rows, width), LOW),
        ],
        scratch_shapes=[
            pltpu.VMEM((part, lanes), LOW),
            pltpu.VMEM((3 * part, lanes), LOW),
            pltpu.VMEM((part // head, lanes), WIDE),
            pltpu.VMEM((GROUP * head, lanes), WIDE),
            pltpu.VMEM((GROUP * head, lanes), WIDE),
        ],
        compiler_params=pltpu.CompilerParams(vmem_limit_bytes=60 * 2**20),
    )(
        bounds,
        slots[None, :],
        slots[:, None],
        first,
        turned,
        mixture,
        log_sum,
        grad_low,
        qkv_w,
        out_w,
    )


def feed_kernel(stream, own, other, gains, up_w, down_w, after, second, hidden, slope, partial):
    summed = stream[...].astype(WIDE) + (own[...].astype(WIDE) + other[...].astype(WIDE))
    after[...] = summed
    unit, _ = centre(summed)
    second[...] = (unit * gains[2:3] + gains[3:4]).astype(LOW)
    units = up_w.shape[1]
    for c in range(0, units, TILE):
        cut = slice(c, c + TILE)
        h, g = gelu_pair(mm(second[...], up_w[:, cut]))
        hidden[:, cut] = h.astype(LOW)
        slope[:, cut] = g.astype(LOW)
    partial[...] = mm(hidden[...], down_w[...], 1, 1).astype(LOW)


def encoder_feed(stream, own, other, gains, up_w, down_w, block):
    rows, width = stream.shape
    units = up_w.shape[1]
    wide, tall = down_rows(block, width), down_rows(block, units)
    return pl.pallas_call(
        feed_kernel,
        grid=(rows // block,),
        in_specs=[wide, wide, wide, fixed((4, width)), fixed(up_w.shape), fixed(down_w.shape)],
        out_specs=[wide, wide, tall, tall, wide],
        out_shape=[
            jax.ShapeDtypeStruct((rows, width), WIDE),
            jax.ShapeDtypeStruct((rows, width), LOW),
            jax.ShapeDtypeStruct((rows, units), LOW),
            jax.ShapeDtypeStruct((rows, units), LOW),
            jax.ShapeDtypeStruct((rows, width), LOW),
        ],
        compiler_params=params(),
    )(stream, own, other, gains, up_w, down_w)


def feed_back_kernel(
    own,
    other,
    second,
    hidden,
    slope,
    up_w,
    down_w,
    grad_up,
    grad_down,
    partial,
    grad_low,
    grad_turned,
    second_turned,
    total,
):
    @pl.when(pl.program_id(0) == 0)
    def _():
        grad_low[...] = (own[...].astype(WIDE) + other[...].astype(WIDE)).astype(LOW)
        grad_turned[...] = jnp.transpose(grad_low[...])
        second_turned[...] = jnp.transpose(second[...])
        total[...] = jnp.zeros_like(total)

    grad_down[...] = mm(grad_turned[...], hidden[...]).astype(LOW)
    grad_z = (mm(grad_low[...], down_w[...]) * slope[...].astype(WIDE)).astype(LOW)
    grad_up[...] = mm(second_turned[...], grad_z).astype(LOW)
    total[...] += mm(grad_z, up_w[...], 1, 1)

    @pl.when(pl.program_id(0) == pl.num_programs(0) - 1)
    def _():
        partial[...] = total[...].astype(LOW)


def encoder_feed_back(own, other, second, hidden, slope, up_w, down_w):
    rows, width = own.shape
    units = up_w.shape[1]
    piece = 256
    whole = fixed((rows, width))
    tall = pl.BlockSpec((rows, piece), lambda i: (0, i))
    weight = pl.BlockSpec((width, piece), lambda i: (0, i))
    return pl.pallas_call(
        feed_back_kernel,
        grid=(units // piece,),
        in_specs=[whole, whole, whole, tall, tall, weight, weight],
        out_specs=[weight, weight, whole],
        out_shape=[
            jax.ShapeDtypeStruct((width, units), LOW),
            jax.ShapeDtypeStruct((width, units), LOW),
            jax.ShapeDtypeStruct((rows, width), LOW),
        ],
        scratch_shapes=[
            pltpu.VMEM((rows, width), LOW),
            pltpu.VMEM((width, rows), LOW),
            pltpu.VMEM((width, rows), LOW),
            pltpu.VMEM((rows, width), WIDE),
        ],
        compiler_params=params(),
    )(own, other, second, hidden, slope, up_w, down_w)


def norm_back_kernel(tokens, own, other, skip_own, skip_other, gains, grad, grad_low, grad_gains, *, at):
    @pl.when(pl.program_id(0) == 0)
    def _():
        grad_gains[...] = jnp.zeros_like(grad_gains)

    pulled = own[...].astype(WIDE) + other[...].astype(WIDE)
    unit, scale = centre(tokens[...].astype(WIDE))
    result = skip_own[...].astype(WIDE)
    if skip_other is not None:
        result = result + skip_other[...].astype(WIDE)
    result = result + centre_back(unit, scale, gains[at : at + 1], pulled)
    grad[...] = result
    if grad_low is not None:
        grad_low[...] = result.astype(LOW)
    grad_gains[0:1] += jnp.sum(pulled * unit, axis=0, keepdims=True)
    grad_gains[1:2] += jnp.sum(pulled, axis=0, keepdims=True)


def encoder_norm_back(tokens, own, other, skip, gains, at, block, low):
    rows, width = tokens.shape
    wide = down_rows(block, width)
    two = len(skip) == 2

    def kernel(*refs):
        refs = list(refs)
        if not two:
            refs.insert(4, None)
        if not low:
            refs.insert(7, None)
        norm_back_kernel(*refs, at=at)

    shapes = [jax.ShapeDtypeStruct((rows, width), WIDE)]
    if low:
        shapes.append(jax.ShapeDtypeStruct((rows, width), LOW))
    shapes.append(jax.ShapeDtypeStruct((8, width), WIDE))
    return pl.pallas_call(
        kernel,
        grid=(rows // block,),
        in_specs=[wide, wide, wide] + [wide] * len(skip) + [fixed((4, width))],
        out_specs=[wide] * (2 if low else 1) + [fixed((8, width))],
        out_shape=shapes,
        compiler_params=params(),
    )(tokens, own, other, *skip, gains)


def from_behind(value, axis, by):
    length = lax.axis_size(axis)
    pairs = [(i, i + by) for i in range(length) if 0 <= i + by < length]
    return lax.ppermute(value, axis, pairs)


def partner(value):
    length = lax.axis_size("mp")
    return lax.ppermute(value, "mp", [(i, (i + 1) % length) for i in range(length)])


def on_side(active, action, *operands):
    def skipped(*values):
        return jax.tree.map(
            lambda leaf: jnp.zeros(leaf.shape, leaf.dtype), jax.eval_shape(action, *values)
        )

    return lax.cond(active, action, skipped, *operands)


def is_fast():
    return lax.axis_size("section") == 2 and lax.axis_size("dp") == 8


def plan(widths, pieces, dec_width, dec_pieces, orders):
    enc = chunk_list(widths, pieces, 0, orders)
    dec = [
        (len(widths), b, c, w, o, k)
        for _, b, c, w, o, k in chunk_list((dec_width,), (dec_pieces,), 1, orders)
    ]
    return enc[:8] + dec + enc[8:]


def gather_all(low_enc, low_dec, norms, widths):
    count = len(widths)
    if not is_fast():
        both = ("section", "dp")
        enc = lax.all_gather(low_enc, both, axis=0, tiled=True)
        dec = lax.all_gather(low_dec, both, axis=0, tiled=True)
        rows = lax.all_gather(norms, both, axis=0, tiled=True)
        parts, column = [], 0
        for w in widths:
            parts.append(enc[:, column : column + w])
            column += w
        return parts, dec, rows
    chunks = plan(widths, (4, 1, 4, 4, 2), low_dec.shape[1], 4, GATHER_ORDERS)
    outputs = [(low_enc.shape[0], w, LOW) for w in widths]
    outputs += [(low_dec.shape[0], low_dec.shape[1], LOW), (8, 128, WIDE)]
    described = [(k // count, k, c, b, w, o, own) for k, b, c, w, o, own in chunks]
    described.append((2, count + 1, 0, 0, 128, "hlyx", BOTH))
    results = gather_weights([low_enc, low_dec, norms], outputs, described, 1, 8)
    return results[:count], results[count], results[count + 1]


def scatter_all(enc_parts, dec, norms, encoder_side):
    widths = [p.shape[1] for p in enc_parts]
    count = len(widths)
    if not is_fast():
        both = ("section", "dp")
        enc = jnp.concatenate(enc_parts, axis=1).astype(WIDE)
        enc = jnp.where(encoder_side, enc, 0.0)
        dec = jnp.where(encoder_side, 0.0, dec.astype(WIDE))
        return [
            lax.psum_scatter(v, both, scatter_dimension=0, tiled=True) for v in (enc, dec, norms)
        ]
    chunks = plan(widths, (4, 1, 4, 4, 2), dec.shape[1], 4, SCATTER_ORDERS)
    described = [(k, k // count, b, c, w, o, own) for k, b, c, w, o, own in chunks]
    described.append((count + 1, 2, 0, 0, 128, "xylh", BOTH))
    rows = enc_parts[0].shape[0] // 16
    outputs = [(rows, sum(widths)), (dec.shape[0] // 16, dec.shape[1]), (8, 128)]
    return scatter_grads([*enc_parts, dec, norms], outputs, described, 2, 8, 2)


def pack_norms(enc_rows, dec_rows, blocks):
    both = [rows.reshape(4, blocks, -1).transpose(1, 0, 2) for rows in (enc_rows, dec_rows)]
    joined = jnp.concatenate(both, axis=2)
    joined = jnp.pad(joined, ((0, 0), (0, 4), (0, 128 - joined.shape[2])))
    return joined.reshape(blocks * 8, 128)


def unpack_norms(packed, blocks, enc_width, dec_width):
    split = packed.reshape(blocks, 8, 128)[:, :4].transpose(1, 0, 2)
    return (
        split[:, :, :enc_width].reshape(4, -1),
        split[:, :, enc_width : enc_width + dec_width].reshape(4, -1),
    )


def key_ranges(slots):
    tiles = slots.reshape(-1, TILE)
    low, high = jnp.min(tiles, axis=1), jnp.max(tiles, axis=1)
    meet = jnp.logical_and(low[:, None] <= high[None, :], high[:, None] >= low[None, :])
    index = jnp.arange(tiles.shape[0], dtype=jnp.int32)[None, :]
    first = jnp.min(jnp.where(meet, index, tiles.shape[0]), axis=1)
    last = jnp.max(jnp.where(meet, index + 1, 0), axis=1)
    return jnp.stack([first, last], axis=1)


def cut_columns(matrix, widths):
    parts, column = [], 0
    for w in widths:
        parts.append(matrix[:, column : column + w])
        column += w
    return parts


def update(
    weight,
    first_moment,
    second_moment,
    gradient,
    factor,
    step_rate,
    fix_first,
    fix_second,
    decay_rate,
):
    clipped = gradient * factor
    new_first = BETA_FIRST * first_moment + (1.0 - BETA_FIRST) * clipped
    new_second = BETA_SECOND * second_moment + (1.0 - BETA_SECOND) * clipped * clipped
    stepped = new_first / fix_first / (jnp.sqrt(new_second / fix_second) + ADAM_EPS)
    return weight - step_rate * (stepped + decay_rate * weight)


def per_device(
    act_in,
    packing,
    enc_weights,
    enc_first,
    enc_second,
    dec_weights,
    dec_first,
    dec_second,
    enc_norms,
    enc_norm_first,
    enc_norm_second,
    dec_norms,
    dec_norm_first,
    dec_norm_second,
    mask_token,
    dec_position,
    learning_rate,
    step_count,
):
    encoder_side = lax.axis_index("section") == 0
    decoder_side = jnp.logical_not(encoder_side)
    mp_rank = lax.axis_index("mp")
    mp_count = lax.axis_size("mp")
    first_half = mp_rank == 0
    slot_ids = packing[0, 0]
    patch_ids = packing[0, 1]
    local_images = IMG // mp_count
    grid_cells = local_images * GRID
    local_slot = slot_ids - mp_rank * local_images
    inside = jnp.logical_and(local_slot >= 0, local_slot < local_images)
    target = jnp.where(inside, local_slot * GRID + patch_ids, grid_cells)

    local_rows, width = act_in.shape[1], act_in.shape[2]
    real_rows = local_rows * mp_count
    rows = -(-real_rows // ROW_BLOCK) * ROW_BLOCK
    lanes = -(-rows // TILE) * TILE
    part = width // mp_count
    units = FF // mp_count
    head = width // HEADS
    dec_width = dec_position.shape[1]
    dec_part = dec_width // mp_count
    dec_units = FFD // mp_count
    widths = (3 * part, part, units, units, dec_part)
    dec_widths = (dec_part,) * 4 + (dec_units,) * 2
    slots = jnp.pad(slot_ids, (0, lanes - real_rows), constant_values=IMG + 1)
    ranges = key_ranges(slots)

    def halves(own, other, axis):
        return jnp.where(
            first_half,
            jnp.concatenate([own, other], axis=axis),
            jnp.concatenate([other, own], axis=axis),
        )

    (qkv_w, out_w, up_w, down_w, projection), dec_own, norm_rows = gather_all(
        enc_weights[:, 0, :].astype(LOW),
        dec_weights[:, 0, :].astype(LOW),
        pack_norms(enc_norms, dec_norms, 1),
        widths,
    )
    enc_gains, dec_gains = (
        v.astype(LOW).astype(WIDE)
        for v in unpack_norms(
            norm_rows, norm_rows.shape[0] // 8, enc_norms.shape[1], dec_norms.shape[1]
        )
    )
    stream = halves(act_in[0], partner(act_in[0]), 0)
    stream = jnp.pad(stream, ((0, rows - real_rows), (0, 0)))
    first, turned, mixture, log_sum, mix_own = encoder_attend(
        stream, slots, ranges, enc_gains, qkv_w, out_w, head
    )
    after, second, hidden, slope, feed_own = encoder_feed(
        stream, mix_own, partner(mix_own), enc_gains, up_w, down_w, ROW_BLOCK
    )
    encoded = (after + (feed_own.astype(WIDE) + partner(feed_own).astype(WIDE))).astype(LOW)
    projected = mm(encoded, projection)[:real_rows].astype(LOW)
    arrived = from_behind(projected, "section", 1)
    visible = halves(arrived, partner(arrived), 1)

    def join(own, other):
        pieces = list(zip(cut_columns(own, dec_widths), cut_columns(other, dec_widths)))
        qkv = jnp.concatenate([p for pair in pieces[:3] for p in pair], axis=1)
        return (qkv, *(jnp.concatenate(pair, axis=1) for pair in pieces[3:]))

    dec_mats = on_side(decoder_side, join, dec_own, partner(dec_own))
    decoded, grad_visible, grad_qkv, grad_out, grad_up, grad_down, dec_gain_grad = decoder_step(
        visible, target, mask_token, dec_position, dec_gains, *dec_mats, act_in[0], local_images
    )

    seen = grad_visible.astype(LOW)
    left, right = seen[:, :dec_part], seen[:, dec_part:]
    returned = jnp.where(first_half, left, right).astype(WIDE) + partner(
        jnp.where(first_half, right, left)
    ).astype(WIDE)
    grad_projected = from_behind(returned.astype(LOW), "section", -1)
    grad_projected = jnp.pad(grad_projected, ((0, rows - real_rows), (0, 0)))

    def dec_packs(grad_qkv, grad_out, grad_up, grad_down):
        pieces = [grad_qkv.T[:, k * dec_part : (k + 1) * dec_part] for k in range(6)]
        pieces += [grad_out.T[:, :dec_part], grad_out.T[:, dec_part:]]
        for matrix in (grad_up, grad_down):
            pieces += [matrix[:, :dec_units], matrix[:, dec_units:]]
        return tuple(
            jnp.concatenate(pieces[k::2], axis=1).astype(kind) for k, kind in ((0, WIDE), (1, LOW))
        )

    pack_own, pack_other = on_side(
        decoder_side, dec_packs, grad_qkv, grad_out, grad_up, grad_down
    )
    dec_grad = (pack_own + partner(pack_other).astype(WIDE)).astype(LOW)
    dec_gain_grad = dec_gain_grad + partner(dec_gain_grad)

    grad_projection = mm(encoded, grad_projected, 0, 0).astype(LOW)
    end_own = mm(grad_projected, projection, 1, 1).astype(LOW)
    end_other = partner(end_own)
    grad_up_w, grad_down_w, back_own = encoder_feed_back(
        end_own, end_other, second, hidden, slope, up_w, down_w
    )
    grad_after, grad_low, gains_two = encoder_norm_back(
        after, back_own, partner(back_own), (end_own, end_other), enc_gains, 2, ROW_BLOCK, True
    )
    grad_qkv_w, grad_out_w, start_own = encoder_attend_back(
        slots, ranges, first, turned, mixture, log_sum, grad_low, qkv_w, out_w, head
    )
    grad_stream, gains_one = encoder_norm_back(
        stream, start_own, partner(start_own), (grad_after,), enc_gains, 0, ROW_BLOCK, False
    )
    enc_gain_grad = jnp.concatenate([gains_one[:2], gains_two[:2]], axis=0)
    norm_grads = pack_norms(
        jnp.where(encoder_side, enc_gain_grad, 0.0),
        jnp.where(decoder_side, dec_gain_grad, 0.0),
        norm_rows.shape[0] // 8,
    )
    enc_shard, dec_shard, norm_shard = scatter_all(
        (grad_qkv_w, grad_out_w, grad_up_w, grad_down_w, grad_projection),
        dec_grad,
        norm_grads,
        encoder_side,
    )
    enc_gain_shard, dec_gain_shard = unpack_norms(
        norm_shard, 1, enc_norms.shape[1], dec_norms.shape[1]
    )
    local_squares = (
        jnp.sum(enc_shard * enc_shard)
        + jnp.sum(dec_shard * dec_shard)
        + (jnp.sum(enc_gain_shard * enc_gain_shard) + jnp.sum(dec_gain_shard * dec_gain_shard))
        / mp_count
    )
    square_total = lax.psum(local_squares, ("section", "dp", "mp"))
    grad_norm = jnp.sqrt(square_total)
    factor = jnp.minimum(1.0, math.sqrt(PARAMS) / (grad_norm + 1e-06))
    step_value = step_count[0].astype(jnp.float32)
    fix_first = 1.0 - jnp.power(BETA_FIRST, step_value)
    fix_second = 1.0 - jnp.power(BETA_SECOND, step_value)

    def renew(weight, first_moment, second_moment, gradient, rate, decay):
        return update(
            weight, first_moment, second_moment, gradient, factor, rate, fix_first, fix_second, decay
        )

    enc_shard, dec_shard = enc_shard[:, None, :], dec_shard[:, None, :]
    step_rate, norm_rate = learning_rate[0], learning_rate[1]
    own_grad = lax.dynamic_slice_in_dim(grad_stream, mp_rank * local_rows, local_rows, axis=0)
    act_out = jnp.where(encoder_side, own_grad, decoded.reshape(local_rows, width))[None]
    return (
        act_out,
        renew(enc_weights, enc_first, enc_second, enc_shard, step_rate, WEIGHT_DECAY),
        renew(dec_weights, dec_first, dec_second, dec_shard, step_rate, WEIGHT_DECAY),
        renew(enc_norms, enc_norm_first, enc_norm_second, enc_gain_shard, norm_rate, 0.0),
        renew(dec_norms, dec_norm_first, dec_norm_second, dec_gain_shard, norm_rate, 0.0),
        enc_shard * factor,
        dec_shard * factor,
        enc_gain_shard * factor,
        dec_gain_shard * factor,
        grad_norm.reshape(1),
    )


def solution(mesh):
    in_specs = (
        P("section", ("dp", "mp"), None),
        P("dp", None, None),
        P(("section", "dp"), "mp", None),
        P(("section", "dp"), "mp", None),
        P(("section", "dp"), "mp", None),
        P(("section", "dp"), "mp", None),
        P(("section", "dp"), "mp", None),
        P(("section", "dp"), "mp", None),
        P(None, ("section", "dp")),
        P(None, ("section", "dp")),
        P(None, ("section", "dp")),
        P(None, ("section", "dp")),
        P(None, ("section", "dp")),
        P(None, ("section", "dp")),
        P(),
        P(),
        P(),
        P(),
    )
    out_specs = (
        P("section", ("dp", "mp"), None),
        P(("section", "dp"), "mp", None),
        P(("section", "dp"), "mp", None),
        P(None, ("section", "dp")),
        P(None, ("section", "dp")),
        P(("section", "dp"), "mp", None),
        P(("section", "dp"), "mp", None),
        P(None, ("section", "dp")),
        P(None, ("section", "dp")),
        P(),
    )
    return jax.shard_map(
        per_device, mesh=mesh, in_specs=in_specs, out_specs=out_specs, check_vma=False
    )
```

```python
import functools
import itertools
import math

import jax
import jax.numpy as jnp
from jax import lax
from jax.experimental import pallas as pl
from jax.experimental.pallas import tpu as pltpu
from jax.sharding import PartitionSpec as P

FF = 4096
FFD = 2048
GRID = 196
IMG = 12
PARAMS = 16259072

BETA_FIRST = 0.9
BETA_SECOND = 0.999
ADAM_EPS = 1e-08
WEIGHT_DECAY = 0.05
ROW_BLOCK = 240
GATHER_ORDERS = ("hlxy", "hlyx", "hlxy", "hlyx", "yxhl")
SCATTER_ORDERS = ("xylh", "yxlh", "xylh", "yxlh", "lhxy")

MESH_ID = pl.DeviceIdType.MESH
EVERY = slice(None)
BOTH = -1
DIMS = "xhly"


class Place:
    def __init__(self):
        s, depth, core = lax.axis_index("section"), lax.axis_index("dp"), lax.axis_index("mp")
        y, low, high = depth % 2, (depth // 2) % 2, depth // 4
        self.at = {"x": s, "h": high, "l": low, "y": y}
        self.s, self.core = s, core
        self.device = {
            "x": (1 - s, depth, core),
            "h": (s, depth + 4 - 8 * high, core),
            "l": (s, depth + 2 - 4 * low, core),
            "y": (s, depth + 1 - 2 * y, core),
            "c": (s, depth, 1 - core),
        }

    def greet(self):
        barrier = pltpu.get_barrier_semaphore()
        for name in self.device:
            pl.semaphore_signal(
                barrier, inc=1, device_id=self.device[name], device_id_type=MESH_ID
            )
        pl.semaphore_wait(barrier, len(self.device))


def run(condition, action):
    if condition is None:
        action()
    else:
        pl.when(condition)(action)


def gather_kernel(chunks, n_in, n_out, ahead, lag, *refs):
    ins, outs = refs[:n_in], refs[n_in : n_in + n_out]
    send, recv, local = refs[n_in + n_out :]
    here = Place()
    count = len(chunks)

    def region(chunk, gathered, sender):
        at = [
            EVERY if d in gathered else 1 - here.at[d] if d == sender else here.at[d] for d in DIMS
        ]
        return outs[chunk[1]].at[(*at, EVERY, pl.ds(chunk[3], chunk[4]))]

    def own(i):
        chunk = chunks[i]
        return pltpu.make_async_copy(
            ins[chunk[0]].at[:, pl.ds(chunk[2], chunk[4])], region(chunk, "", None), local.at[i]
        )

    def copy(i, stage, incoming):
        chunk = chunks[i]
        order = chunk[5]
        axis = order[stage]
        block = region(chunk, order[:stage], axis if incoming else None)
        source = block
        if stage == 0 and not incoming:
            source = ins[chunk[0]].at[:, pl.ds(chunk[2], chunk[4])]
        return pltpu.make_async_remote_copy(
            src_ref=source,
            dst_ref=block,
            send_sem=send.at[i, stage],
            recv_sem=recv.at[i, stage],
            device_id=here.device[axis],
            device_id_type=MESH_ID,
        )

    def roles(i, stage):
        order, owner = chunks[i][5], chunks[i][6]
        if owner == BOTH:
            return None, None
        if order[stage] == "x":
            return here.s != owner, here.s == owner
        if "x" in order[:stage]:
            return here.s == owner, here.s == owner
        return None, None

    def begin(i, stage):
        run(roles(i, stage)[0], lambda: copy(i, stage, False).start())

    def arrive(i, stage):
        run(roles(i, stage)[1], lambda: copy(i, stage, True).wait_recv())
        if stage == 0:
            own(i).wait()

    here.greet()
    for i in range(count):
        own(i).start()
    for i in range(min(ahead, count)):
        begin(i, 0)
    for step in range(count + sum(lag)):
        for stage in range(3):
            i = step - sum(lag[:stage])
            if not 0 <= i < count:
                continue
            arrive(i, stage)
            begin(i, stage + 1)
            if stage == 0 and i + ahead < count:
                begin(i + ahead, 0)
    for i in range(count):
        arrive(i, 3)
    for i in range(count):
        for stage in range(4):
            run(
                roles(i, stage)[0],
                lambda i=i, stage=stage: copy(i, stage, False).wait_send(),
            )


def gather_weights(shards, outputs, chunks, collective_id, ahead=4, lag=(1, 1)):
    count = len(chunks)
    call = pl.pallas_call(
        functools.partial(gather_kernel, chunks, len(shards), len(outputs), ahead, lag),
        out_shape=[
            jax.ShapeDtypeStruct((2, 2, 2, 2, rows, width), dtype) for rows, width, dtype in outputs
        ],
        in_specs=[pl.BlockSpec(memory_space=pltpu.VMEM)] * len(shards),
        out_specs=[pl.BlockSpec(memory_space=pl.ANY)] * len(outputs),
        scratch_shapes=[
            pltpu.SemaphoreType.DMA((count, 4)),
            pltpu.SemaphoreType.DMA((count, 4)),
            pltpu.SemaphoreType.DMA((count,)),
        ],
        compiler_params=pltpu.CompilerParams(
            collective_id=collective_id, has_side_effects=True, vmem_limit_bytes=40 * 2**20
        ),
    )
    results = call(*shards)
    return [
        r.reshape(16 * rows, width) for r, (rows, width, _) in zip(results, outputs, strict=True)
    ]


def spread(total, pieces, unit=128):
    units = total // unit
    widths = [units // pieces + (1 if k < units % pieces else 0) for k in range(pieces)]
    return [w * unit for w in widths if w]


def chunk_list(widths, pieces, owner, orders):
    chunks = []
    column = turn = 0
    for index, (width, count) in enumerate(zip(widths, pieces, strict=True)):
        begin = 0
        for piece in spread(width, count):
            chunks.append((index, begin, column, piece, orders[turn % len(orders)], owner))
            begin += piece
            column += piece
            turn += 1
    return chunks


def left_after(order, stage):
    return [d for d in DIMS if d not in order[: stage + 1]]


def scatter_buffers(order, owner):
    shapes = [(2,) * 3]
    for stage in range(4):
        if order[stage] == "x" and owner != BOTH:
            continue
        shapes.append((2,) * (3 - stage))
    return shapes


def squares(ref):
    def step(k, total):
        block = ref[:, pl.ds(pl.multiple_of(k * 128, 128), 128)].astype(jnp.float32)
        block = block * block
        for r in range(0, block.shape[0], 8):
            total = total + block[r : r + 8]
        return total

    return lax.fori_loop(0, ref.shape[1] // 128, step, jnp.zeros((8, 128), jnp.float32))


def scatter_kernel(chunks, n_in, n_out, ahead, lag, cores, *refs):
    ins, summed, outs = refs[:n_in], refs[n_in], refs[n_in + 1 : n_in + 1 + n_out]
    square_total = refs[n_in + 1 + n_out]
    rest = refs[n_in + n_out + 2 :]
    send, recv, local, square_send, square_recv, square_mine, square_there = rest[:7]
    here = Place()
    s = here.s
    count = len(chunks)
    own, got = [], []
    position = 7
    for chunk in chunks:
        order, owner = chunk[5], chunk[6]
        own.append(rest[position])
        position += 1
        mine = []
        for stage in range(4):
            if order[stage] == "x" and owner != BOTH:
                mine.append(None)
                continue
            mine.append(rest[position])
            position += 1
        got.append(mine)

    def source(i, axis, keep):
        chunk = chunks[i]
        at = [
            (here.at[d] if keep else 1 - here.at[d]) if d == axis else EVERY for d in DIMS
        ]
        return ins[chunk[0]].at[(*at, EVERY, pl.ds(chunk[2], chunk[4]))]

    def load(i):
        return pltpu.make_async_copy(source(i, chunks[i][5][0], True), own[i], local.at[i])

    def spot(i, stage, flip):
        order = chunks[i][5]
        at = []
        for d in DIMS:
            if d == order[0]:
                continue
            if d in order[:stage]:
                at.append(here.at[d])
            elif d == order[stage]:
                at.append(1 - here.at[d] if flip else here.at[d])
            else:
                at.append(EVERY)
        return tuple(at)

    def copy(i, stage, incoming):
        order = chunks[i][5]
        axis = order[stage]
        moved = got[i][stage] is None
        src = source(i, axis, False) if stage == 0 else own[i].at[spot(i, stage, True)]
        if not moved:
            there = mine = got[i][stage]
        elif stage == 0:
            there = mine = own[i]
        else:
            there, mine = own[i].at[spot(i, stage, True)], own[i].at[spot(i, stage, False)]
        return pltpu.make_async_remote_copy(
            src_ref=mine if incoming else src,
            dst_ref=mine if incoming else there,
            send_sem=send.at[i, stage],
            recv_sem=recv.at[i, stage],
            device_id=here.device[axis],
            device_id_type=MESH_ID,
        )

    def roles(i, stage):
        order, owner = chunks[i][5], chunks[i][6]
        if owner == BOTH:
            return None, None
        if order[stage] == "x":
            return s == owner, s != owner
        if "x" in order[:stage]:
            return None, None
        return s == owner, s == owner

    def begin(i, stage):
        run(roles(i, stage)[0], lambda: copy(i, stage, False).start())

    def arrive(i, stage):
        chunk, a, r = chunks[i], own[i], got[i][stage]
        order, owner = chunk[5], chunk[6]
        run(roles(i, stage)[1], lambda: copy(i, stage, True).wait_recv())
        if stage == 0:
            run(None if owner == BOTH else s == owner, lambda: load(i).wait())
        out = outs[chunk[1]].at[:, pl.ds(chunk[3], chunk[4])]
        place = spot(i, stage, False)
        if stage == 3:
            result = a[place].astype(jnp.float32)
            if r is not None:
                result = result + r[...].astype(jnp.float32)
            out[...] = result
            return
        if r is None:
            return

        def add():
            free = [k for k, p in enumerate(place) if p is EVERY]
            for combo in itertools.product(range(2), repeat=len(free)):
                at = list(place)
                for k, c in zip(free, combo):
                    at[k] = c
                at = tuple(at)
                a[at] = (a[at].astype(jnp.float32) + r[combo].astype(jnp.float32)).astype(a.dtype)

        run(roles(i, stage)[1], add)

    here.greet()
    for i in range(count):
        run(
            None if chunks[i][6] == BOTH else s == chunks[i][6],
            lambda i=i: load(i).start(),
        )
    for i in range(min(ahead, count)):
        begin(i, 0)
    for step in range(count + sum(lag)):
        for stage in range(3, -1, -1):
            i = step - sum(lag[:stage])
            if not 0 <= i < count:
                continue
            arrive(i, stage)
            if stage < 3:
                begin(i, stage + 1)
            if stage == 0 and i + ahead < count:
                begin(i + ahead, 0)
    for i in range(count):
        for stage in range(4):
            run(
                roles(i, stage)[0],
                lambda i=i, stage=stage: copy(i, stage, False).wait_send(),
            )

    value = squares(summed)
    for k, out in enumerate(outs):
        value = value + squares(out) * (1.0 / cores if k == n_out - 1 else 1.0)
    value = jnp.broadcast_to(jnp.sum(value, keepdims=True), (8, 128))
    for k, axis in enumerate("cyxlh"):
        square_mine[k] = value
        move = pltpu.make_async_remote_copy(
            src_ref=square_mine.at[k],
            dst_ref=square_there.at[k],
            send_sem=square_send.at[k],
            recv_sem=square_recv.at[k],
            device_id=here.device[axis],
            device_id_type=MESH_ID,
        )
        move.start()
        move.wait()
        value = value + square_there[k]
    square_total[...] = value


def scatter_grads(parts, summed, outputs, chunks, collective_id, ahead=4, lag=(1, 1, 1)):
    count = len(chunks)
    views = [p.reshape(2, 2, 2, 2, p.shape[0] // 16, p.shape[1]) for p in parts]
    buffers = []
    for chunk in chunks:
        view = views[chunk[0]]
        for lead in scatter_buffers(chunk[5], chunk[6]):
            buffers.append(pltpu.VMEM((*lead, view.shape[4], chunk[4]), view.dtype))
    call = pl.pallas_call(
        functools.partial(scatter_kernel, chunks, len(parts), len(outputs), ahead, lag, lax.axis_size("mp")),
        out_shape=[
            jax.ShapeDtypeStruct((rows, width), jnp.float32) for rows, width in [*outputs, (8, 128)]
        ],
        in_specs=[pl.BlockSpec(memory_space=pl.ANY)] * len(parts)
        + [pl.BlockSpec(memory_space=pltpu.VMEM)],
        out_specs=[pl.BlockSpec(memory_space=pltpu.VMEM)] * (len(outputs) + 1),
        scratch_shapes=[
            pltpu.SemaphoreType.DMA((count, 4)),
            pltpu.SemaphoreType.DMA((count, 4)),
            pltpu.SemaphoreType.DMA((count,)),
            pltpu.SemaphoreType.DMA((5,)),
            pltpu.SemaphoreType.DMA((5,)),
            pltpu.VMEM((5, 8, 128), jnp.float32),
            pltpu.VMEM((5, 8, 128), jnp.float32),
            *buffers,
        ],
        compiler_params=pltpu.CompilerParams(
            collective_id=collective_id, has_side_effects=True, vmem_limit_bytes=56 * 2**20
        ),
    )
    return call(*views, summed)


HEADS = 16
NORM_EPS = 1e-06
MASKED = -1e30
LOW = jnp.bfloat16
WIDE = jnp.float32


def mm(left, right, left_dim=1, right_dim=0):
    return lax.dot_general(
        left, right, (((left_dim,), (right_dim,)), ((), ())), preferred_element_type=WIDE
    )


def centre(tokens):
    average = jnp.mean(tokens, axis=-1, keepdims=True)
    centred = tokens - average
    spread_ = jnp.mean(centred * centred, axis=-1, keepdims=True)
    scale = lax.rsqrt(spread_ + NORM_EPS)
    return centred * scale, scale


def centre_back(unit, scale, gain, grad):
    pulled = grad * gain
    first = jnp.mean(pulled, axis=-1, keepdims=True)
    second = jnp.mean(pulled * unit, axis=-1, keepdims=True)
    return scale * (pulled - first - unit * second)


def gelu_pair(z):
    cdf = 0.5 * (1.0 + lax.erf(z * math.sqrt(0.5)))
    return z * cdf, cdf + z * (jnp.exp(-0.5 * z * z) * (1.0 / math.sqrt(2.0 * math.pi)))


def decoder_kernel(
    grid_cells,
    length,
    target_row,
    target_column,
    visible,
    mask,
    position,
    gains,
    qkv_t,
    qkv_w,
    out_t,
    out_w,
    up_w,
    down_w,
    cotangent,
    decoded,
    grad_visible,
    grad_qkv,
    grad_out,
    grad_up,
    grad_down,
    grad_gains,
    qkv_rows,
    shares,
    mixture,
    hidden,
    slope,
    grad_rows,
):
    image = pl.program_id(0)
    rows, width = decoded.shape[1], decoded.shape[2]
    head = width // HEADS
    units = hidden.shape[1]
    scaling = head ** (-0.5)

    @pl.when(image == 0)
    def _():
        for ref in (grad_visible, grad_qkv, grad_out, grad_up, grad_down, grad_gains):
            ref[...] = jnp.zeros_like(ref)

    packed = target_row.shape[1]
    cell = lax.broadcasted_iota(jnp.int32, (rows, packed), 0)
    wanted = jnp.where(cell < length, cell + image * length, -7)
    chosen = (target_row[...] == wanted).astype(WIDE)
    seen = jnp.max(chosen, axis=1, keepdims=True)
    placed = mm(chosen.astype(LOW), visible[...])
    stream = jnp.where(seen > 0.0, placed, mask[...]) + position[...]

    unit_one, scale_one = centre(stream)
    first = (unit_one * gains[0:1] + gains[1:2]).astype(LOW)
    qkv_rows[...] = mm(qkv_t[...], first, 1, 1).astype(LOW)

    key_index = lax.broadcasted_iota(jnp.int32, (rows, rows), 0)

    def attend(h, carry):
        begin = pl.multiple_of(h * head, head)
        q = qkv_rows[pl.ds(begin, head), :]
        k = qkv_rows[pl.ds(pl.multiple_of(width + begin, head), head), :]
        v = qkv_rows[pl.ds(pl.multiple_of(2 * width + begin, head), head), :]
        scores = mm(k, q, 0, 0) * scaling
        scores = jnp.where(key_index < length, scores, MASKED)
        weights = jnp.exp(scores - jnp.max(scores, axis=0, keepdims=True))
        share = weights * (1.0 / jnp.sum(weights, axis=0, keepdims=True))
        shares[h] = share
        mixture[pl.ds(begin, head), :] = mm(v, share.astype(LOW)).astype(LOW)
        return carry

    lax.fori_loop(0, HEADS, attend, 0, unroll=4)
    mixed = mixture[...]
    after = stream + mm(jnp.transpose(mixed), out_w[...], 1, 1)
    unit_two, scale_two = centre(after)
    second = (unit_two * gains[2:3] + gains[3:4]).astype(LOW)
    piece = 256
    result = after
    for c in range(0, units, piece):
        z = mm(second, up_w[:, c : c + piece])
        h, g = gelu_pair(z)
        hidden[:, c : c + piece] = h.astype(LOW)
        slope[:, c : c + piece] = g
    decoded[0] = after + mm(hidden[...], down_w[...], 1, 1)

    grad_low = cotangent[0]
    grad_result = grad_low.astype(WIDE)
    turned = jnp.transpose(grad_low)
    second_turned = jnp.transpose(second)
    for c in range(0, units, piece):
        cut = slice(c, c + piece)
        grad_down[:, cut] += mm(turned, hidden[:, cut])
        grad_z = (mm(grad_low, down_w[:, cut]) * slope[:, cut]).astype(LOW)
        hidden[:, cut] = grad_z
        grad_up[:, cut] += mm(second_turned, grad_z)
    grad_second = mm(hidden[...], up_w[...], 1, 1)
    grad_after = grad_result + centre_back(unit_two, scale_two, gains[2:3], grad_second)
    grad_gains[2:3] += jnp.sum(grad_second * unit_two, axis=0, keepdims=True)
    grad_gains[3:4] += jnp.sum(grad_second, axis=0, keepdims=True)

    after_low = grad_after.astype(LOW)
    grad_out[...] += mm(mixed, after_low)
    grad_rows[...] = mm(out_t[...], after_low, 1, 1).astype(LOW)

    def attend_back(h, carry):
        begin = pl.multiple_of(h * head, head)
        key_at = pl.multiple_of(width + begin, head)
        value_at = pl.multiple_of(2 * width + begin, head)
        q = qkv_rows[pl.ds(begin, head), :]
        k = qkv_rows[pl.ds(key_at, head), :]
        v = qkv_rows[pl.ds(value_at, head), :]
        grad_mixture = grad_rows[pl.ds(begin, head), :]
        share = shares[h]
        grad_share = mm(v, grad_mixture, 0, 0)
        grad_value = mm(grad_mixture, share.astype(LOW), 1, 1)
        inner = jnp.sum(share * grad_share, axis=0, keepdims=True)
        grad_score = (share * (grad_share - inner)).astype(LOW)
        grad_query = mm(k, grad_score) * scaling
        grad_key = mm(q, grad_score, 1, 1) * scaling
        qkv_rows[pl.ds(begin, head), :] = grad_query.astype(LOW)
        qkv_rows[pl.ds(key_at, head), :] = grad_key.astype(LOW)
        qkv_rows[pl.ds(value_at, head), :] = grad_value.astype(LOW)
        return carry

    lax.fori_loop(0, HEADS, attend_back, 0, unroll=4)
    grads = qkv_rows[...]
    grad_qkv[...] += mm(grads, first)
    grad_first = jnp.transpose(mm(qkv_w[...], grads))
    grad_stream = grad_after + centre_back(unit_one, scale_one, gains[0:1], grad_first)
    grad_gains[0:1] += jnp.sum(grad_first * unit_one, axis=0, keepdims=True)
    grad_gains[1:2] += jnp.sum(grad_first, axis=0, keepdims=True)

    cell_lane = lax.broadcasted_iota(jnp.int32, (packed, rows), 1)
    wanted_lane = jnp.where(cell_lane < length, cell_lane + image * length, -7)
    chosen_back = (target_column[...] == wanted_lane).astype(WIDE).astype(LOW)
    grad_visible[...] += mm(chosen_back, grad_stream.astype(LOW))


def decoder_step(
    visible, target, mask, position, gains, qkv_w, out_w, up_w, down_w, cotangent, images
):
    length, width = position.shape
    rows = -(-length // 16) * 16
    packed = -(-visible.shape[0] // 128) * 128
    spare = packed - visible.shape[0]
    units = up_w.shape[1]
    visible = jnp.pad(visible, ((0, spare), (0, 0)))
    target = jnp.pad(target, (0, spare), constant_values=-1)
    longer = ((0, 0), (0, rows - length), (0, 0))
    cotangent = jnp.pad(cotangent.reshape(images, length, width), longer)
    position = jnp.pad(position, ((0, rows - length), (0, 0)))

    def fixed(shape):
        return pl.BlockSpec(shape, lambda i: (0,) * len(shape), pipeline_mode=pl.Buffered(1))

    per_image = pl.BlockSpec((1, rows, width), lambda i: (i, 0, 0))
    grads = [
        ((packed, width), WIDE),
        ((3 * width, width), WIDE),
        ((width, width), WIDE),
        ((width, units), WIDE),
        ((width, units), WIDE),
        ((8, width), WIDE),
    ]
    results = pl.pallas_call(
        functools.partial(decoder_kernel, images * length, length),
        grid=(images,),
        out_shape=[jax.ShapeDtypeStruct((images, rows, width), WIDE)]
        + [jax.ShapeDtypeStruct(s, d) for s, d in grads],
        in_specs=[
            fixed((1, packed)),
            fixed((packed, 1)),
            fixed((packed, width)),
            fixed((1, width)),
            fixed((rows, width)),
            fixed((4, width)),
            fixed((3 * width, width)),
            fixed((width, 3 * width)),
            fixed((width, width)),
            fixed((width, width)),
            fixed((width, units)),
            fixed((width, units)),
            per_image,
        ],
        out_specs=[per_image] + [fixed(s) for s, _ in grads],
        scratch_shapes=[
            pltpu.VMEM((3 * width, rows), LOW),
            pltpu.VMEM((HEADS, rows, rows), WIDE),
            pltpu.VMEM((width, rows), LOW),
            pltpu.VMEM((rows, units), LOW),
            pltpu.VMEM((rows, units), WIDE),
            pltpu.VMEM((width, rows), LOW),
        ],
        compiler_params=pltpu.CompilerParams(
            dimension_semantics=("arbitrary",), vmem_limit_bytes=60 * 2**20
        ),
    )(
        target[None, :],
        target[:, None],
        visible,
        mask[None, :],
        position,
        gains,
        qkv_w.T,
        qkv_w,
        out_w.T,
        out_w,
        up_w,
        down_w,
        cotangent,
    )
    decoded, grad_visible, grad_qkv, grad_out, grad_up, grad_down, grad_gains = results
    return (
        decoded[:, :length].reshape(images * length, width),
        grad_visible[: packed - spare],
        grad_qkv,
        grad_out,
        grad_up,
        grad_down,
        grad_gains[:4],
    )


TILE = 256
GROUP = 4


def fixed(shape):
    return pl.BlockSpec(shape, lambda i: (0,) * len(shape), pipeline_mode=pl.Buffered(1))


def down_rows(rows, width):
    return pl.BlockSpec((rows, width), lambda i: (i, 0))


def params(megabytes=60):
    return pltpu.CompilerParams(
        dimension_semantics=("arbitrary",), vmem_limit_bytes=megabytes * 2**20
    )


def attend_kernel(
    head, bounds, stream, slots_row, slots_column, gains, qkv_w, out_w, first, turned, mixture, log_sum, partial
):
    rows, width = stream.shape
    part, lanes = mixture.shape
    tiles = lanes // TILE
    scaling = head ** (-0.5)
    unit, _ = centre(stream[...].astype(WIDE))
    first[...] = (unit * gains[0:1] + gains[1:2]).astype(LOW)
    turned[:, rows:] = jnp.zeros((3 * part, lanes - rows), LOW)
    for c in range(0, 3 * part, TILE):
        weight = jnp.transpose(qkv_w[:, c : c + TILE])
        turned[c : c + TILE, :rows] = mm(weight, first[...], 1, 1).astype(LOW)

    def at(which, h, tile):
        return (
            pl.ds(pl.multiple_of(which * part + h * head, head), head),
            pl.ds(pl.multiple_of(tile * TILE, TILE), TILE),
        )

    def step(n, carry):
        group, i = n // tiles, n % tiles
        heads = [group * GROUP + g for g in range(GROUP)]
        lane_i = pl.ds(pl.multiple_of(i * TILE, TILE), TILE)
        queries = [turned[at(0, h, i)] for h in heads]
        slot_i = slots_row[:, lane_i]

        def inner(j, state):
            same = slots_column[pl.ds(pl.multiple_of(j * TILE, TILE), TILE), :] == slot_i
            result = []
            for g, h in enumerate(heads):
                high, total, mixed = state[g]
                scores = mm(turned[at(1, h, j)], queries[g], 0, 0) * scaling
                scores = jnp.where(same, scores, MASKED)
                higher = jnp.maximum(high, jnp.max(scores, axis=0, keepdims=True))
                weights = jnp.exp(scores - higher)
                fix = jnp.exp(high - higher)
                total = total * fix + jnp.sum(weights, axis=0, keepdims=True)
                mixed = mixed * fix + mm(turned[at(2, h, j)], weights.astype(LOW))
                result.append((higher, total, mixed))
            return tuple(result)

        begin = (
            jnp.full((1, TILE), MASKED, WIDE),
            jnp.zeros((1, TILE), WIDE),
            jnp.zeros((head, TILE), WIDE),
        )
        state = lax.fori_loop(bounds[i, 0], bounds[i, 1], inner, (begin,) * GROUP)
        for g, h in enumerate(heads):
            high, total, mixed = state[g]
            mixture[at(0, h, i)] = (mixed / total).astype(LOW)
            log_sum[pl.ds(h, 1), lane_i] = high + jnp.log(total)
        return carry

    lax.fori_loop(0, part // head // GROUP * tiles, step, 0)
    mixed = jnp.transpose(mixture[...])[:rows]
    for c in range(0, width, TILE):
        partial[:, c : c + TILE] = mm(mixed, out_w[c : c + TILE, :], 1, 1).astype(LOW)


def encoder_attend(stream, slots, bounds, gains, qkv_w, out_w, head):
    rows, width = stream.shape
    lanes = slots.shape[0]
    part = out_w.shape[1]
    return pl.pallas_call(
        functools.partial(attend_kernel, head),
        in_specs=[pl.BlockSpec(memory_space=pltpu.SMEM)]
        + [pl.BlockSpec(memory_space=pltpu.VMEM)] * 6,
        out_specs=[pl.BlockSpec(memory_space=pltpu.VMEM)] * 5,
        out_shape=[
            jax.ShapeDtypeStruct((rows, width), LOW),
            jax.ShapeDtypeStruct((3 * part, lanes), LOW),
            jax.ShapeDtypeStruct((part, lanes), LOW),
            jax.ShapeDtypeStruct((part // head, lanes), WIDE),
            jax.ShapeDtypeStruct((rows, width), LOW),
        ],
        compiler_params=pltpu.CompilerParams(vmem_limit_bytes=60 * 2**20),
    )(bounds, stream, slots[None, :], slots[:, None], gains, qkv_w, out_w)


def attend_back_kernel(
    head,
    bounds,
    slots_row,
    slots_column,
    first,
    turned,
    mixture,
    log_sum,
    grad_low,
    qkv_w,
    out_w,
    grad_qkv_w,
    grad_out_w,
    partial,
    grad_mixture,
    grad_turned,
    inner_sum,
    key_sum,
    value_sum,
):
    rows, width = grad_low.shape
    part, lanes = mixture.shape
    tiles = lanes // TILE
    scaling = head ** (-0.5)
    grad_mixture[:, rows:] = jnp.zeros((part, lanes - rows), LOW)
    for c in range(0, width, TILE):
        grad_out_w[c : c + TILE, :] = jnp.transpose(
            mm(mixture[:, :rows], grad_low[:, c : c + TILE]).astype(LOW)
        )
    for c in range(0, part, TILE):
        weight = jnp.transpose(out_w[:, c : c + TILE])
        grad_mixture[c : c + TILE, :rows] = mm(weight, grad_low[...], 1, 1).astype(LOW)
    for h in range(part // head):
        cut = slice(h * head, (h + 1) * head)
        inner_sum[h : h + 1, :] = jnp.sum(
            grad_mixture[cut, :].astype(WIDE) * mixture[cut, :].astype(WIDE), axis=0, keepdims=True
        )

    def at(which, h, tile):
        return (
            pl.ds(pl.multiple_of(which * part + h * head, head), head),
            pl.ds(pl.multiple_of(tile * TILE, TILE), TILE),
        )

    def over_group(group, carry):
        heads = [group * GROUP + g for g in range(GROUP)]
        key_sum[...] = jnp.zeros_like(key_sum)
        value_sum[...] = jnp.zeros_like(value_sum)

        def over_queries(i, carry):
            lane_i = pl.ds(pl.multiple_of(i * TILE, TILE), TILE)
            slot_i = slots_row[:, lane_i]
            queries = [turned[at(0, h, i)] for h in heads]
            grads = [grad_mixture[at(0, h, i)] for h in heads]
            logs = [log_sum[pl.ds(h, 1), lane_i] for h in heads]
            sums = [inner_sum[pl.ds(h, 1), lane_i] for h in heads]

            def inner(j, state):
                lane_j = pl.ds(pl.multiple_of(j * TILE, TILE), TILE)
                same = slots_column[lane_j, :] == slot_i
                result = []
                for g, h in enumerate(heads):
                    cut = slice(g * head, (g + 1) * head)
                    keys, values = turned[at(1, h, j)], turned[at(2, h, j)]
                    scores = jnp.where(same, mm(keys, queries[g], 0, 0) * scaling, MASKED)
                    share = jnp.exp(scores - logs[g])
                    grad_share = mm(values, grads[g], 0, 0)
                    grad_score = (share * (grad_share - sums[g])).astype(LOW)
                    value_sum[cut, lane_j] += mm(grads[g], share.astype(LOW), 1, 1)
                    key_sum[cut, lane_j] += mm(queries[g], grad_score, 1, 1)
                    result.append(state[g] + mm(keys, grad_score))
                return tuple(result)

            begin = (jnp.zeros((head, TILE), WIDE),) * GROUP
            state = lax.fori_loop(bounds[i, 0], bounds[i, 1], inner, begin)
            for g, h in enumerate(heads):
                grad_turned[at(0, h, i)] = (state[g] * scaling).astype(LOW)
            return carry

        lax.fori_loop(0, tiles, over_queries, 0)
        size = GROUP * head
        key_at = pl.ds(pl.multiple_of(part + group * size, size), size)
        value_at = pl.ds(pl.multiple_of(2 * part + group * size, size), size)
        grad_turned[key_at, :] = (key_sum[...] * scaling).astype(LOW)
        grad_turned[value_at, :] = value_sum[...].astype(LOW)
        return carry

    lax.fori_loop(0, part // head // GROUP, over_group, 0)
    for c in range(0, 3 * part, TILE):
        grad_qkv_w[:, c : c + TILE] = jnp.transpose(
            mm(grad_turned[c : c + TILE, :rows], first[...]).astype(LOW)
        )
    for c in range(0, width, TILE):
        partial[:, c : c + TILE] = jnp.transpose(
            mm(qkv_w[c : c + TILE, :], grad_turned[:, :rows]).astype(LOW)
        )


def encoder_attend_back(
    slots, bounds, first, turned, mixture, log_sum, grad_low, qkv_w, out_w, head
):
    rows, width = first.shape
    part, lanes = mixture.shape
    return pl.pallas_call(
        functools.partial(attend_back_kernel, head),
        in_specs=[pl.BlockSpec(memory_space=pltpu.SMEM)]
        + [pl.BlockSpec(memory_space=pltpu.VMEM)] * 9,
        out_specs=[pl.BlockSpec(memory_space=pltpu.VMEM)] * 3,
        out_shape=[
            jax.ShapeDtypeStruct((width, 3 * part), LOW),
            jax.ShapeDtypeStruct((width, part), LOW),
            jax.ShapeDtypeStruct((rows, width), LOW),
        ],
        scratch_shapes=[
            pltpu.VMEM((part, lanes), LOW),
            pltpu.VMEM((3 * part, lanes), LOW),
            pltpu.VMEM((part // head, lanes), WIDE),
            pltpu.VMEM((GROUP * head, lanes), WIDE),
            pltpu.VMEM((GROUP * head, lanes), WIDE),
        ],
        compiler_params=pltpu.CompilerParams(vmem_limit_bytes=60 * 2**20),
    )(
        bounds,
        slots[None, :],
        slots[:, None],
        first,
        turned,
        mixture,
        log_sum,
        grad_low,
        qkv_w,
        out_w,
    )


def feed_kernel(stream, own, other, gains, up_w, down_w, after, second, hidden, slope, partial):
    summed = stream[...].astype(WIDE) + (own[...].astype(WIDE) + other[...].astype(WIDE))
    after[...] = summed
    unit, _ = centre(summed)
    second[...] = (unit * gains[2:3] + gains[3:4]).astype(LOW)
    units = up_w.shape[1]
    for c in range(0, units, TILE):
        cut = slice(c, c + TILE)
        h, g = gelu_pair(mm(second[...], up_w[:, cut]))
        hidden[:, cut] = h.astype(LOW)
        slope[:, cut] = g.astype(LOW)
    partial[...] = mm(hidden[...], down_w[...], 1, 1).astype(LOW)


def encoder_feed(stream, own, other, gains, up_w, down_w, block):
    rows, width = stream.shape
    units = up_w.shape[1]
    wide, tall = down_rows(block, width), down_rows(block, units)
    return pl.pallas_call(
        feed_kernel,
        grid=(rows // block,),
        in_specs=[wide, wide, wide, fixed((4, width)), fixed(up_w.shape), fixed(down_w.shape)],
        out_specs=[wide, wide, tall, tall, wide],
        out_shape=[
            jax.ShapeDtypeStruct((rows, width), WIDE),
            jax.ShapeDtypeStruct((rows, width), LOW),
            jax.ShapeDtypeStruct((rows, units), LOW),
            jax.ShapeDtypeStruct((rows, units), LOW),
            jax.ShapeDtypeStruct((rows, width), LOW),
        ],
        compiler_params=params(),
    )(stream, own, other, gains, up_w, down_w)


def feed_back_kernel(
    counts,
    own,
    other,
    second,
    hidden,
    slope,
    up_w,
    down_w,
    grad_up,
    grad_down,
    partial,
    grad_low,
    grad_turned,
    second_turned,
    total,
):
    @pl.when(pl.program_id(0) == 0)
    def _():
        grad_low[...] = (own[...].astype(WIDE) + other[...].astype(WIDE)).astype(LOW)
        grad_turned[...] = jnp.transpose(grad_low[...])
        second_turned[...] = jnp.transpose(second[...])
        total[...] = jnp.zeros_like(total)

    down = mm(grad_turned[...], hidden[...])
    grad_down[...] = jnp.where(counts[0] > 0, down, jnp.zeros_like(down)).astype(LOW)
    grad_z = (mm(grad_low[...], down_w[...]) * slope[...].astype(WIDE)).astype(LOW)
    grad_up[...] = mm(second_turned[...], grad_z).astype(LOW)
    total[...] += mm(grad_z, up_w[...], 1, 1)

    @pl.when(pl.program_id(0) == pl.num_programs(0) - 1)
    def _():
        partial[...] = total[...].astype(LOW)


def encoder_feed_back(counts, own, other, second, hidden, slope, up_w, down_w):
    rows, width = own.shape
    units = up_w.shape[1]
    piece = 256
    whole = fixed((rows, width))
    tall = pl.BlockSpec((rows, piece), lambda i: (0, i))
    weight = pl.BlockSpec((width, piece), lambda i: (0, i))
    return pl.pallas_call(
        feed_back_kernel,
        grid=(units // piece,),
        in_specs=[pl.BlockSpec(memory_space=pltpu.SMEM)]
        + [whole, whole, whole, tall, tall, weight, weight],
        out_specs=[weight, weight, whole],
        out_shape=[
            jax.ShapeDtypeStruct((width, units), LOW),
            jax.ShapeDtypeStruct((width, units), LOW),
            jax.ShapeDtypeStruct((rows, width), LOW),
        ],
        scratch_shapes=[
            pltpu.VMEM((rows, width), LOW),
            pltpu.VMEM((width, rows), LOW),
            pltpu.VMEM((width, rows), LOW),
            pltpu.VMEM((rows, width), WIDE),
        ],
        compiler_params=params(),
    )(counts, own, other, second, hidden, slope, up_w, down_w)


def norm_back_kernel(tokens, own, other, skip_own, skip_other, gains, grad, grad_low, grad_gains, *, at):
    @pl.when(pl.program_id(0) == 0)
    def _():
        grad_gains[...] = jnp.zeros_like(grad_gains)

    pulled = own[...].astype(WIDE) + other[...].astype(WIDE)
    unit, scale = centre(tokens[...].astype(WIDE))
    result = skip_own[...].astype(WIDE)
    if skip_other is not None:
        result = result + skip_other[...].astype(WIDE)
    result = result + centre_back(unit, scale, gains[at : at + 1], pulled)
    grad[...] = result
    if grad_low is not None:
        grad_low[...] = result.astype(LOW)
    grad_gains[0:1] += jnp.sum(pulled * unit, axis=0, keepdims=True)
    grad_gains[1:2] += jnp.sum(pulled, axis=0, keepdims=True)


def encoder_norm_back(tokens, own, other, skip, gains, at, block, low):
    rows, width = tokens.shape
    wide = down_rows(block, width)
    two = len(skip) == 2

    def kernel(*refs):
        refs = list(refs)
        if not two:
            refs.insert(4, None)
        if not low:
            refs.insert(7, None)
        norm_back_kernel(*refs, at=at)

    shapes = [jax.ShapeDtypeStruct((rows, width), WIDE)]
    if low:
        shapes.append(jax.ShapeDtypeStruct((rows, width), LOW))
    shapes.append(jax.ShapeDtypeStruct((8, width), WIDE))
    return pl.pallas_call(
        kernel,
        grid=(rows // block,),
        in_specs=[wide, wide, wide] + [wide] * len(skip) + [fixed((4, width))],
        out_specs=[wide] * (2 if low else 1) + [fixed((8, width))],
        out_shape=shapes,
        compiler_params=params(),
    )(tokens, own, other, *skip, gains)


def from_behind(value, axis, by):
    length = lax.axis_size(axis)
    pairs = [(i, i + by) for i in range(length) if 0 <= i + by < length]
    return lax.ppermute(value, axis, pairs)


def partner(value):
    length = lax.axis_size("mp")
    return lax.ppermute(value, "mp", [(i, (i + 1) % length) for i in range(length)])


def on_side(active, action, *operands):
    def skipped(*values):
        return jax.tree.map(
            lambda leaf: jnp.zeros(leaf.shape, leaf.dtype), jax.eval_shape(action, *values)
        )

    return lax.cond(active, action, skipped, *operands)


def is_fast():
    return lax.axis_size("section") == 2 and lax.axis_size("dp") == 8


def plan(widths, pieces, dec_width, dec_pieces, orders):
    enc = chunk_list(widths, pieces, 0, orders)
    dec = [
        (len(widths), b, c, w, o, k)
        for _, b, c, w, o, k in chunk_list((dec_width,), (dec_pieces,), 1, orders)
    ]
    return enc[:8] + dec + enc[8:]


def gather_all(low_enc, low_dec, norms, widths):
    count = len(widths)
    if not is_fast():
        both = ("section", "dp")
        enc = lax.all_gather(low_enc, both, axis=0, tiled=True)
        dec = lax.all_gather(low_dec, both, axis=0, tiled=True)
        rows = lax.all_gather(norms, both, axis=0, tiled=True)
        parts, column = [], 0
        for w in widths:
            parts.append(enc[:, column : column + w])
            column += w
        return parts, dec, rows
    columns = [sum(widths[:k]) for k in range(count + 1)]
    ahead = [low_enc[:, : columns[3]], low_enc[:, columns[4] :]]
    near = (*widths[:3], widths[4])
    chunks = plan(near, (4, 1, 4, 2), low_dec.shape[1], 4, GATHER_ORDERS)
    outputs = [(low_enc.shape[0], w, LOW) for w in near]
    outputs += [(low_dec.shape[0], low_dec.shape[1], LOW), (8, 128, WIDE)]
    described = [(k // 4, k, c, b, w, o, own) for k, b, c, w, o, own in chunks]
    described.append((2, 5, 0, 0, 128, "hlyx", BOTH))
    shards = [jnp.concatenate(ahead, axis=1), low_dec, norms]
    results = gather_weights(shards, outputs, described, 1, 4, (1, 3))
    low_down, norm_rows = lax.optimization_barrier(
        (low_enc[:, columns[3] : columns[4]], results[5])
    )
    down = lax.all_gather(low_down, ("section", "dp"), axis=0, tiled=True)
    return [*results[:3], down, results[3]], results[4], norm_rows


def scatter_all(enc_parts, dec, norms, encoder_side):
    widths = [p.shape[1] for p in enc_parts]
    both = ("section", "dp")

    def scattered(v):
        return lax.psum_scatter(v, both, scatter_dimension=0, tiled=True)

    if not is_fast():
        parts = [scattered(jnp.where(encoder_side, p.astype(WIDE), 0.0)) for p in enc_parts]
        dec = scattered(jnp.where(encoder_side, 0.0, dec.astype(WIDE)))
        norms = scattered(norms)
        local = sum(jnp.sum(v * v) for v in (*parts, dec))
        local = local + jnp.sum(norms * norms) / lax.axis_size("mp")
        return jnp.concatenate(parts, axis=1), dec, norms, lax.psum(local, (*both, "mp"))
    down = scattered(enc_parts[3])
    near = (*enc_parts[:3], enc_parts[4])
    near_widths = (*widths[:3], widths[4])
    chunks = plan(near_widths, (4, 1, 4, 2), dec.shape[1], 4, SCATTER_ORDERS)
    described = [(k, k // 4, b, c, w, o, own) for k, b, c, w, o, own in chunks]
    described.append((5, 2, 0, 0, 128, "xylh", BOTH))
    rows = near[0].shape[0] // 16
    outputs = [(rows, sum(near_widths)), (dec.shape[0] // 16, dec.shape[1]), (8, 128)]
    enc, dec, norms, total = scatter_grads(
        [*near, dec, norms], down, outputs, described, 2, 4, (2, 2, 2)
    )
    cut = sum(widths[:3])
    enc = jnp.concatenate([enc[:, :cut], down.astype(WIDE), enc[:, cut:]], axis=1)
    return enc, dec, norms, total[0, 0]


def pack_norms(enc_rows, dec_rows, blocks):
    both = [rows.reshape(4, blocks, -1).transpose(1, 0, 2) for rows in (enc_rows, dec_rows)]
    joined = jnp.concatenate(both, axis=2)
    joined = jnp.pad(joined, ((0, 0), (0, 4), (0, 128 - joined.shape[2])))
    return joined.reshape(blocks * 8, 128)


def unpack_norms(packed, blocks, enc_width, dec_width):
    split = packed.reshape(blocks, 8, 128)[:, :4].transpose(1, 0, 2)
    return (
        split[:, :, :enc_width].reshape(4, -1),
        split[:, :, enc_width : enc_width + dec_width].reshape(4, -1),
    )


def key_ranges(slots):
    tiles = slots.reshape(-1, TILE)
    low, high = jnp.min(tiles, axis=1), jnp.max(tiles, axis=1)
    meet = jnp.logical_and(low[:, None] <= high[None, :], high[:, None] >= low[None, :])
    index = jnp.arange(tiles.shape[0], dtype=jnp.int32)[None, :]
    first = jnp.min(jnp.where(meet, index, tiles.shape[0]), axis=1)
    last = jnp.max(jnp.where(meet, index + 1, 0), axis=1)
    return jnp.stack([first, last], axis=1)


def cut_columns(matrix, widths):
    parts, column = [], 0
    for w in widths:
        parts.append(matrix[:, column : column + w])
        column += w
    return parts


def update(
    weight,
    first_moment,
    second_moment,
    gradient,
    factor,
    step_rate,
    fix_first,
    fix_second,
    decay_rate,
):
    clipped = gradient * factor
    new_first = BETA_FIRST * first_moment + (1.0 - BETA_FIRST) * clipped
    new_second = BETA_SECOND * second_moment + (1.0 - BETA_SECOND) * clipped * clipped
    stepped = new_first / fix_first / (jnp.sqrt(new_second / fix_second) + ADAM_EPS)
    return weight - step_rate * (stepped + decay_rate * weight)


def per_device(
    act_in,
    packing,
    enc_weights,
    enc_first,
    enc_second,
    dec_weights,
    dec_first,
    dec_second,
    enc_norms,
    enc_norm_first,
    enc_norm_second,
    dec_norms,
    dec_norm_first,
    dec_norm_second,
    mask_token,
    dec_position,
    learning_rate,
    step_count,
):
    encoder_side = lax.axis_index("section") == 0
    decoder_side = jnp.logical_not(encoder_side)
    mp_rank = lax.axis_index("mp")
    mp_count = lax.axis_size("mp")
    first_half = mp_rank == 0
    slot_ids = packing[0, 0]
    patch_ids = packing[0, 1]
    local_images = IMG // mp_count
    grid_cells = local_images * GRID
    local_slot = slot_ids - mp_rank * local_images
    inside = jnp.logical_and(local_slot >= 0, local_slot < local_images)
    target = jnp.where(inside, local_slot * GRID + patch_ids, grid_cells)

    local_rows, width = act_in.shape[1], act_in.shape[2]
    real_rows = local_rows * mp_count
    rows = -(-real_rows // ROW_BLOCK) * ROW_BLOCK
    lanes = -(-rows // TILE) * TILE
    part = width // mp_count
    units = FF // mp_count
    head = width // HEADS
    dec_width = dec_position.shape[1]
    dec_part = dec_width // mp_count
    dec_units = FFD // mp_count
    widths = (3 * part, part, units, units, dec_part)
    dec_widths = (dec_part,) * 4 + (dec_units,) * 2
    slots = jnp.pad(slot_ids, (0, lanes - real_rows), constant_values=IMG + 1)
    ranges = key_ranges(slots)

    def halves(own, other, axis):
        return jnp.where(
            first_half,
            jnp.concatenate([own, other], axis=axis),
            jnp.concatenate([other, own], axis=axis),
        )

    (qkv_w, out_w, up_w, down_w, projection), dec_own, norm_rows = gather_all(
        enc_weights[:, 0, :].astype(LOW),
        dec_weights[:, 0, :].astype(LOW),
        pack_norms(enc_norms, dec_norms, 1),
        widths,
    )
    enc_gains, dec_gains = (
        v.astype(LOW).astype(WIDE)
        for v in unpack_norms(
            norm_rows, norm_rows.shape[0] // 8, enc_norms.shape[1], dec_norms.shape[1]
        )
    )
    stream = halves(act_in[0], partner(act_in[0]), 0)
    stream = jnp.pad(stream, ((0, rows - real_rows), (0, 0)))
    first, turned, mixture, log_sum, mix_own = encoder_attend(
        stream, slots, ranges, enc_gains, qkv_w, out_w, head
    )
    after, second, hidden, slope, feed_own = encoder_feed(
        stream, mix_own, partner(mix_own), enc_gains, up_w, down_w, ROW_BLOCK
    )
    encoded = (after + (feed_own.astype(WIDE) + partner(feed_own).astype(WIDE))).astype(LOW)
    projected = mm(encoded, projection)[:real_rows].astype(LOW)
    arrived = from_behind(projected, "section", 1)
    visible = halves(arrived, partner(arrived), 1)

    def join(own, other):
        pieces = list(zip(cut_columns(own, dec_widths), cut_columns(other, dec_widths)))
        qkv = jnp.concatenate([p for pair in pieces[:3] for p in pair], axis=1)
        return (qkv, *(jnp.concatenate(pair, axis=1) for pair in pieces[3:]))

    dec_mats = on_side(decoder_side, join, dec_own, partner(dec_own))
    decoded, grad_visible, grad_qkv, grad_out, grad_up, grad_down, dec_gain_grad = decoder_step(
        visible, target, mask_token, dec_position, dec_gains, *dec_mats, act_in[0], local_images
    )

    seen = grad_visible.astype(LOW)
    left, right = seen[:, :dec_part], seen[:, dec_part:]
    returned = jnp.where(first_half, left, right).astype(WIDE) + partner(
        jnp.where(first_half, right, left)
    ).astype(WIDE)
    grad_projected = from_behind(returned.astype(LOW), "section", -1)
    grad_projected = jnp.pad(grad_projected, ((0, rows - real_rows), (0, 0)))

    def dec_packs(grad_qkv, grad_out, grad_up, grad_down):
        pieces = [grad_qkv.T[:, k * dec_part : (k + 1) * dec_part] for k in range(6)]
        pieces += [grad_out.T[:, :dec_part], grad_out.T[:, dec_part:]]
        for matrix in (grad_up, grad_down):
            pieces += [matrix[:, :dec_units], matrix[:, dec_units:]]
        return tuple(
            jnp.concatenate(pieces[k::2], axis=1).astype(kind) for k, kind in ((0, WIDE), (1, LOW))
        )

    pack_own, pack_other = on_side(
        decoder_side, dec_packs, grad_qkv, grad_out, grad_up, grad_down
    )
    dec_grad = (pack_own + partner(pack_other).astype(WIDE)).astype(LOW)
    dec_gain_grad = dec_gain_grad + partner(dec_gain_grad)

    grad_projection = mm(encoded, grad_projected, 0, 0).astype(LOW)
    end_own = mm(grad_projected, projection, 1, 1).astype(LOW)
    end_other = partner(end_own)
    grad_up_w, grad_down_w, back_own = encoder_feed_back(
        jnp.where(encoder_side, 1, 0).astype(jnp.int32).reshape(1),
        end_own,
        end_other,
        second,
        hidden,
        slope,
        up_w,
        down_w,
    )
    grad_after, grad_low, gains_two = encoder_norm_back(
        after, back_own, partner(back_own), (end_own, end_other), enc_gains, 2, ROW_BLOCK, True
    )
    grad_qkv_w, grad_out_w, start_own = encoder_attend_back(
        slots, ranges, first, turned, mixture, log_sum, grad_low, qkv_w, out_w, head
    )
    grad_stream, gains_one = encoder_norm_back(
        stream, start_own, partner(start_own), (grad_after,), enc_gains, 0, ROW_BLOCK, False
    )
    enc_gain_grad = jnp.concatenate([gains_one[:2], gains_two[:2]], axis=0)
    norm_grads = pack_norms(
        jnp.where(encoder_side, enc_gain_grad, 0.0),
        jnp.where(decoder_side, dec_gain_grad, 0.0),
        norm_rows.shape[0] // 8,
    )
    enc_shard, dec_shard, norm_shard, square_total = scatter_all(
        (grad_qkv_w, grad_out_w, grad_up_w, grad_down_w, grad_projection),
        dec_grad,
        norm_grads,
        encoder_side,
    )
    enc_gain_shard, dec_gain_shard = unpack_norms(
        norm_shard, 1, enc_norms.shape[1], dec_norms.shape[1]
    )
    grad_norm = jnp.sqrt(square_total)
    factor = jnp.minimum(1.0, math.sqrt(PARAMS) / (grad_norm + 1e-06))
    step_value = step_count[0].astype(jnp.float32)
    fix_first = 1.0 - jnp.power(BETA_FIRST, step_value)
    fix_second = 1.0 - jnp.power(BETA_SECOND, step_value)

    def renew(weight, first_moment, second_moment, gradient, rate, decay):
        flat = (-1, 128) if gradient.size % 1024 == 0 else gradient.shape
        gradient = gradient.reshape(flat)
        renewed = update(
            weight.reshape(flat),
            first_moment.reshape(flat),
            second_moment.reshape(flat),
            gradient,
            factor,
            rate,
            fix_first,
            fix_second,
            decay,
        )
        return renewed.reshape(weight.shape), (gradient * factor).reshape(weight.shape)

    step_rate, norm_rate = learning_rate[0], learning_rate[1]
    new_enc, enc_clipped = renew(
        enc_weights, enc_first, enc_second, enc_shard, step_rate, WEIGHT_DECAY
    )
    new_dec, dec_clipped = renew(
        dec_weights, dec_first, dec_second, dec_shard, step_rate, WEIGHT_DECAY
    )
    new_enc_norms, enc_norm_clipped = renew(
        enc_norms, enc_norm_first, enc_norm_second, enc_gain_shard, norm_rate, 0.0
    )
    new_dec_norms, dec_norm_clipped = renew(
        dec_norms, dec_norm_first, dec_norm_second, dec_gain_shard, norm_rate, 0.0
    )
    own_grad = lax.dynamic_slice_in_dim(grad_stream, mp_rank * local_rows, local_rows, axis=0)
    act_out = jnp.where(encoder_side, own_grad, decoded.reshape(local_rows, width))[None]
    return (
        act_out,
        new_enc,
        new_dec,
        new_enc_norms,
        new_dec_norms,
        enc_clipped,
        dec_clipped,
        enc_norm_clipped,
        dec_norm_clipped,
        grad_norm.reshape(1),
    )


def solution(mesh):
    in_specs = (
        P("section", ("dp", "mp"), None),
        P("dp", None, None),
        P(("section", "dp"), "mp", None),
        P(("section", "dp"), "mp", None),
        P(("section", "dp"), "mp", None),
        P(("section", "dp"), "mp", None),
        P(("section", "dp"), "mp", None),
        P(("section", "dp"), "mp", None),
        P(None, ("section", "dp")),
        P(None, ("section", "dp")),
        P(None, ("section", "dp")),
        P(None, ("section", "dp")),
        P(None, ("section", "dp")),
        P(None, ("section", "dp")),
        P(),
        P(),
        P(),
        P(),
    )
    out_specs = (
        P("section", ("dp", "mp"), None),
        P(("section", "dp"), "mp", None),
        P(("section", "dp"), "mp", None),
        P(None, ("section", "dp")),
        P(None, ("section", "dp")),
        P(("section", "dp"), "mp", None),
        P(("section", "dp"), "mp", None),
        P(None, ("section", "dp")),
        P(None, ("section", "dp")),
        P(),
    )
    return jax.shard_map(
        per_device, mesh=mesh, in_specs=in_specs, out_specs=out_specs, check_vma=False
    )
```

```python
import functools
import itertools
import math

import jax
import jax.numpy as jnp
from jax import lax
from jax.experimental import pallas as pl
from jax.experimental.pallas import tpu as pltpu
from jax.sharding import PartitionSpec as P

FF = 4096
GRID = 196
IMG = 12
PARAMS = 16259072

BETA_FIRST = 0.9
BETA_SECOND = 0.999
ADAM_EPS = 1e-08
WEIGHT_DECAY = 0.05
ROW_BLOCK = 240
MOST_VISIBLE = 73
GATHER_ORDERS = ("hlxy", "hlyx", "hlxy", "hlyx", "yxhl")
SCATTER_ORDERS = ("xylh", "yxlh", "xylh", "yxlh", "lhxy")

MESH_ID = pl.DeviceIdType.MESH
EVERY = slice(None)
BOTH = -1
DIMS = "xhly"


class Place:
    def __init__(self):
        s, depth, core = lax.axis_index("section"), lax.axis_index("dp"), lax.axis_index("mp")
        y, low, high = depth % 2, (depth // 2) % 2, depth // 4
        self.at = {"x": s, "h": high, "l": low, "y": y}
        self.s, self.core = s, core
        self.device = {
            "x": (1 - s, depth, core),
            "h": (s, depth + 4 - 8 * high, core),
            "l": (s, depth + 2 - 4 * low, core),
            "y": (s, depth + 1 - 2 * y, core),
            "c": (s, depth, 1 - core),
        }

    def greet(self):
        barrier = pltpu.get_barrier_semaphore()
        for name in self.device:
            pl.semaphore_signal(
                barrier, inc=1, device_id=self.device[name], device_id_type=MESH_ID
            )
        pl.semaphore_wait(barrier, len(self.device))


def run(condition, action):
    if condition is None:
        action()
    else:
        pl.when(condition)(action)


def gather_kernel(chunks, n_in, n_out, ahead, lag, *refs):
    ins, outs = refs[:n_in], refs[n_in : n_in + n_out]
    send, recv, local = refs[n_in + n_out :]
    here = Place()
    count = len(chunks)

    def region(chunk, gathered, sender):
        at = [
            EVERY if d in gathered else 1 - here.at[d] if d == sender else here.at[d] for d in DIMS
        ]
        return outs[chunk[1]].at[(*at, EVERY, pl.ds(chunk[3], chunk[4]))]

    def own(i):
        chunk = chunks[i]
        return pltpu.make_async_copy(
            ins[chunk[0]].at[:, pl.ds(chunk[2], chunk[4])], region(chunk, "", None), local.at[i]
        )

    def copy(i, stage, incoming):
        chunk = chunks[i]
        order = chunk[5]
        axis = order[stage]
        block = region(chunk, order[:stage], axis if incoming else None)
        source = block
        if stage == 0 and not incoming:
            source = ins[chunk[0]].at[:, pl.ds(chunk[2], chunk[4])]
        return pltpu.make_async_remote_copy(
            src_ref=source,
            dst_ref=block,
            send_sem=send.at[i, stage],
            recv_sem=recv.at[i, stage],
            device_id=here.device[axis],
            device_id_type=MESH_ID,
        )

    def roles(i, stage):
        order, owner = chunks[i][5], chunks[i][6]
        if owner == BOTH:
            return None, None
        if order[stage] == "x":
            return here.s != owner, here.s == owner
        if "x" in order[:stage]:
            return here.s == owner, here.s == owner
        return None, None

    def begin(i, stage):
        run(roles(i, stage)[0], lambda: copy(i, stage, False).start())

    def arrive(i, stage):
        run(roles(i, stage)[1], lambda: copy(i, stage, True).wait_recv())
        if stage == 0:
            own(i).wait()

    here.greet()
    for i in range(count):
        own(i).start()
    for i in range(min(ahead, count)):
        begin(i, 0)
    for step in range(count + sum(lag)):
        for stage in range(3):
            i = step - sum(lag[:stage])
            if not 0 <= i < count:
                continue
            arrive(i, stage)
            begin(i, stage + 1)
            if stage == 0 and i + ahead < count:
                begin(i + ahead, 0)
    for i in range(count):
        arrive(i, 3)
    for i in range(count):
        for stage in range(4):
            run(
                roles(i, stage)[0],
                lambda i=i, stage=stage: copy(i, stage, False).wait_send(),
            )


def gather_weights(shards, outputs, chunks, collective_id, ahead=4, lag=(1, 1)):
    count = len(chunks)
    call = pl.pallas_call(
        functools.partial(gather_kernel, chunks, len(shards), len(outputs), ahead, lag),
        out_shape=[
            jax.ShapeDtypeStruct((2, 2, 2, 2, rows, width), dtype) for rows, width, dtype in outputs
        ],
        in_specs=[pl.BlockSpec(memory_space=pltpu.VMEM)] * len(shards),
        out_specs=[pl.BlockSpec(memory_space=pl.ANY)] * len(outputs),
        scratch_shapes=[
            pltpu.SemaphoreType.DMA((count, 4)),
            pltpu.SemaphoreType.DMA((count, 4)),
            pltpu.SemaphoreType.DMA((count,)),
        ],
        compiler_params=pltpu.CompilerParams(
            collective_id=collective_id, has_side_effects=True, vmem_limit_bytes=40 * 2**20
        ),
    )
    results = call(*shards)
    return [
        r.reshape(16 * rows, width) for r, (rows, width, _) in zip(results, outputs, strict=True)
    ]


def spread(total, pieces, unit=128):
    units = total // unit
    widths = [units // pieces + (1 if k < units % pieces else 0) for k in range(pieces)]
    return [w * unit for w in widths if w]


def chunk_list(widths, pieces, owner, orders):
    chunks = []
    column = turn = 0
    for index, (width, count) in enumerate(zip(widths, pieces, strict=True)):
        begin = 0
        for piece in spread(width, count):
            chunks.append((index, begin, column, piece, orders[turn % len(orders)], owner))
            begin += piece
            column += piece
            turn += 1
    return chunks


def left_after(order, stage):
    return [d for d in DIMS if d not in order[: stage + 1]]


def scatter_buffers(order, owner):
    shapes = [(2,) * 3]
    for stage in range(4):
        if order[stage] == "x" and owner != BOTH:
            continue
        shapes.append((2,) * (3 - stage))
    return shapes


def squares(ref):
    def step(k, total):
        block = ref[:, pl.ds(pl.multiple_of(k * 128, 128), 128)].astype(jnp.float32)
        block = block * block
        for r in range(0, block.shape[0], 8):
            total = total + block[r : r + 8]
        return total

    return lax.fori_loop(0, ref.shape[1] // 128, step, jnp.zeros((8, 128), jnp.float32))


def scatter_kernel(chunks, n_in, n_out, ahead, lag, cores, *refs):
    ins, summed, outs = refs[:n_in], refs[n_in], refs[n_in + 1 : n_in + 1 + n_out]
    square_total = refs[n_in + 1 + n_out]
    rest = refs[n_in + n_out + 2 :]
    send, recv, local, square_send, square_recv, square_mine, square_there = rest[:7]
    here = Place()
    s = here.s
    count = len(chunks)
    own, got = [], []
    position = 7
    for chunk in chunks:
        order, owner = chunk[5], chunk[6]
        own.append(rest[position])
        position += 1
        mine = []
        for stage in range(4):
            if order[stage] == "x" and owner != BOTH:
                mine.append(None)
                continue
            mine.append(rest[position])
            position += 1
        got.append(mine)

    def source(i, axis, keep):
        chunk = chunks[i]
        at = [
            (here.at[d] if keep else 1 - here.at[d]) if d == axis else EVERY for d in DIMS
        ]
        return ins[chunk[0]].at[(*at, EVERY, pl.ds(chunk[2], chunk[4]))]

    def load(i):
        return pltpu.make_async_copy(source(i, chunks[i][5][0], True), own[i], local.at[i])

    def spot(i, stage, flip):
        order = chunks[i][5]
        at = []
        for d in DIMS:
            if d == order[0]:
                continue
            if d in order[:stage]:
                at.append(here.at[d])
            elif d == order[stage]:
                at.append(1 - here.at[d] if flip else here.at[d])
            else:
                at.append(EVERY)
        return tuple(at)

    def copy(i, stage, incoming):
        order = chunks[i][5]
        axis = order[stage]
        moved = got[i][stage] is None
        src = source(i, axis, False) if stage == 0 else own[i].at[spot(i, stage, True)]
        if not moved:
            there = mine = got[i][stage]
        elif stage == 0:
            there = mine = own[i]
        else:
            there, mine = own[i].at[spot(i, stage, True)], own[i].at[spot(i, stage, False)]
        return pltpu.make_async_remote_copy(
            src_ref=mine if incoming else src,
            dst_ref=mine if incoming else there,
            send_sem=send.at[i, stage],
            recv_sem=recv.at[i, stage],
            device_id=here.device[axis],
            device_id_type=MESH_ID,
        )

    def roles(i, stage):
        order, owner = chunks[i][5], chunks[i][6]
        if owner == BOTH:
            return None, None
        if order[stage] == "x":
            return s == owner, s != owner
        if "x" in order[:stage]:
            return None, None
        return s == owner, s == owner

    def begin(i, stage):
        run(roles(i, stage)[0], lambda: copy(i, stage, False).start())

    def arrive(i, stage):
        chunk, a, r = chunks[i], own[i], got[i][stage]
        order, owner = chunk[5], chunk[6]
        run(roles(i, stage)[1], lambda: copy(i, stage, True).wait_recv())
        if stage == 0:
            run(None if owner == BOTH else s == owner, lambda: load(i).wait())
        out = outs[chunk[1]].at[:, pl.ds(chunk[3], chunk[4])]
        place = spot(i, stage, False)
        if stage == 3:
            result = a[place].astype(jnp.float32)
            if r is not None:
                result = result + r[...].astype(jnp.float32)
            out[...] = result
            return
        if r is None:
            return

        def add():
            free = [k for k, p in enumerate(place) if p is EVERY]
            for combo in itertools.product(range(2), repeat=len(free)):
                at = list(place)
                for k, c in zip(free, combo):
                    at[k] = c
                at = tuple(at)
                a[at] = (a[at].astype(jnp.float32) + r[combo].astype(jnp.float32)).astype(a.dtype)

        run(roles(i, stage)[1], add)

    here.greet()
    for i in range(count):
        run(
            None if chunks[i][6] == BOTH else s == chunks[i][6],
            lambda i=i: load(i).start(),
        )
    for i in range(min(ahead, count)):
        begin(i, 0)
    for step in range(count + sum(lag)):
        for stage in range(3, -1, -1):
            i = step - sum(lag[:stage])
            if not 0 <= i < count:
                continue
            arrive(i, stage)
            if stage < 3:
                begin(i, stage + 1)
            if stage == 0 and i + ahead < count:
                begin(i + ahead, 0)
    for i in range(count):
        for stage in range(4):
            run(
                roles(i, stage)[0],
                lambda i=i, stage=stage: copy(i, stage, False).wait_send(),
            )

    value = squares(summed)
    for k, out in enumerate(outs):
        value = value + squares(out) * (1.0 / cores if k == n_out - 1 else 1.0)
    value = jnp.broadcast_to(jnp.sum(value, keepdims=True), (8, 128))
    for k, axis in enumerate("cyxlh"):
        square_mine[k] = value
        move = pltpu.make_async_remote_copy(
            src_ref=square_mine.at[k],
            dst_ref=square_there.at[k],
            send_sem=square_send.at[k],
            recv_sem=square_recv.at[k],
            device_id=here.device[axis],
            device_id_type=MESH_ID,
        )
        move.start()
        move.wait()
        value = value + square_there[k]
    square_total[...] = value


def scatter_grads(parts, summed, outputs, chunks, collective_id, ahead=4, lag=(1, 1, 1)):
    count = len(chunks)
    views = [p.reshape(2, 2, 2, 2, p.shape[0] // 16, p.shape[1]) for p in parts]
    buffers = []
    for chunk in chunks:
        view = views[chunk[0]]
        for lead in scatter_buffers(chunk[5], chunk[6]):
            buffers.append(pltpu.VMEM((*lead, view.shape[4], chunk[4]), view.dtype))
    call = pl.pallas_call(
        functools.partial(scatter_kernel, chunks, len(parts), len(outputs), ahead, lag, lax.axis_size("mp")),
        out_shape=[
            jax.ShapeDtypeStruct((rows, width), jnp.float32) for rows, width in [*outputs, (8, 128)]
        ],
        in_specs=[pl.BlockSpec(memory_space=pl.ANY)] * len(parts)
        + [pl.BlockSpec(memory_space=pltpu.VMEM)],
        out_specs=[pl.BlockSpec(memory_space=pltpu.VMEM)] * (len(outputs) + 1),
        scratch_shapes=[
            pltpu.SemaphoreType.DMA((count, 4)),
            pltpu.SemaphoreType.DMA((count, 4)),
            pltpu.SemaphoreType.DMA((count,)),
            pltpu.SemaphoreType.DMA((5,)),
            pltpu.SemaphoreType.DMA((5,)),
            pltpu.VMEM((5, 8, 128), jnp.float32),
            pltpu.VMEM((5, 8, 128), jnp.float32),
            *buffers,
        ],
        compiler_params=pltpu.CompilerParams(
            collective_id=collective_id, has_side_effects=True, vmem_limit_bytes=56 * 2**20
        ),
    )
    return call(*views, summed)


HEADS = 16
TOGETHER = 4
NORM_EPS = 1e-06
MASKED = -1e30
LOW = jnp.bfloat16
WIDE = jnp.float32


def mm(left, right, left_dim=1, right_dim=0):
    return lax.dot_general(
        left, right, (((left_dim,), (right_dim,)), ((), ())), preferred_element_type=WIDE
    )


def centre(tokens):
    average = jnp.mean(tokens, axis=-1, keepdims=True)
    centred = tokens - average
    spread_ = jnp.mean(centred * centred, axis=-1, keepdims=True)
    scale = lax.rsqrt(spread_ + NORM_EPS)
    return centred * scale, scale


def centre_back(unit, scale, gain, grad):
    pulled = grad * gain
    first = jnp.mean(pulled, axis=-1, keepdims=True)
    second = jnp.mean(pulled * unit, axis=-1, keepdims=True)
    return scale * (pulled - first - unit * second)


def gelu_pair(z):
    cdf = 0.5 * (1.0 + lax.erf(z * math.sqrt(0.5)))
    return z * cdf, cdf + z * (jnp.exp(-0.5 * z * z) * (1.0 / math.sqrt(2.0 * math.pi)))


def decoder_kernel(
    length,
    flag,
    target_row,
    target_column,
    visible_own,
    visible_other,
    mask,
    position,
    gains,
    pack_own,
    pack_other,
    cotangent,
    decoded,
    grad_keep,
    grad_send,
    grad_own,
    grad_other,
    grad_gains,
    qkv_t,
    out_t,
    qkv_rows,
    shares,
    mixture,
    hidden,
    slope,
    grad_rows,
    grad_visible,
    grad_qkv,
    grad_out,
    grad_up,
    grad_down,
):
    image = pl.program_id(0)
    rows, width = decoded.shape[1], decoded.shape[2]
    head = width // HEADS
    units = hidden.shape[1]
    part, half = width // 2, units // 2
    up_at, down_at = 4 * part, 4 * part + half
    scaling = head ** (-0.5)
    packs = (pack_own, pack_other)
    halves = ((slice(0, half), pack_own), (slice(half, units), pack_other))

    @pl.when(image == 0)
    def _():
        for ref in (grad_visible, grad_qkv, grad_out, grad_up, grad_down, grad_gains):
            ref[...] = jnp.zeros_like(ref)
        for which in range(4):
            for k, pack in enumerate(packs):
                at = (2 * which + k) * part
                piece = jnp.transpose(pack[:, which * part : (which + 1) * part])
                if which < 3:
                    qkv_t[at : at + part, :] = piece
                else:
                    out_t[k * part : (k + 1) * part, :] = piece

    packed = target_row.shape[1]
    cell = lax.broadcasted_iota(jnp.int32, (rows, packed), 0)
    wanted = jnp.where(cell < length, cell + image * length, -7)
    chosen = (target_row[...] == wanted).astype(WIDE)
    seen = jnp.max(chosen, axis=1, keepdims=True)
    chosen = chosen.astype(LOW)
    placed_own, placed_other = mm(chosen, visible_own[...]), mm(chosen, visible_other[...])
    left = flag[0] > 0
    placed = jnp.concatenate(
        [
            jnp.where(left, placed_own, placed_other),
            jnp.where(left, placed_other, placed_own),
        ],
        axis=1,
    )
    stream = jnp.where(seen > 0.0, placed, mask[...]) + position[...]

    unit_one, scale_one = centre(stream)
    first = (unit_one * gains[0:1] + gains[1:2]).astype(LOW)
    qkv_rows[...] = mm(qkv_t[...], first, 1, 1).astype(LOW)

    key_index = lax.broadcasted_iota(jnp.int32, (rows, rows), 0)

    def lines(which, h):
        return slice(which * width + h * head, which * width + (h + 1) * head)

    for begin in range(0, HEADS, TOGETHER):
        group = range(begin, begin + TOGETHER)
        scores = [mm(qkv_rows[lines(1, h), :], qkv_rows[lines(0, h), :], 0, 0) * scaling for h in group]
        scores = [jnp.where(key_index < length, s, MASKED) for s in scores]
        weights = [jnp.exp(s - jnp.max(s, axis=0, keepdims=True)) for s in scores]
        group_shares = [w * (1.0 / jnp.sum(w, axis=0, keepdims=True)) for w in weights]
        for h, share in zip(group, group_shares):
            shares[h] = share
            mixture[lines(0, h), :] = mm(qkv_rows[lines(2, h), :], share.astype(LOW)).astype(LOW)
    mixed = mixture[...]
    after = stream + mm(mixed, out_t[...], 0, 0)
    unit_two, scale_two = centre(after)
    second = (unit_two * gains[2:3] + gains[3:4]).astype(LOW)
    piece = 256
    for c in range(0, units, piece):
        pack, at = packs[c // half], up_at + c % half
        z = mm(second, pack[:, at : at + piece])
        h, g = gelu_pair(z)
        hidden[:, c : c + piece] = h.astype(LOW)
        slope[:, c : c + piece] = g
    fed = [mm(hidden[:, cut], pack[:, down_at : down_at + half], 1, 1) for cut, pack in halves]
    decoded[0] = after + (fed[0] + fed[1])

    grad_low = cotangent[0]
    grad_result = grad_low.astype(WIDE)
    turned = jnp.transpose(grad_low)
    second_turned = jnp.transpose(second)
    for c in range(0, units, piece):
        cut = slice(c, c + piece)
        grad_down[:, cut] += mm(turned, hidden[:, cut])
        pack, at = packs[c // half], down_at + c % half
        grad_z = (mm(grad_low, pack[:, at : at + piece]) * slope[:, cut]).astype(LOW)
        hidden[:, cut] = grad_z
        grad_up[:, cut] += mm(second_turned, grad_z)
    pulled = [mm(hidden[:, cut], pack[:, up_at : up_at + half], 1, 1) for cut, pack in halves]
    grad_second = pulled[0] + pulled[1]
    grad_after = grad_result + centre_back(unit_two, scale_two, gains[2:3], grad_second)
    grad_gains[2:3] += jnp.sum(grad_second * unit_two, axis=0, keepdims=True)
    grad_gains[3:4] += jnp.sum(grad_second, axis=0, keepdims=True)

    after_low = grad_after.astype(LOW)
    grad_out[...] += mm(mixed, after_low)
    grad_rows[...] = mm(out_t[...], after_low, 1, 1).astype(LOW)

    for begin in range(0, HEADS, TOGETHER):
        group = range(begin, begin + TOGETHER)
        queries = [qkv_rows[lines(0, h), :] for h in group]
        keys = [qkv_rows[lines(1, h), :] for h in group]
        values = [qkv_rows[lines(2, h), :] for h in group]
        grads_in = [grad_rows[lines(0, h), :] for h in group]
        grad_shares = [mm(v, g, 0, 0) for v, g in zip(values, grads_in)]
        grad_values = [mm(g, shares[h].astype(LOW), 1, 1) for g, h in zip(grads_in, group)]
        grad_scores = []
        for h, g in zip(group, grad_shares):
            share = shares[h]
            inner = jnp.sum(share * g, axis=0, keepdims=True)
            grad_scores.append((share * (g - inner)).astype(LOW))
        for k, h in enumerate(group):
            qkv_rows[lines(0, h), :] = (mm(keys[k], grad_scores[k]) * scaling).astype(LOW)
            qkv_rows[lines(1, h), :] = (mm(queries[k], grad_scores[k], 1, 1) * scaling).astype(LOW)
            qkv_rows[lines(2, h), :] = grad_values[k].astype(LOW)
    grads = qkv_rows[...]
    grad_qkv[...] += mm(grads, first)
    grad_first = mm(grads, qkv_t[...], 0, 0)
    grad_stream = grad_after + centre_back(unit_one, scale_one, gains[0:1], grad_first)
    grad_gains[0:1] += jnp.sum(grad_first * unit_one, axis=0, keepdims=True)
    grad_gains[1:2] += jnp.sum(grad_first, axis=0, keepdims=True)

    cell_lane = lax.broadcasted_iota(jnp.int32, (packed, rows), 1)
    wanted_lane = jnp.where(cell_lane < length, cell_lane + image * length, -7)
    chosen_back = (target_column[...] == wanted_lane).astype(WIDE).astype(LOW)
    grad_visible[...] += mm(chosen_back, grad_stream.astype(LOW))

    @pl.when(image == pl.num_programs(0) - 1)
    def _():
        gathered = grad_visible[...].astype(LOW)
        one, two = gathered[:, :part], gathered[:, part:]
        grad_keep[...] = jnp.where(left, one, two)
        grad_send[...] = jnp.where(left, two, one)
        for k, ref in enumerate((grad_own, grad_other)):
            for which in range(4):
                at = (2 * which + k) * part
                piece = grad_qkv[at : at + part, :] if which < 3 else grad_out[k * part : (k + 1) * part, :]
                ref[:, which * part : (which + 1) * part] = jnp.transpose(piece.astype(LOW))
            cut = slice(k * half, (k + 1) * half)
            ref[:, up_at:down_at] = grad_up[:, cut].astype(LOW)
            ref[:, down_at:] = grad_down[:, cut].astype(LOW)


def decoder_step(
    left, visible_own, visible_other, target, mask, position, gains, pack_own, pack_other, cotangent, images
):
    length, width = position.shape
    rows = -(-length // 16) * 16
    packed = visible_own.shape[0]
    columns = pack_own.shape[1]
    units = columns - 2 * width
    cotangent = jnp.pad(
        cotangent.reshape(images, length, width), ((0, 0), (0, rows - length), (0, 0))
    )
    position = jnp.pad(position, ((0, rows - length), (0, 0)))

    def fixed(shape):
        return pl.BlockSpec(shape, lambda i: (0,) * len(shape), pipeline_mode=pl.Buffered(1))

    per_image = pl.BlockSpec((1, rows, width), lambda i: (i, 0, 0))
    grads = [
        ((packed, width // 2), LOW),
        ((packed, width // 2), LOW),
        ((width, columns), LOW),
        ((width, columns), LOW),
        ((8, width), WIDE),
    ]
    decoded, keep, send, grad_own, grad_other, grad_gains = pl.pallas_call(
        functools.partial(decoder_kernel, length),
        grid=(images,),
        out_shape=[jax.ShapeDtypeStruct((images, rows, width), WIDE)]
        + [jax.ShapeDtypeStruct(s, d) for s, d in grads],
        in_specs=[
            pl.BlockSpec(memory_space=pltpu.SMEM),
            fixed((1, packed)),
            fixed((packed, 1)),
            fixed((packed, width // 2)),
            fixed((packed, width // 2)),
            fixed((1, width)),
            fixed((rows, width)),
            fixed((4, width)),
            fixed((width, columns)),
            fixed((width, columns)),
            per_image,
        ],
        out_specs=[per_image] + [fixed(s) for s, _ in grads],
        scratch_shapes=[
            pltpu.VMEM((3 * width, width), LOW),
            pltpu.VMEM((width, width), LOW),
            pltpu.VMEM((3 * width, rows), LOW),
            pltpu.VMEM((HEADS, rows, rows), WIDE),
            pltpu.VMEM((width, rows), LOW),
            pltpu.VMEM((rows, units), LOW),
            pltpu.VMEM((rows, units), WIDE),
            pltpu.VMEM((width, rows), LOW),
            pltpu.VMEM((packed, width), WIDE),
            pltpu.VMEM((3 * width, width), WIDE),
            pltpu.VMEM((width, width), WIDE),
            pltpu.VMEM((width, units), WIDE),
            pltpu.VMEM((width, units), WIDE),
        ],
        compiler_params=pltpu.CompilerParams(
            dimension_semantics=("arbitrary",), vmem_limit_bytes=60 * 2**20
        ),
    )(
        left.astype(jnp.int32).reshape(1),
        target[None, :],
        target[:, None],
        visible_own,
        visible_other,
        mask[None, :],
        position,
        gains,
        pack_own,
        pack_other,
        cotangent,
    )
    decoded = decoded[:, :length].reshape(images * length, width)
    return decoded, keep, send, grad_own, grad_other, grad_gains[:4]


TILE = 256
GROUP = 4


def fixed(shape):
    return pl.BlockSpec(shape, lambda i: (0,) * len(shape), pipeline_mode=pl.Buffered(1))


def down_rows(rows, width):
    return pl.BlockSpec((rows, width), lambda i: (i, 0))


def params(megabytes=60):
    return pltpu.CompilerParams(
        dimension_semantics=("arbitrary",), vmem_limit_bytes=megabytes * 2**20
    )


def attend_kernel(
    head, bounds, stream, slots_row, slots_column, gains, qkv_w, out_w, first, turned, mixture, log_sum, partial
):
    rows, width = stream.shape
    part, lanes = mixture.shape
    tiles = lanes // TILE
    scaling = head ** (-0.5)
    unit, _ = centre(stream[...].astype(WIDE))
    first[...] = (unit * gains[0:1] + gains[1:2]).astype(LOW)
    turned[:, rows:] = jnp.zeros((3 * part, lanes - rows), LOW)
    for c in range(0, 3 * part, TILE):
        weight = jnp.transpose(qkv_w[:, c : c + TILE])
        turned[c : c + TILE, :rows] = mm(weight, first[...], 1, 1).astype(LOW)

    def at(which, h, tile):
        return (
            pl.ds(pl.multiple_of(which * part + h * head, head), head),
            pl.ds(pl.multiple_of(tile * TILE, TILE), TILE),
        )

    def step(n, carry):
        group, i = n // tiles, n % tiles
        heads = [group * GROUP + g for g in range(GROUP)]
        lane_i = pl.ds(pl.multiple_of(i * TILE, TILE), TILE)
        queries = [turned[at(0, h, i)] for h in heads]
        slot_i = slots_row[:, lane_i]

        def inner(j, state):
            same = slots_column[pl.ds(pl.multiple_of(j * TILE, TILE), TILE), :] == slot_i
            scores = [mm(turned[at(1, h, j)], q, 0, 0) * scaling for h, q in zip(heads, queries)]
            scores = [jnp.where(same, s, MASKED) for s in scores]
            highs = [
                jnp.maximum(state[g][0], jnp.max(s, axis=0, keepdims=True))
                for g, s in enumerate(scores)
            ]
            weights = [jnp.exp(s - high) for s, high in zip(scores, highs)]
            fixes = [jnp.exp(state[g][0] - high) for g, high in enumerate(highs)]
            sums = [jnp.sum(w, axis=0, keepdims=True) for w in weights]
            mixes = [mm(turned[at(2, h, j)], w.astype(LOW)) for h, w in zip(heads, weights)]
            return tuple(
                (highs[g], state[g][1] * fixes[g] + sums[g], state[g][2] * fixes[g] + mixes[g])
                for g in range(GROUP)
            )

        begin = (
            jnp.full((1, TILE), MASKED, WIDE),
            jnp.zeros((1, TILE), WIDE),
            jnp.zeros((head, TILE), WIDE),
        )
        state = lax.fori_loop(bounds[i, 0], bounds[i, 1], inner, (begin,) * GROUP)
        for g, h in enumerate(heads):
            high, total, mixed = state[g]
            mixture[at(0, h, i)] = (mixed / total).astype(LOW)
            log_sum[pl.ds(h, 1), lane_i] = high + jnp.log(total)
        return carry

    lax.fori_loop(0, part // head // GROUP * tiles, step, 0)
    mixed = jnp.transpose(mixture[...])[:rows]
    for c in range(0, width, TILE):
        partial[:, c : c + TILE] = mm(mixed, out_w[c : c + TILE, :], 1, 1).astype(LOW)


def encoder_attend(stream, slots, bounds, gains, qkv_w, out_w, head):
    rows, width = stream.shape
    lanes = slots.shape[0]
    part = out_w.shape[1]
    return pl.pallas_call(
        functools.partial(attend_kernel, head),
        in_specs=[pl.BlockSpec(memory_space=pltpu.SMEM)]
        + [pl.BlockSpec(memory_space=pltpu.VMEM)] * 6,
        out_specs=[pl.BlockSpec(memory_space=pltpu.VMEM)] * 5,
        out_shape=[
            jax.ShapeDtypeStruct((rows, width), LOW),
            jax.ShapeDtypeStruct((3 * part, lanes), LOW),
            jax.ShapeDtypeStruct((part, lanes), LOW),
            jax.ShapeDtypeStruct((part // head, lanes), WIDE),
            jax.ShapeDtypeStruct((rows, width), LOW),
        ],
        compiler_params=pltpu.CompilerParams(vmem_limit_bytes=60 * 2**20),
    )(bounds, stream, slots[None, :], slots[:, None], gains, qkv_w, out_w)


def attend_back_kernel(
    head,
    bounds,
    slots_row,
    slots_column,
    first,
    turned,
    mixture,
    log_sum,
    grad_low,
    qkv_w,
    out_w,
    grad_qkv_w,
    grad_out_w,
    partial,
    grad_mixture,
    grad_turned,
    inner_sum,
    key_sum,
    value_sum,
):
    rows, width = grad_low.shape
    part, lanes = mixture.shape
    tiles = lanes // TILE
    scaling = head ** (-0.5)
    grad_mixture[:, rows:] = jnp.zeros((part, lanes - rows), LOW)
    for c in range(0, width, TILE):
        grad_out_w[c : c + TILE, :] = jnp.transpose(
            mm(mixture[:, :rows], grad_low[:, c : c + TILE]).astype(LOW)
        )
    for c in range(0, part, TILE):
        weight = jnp.transpose(out_w[:, c : c + TILE])
        grad_mixture[c : c + TILE, :rows] = mm(weight, grad_low[...], 1, 1).astype(LOW)
    for h in range(part // head):
        cut = slice(h * head, (h + 1) * head)
        inner_sum[h : h + 1, :] = jnp.sum(
            grad_mixture[cut, :].astype(WIDE) * mixture[cut, :].astype(WIDE), axis=0, keepdims=True
        )

    def at(which, h, tile):
        return (
            pl.ds(pl.multiple_of(which * part + h * head, head), head),
            pl.ds(pl.multiple_of(tile * TILE, TILE), TILE),
        )

    def over_group(group, carry):
        heads = [group * GROUP + g for g in range(GROUP)]
        key_sum[...] = jnp.zeros_like(key_sum)
        value_sum[...] = jnp.zeros_like(value_sum)

        def over_queries(i, carry):
            lane_i = pl.ds(pl.multiple_of(i * TILE, TILE), TILE)
            slot_i = slots_row[:, lane_i]
            queries = [turned[at(0, h, i)] for h in heads]
            grads = [grad_mixture[at(0, h, i)] for h in heads]
            logs = [log_sum[pl.ds(h, 1), lane_i] for h in heads]
            sums = [inner_sum[pl.ds(h, 1), lane_i] for h in heads]

            def inner(j, state):
                lane_j = pl.ds(pl.multiple_of(j * TILE, TILE), TILE)
                same = slots_column[lane_j, :] == slot_i
                cuts = [slice(g * head, (g + 1) * head) for g in range(GROUP)]
                keys = [turned[at(1, h, j)] for h in heads]
                values = [turned[at(2, h, j)] for h in heads]
                scores = [mm(k, q, 0, 0) * scaling for k, q in zip(keys, queries)]
                grad_shares = [mm(v, g, 0, 0) for v, g in zip(values, grads)]
                shares = [
                    jnp.exp(jnp.where(same, s, MASKED) - log) for s, log in zip(scores, logs)
                ]
                grad_scores = [
                    (s * (g - total)).astype(LOW) for s, g, total in zip(shares, grad_shares, sums)
                ]
                for g, cut in enumerate(cuts):
                    value_sum[cut, lane_j] += mm(grads[g], shares[g].astype(LOW), 1, 1)
                for g, cut in enumerate(cuts):
                    key_sum[cut, lane_j] += mm(queries[g], grad_scores[g], 1, 1)
                return tuple(
                    state[g] + mm(keys[g], grad_scores[g]) for g in range(GROUP)
                )

            begin = (jnp.zeros((head, TILE), WIDE),) * GROUP
            state = lax.fori_loop(bounds[i, 0], bounds[i, 1], inner, begin)
            for g, h in enumerate(heads):
                grad_turned[at(0, h, i)] = (state[g] * scaling).astype(LOW)
            return carry

        lax.fori_loop(0, tiles, over_queries, 0)
        size = GROUP * head
        key_at = pl.ds(pl.multiple_of(part + group * size, size), size)
        value_at = pl.ds(pl.multiple_of(2 * part + group * size, size), size)
        grad_turned[key_at, :] = (key_sum[...] * scaling).astype(LOW)
        grad_turned[value_at, :] = value_sum[...].astype(LOW)
        return carry

    lax.fori_loop(0, part // head // GROUP, over_group, 0)
    for c in range(0, 3 * part, TILE):
        grad_qkv_w[:, c : c + TILE] = jnp.transpose(
            mm(grad_turned[c : c + TILE, :rows], first[...]).astype(LOW)
        )
    for c in range(0, width, TILE):
        partial[:, c : c + TILE] = jnp.transpose(
            mm(qkv_w[c : c + TILE, :], grad_turned[:, :rows]).astype(LOW)
        )


def encoder_attend_back(
    slots, bounds, first, turned, mixture, log_sum, grad_low, qkv_w, out_w, head
):
    rows, width = first.shape
    part, lanes = mixture.shape
    return pl.pallas_call(
        functools.partial(attend_back_kernel, head),
        in_specs=[pl.BlockSpec(memory_space=pltpu.SMEM)]
        + [pl.BlockSpec(memory_space=pltpu.VMEM)] * 9,
        out_specs=[pl.BlockSpec(memory_space=pltpu.VMEM)] * 3,
        out_shape=[
            jax.ShapeDtypeStruct((width, 3 * part), LOW),
            jax.ShapeDtypeStruct((width, part), LOW),
            jax.ShapeDtypeStruct((rows, width), LOW),
        ],
        scratch_shapes=[
            pltpu.VMEM((part, lanes), LOW),
            pltpu.VMEM((3 * part, lanes), LOW),
            pltpu.VMEM((part // head, lanes), WIDE),
            pltpu.VMEM((GROUP * head, lanes), WIDE),
            pltpu.VMEM((GROUP * head, lanes), WIDE),
        ],
        compiler_params=pltpu.CompilerParams(vmem_limit_bytes=60 * 2**20),
    )(
        bounds,
        slots[None, :],
        slots[:, None],
        first,
        turned,
        mixture,
        log_sum,
        grad_low,
        qkv_w,
        out_w,
    )


def feed_kernel(stream, own, other, gains, up_w, down_w, after, second, hidden, slope, partial):
    summed = stream[...].astype(WIDE) + (own[...].astype(WIDE) + other[...].astype(WIDE))
    after[...] = summed
    unit, _ = centre(summed)
    second[...] = (unit * gains[2:3] + gains[3:4]).astype(LOW)
    units = up_w.shape[1]
    for c in range(0, units, TILE):
        cut = slice(c, c + TILE)
        h, g = gelu_pair(mm(second[...], up_w[:, cut]))
        hidden[:, cut] = h.astype(LOW)
        slope[:, cut] = g.astype(LOW)
    partial[...] = mm(hidden[...], down_w[...], 1, 1).astype(LOW)


def encoder_feed(stream, own, other, gains, up_w, down_w, block):
    rows, width = stream.shape
    units = up_w.shape[1]
    wide, tall = down_rows(block, width), down_rows(block, units)
    return pl.pallas_call(
        feed_kernel,
        grid=(rows // block,),
        in_specs=[wide, wide, wide, fixed((4, width)), fixed(up_w.shape), fixed(down_w.shape)],
        out_specs=[wide, wide, tall, tall, wide],
        out_shape=[
            jax.ShapeDtypeStruct((rows, width), WIDE),
            jax.ShapeDtypeStruct((rows, width), LOW),
            jax.ShapeDtypeStruct((rows, units), LOW),
            jax.ShapeDtypeStruct((rows, units), LOW),
            jax.ShapeDtypeStruct((rows, width), LOW),
        ],
        compiler_params=params(),
    )(stream, own, other, gains, up_w, down_w)


def feed_back_kernel(
    counts,
    own,
    other,
    second,
    hidden,
    slope,
    up_w,
    down_w,
    grad_up,
    grad_down,
    partial,
    grad_low,
    grad_turned,
    second_turned,
    total,
):
    @pl.when(pl.program_id(0) == 0)
    def _():
        grad_low[...] = (own[...].astype(WIDE) + other[...].astype(WIDE)).astype(LOW)
        grad_turned[...] = jnp.transpose(grad_low[...])
        second_turned[...] = jnp.transpose(second[...])
        total[...] = jnp.zeros_like(total)

    down = mm(grad_turned[...], hidden[...])
    grad_down[...] = jnp.where(counts[0] > 0, down, jnp.zeros_like(down)).astype(LOW)
    grad_z = (mm(grad_low[...], down_w[...]) * slope[...].astype(WIDE)).astype(LOW)
    grad_up[...] = mm(second_turned[...], grad_z).astype(LOW)
    total[...] += mm(grad_z, up_w[...], 1, 1)

    @pl.when(pl.program_id(0) == pl.num_programs(0) - 1)
    def _():
        partial[...] = total[...].astype(LOW)


def encoder_feed_back(counts, own, other, second, hidden, slope, up_w, down_w):
    rows, width = own.shape
    units = up_w.shape[1]
    piece = 256
    whole = fixed((rows, width))
    tall = pl.BlockSpec((rows, piece), lambda i: (0, i))
    weight = pl.BlockSpec((width, piece), lambda i: (0, i))
    return pl.pallas_call(
        feed_back_kernel,
        grid=(units // piece,),
        in_specs=[pl.BlockSpec(memory_space=pltpu.SMEM)]
        + [whole, whole, whole, tall, tall, weight, weight],
        out_specs=[weight, weight, whole],
        out_shape=[
            jax.ShapeDtypeStruct((width, units), LOW),
            jax.ShapeDtypeStruct((width, units), LOW),
            jax.ShapeDtypeStruct((rows, width), LOW),
        ],
        scratch_shapes=[
            pltpu.VMEM((rows, width), LOW),
            pltpu.VMEM((width, rows), LOW),
            pltpu.VMEM((width, rows), LOW),
            pltpu.VMEM((rows, width), WIDE),
        ],
        compiler_params=params(),
    )(counts, own, other, second, hidden, slope, up_w, down_w)


def norm_back_kernel(tokens, own, other, skip_own, skip_other, gains, grad, grad_low, grad_gains, *, at):
    @pl.when(pl.program_id(0) == 0)
    def _():
        grad_gains[...] = jnp.zeros_like(grad_gains)

    pulled = own[...].astype(WIDE) + other[...].astype(WIDE)
    unit, scale = centre(tokens[...].astype(WIDE))
    result = skip_own[...].astype(WIDE)
    if skip_other is not None:
        result = result + skip_other[...].astype(WIDE)
    result = result + centre_back(unit, scale, gains[at : at + 1], pulled)
    grad[...] = result
    if grad_low is not None:
        grad_low[...] = result.astype(LOW)
    grad_gains[0:1] += jnp.sum(pulled * unit, axis=0, keepdims=True)
    grad_gains[1:2] += jnp.sum(pulled, axis=0, keepdims=True)


def encoder_norm_back(tokens, own, other, skip, gains, at, block, low):
    rows, width = tokens.shape
    wide = down_rows(block, width)
    two = len(skip) == 2

    def kernel(*refs):
        refs = list(refs)
        if not two:
            refs.insert(4, None)
        if not low:
            refs.insert(7, None)
        norm_back_kernel(*refs, at=at)

    shapes = [jax.ShapeDtypeStruct((rows, width), WIDE)]
    if low:
        shapes.append(jax.ShapeDtypeStruct((rows, width), LOW))
    shapes.append(jax.ShapeDtypeStruct((8, width), WIDE))
    return pl.pallas_call(
        kernel,
        grid=(rows // block,),
        in_specs=[wide, wide, wide] + [wide] * len(skip) + [fixed((4, width))],
        out_specs=[wide] * (2 if low else 1) + [fixed((8, width))],
        out_shape=shapes,
        compiler_params=params(),
    )(tokens, own, other, *skip, gains)


def from_behind(value, axis, by):
    length = lax.axis_size(axis)
    pairs = [(i, i + by) for i in range(length) if 0 <= i + by < length]
    return lax.ppermute(value, axis, pairs)


def partner(value):
    length = lax.axis_size("mp")
    return lax.ppermute(value, "mp", [(i, (i + 1) % length) for i in range(length)])


def is_fast():
    return lax.axis_size("section") == 2 and lax.axis_size("dp") == 8


def plan(widths, pieces, dec_width, dec_pieces, orders):
    enc = chunk_list(widths, pieces, 0, orders)
    dec = [
        (len(widths), b, c, w, o, k)
        for _, b, c, w, o, k in chunk_list((dec_width,), (dec_pieces,), 1, orders)
    ]
    return enc[:8] + dec + enc[8:]


def gather_all(low_enc, low_dec, norms, widths):
    count = len(widths)
    if not is_fast():
        both = ("section", "dp")
        enc = lax.all_gather(low_enc, both, axis=0, tiled=True)
        dec = lax.all_gather(low_dec, both, axis=0, tiled=True)
        rows = lax.all_gather(norms, both, axis=0, tiled=True)
        parts, column = [], 0
        for w in widths:
            parts.append(enc[:, column : column + w])
            column += w
        return parts, dec, rows
    columns = [sum(widths[:k]) for k in range(count + 1)]
    ahead = [low_enc[:, : columns[3]], low_enc[:, columns[4] :]]
    near = (*widths[:3], widths[4])
    chunks = plan(near, (4, 1, 4, 2), low_dec.shape[1], 4, GATHER_ORDERS)
    outputs = [(low_enc.shape[0], w, LOW) for w in near]
    outputs += [(low_dec.shape[0], low_dec.shape[1], LOW), (8, 128, WIDE)]
    described = [(k // 4, k, c, b, w, o, own) for k, b, c, w, o, own in chunks]
    described.append((2, 5, 0, 0, 128, "hlyx", BOTH))
    shards = [jnp.concatenate(ahead, axis=1), low_dec, norms]
    results = gather_weights(shards, outputs, described, 1, 4, (1, 3))
    low_down, norm_rows = lax.optimization_barrier(
        (low_enc[:, columns[3] : columns[4]], results[5])
    )
    down = lax.all_gather(low_down, ("section", "dp"), axis=0, tiled=True)
    return [*results[:3], down, results[3]], results[4], norm_rows


def scatter_all(enc_parts, dec, norms, encoder_side):
    widths = [p.shape[1] for p in enc_parts]
    both = ("section", "dp")

    def scattered(v):
        return lax.psum_scatter(v, both, scatter_dimension=0, tiled=True)

    if not is_fast():
        parts = [scattered(jnp.where(encoder_side, p.astype(WIDE), 0.0)) for p in enc_parts]
        dec = scattered(jnp.where(encoder_side, 0.0, dec.astype(WIDE)))
        norms = scattered(norms)
        local = sum(jnp.sum(v * v) for v in (*parts, dec))
        local = local + jnp.sum(norms * norms) / lax.axis_size("mp")
        return jnp.concatenate(parts, axis=1), dec, norms, lax.psum(local, (*both, "mp"))
    down = scattered(enc_parts[3])
    near = (*enc_parts[:3], enc_parts[4])
    near_widths = (*widths[:3], widths[4])
    chunks = plan(near_widths, (4, 1, 4, 2), dec.shape[1], 4, SCATTER_ORDERS)
    described = [(k, k // 4, b, c, w, o, own) for k, b, c, w, o, own in chunks]
    described.append((5, 2, 0, 0, 128, "xylh", BOTH))
    rows = near[0].shape[0] // 16
    outputs = [(rows, sum(near_widths)), (dec.shape[0] // 16, dec.shape[1]), (8, 128)]
    enc, dec, norms, total = scatter_grads(
        [*near, dec, norms], down, outputs, described, 2, 4, (2, 2, 2)
    )
    cut = sum(widths[:3])
    enc = jnp.concatenate([enc[:, :cut], down.astype(WIDE), enc[:, cut:]], axis=1)
    return enc, dec, norms, total[0, 0]


def pack_norms(enc_rows, dec_rows, blocks):
    both = [rows.reshape(4, blocks, -1).transpose(1, 0, 2) for rows in (enc_rows, dec_rows)]
    joined = jnp.concatenate(both, axis=2)
    joined = jnp.pad(joined, ((0, 0), (0, 4), (0, 128 - joined.shape[2])))
    return joined.reshape(blocks * 8, 128)


def unpack_norms(packed, blocks, enc_width, dec_width):
    split = packed.reshape(blocks, 8, 128)[:, :4].transpose(1, 0, 2)
    return (
        split[:, :, :enc_width].reshape(4, -1),
        split[:, :, enc_width : enc_width + dec_width].reshape(4, -1),
    )


def key_ranges(slots):
    tiles = slots.reshape(-1, TILE)
    low, high = jnp.min(tiles, axis=1), jnp.max(tiles, axis=1)
    meet = jnp.logical_and(low[:, None] <= high[None, :], high[:, None] >= low[None, :])
    index = jnp.arange(tiles.shape[0], dtype=jnp.int32)[None, :]
    first = jnp.min(jnp.where(meet, index, tiles.shape[0]), axis=1)
    last = jnp.max(jnp.where(meet, index + 1, 0), axis=1)
    return jnp.stack([first, last], axis=1)


def update(
    weight,
    first_moment,
    second_moment,
    gradient,
    factor,
    step_rate,
    fix_first,
    fix_second,
    decay_rate,
):
    clipped = gradient * factor
    new_first = BETA_FIRST * first_moment + (1.0 - BETA_FIRST) * clipped
    new_second = BETA_SECOND * second_moment + (1.0 - BETA_SECOND) * clipped * clipped
    stepped = new_first / fix_first / (jnp.sqrt(new_second / fix_second) + ADAM_EPS)
    return weight - step_rate * (stepped + decay_rate * weight)


def per_device(
    act_in,
    packing,
    enc_weights,
    enc_first,
    enc_second,
    dec_weights,
    dec_first,
    dec_second,
    enc_norms,
    enc_norm_first,
    enc_norm_second,
    dec_norms,
    dec_norm_first,
    dec_norm_second,
    mask_token,
    dec_position,
    learning_rate,
    step_count,
):
    encoder_side = lax.axis_index("section") == 0
    decoder_side = jnp.logical_not(encoder_side)
    mp_rank = lax.axis_index("mp")
    mp_count = lax.axis_size("mp")
    first_half = mp_rank == 0
    slot_ids = packing[0, 0]
    patch_ids = packing[0, 1]
    local_images = IMG // mp_count
    grid_cells = local_images * GRID
    local_slot = slot_ids - mp_rank * local_images
    inside = jnp.logical_and(local_slot >= 0, local_slot < local_images)
    target = jnp.where(inside, local_slot * GRID + patch_ids, grid_cells)

    local_rows, width = act_in.shape[1], act_in.shape[2]
    real_rows = local_rows * mp_count
    rows = -(-real_rows // ROW_BLOCK) * ROW_BLOCK
    lanes = -(-rows // TILE) * TILE
    part = width // mp_count
    units = FF // mp_count
    head = width // HEADS
    dec_width = dec_position.shape[1]
    dec_part = dec_width // mp_count
    widths = (3 * part, part, units, units, dec_part)
    slots = jnp.pad(slot_ids, (0, lanes - real_rows), constant_values=IMG + 1)
    ranges = key_ranges(slots)

    def halves(own, other, axis):
        return jnp.where(
            first_half,
            jnp.concatenate([own, other], axis=axis),
            jnp.concatenate([other, own], axis=axis),
        )

    (qkv_w, out_w, up_w, down_w, projection), dec_own, norm_rows = gather_all(
        enc_weights[:, 0, :].astype(LOW),
        dec_weights[:, 0, :].astype(LOW),
        pack_norms(enc_norms, dec_norms, 1),
        widths,
    )
    enc_gains, dec_gains = (
        v.astype(LOW).astype(WIDE)
        for v in unpack_norms(
            norm_rows, norm_rows.shape[0] // 8, enc_norms.shape[1], dec_norms.shape[1]
        )
    )
    stream = halves(act_in[0], partner(act_in[0]), 0)
    stream = jnp.pad(stream, ((0, rows - real_rows), (0, 0)))
    first, turned, mixture, log_sum, mix_own = encoder_attend(
        stream, slots, ranges, enc_gains, qkv_w, out_w, head
    )
    after, second, hidden, slope, feed_own = encoder_feed(
        stream, mix_own, partner(mix_own), enc_gains, up_w, down_w, ROW_BLOCK
    )
    encoded = (after + (feed_own.astype(WIDE) + partner(feed_own).astype(WIDE))).astype(LOW)
    shown = min(real_rows, -(-IMG * MOST_VISIBLE // 16) * 16)
    packed = -(-shown // 128) * 128
    projected = mm(encoded[:shown], projection).astype(LOW)
    arrived = from_behind(projected, "section", 1)
    arrived = jnp.pad(arrived, ((0, packed - shown), (0, 0)))
    seen_target = jnp.pad(target[:shown], (0, packed - shown), constant_values=-1)
    decoded, grad_keep, grad_send, dec_grad_own, dec_grad_other, dec_gain_grad = decoder_step(
        first_half,
        arrived,
        partner(arrived),
        seen_target,
        mask_token,
        dec_position,
        dec_gains,
        dec_own,
        partner(dec_own),
        act_in[0],
        local_images,
    )
    returned = grad_keep[:shown] + partner(grad_send[:shown])
    grad_projected = from_behind(returned, "section", -1)
    grad_projected = jnp.pad(grad_projected, ((0, rows - shown), (0, 0)))
    dec_grad = dec_grad_own.astype(WIDE) + partner(dec_grad_other).astype(WIDE)
    dec_grad = dec_grad.astype(LOW)
    dec_gain_grad = dec_gain_grad + partner(dec_gain_grad)

    grad_projection = mm(encoded, grad_projected, 0, 0).astype(LOW)
    end_own = mm(grad_projected, projection, 1, 1).astype(LOW)
    end_other = partner(end_own)
    grad_up_w, grad_down_w, back_own = encoder_feed_back(
        jnp.where(encoder_side, 1, 0).astype(jnp.int32).reshape(1),
        end_own,
        end_other,
        second,
        hidden,
        slope,
        up_w,
        down_w,
    )
    grad_after, grad_low, gains_two = encoder_norm_back(
        after, back_own, partner(back_own), (end_own, end_other), enc_gains, 2, ROW_BLOCK, True
    )
    grad_qkv_w, grad_out_w, start_own = encoder_attend_back(
        slots, ranges, first, turned, mixture, log_sum, grad_low, qkv_w, out_w, head
    )
    grad_stream, gains_one = encoder_norm_back(
        stream, start_own, partner(start_own), (grad_after,), enc_gains, 0, ROW_BLOCK, False
    )
    enc_gain_grad = jnp.concatenate([gains_one[:2], gains_two[:2]], axis=0)
    norm_grads = pack_norms(
        jnp.where(encoder_side, enc_gain_grad, 0.0),
        jnp.where(decoder_side, dec_gain_grad, 0.0),
        norm_rows.shape[0] // 8,
    )
    enc_shard, dec_shard, norm_shard, square_total = scatter_all(
        (grad_qkv_w, grad_out_w, grad_up_w, grad_down_w, grad_projection),
        dec_grad,
        norm_grads,
        encoder_side,
    )
    enc_gain_shard, dec_gain_shard = unpack_norms(
        norm_shard, 1, enc_norms.shape[1], dec_norms.shape[1]
    )
    grad_norm = jnp.sqrt(square_total)
    factor = jnp.minimum(1.0, math.sqrt(PARAMS) / (grad_norm + 1e-06))
    step_value = step_count[0].astype(jnp.float32)
    fix_first = 1.0 - jnp.power(BETA_FIRST, step_value)
    fix_second = 1.0 - jnp.power(BETA_SECOND, step_value)

    def renew(weight, first_moment, second_moment, gradient, rate, decay):
        flat = (-1, 128) if gradient.size % 1024 == 0 else gradient.shape
        gradient = gradient.reshape(flat)
        renewed = update(
            weight.reshape(flat),
            first_moment.reshape(flat),
            second_moment.reshape(flat),
            gradient,
            factor,
            rate,
            fix_first,
            fix_second,
            decay,
        )
        return renewed.reshape(weight.shape), (gradient * factor).reshape(weight.shape)

    step_rate, norm_rate = learning_rate[0], learning_rate[1]
    new_enc, enc_clipped = renew(
        enc_weights, enc_first, enc_second, enc_shard, step_rate, WEIGHT_DECAY
    )
    new_dec, dec_clipped = renew(
        dec_weights, dec_first, dec_second, dec_shard, step_rate, WEIGHT_DECAY
    )
    new_enc_norms, enc_norm_clipped = renew(
        enc_norms, enc_norm_first, enc_norm_second, enc_gain_shard, norm_rate, 0.0
    )
    new_dec_norms, dec_norm_clipped = renew(
        dec_norms, dec_norm_first, dec_norm_second, dec_gain_shard, norm_rate, 0.0
    )
    own_grad = lax.dynamic_slice_in_dim(grad_stream, mp_rank * local_rows, local_rows, axis=0)
    act_out = jnp.where(encoder_side, own_grad, decoded.reshape(local_rows, width))[None]
    return (
        act_out,
        new_enc,
        new_dec,
        new_enc_norms,
        new_dec_norms,
        enc_clipped,
        dec_clipped,
        enc_norm_clipped,
        dec_norm_clipped,
        grad_norm.reshape(1),
    )


def solution(mesh):
    in_specs = (
        P("section", ("dp", "mp"), None),
        P("dp", None, None),
        P(("section", "dp"), "mp", None),
        P(("section", "dp"), "mp", None),
        P(("section", "dp"), "mp", None),
        P(("section", "dp"), "mp", None),
        P(("section", "dp"), "mp", None),
        P(("section", "dp"), "mp", None),
        P(None, ("section", "dp")),
        P(None, ("section", "dp")),
        P(None, ("section", "dp")),
        P(None, ("section", "dp")),
        P(None, ("section", "dp")),
        P(None, ("section", "dp")),
        P(),
        P(),
        P(),
        P(),
    )
    out_specs = (
        P("section", ("dp", "mp"), None),
        P(("section", "dp"), "mp", None),
        P(("section", "dp"), "mp", None),
        P(None, ("section", "dp")),
        P(None, ("section", "dp")),
        P(("section", "dp"), "mp", None),
        P(("section", "dp"), "mp", None),
        P(None, ("section", "dp")),
        P(None, ("section", "dp")),
        P(),
    )
    return jax.shard_map(
        per_device, mesh=mesh, in_specs=in_specs, out_specs=out_specs, check_vma=False
    )
```

```python
import functools
import itertools
import math

import jax
import jax.numpy as jnp
from jax import lax
from jax.experimental import pallas as pl
from jax.experimental.pallas import tpu as pltpu
from jax.sharding import PartitionSpec as P

FF = 4096
GRID = 196
IMG = 12
PARAMS = 16259072

BETA_FIRST = 0.9
BETA_SECOND = 0.999
ADAM_EPS = 1e-08
WEIGHT_DECAY = 0.05
ROW_BLOCK = 240
MOST_VISIBLE = 73
GATHER_ORDERS = ("hlxy", "hlyx", "hlxy", "hlyx", "yxhl")
DEC_GATHER_ORDERS = ("xhly", "xyhl")
DEC_SCATTER_ORDERS = ("ylhx", "ylhx")
GATHER_AHEAD, GATHER_LAG = 4, (1, 3)
SCATTER_AHEAD, SCATTER_LAG = 4, (2, 2, 2)
SCATTER_ORDERS = ("xylh", "yxlh", "xylh", "yxlh", "lhxy")

MESH_ID = pl.DeviceIdType.MESH
EVERY = slice(None)
BOTH = -1
DIMS = "xhly"


class Place:
    def __init__(self):
        s, depth, core = lax.axis_index("section"), lax.axis_index("dp"), lax.axis_index("mp")
        y, low, high = depth % 2, (depth // 2) % 2, depth // 4
        self.at = {"x": s, "h": high, "l": low, "y": y}
        self.s, self.core = s, core
        self.device = {
            "x": (1 - s, depth, core),
            "h": (s, depth + 4 - 8 * high, core),
            "l": (s, depth + 2 - 4 * low, core),
            "y": (s, depth + 1 - 2 * y, core),
            "c": (s, depth, 1 - core),
        }

    def greet(self):
        barrier = pltpu.get_barrier_semaphore()
        for name in self.device:
            pl.semaphore_signal(
                barrier, inc=1, device_id=self.device[name], device_id_type=MESH_ID
            )
        pl.semaphore_wait(barrier, len(self.device))


def run(condition, action):
    if condition is None:
        action()
    else:
        pl.when(condition)(action)


def gather_kernel(chunks, n_in, n_out, ahead, lag, *refs):
    ins, outs = refs[:n_in], refs[n_in : n_in + n_out]
    send, recv, local = refs[n_in + n_out :]
    here = Place()
    count = len(chunks)

    def region(chunk, gathered, sender):
        at = [
            EVERY if d in gathered else 1 - here.at[d] if d == sender else here.at[d] for d in DIMS
        ]
        return outs[chunk[1]].at[(*at, EVERY, pl.ds(chunk[3], chunk[4]))]

    def own(i):
        chunk = chunks[i]
        return pltpu.make_async_copy(
            ins[chunk[0]].at[:, pl.ds(chunk[2], chunk[4])], region(chunk, "", None), local.at[i]
        )

    def copy(i, stage, incoming):
        chunk = chunks[i]
        order = chunk[5]
        axis = order[stage]
        block = region(chunk, order[:stage], axis if incoming else None)
        source = block
        if stage == 0 and not incoming:
            source = ins[chunk[0]].at[:, pl.ds(chunk[2], chunk[4])]
        return pltpu.make_async_remote_copy(
            src_ref=source,
            dst_ref=block,
            send_sem=send.at[i, stage],
            recv_sem=recv.at[i, stage],
            device_id=here.device[axis],
            device_id_type=MESH_ID,
        )

    def roles(i, stage):
        order, owner = chunks[i][5], chunks[i][6]
        if owner == BOTH:
            return None, None
        if order[stage] == "x":
            return here.s != owner, here.s == owner
        if "x" in order[:stage]:
            return here.s == owner, here.s == owner
        return None, None

    def begin(i, stage):
        run(roles(i, stage)[0], lambda: copy(i, stage, False).start())

    def arrive(i, stage):
        run(roles(i, stage)[1], lambda: copy(i, stage, True).wait_recv())
        if stage == 0:
            own(i).wait()

    here.greet()
    for i in range(count):
        own(i).start()
    for i in range(min(ahead, count)):
        begin(i, 0)
    for step in range(count + sum(lag)):
        for stage in range(3):
            i = step - sum(lag[:stage])
            if not 0 <= i < count:
                continue
            arrive(i, stage)
            begin(i, stage + 1)
            if stage == 0 and i + ahead < count:
                begin(i + ahead, 0)
    for i in range(count):
        arrive(i, 3)
    for i in range(count):
        for stage in range(4):
            run(
                roles(i, stage)[0],
                lambda i=i, stage=stage: copy(i, stage, False).wait_send(),
            )


def gather_weights(shards, outputs, chunks, collective_id, ahead=4, lag=(1, 1)):
    count = len(chunks)
    call = pl.pallas_call(
        functools.partial(gather_kernel, chunks, len(shards), len(outputs), ahead, lag),
        out_shape=[
            jax.ShapeDtypeStruct((2, 2, 2, 2, rows, width), dtype) for rows, width, dtype in outputs
        ],
        in_specs=[pl.BlockSpec(memory_space=pltpu.VMEM)] * len(shards),
        out_specs=[pl.BlockSpec(memory_space=pl.ANY)] * len(outputs),
        scratch_shapes=[
            pltpu.SemaphoreType.DMA((count, 4)),
            pltpu.SemaphoreType.DMA((count, 4)),
            pltpu.SemaphoreType.DMA((count,)),
        ],
        compiler_params=pltpu.CompilerParams(
            collective_id=collective_id, has_side_effects=True, vmem_limit_bytes=40 * 2**20
        ),
    )
    results = call(*shards)
    return [
        r.reshape(16 * rows, width) for r, (rows, width, _) in zip(results, outputs, strict=True)
    ]


def spread(total, pieces, unit=128):
    units = total // unit
    widths = [units // pieces + (1 if k < units % pieces else 0) for k in range(pieces)]
    return [w * unit for w in widths if w]


def chunk_list(widths, pieces, owner, orders):
    chunks = []
    column = turn = 0
    for index, (width, count) in enumerate(zip(widths, pieces, strict=True)):
        begin = 0
        for piece in spread(width, count):
            chunks.append((index, begin, column, piece, orders[turn % len(orders)], owner))
            begin += piece
            column += piece
            turn += 1
    return chunks


def left_after(order, stage):
    return [d for d in DIMS if d not in order[: stage + 1]]


def scatter_buffers(order, owner):
    shapes = [(2,) * 3]
    for stage in range(4):
        if order[stage] == "x" and owner != BOTH:
            continue
        shapes.append((2,) * (3 - stage))
    return shapes


def squares(ref):
    def step(k, total):
        block = ref[:, pl.ds(pl.multiple_of(k * 128, 128), 128)].astype(jnp.float32)
        block = block * block
        for r in range(0, block.shape[0], 8):
            total = total + block[r : r + 8]
        return total

    return lax.fori_loop(0, ref.shape[1] // 128, step, jnp.zeros((8, 128), jnp.float32))


def scatter_kernel(chunks, n_in, n_out, ahead, lag, cores, *refs):
    ins, summed, outs = refs[:n_in], refs[n_in], refs[n_in + 1 : n_in + 1 + n_out]
    square_total = refs[n_in + 1 + n_out]
    rest = refs[n_in + n_out + 2 :]
    send, recv, local, square_send, square_recv, square_mine, square_there = rest[:7]
    here = Place()
    s = here.s
    count = len(chunks)
    own, got = [], []
    position = 7
    for chunk in chunks:
        order, owner = chunk[5], chunk[6]
        own.append(rest[position])
        position += 1
        mine = []
        for stage in range(4):
            if order[stage] == "x" and owner != BOTH:
                mine.append(None)
                continue
            mine.append(rest[position])
            position += 1
        got.append(mine)

    def source(i, axis, keep):
        chunk = chunks[i]
        at = [
            (here.at[d] if keep else 1 - here.at[d]) if d == axis else EVERY for d in DIMS
        ]
        return ins[chunk[0]].at[(*at, EVERY, pl.ds(chunk[2], chunk[4]))]

    def load(i):
        return pltpu.make_async_copy(source(i, chunks[i][5][0], True), own[i], local.at[i])

    def spot(i, stage, flip):
        order = chunks[i][5]
        at = []
        for d in DIMS:
            if d == order[0]:
                continue
            if d in order[:stage]:
                at.append(here.at[d])
            elif d == order[stage]:
                at.append(1 - here.at[d] if flip else here.at[d])
            else:
                at.append(EVERY)
        return tuple(at)

    def copy(i, stage, incoming):
        order = chunks[i][5]
        axis = order[stage]
        moved = got[i][stage] is None
        src = source(i, axis, False) if stage == 0 else own[i].at[spot(i, stage, True)]
        if not moved:
            there = mine = got[i][stage]
        elif stage == 0:
            there = mine = own[i]
        else:
            there, mine = own[i].at[spot(i, stage, True)], own[i].at[spot(i, stage, False)]
        return pltpu.make_async_remote_copy(
            src_ref=mine if incoming else src,
            dst_ref=mine if incoming else there,
            send_sem=send.at[i, stage],
            recv_sem=recv.at[i, stage],
            device_id=here.device[axis],
            device_id_type=MESH_ID,
        )

    def roles(i, stage):
        order, owner = chunks[i][5], chunks[i][6]
        if owner == BOTH:
            return None, None
        if order[stage] == "x":
            return s == owner, s != owner
        if "x" in order[:stage]:
            return None, None
        return s == owner, s == owner

    def begin(i, stage):
        run(roles(i, stage)[0], lambda: copy(i, stage, False).start())

    def arrive(i, stage):
        chunk, a, r = chunks[i], own[i], got[i][stage]
        order, owner = chunk[5], chunk[6]
        run(roles(i, stage)[1], lambda: copy(i, stage, True).wait_recv())
        if stage == 0:
            run(None if owner == BOTH else s == owner, lambda: load(i).wait())
        out = outs[chunk[1]].at[:, pl.ds(chunk[3], chunk[4])]
        place = spot(i, stage, False)
        if stage == 3:
            result = a[place].astype(jnp.float32)
            if r is not None:
                result = result + r[...].astype(jnp.float32)
            out[...] = result
            return
        if r is None:
            return

        def add():
            free = [k for k, p in enumerate(place) if p is EVERY]
            for combo in itertools.product(range(2), repeat=len(free)):
                at = list(place)
                for k, c in zip(free, combo):
                    at[k] = c
                at = tuple(at)
                a[at] = (a[at].astype(jnp.float32) + r[combo].astype(jnp.float32)).astype(a.dtype)

        run(roles(i, stage)[1], add)

    here.greet()
    for i in range(count):
        run(
            None if chunks[i][6] == BOTH else s == chunks[i][6],
            lambda i=i: load(i).start(),
        )
    for i in range(min(ahead, count)):
        begin(i, 0)
    for step in range(count + sum(lag)):
        for stage in range(3, -1, -1):
            i = step - sum(lag[:stage])
            if not 0 <= i < count:
                continue
            arrive(i, stage)
            if stage < 3:
                begin(i, stage + 1)
            if stage == 0 and i + ahead < count:
                begin(i + ahead, 0)
    for i in range(count):
        for stage in range(4):
            run(
                roles(i, stage)[0],
                lambda i=i, stage=stage: copy(i, stage, False).wait_send(),
            )

    value = squares(summed)
    for k, out in enumerate(outs):
        value = value + squares(out) * (1.0 / cores if k == n_out - 1 else 1.0)
    value = jnp.broadcast_to(jnp.sum(value, keepdims=True), (8, 128))
    for k, axis in enumerate("cyxlh"):
        square_mine[k] = value
        move = pltpu.make_async_remote_copy(
            src_ref=square_mine.at[k],
            dst_ref=square_there.at[k],
            send_sem=square_send.at[k],
            recv_sem=square_recv.at[k],
            device_id=here.device[axis],
            device_id_type=MESH_ID,
        )
        move.start()
        move.wait()
        value = value + square_there[k]
    square_total[...] = value


def scatter_grads(parts, summed, outputs, chunks, collective_id, ahead=4, lag=(1, 1, 1)):
    count = len(chunks)
    views = [p.reshape(2, 2, 2, 2, p.shape[0] // 16, p.shape[1]) for p in parts]
    buffers = []
    for chunk in chunks:
        view = views[chunk[0]]
        for lead in scatter_buffers(chunk[5], chunk[6]):
            buffers.append(pltpu.VMEM((*lead, view.shape[4], chunk[4]), view.dtype))
    call = pl.pallas_call(
        functools.partial(scatter_kernel, chunks, len(parts), len(outputs), ahead, lag, lax.axis_size("mp")),
        out_shape=[
            jax.ShapeDtypeStruct((rows, width), jnp.float32) for rows, width in [*outputs, (8, 128)]
        ],
        in_specs=[pl.BlockSpec(memory_space=pl.ANY)] * len(parts)
        + [pl.BlockSpec(memory_space=pltpu.VMEM)],
        out_specs=[pl.BlockSpec(memory_space=pltpu.VMEM)] * (len(outputs) + 1),
        scratch_shapes=[
            pltpu.SemaphoreType.DMA((count, 4)),
            pltpu.SemaphoreType.DMA((count, 4)),
            pltpu.SemaphoreType.DMA((count,)),
            pltpu.SemaphoreType.DMA((5,)),
            pltpu.SemaphoreType.DMA((5,)),
            pltpu.VMEM((5, 8, 128), jnp.float32),
            pltpu.VMEM((5, 8, 128), jnp.float32),
            *buffers,
        ],
        compiler_params=pltpu.CompilerParams(
            collective_id=collective_id, has_side_effects=True, vmem_limit_bytes=56 * 2**20
        ),
    )
    return call(*views, summed)


HEADS = 16
TOGETHER = 8
NORM_EPS = 1e-06
MASKED = -1e30
LOW = jnp.bfloat16
WIDE = jnp.float32


def mm(left, right, left_dim=1, right_dim=0):
    return lax.dot_general(
        left, right, (((left_dim,), (right_dim,)), ((), ())), preferred_element_type=WIDE
    )


def centre(tokens):
    average = jnp.mean(tokens, axis=-1, keepdims=True)
    centred = tokens - average
    spread_ = jnp.mean(centred * centred, axis=-1, keepdims=True)
    scale = lax.rsqrt(spread_ + NORM_EPS)
    return centred * scale, scale


def centre_back(unit, scale, gain, grad):
    pulled = grad * gain
    first = jnp.mean(pulled, axis=-1, keepdims=True)
    second = jnp.mean(pulled * unit, axis=-1, keepdims=True)
    return scale * (pulled - first - unit * second)


def gelu_pair(z):
    cdf = 0.5 * (1.0 + lax.erf(z * math.sqrt(0.5)))
    return z * cdf, cdf + z * (jnp.exp(-0.5 * z * z) * (1.0 / math.sqrt(2.0 * math.pi)))


def decoder_kernel(
    length,
    flag,
    target_row,
    target_column,
    visible_own,
    visible_other,
    mask,
    position,
    gains,
    pack_own,
    pack_other,
    cotangent,
    decoded,
    grad_keep,
    grad_send,
    grad_own,
    grad_other,
    grad_gains,
    qkv_t,
    out_t,
    qkv_rows,
    shares,
    mixture,
    hidden,
    slope,
    grad_mixture,
    stream,
    first,
    after,
    grad_low,
    grad_first,
    grad_visible,
    grad_qkv,
    grad_out,
    grad_up,
    grad_down,
):
    step = pl.program_id(0)
    images, rows, width = decoded.shape
    head = width // HEADS
    units = hidden.shape[1]
    part, half = width // 2, units // 2
    up_at, down_at = 4 * part, 4 * part + half
    scaling = head ** (-0.5)
    packs = (pack_own, pack_other)
    halves = ((slice(0, half), pack_own), (slice(half, units), pack_other))

    @pl.when(step == 0)
    def _():
        for ref in (grad_visible, grad_qkv, grad_out, grad_up, grad_down, grad_gains):
            ref[...] = jnp.zeros_like(ref)
        for which in range(4):
            for k, pack in enumerate(packs):
                at = (2 * which + k) * part
                piece = jnp.transpose(pack[:, which * part : (which + 1) * part])
                if which < 3:
                    qkv_t[at : at + part, :] = piece
                else:
                    out_t[k * part : (k + 1) * part, :] = piece

    packed = target_row.shape[1]
    left = flag[0] > 0
    spans = [slice(k * rows, (k + 1) * rows) for k in range(images)]
    for k, span in enumerate(spans):
        number = step * images + k
        cell = lax.broadcasted_iota(jnp.int32, (rows, packed), 0)
        wanted = jnp.where(cell < length, cell + number * length, -7)
        chosen = (target_row[...] == wanted).astype(WIDE)
        seen = jnp.max(chosen, axis=1, keepdims=True)
        chosen = chosen.astype(LOW)
        placed_own, placed_other = mm(chosen, visible_own[...]), mm(chosen, visible_other[...])
        placed = jnp.concatenate(
            [
                jnp.where(left, placed_own, placed_other),
                jnp.where(left, placed_other, placed_own),
            ],
            axis=1,
        )
        stream[span, :] = jnp.where(seen > 0.0, placed, mask[...]) + position[...]

    unit_one, scale_one = centre(stream[...])
    first[...] = (unit_one * gains[0:1] + gains[1:2]).astype(LOW)
    key_index = lax.broadcasted_iota(jnp.int32, (rows, rows), 0)

    def lines(which, h):
        return slice(which * width + h * head, which * width + (h + 1) * head)

    for k, span in enumerate(spans):
        qkv, mixed = qkv_rows.at[k], mixture.at[k]
        qkv[...] = mm(qkv_t[...], first[span, :], 1, 1).astype(LOW)
        for begin in range(0, HEADS, TOGETHER):
            group = range(begin, begin + TOGETHER)
            scores = [mm(qkv[lines(1, h), :], qkv[lines(0, h), :], 0, 0) * scaling for h in group]
            scores = [jnp.where(key_index < length, s, MASKED) for s in scores]
            weights = [jnp.exp(s - jnp.max(s, axis=0, keepdims=True)) for s in scores]
            group_shares = [w * (1.0 / jnp.sum(w, axis=0, keepdims=True)) for w in weights]
            for h, share in zip(group, group_shares):
                shares[k, h] = share
                mixed[lines(0, h), :] = mm(qkv[lines(2, h), :], share.astype(LOW)).astype(LOW)
        after[span, :] = stream[span, :] + mm(mixed[...], out_t[...], 0, 0)

    unit_two, scale_two = centre(after[...])
    second = (unit_two * gains[2:3] + gains[3:4]).astype(LOW)
    piece = 256
    for c in range(0, units, piece):
        pack, at = packs[c // half], up_at + c % half
        z = mm(second, pack[:, at : at + piece])
        h, g = gelu_pair(z)
        hidden[:, c : c + piece] = h.astype(LOW)
        slope[:, c : c + piece] = g
    fed = [mm(hidden[:, cut], pack[:, down_at : down_at + half], 1, 1) for cut, pack in halves]
    result = after[...] + (fed[0] + fed[1])
    for k, span in enumerate(spans):
        decoded[k] = result[span]

    for k, span in enumerate(spans):
        grad_low[span, :] = cotangent[k]
    turned = jnp.transpose(grad_low[...])
    second_turned = jnp.transpose(second)
    for c in range(0, units, piece):
        cut = slice(c, c + piece)
        grad_down[:, cut] += mm(turned, hidden[:, cut])
        pack, at = packs[c // half], down_at + c % half
        grad_z = (mm(grad_low[...], pack[:, at : at + piece]) * slope[:, cut]).astype(LOW)
        hidden[:, cut] = grad_z
        grad_up[:, cut] += mm(second_turned, grad_z)
    pulled = [mm(hidden[:, cut], pack[:, up_at : up_at + half], 1, 1) for cut, pack in halves]
    grad_second = pulled[0] + pulled[1]
    grad_gains[2:3] += jnp.sum(grad_second * unit_two, axis=0, keepdims=True)
    grad_gains[3:4] += jnp.sum(grad_second, axis=0, keepdims=True)
    after[...] = grad_low[...].astype(WIDE) + centre_back(
        unit_two, scale_two, gains[2:3], grad_second
    )

    for k, span in enumerate(spans):
        qkv, mixed, grad_rows = qkv_rows.at[k], mixture.at[k], grad_mixture.at[k]
        after_low = after[span, :].astype(LOW)
        grad_out[...] += mm(mixed[...], after_low)
        grad_rows[...] = mm(out_t[...], after_low, 1, 1).astype(LOW)
        for begin in range(0, HEADS, TOGETHER):
            group = range(begin, begin + TOGETHER)
            queries = [qkv[lines(0, h), :] for h in group]
            keys = [qkv[lines(1, h), :] for h in group]
            values = [qkv[lines(2, h), :] for h in group]
            grads_in = [grad_rows[lines(0, h), :] for h in group]
            grad_shares = [mm(v, g, 0, 0) for v, g in zip(values, grads_in)]
            grad_values = [mm(g, shares[k, h].astype(LOW), 1, 1) for g, h in zip(grads_in, group)]
            grad_scores = []
            for h, g in zip(group, grad_shares):
                share = shares[k, h]
                inner = jnp.sum(share * g, axis=0, keepdims=True)
                grad_scores.append((share * (g - inner)).astype(LOW))
            for n, h in enumerate(group):
                qkv[lines(0, h), :] = (mm(keys[n], grad_scores[n]) * scaling).astype(LOW)
                qkv[lines(1, h), :] = (mm(queries[n], grad_scores[n], 1, 1) * scaling).astype(LOW)
                qkv[lines(2, h), :] = grad_values[n].astype(LOW)
        grad_qkv[...] += mm(qkv[...], first[span, :])
        grad_first[span, :] = mm(qkv[...], qkv_t[...], 0, 0)

    unit_one, scale_one = centre(stream[...])
    pulled = grad_first[...]
    grad_stream = after[...] + centre_back(unit_one, scale_one, gains[0:1], pulled)
    grad_gains[0:1] += jnp.sum(pulled * unit_one, axis=0, keepdims=True)
    grad_gains[1:2] += jnp.sum(pulled, axis=0, keepdims=True)

    for k, span in enumerate(spans):
        cell_lane = lax.broadcasted_iota(jnp.int32, (packed, rows), 1)
        wanted_lane = jnp.where(cell_lane < length, cell_lane + (step * images + k) * length, -7)
        chosen_back = (target_column[...] == wanted_lane).astype(WIDE).astype(LOW)
        grad_visible[...] += mm(chosen_back, grad_stream[span].astype(LOW))

    @pl.when(step == pl.num_programs(0) - 1)
    def _():
        gathered = grad_visible[...].astype(LOW)
        one, two = gathered[:, :part], gathered[:, part:]
        grad_keep[...] = jnp.where(left, one, two)
        grad_send[...] = jnp.where(left, two, one)
        for k, ref in enumerate((grad_own, grad_other)):
            for which in range(4):
                at = (2 * which + k) * part
                piece = grad_qkv[at : at + part, :] if which < 3 else grad_out[k * part : (k + 1) * part, :]
                ref[:, which * part : (which + 1) * part] = jnp.transpose(piece.astype(LOW))
            cut = slice(k * half, (k + 1) * half)
            ref[:, up_at:down_at] = grad_up[:, cut].astype(LOW)
            ref[:, down_at:] = grad_down[:, cut].astype(LOW)


def decoder_step(
    left, visible_own, visible_other, target, mask, position, gains, pack_own, pack_other, cotangent, images
):
    length, width = position.shape
    rows = -(-length // 16) * 16
    packed = visible_own.shape[0]
    columns = pack_own.shape[1]
    units = columns - 2 * width
    cotangent = jnp.pad(
        cotangent.reshape(images, length, width), ((0, 0), (0, rows - length), (0, 0))
    )
    position = jnp.pad(position, ((0, rows - length), (0, 0)))

    def fixed(shape):
        return pl.BlockSpec(shape, lambda i: (0,) * len(shape), pipeline_mode=pl.Buffered(1))

    at_once = 2 if images % 2 == 0 else 1
    per_image = pl.BlockSpec((at_once, rows, width), lambda i: (i, 0, 0))
    tall = at_once * rows
    grads = [
        ((packed, width // 2), LOW),
        ((packed, width // 2), LOW),
        ((width, columns), LOW),
        ((width, columns), LOW),
        ((8, width), WIDE),
    ]
    decoded, keep, send, grad_own, grad_other, grad_gains = pl.pallas_call(
        functools.partial(decoder_kernel, length),
        grid=(images // at_once,),
        out_shape=[jax.ShapeDtypeStruct((images, rows, width), WIDE)]
        + [jax.ShapeDtypeStruct(s, d) for s, d in grads],
        in_specs=[
            pl.BlockSpec(memory_space=pltpu.SMEM),
            fixed((1, packed)),
            fixed((packed, 1)),
            fixed((packed, width // 2)),
            fixed((packed, width // 2)),
            fixed((1, width)),
            fixed((rows, width)),
            fixed((4, width)),
            fixed((width, columns)),
            fixed((width, columns)),
            per_image,
        ],
        out_specs=[per_image] + [fixed(s) for s, _ in grads],
        scratch_shapes=[
            pltpu.VMEM((3 * width, width), LOW),
            pltpu.VMEM((width, width), LOW),
            pltpu.VMEM((at_once, 3 * width, rows), LOW),
            pltpu.VMEM((at_once, HEADS, rows, rows), WIDE),
            pltpu.VMEM((at_once, width, rows), LOW),
            pltpu.VMEM((tall, units), LOW),
            pltpu.VMEM((tall, units), WIDE),
            pltpu.VMEM((at_once, width, rows), LOW),
            pltpu.VMEM((tall, width), WIDE),
            pltpu.VMEM((tall, width), LOW),
            pltpu.VMEM((tall, width), WIDE),
            pltpu.VMEM((tall, width), LOW),
            pltpu.VMEM((tall, width), WIDE),
            pltpu.VMEM((packed, width), WIDE),
            pltpu.VMEM((3 * width, width), WIDE),
            pltpu.VMEM((width, width), WIDE),
            pltpu.VMEM((width, units), WIDE),
            pltpu.VMEM((width, units), WIDE),
        ],
        compiler_params=pltpu.CompilerParams(
            dimension_semantics=("arbitrary",), vmem_limit_bytes=60 * 2**20
        ),
    )(
        left.astype(jnp.int32).reshape(1),
        target[None, :],
        target[:, None],
        visible_own,
        visible_other,
        mask[None, :],
        position,
        gains,
        pack_own,
        pack_other,
        cotangent,
    )
    decoded = decoded[:, :length].reshape(images * length, width)
    return decoded, keep, send, grad_own, grad_other, grad_gains[:4]


TILE = 256
GROUP = 4


def fixed(shape):
    return pl.BlockSpec(shape, lambda i: (0,) * len(shape), pipeline_mode=pl.Buffered(1))


def down_rows(rows, width):
    return pl.BlockSpec((rows, width), lambda i: (i, 0))


def params(megabytes=60):
    return pltpu.CompilerParams(
        dimension_semantics=("arbitrary",), vmem_limit_bytes=megabytes * 2**20
    )


def attend_kernel(
    head, bounds, stream, slots_row, slots_column, gains, qkv_w, out_w, first, turned, mixture, log_sum, partial
):
    rows, width = stream.shape
    part, lanes = mixture.shape
    tiles = lanes // TILE
    scaling = head ** (-0.5)
    unit, _ = centre(stream[...].astype(WIDE))
    first[...] = (unit * gains[0:1] + gains[1:2]).astype(LOW)
    turned[:, rows:] = jnp.zeros((3 * part, lanes - rows), LOW)
    for c in range(0, 3 * part, TILE):
        weight = jnp.transpose(qkv_w[:, c : c + TILE])
        turned[c : c + TILE, :rows] = mm(weight, first[...], 1, 1).astype(LOW)

    def at(which, h, tile):
        return (
            pl.ds(pl.multiple_of(which * part + h * head, head), head),
            pl.ds(pl.multiple_of(tile * TILE, TILE), TILE),
        )

    def step(n, carry):
        group, i = n // tiles, n % tiles
        heads = [group * GROUP + g for g in range(GROUP)]
        lane_i = pl.ds(pl.multiple_of(i * TILE, TILE), TILE)
        queries = [turned[at(0, h, i)] for h in heads]
        slot_i = slots_row[:, lane_i]

        def inner(j, state):
            same = slots_column[pl.ds(pl.multiple_of(j * TILE, TILE), TILE), :] == slot_i
            scores = [mm(turned[at(1, h, j)], q, 0, 0) * scaling for h, q in zip(heads, queries)]
            scores = [jnp.where(same, s, MASKED) for s in scores]
            highs = [
                jnp.maximum(state[g][0], jnp.max(s, axis=0, keepdims=True))
                for g, s in enumerate(scores)
            ]
            weights = [jnp.exp(s - high) for s, high in zip(scores, highs)]
            fixes = [jnp.exp(state[g][0] - high) for g, high in enumerate(highs)]
            sums = [jnp.sum(w, axis=0, keepdims=True) for w in weights]
            mixes = [mm(turned[at(2, h, j)], w.astype(LOW)) for h, w in zip(heads, weights)]
            return tuple(
                (highs[g], state[g][1] * fixes[g] + sums[g], state[g][2] * fixes[g] + mixes[g])
                for g in range(GROUP)
            )

        begin = (
            jnp.full((1, TILE), MASKED, WIDE),
            jnp.zeros((1, TILE), WIDE),
            jnp.zeros((head, TILE), WIDE),
        )
        state = lax.fori_loop(bounds[i, 0], bounds[i, 1], inner, (begin,) * GROUP)
        for g, h in enumerate(heads):
            high, total, mixed = state[g]
            mixture[at(0, h, i)] = (mixed / total).astype(LOW)
            log_sum[pl.ds(h, 1), lane_i] = high + jnp.log(total)
        return carry

    lax.fori_loop(0, part // head // GROUP * tiles, step, 0)
    mixed = jnp.transpose(mixture[...])[:rows]
    for c in range(0, width, TILE):
        partial[:, c : c + TILE] = mm(mixed, out_w[c : c + TILE, :], 1, 1).astype(LOW)


def encoder_attend(stream, slots, bounds, gains, qkv_w, out_w, head):
    rows, width = stream.shape
    lanes = slots.shape[0]
    part = out_w.shape[1]
    return pl.pallas_call(
        functools.partial(attend_kernel, head),
        in_specs=[pl.BlockSpec(memory_space=pltpu.SMEM)]
        + [pl.BlockSpec(memory_space=pltpu.VMEM)] * 6,
        out_specs=[pl.BlockSpec(memory_space=pltpu.VMEM)] * 5,
        out_shape=[
            jax.ShapeDtypeStruct((rows, width), LOW),
            jax.ShapeDtypeStruct((3 * part, lanes), LOW),
            jax.ShapeDtypeStruct((part, lanes), LOW),
            jax.ShapeDtypeStruct((part // head, lanes), WIDE),
            jax.ShapeDtypeStruct((rows, width), LOW),
        ],
        compiler_params=pltpu.CompilerParams(vmem_limit_bytes=60 * 2**20),
    )(bounds, stream, slots[None, :], slots[:, None], gains, qkv_w, out_w)


def attend_back_kernel(
    head,
    bounds,
    slots_row,
    slots_column,
    first,
    turned,
    mixture,
    log_sum,
    grad_low,
    qkv_w,
    out_w,
    grad_qkv_w,
    grad_out_w,
    partial,
    grad_mixture,
    grad_turned,
    inner_sum,
    key_sum,
    value_sum,
):
    rows, width = grad_low.shape
    part, lanes = mixture.shape
    tiles = lanes // TILE
    scaling = head ** (-0.5)
    grad_mixture[:, rows:] = jnp.zeros((part, lanes - rows), LOW)
    for c in range(0, width, TILE):
        grad_out_w[c : c + TILE, :] = jnp.transpose(
            mm(mixture[:, :rows], grad_low[:, c : c + TILE]).astype(LOW)
        )
    for c in range(0, part, TILE):
        weight = jnp.transpose(out_w[:, c : c + TILE])
        grad_mixture[c : c + TILE, :rows] = mm(weight, grad_low[...], 1, 1).astype(LOW)
    for h in range(part // head):
        cut = slice(h * head, (h + 1) * head)
        inner_sum[h : h + 1, :] = jnp.sum(
            grad_mixture[cut, :].astype(WIDE) * mixture[cut, :].astype(WIDE), axis=0, keepdims=True
        )

    def at(which, h, tile):
        return (
            pl.ds(pl.multiple_of(which * part + h * head, head), head),
            pl.ds(pl.multiple_of(tile * TILE, TILE), TILE),
        )

    def over_group(group, carry):
        heads = [group * GROUP + g for g in range(GROUP)]
        key_sum[...] = jnp.zeros_like(key_sum)
        value_sum[...] = jnp.zeros_like(value_sum)

        def over_queries(i, carry):
            lane_i = pl.ds(pl.multiple_of(i * TILE, TILE), TILE)
            slot_i = slots_row[:, lane_i]
            queries = [turned[at(0, h, i)] for h in heads]
            grads = [grad_mixture[at(0, h, i)] for h in heads]
            logs = [log_sum[pl.ds(h, 1), lane_i] for h in heads]
            sums = [inner_sum[pl.ds(h, 1), lane_i] for h in heads]

            def inner(j, state):
                lane_j = pl.ds(pl.multiple_of(j * TILE, TILE), TILE)
                same = slots_column[lane_j, :] == slot_i
                cuts = [slice(g * head, (g + 1) * head) for g in range(GROUP)]
                keys = [turned[at(1, h, j)] for h in heads]
                values = [turned[at(2, h, j)] for h in heads]
                scores = [mm(k, q, 0, 0) * scaling for k, q in zip(keys, queries)]
                grad_shares = [mm(v, g, 0, 0) for v, g in zip(values, grads)]
                shares = [
                    jnp.exp(jnp.where(same, s, MASKED) - log) for s, log in zip(scores, logs)
                ]
                grad_scores = [
                    (s * (g - total)).astype(LOW) for s, g, total in zip(shares, grad_shares, sums)
                ]
                for g, cut in enumerate(cuts):
                    value_sum[cut, lane_j] += mm(grads[g], shares[g].astype(LOW), 1, 1)
                for g, cut in enumerate(cuts):
                    key_sum[cut, lane_j] += mm(queries[g], grad_scores[g], 1, 1)
                return tuple(
                    state[g] + mm(keys[g], grad_scores[g]) for g in range(GROUP)
                )

            begin = (jnp.zeros((head, TILE), WIDE),) * GROUP
            state = lax.fori_loop(bounds[i, 0], bounds[i, 1], inner, begin)
            for g, h in enumerate(heads):
                grad_turned[at(0, h, i)] = (state[g] * scaling).astype(LOW)
            return carry

        lax.fori_loop(0, tiles, over_queries, 0)
        size = GROUP * head
        key_at = pl.ds(pl.multiple_of(part + group * size, size), size)
        value_at = pl.ds(pl.multiple_of(2 * part + group * size, size), size)
        grad_turned[key_at, :] = (key_sum[...] * scaling).astype(LOW)
        grad_turned[value_at, :] = value_sum[...].astype(LOW)
        return carry

    lax.fori_loop(0, part // head // GROUP, over_group, 0)
    for c in range(0, 3 * part, TILE):
        grad_qkv_w[:, c : c + TILE] = jnp.transpose(
            mm(grad_turned[c : c + TILE, :rows], first[...]).astype(LOW)
        )
    for c in range(0, width, TILE):
        partial[:, c : c + TILE] = jnp.transpose(
            mm(qkv_w[c : c + TILE, :], grad_turned[:, :rows]).astype(LOW)
        )


def encoder_attend_back(
    slots, bounds, first, turned, mixture, log_sum, grad_low, qkv_w, out_w, head
):
    rows, width = first.shape
    part, lanes = mixture.shape
    return pl.pallas_call(
        functools.partial(attend_back_kernel, head),
        in_specs=[pl.BlockSpec(memory_space=pltpu.SMEM)]
        + [pl.BlockSpec(memory_space=pltpu.VMEM)] * 9,
        out_specs=[pl.BlockSpec(memory_space=pltpu.VMEM)] * 3,
        out_shape=[
            jax.ShapeDtypeStruct((width, 3 * part), LOW),
            jax.ShapeDtypeStruct((width, part), LOW),
            jax.ShapeDtypeStruct((rows, width), LOW),
        ],
        scratch_shapes=[
            pltpu.VMEM((part, lanes), LOW),
            pltpu.VMEM((3 * part, lanes), LOW),
            pltpu.VMEM((part // head, lanes), WIDE),
            pltpu.VMEM((GROUP * head, lanes), WIDE),
            pltpu.VMEM((GROUP * head, lanes), WIDE),
        ],
        compiler_params=pltpu.CompilerParams(vmem_limit_bytes=60 * 2**20),
    )(
        bounds,
        slots[None, :],
        slots[:, None],
        first,
        turned,
        mixture,
        log_sum,
        grad_low,
        qkv_w,
        out_w,
    )


def feed_kernel(stream, own, other, gains, up_w, down_w, after, second, hidden, slope, partial):
    summed = stream[...].astype(WIDE) + (own[...].astype(WIDE) + other[...].astype(WIDE))
    after[...] = summed
    unit, _ = centre(summed)
    second[...] = (unit * gains[2:3] + gains[3:4]).astype(LOW)
    units = up_w.shape[1]
    for c in range(0, units, TILE):
        cut = slice(c, c + TILE)
        h, g = gelu_pair(mm(second[...], up_w[:, cut]))
        hidden[:, cut] = h.astype(LOW)
        slope[:, cut] = g.astype(LOW)
    partial[...] = mm(hidden[...], down_w[...], 1, 1).astype(LOW)


def encoder_feed(stream, own, other, gains, up_w, down_w, block):
    rows, width = stream.shape
    units = up_w.shape[1]
    wide, tall = down_rows(block, width), down_rows(block, units)
    return pl.pallas_call(
        feed_kernel,
        grid=(rows // block,),
        in_specs=[wide, wide, wide, fixed((4, width)), fixed(up_w.shape), fixed(down_w.shape)],
        out_specs=[wide, wide, tall, tall, wide],
        out_shape=[
            jax.ShapeDtypeStruct((rows, width), WIDE),
            jax.ShapeDtypeStruct((rows, width), LOW),
            jax.ShapeDtypeStruct((rows, units), LOW),
            jax.ShapeDtypeStruct((rows, units), LOW),
            jax.ShapeDtypeStruct((rows, width), LOW),
        ],
        compiler_params=params(),
    )(stream, own, other, gains, up_w, down_w)


def feed_back_kernel(
    counts,
    own,
    other,
    second,
    hidden,
    slope,
    up_w,
    down_w,
    grad_up,
    grad_down,
    partial,
    grad_low,
    grad_turned,
    second_turned,
    total,
):
    @pl.when(pl.program_id(0) == 0)
    def _():
        grad_low[...] = (own[...].astype(WIDE) + other[...].astype(WIDE)).astype(LOW)
        grad_turned[...] = jnp.transpose(grad_low[...])
        second_turned[...] = jnp.transpose(second[...])
        total[...] = jnp.zeros_like(total)

    down = mm(grad_turned[...], hidden[...])
    grad_down[...] = jnp.where(counts[0] > 0, down, jnp.zeros_like(down)).astype(LOW)
    grad_z = (mm(grad_low[...], down_w[...]) * slope[...].astype(WIDE)).astype(LOW)
    grad_up[...] = mm(second_turned[...], grad_z).astype(LOW)
    total[...] += mm(grad_z, up_w[...], 1, 1)

    @pl.when(pl.program_id(0) == pl.num_programs(0) - 1)
    def _():
        partial[...] = total[...].astype(LOW)


def encoder_feed_back(counts, own, other, second, hidden, slope, up_w, down_w):
    rows, width = own.shape
    units = up_w.shape[1]
    piece = 256
    whole = fixed((rows, width))
    tall = pl.BlockSpec((rows, piece), lambda i: (0, i))
    weight = pl.BlockSpec((width, piece), lambda i: (0, i))
    return pl.pallas_call(
        feed_back_kernel,
        grid=(units // piece,),
        in_specs=[pl.BlockSpec(memory_space=pltpu.SMEM)]
        + [whole, whole, whole, tall, tall, weight, weight],
        out_specs=[weight, weight, whole],
        out_shape=[
            jax.ShapeDtypeStruct((width, units), LOW),
            jax.ShapeDtypeStruct((width, units), LOW),
            jax.ShapeDtypeStruct((rows, width), LOW),
        ],
        scratch_shapes=[
            pltpu.VMEM((rows, width), LOW),
            pltpu.VMEM((width, rows), LOW),
            pltpu.VMEM((width, rows), LOW),
            pltpu.VMEM((rows, width), WIDE),
        ],
        compiler_params=params(),
    )(counts, own, other, second, hidden, slope, up_w, down_w)


def norm_back_kernel(tokens, own, other, skip_own, skip_other, gains, grad, grad_low, grad_gains, *, at):
    @pl.when(pl.program_id(0) == 0)
    def _():
        grad_gains[...] = jnp.zeros_like(grad_gains)

    pulled = own[...].astype(WIDE) + other[...].astype(WIDE)
    unit, scale = centre(tokens[...].astype(WIDE))
    result = skip_own[...].astype(WIDE)
    if skip_other is not None:
        result = result + skip_other[...].astype(WIDE)
    result = result + centre_back(unit, scale, gains[at : at + 1], pulled)
    grad[...] = result
    if grad_low is not None:
        grad_low[...] = result.astype(LOW)
    grad_gains[0:1] += jnp.sum(pulled * unit, axis=0, keepdims=True)
    grad_gains[1:2] += jnp.sum(pulled, axis=0, keepdims=True)


def encoder_norm_back(tokens, own, other, skip, gains, at, block, low):
    rows, width = tokens.shape
    wide = down_rows(block, width)
    two = len(skip) == 2

    def kernel(*refs):
        refs = list(refs)
        if not two:
            refs.insert(4, None)
        if not low:
            refs.insert(7, None)
        norm_back_kernel(*refs, at=at)

    shapes = [jax.ShapeDtypeStruct((rows, width), WIDE)]
    if low:
        shapes.append(jax.ShapeDtypeStruct((rows, width), LOW))
    shapes.append(jax.ShapeDtypeStruct((8, width), WIDE))
    return pl.pallas_call(
        kernel,
        grid=(rows // block,),
        in_specs=[wide, wide, wide] + [wide] * len(skip) + [fixed((4, width))],
        out_specs=[wide] * (2 if low else 1) + [fixed((8, width))],
        out_shape=shapes,
        compiler_params=params(),
    )(tokens, own, other, *skip, gains)


def from_behind(value, axis, by):
    length = lax.axis_size(axis)
    pairs = [(i, i + by) for i in range(length) if 0 <= i + by < length]
    return lax.ppermute(value, axis, pairs)


def partner(value):
    length = lax.axis_size("mp")
    return lax.ppermute(value, "mp", [(i, (i + 1) % length) for i in range(length)])


def is_fast():
    return lax.axis_size("section") == 2 and lax.axis_size("dp") == 8


def plan(widths, pieces, dec_width, orders, dec_orders):
    enc = chunk_list(widths, pieces, 0, orders)
    dec = [
        (len(widths), b, c, w, o, k)
        for _, b, c, w, o, k in chunk_list((dec_width,), (4,), 1, dec_orders)
    ]
    for k, chunk in enumerate(dec):
        enc.insert(3 * k + 2, chunk)
    return enc


def gather_all(low_enc, low_dec, norms, widths):
    count = len(widths)
    if not is_fast():
        both = ("section", "dp")
        enc = lax.all_gather(low_enc, both, axis=0, tiled=True)
        dec = lax.all_gather(low_dec, both, axis=0, tiled=True)
        rows = lax.all_gather(norms, both, axis=0, tiled=True)
        parts, column = [], 0
        for w in widths:
            parts.append(enc[:, column : column + w])
            column += w
        return parts, dec, rows
    columns = [sum(widths[:k]) for k in range(count + 1)]
    ahead = [low_enc[:, : columns[3]], low_enc[:, columns[4] :]]
    near = (*widths[:3], widths[4])
    chunks = plan(near, (4, 1, 4, 2), low_dec.shape[1], GATHER_ORDERS, DEC_GATHER_ORDERS)
    outputs = [(low_enc.shape[0], w, LOW) for w in near]
    outputs += [(low_dec.shape[0], low_dec.shape[1], LOW), (8, 128, WIDE)]
    described = [(k // 4, k, c, b, w, o, own) for k, b, c, w, o, own in chunks]
    described.append((2, 5, 0, 0, 128, "hlyx", BOTH))
    shards = [jnp.concatenate(ahead, axis=1), low_dec, norms]
    results = gather_weights(shards, outputs, described, 1, GATHER_AHEAD, GATHER_LAG)
    low_down, norm_rows = lax.optimization_barrier(
        (low_enc[:, columns[3] : columns[4]], results[5])
    )
    down = lax.all_gather(low_down, ("section", "dp"), axis=0, tiled=True)
    return [*results[:3], down, results[3]], results[4], norm_rows


def scatter_all(enc_parts, dec, norms, encoder_side):
    widths = [p.shape[1] for p in enc_parts]
    both = ("section", "dp")

    def scattered(v):
        return lax.psum_scatter(v, both, scatter_dimension=0, tiled=True)

    if not is_fast():
        parts = [scattered(jnp.where(encoder_side, p.astype(WIDE), 0.0)) for p in enc_parts]
        dec = scattered(jnp.where(encoder_side, 0.0, dec.astype(WIDE)))
        norms = scattered(norms)
        local = sum(jnp.sum(v * v) for v in (*parts, dec))
        local = local + jnp.sum(norms * norms) / lax.axis_size("mp")
        total = jnp.full((8, 128), lax.psum(local, (*both, "mp")))
        return jnp.concatenate([*parts[:3], parts[4]], axis=1), parts[3], dec, norms, total
    down = scattered(enc_parts[3])
    near = (*enc_parts[:3], enc_parts[4])
    near_widths = (*widths[:3], widths[4])
    chunks = plan(near_widths, (4, 1, 4, 2), dec.shape[1], SCATTER_ORDERS, DEC_SCATTER_ORDERS)
    described = [(k, k // 4, b, c, w, o, own) for k, b, c, w, o, own in chunks]
    described.append((5, 2, 0, 0, 128, "xylh", BOTH))
    rows = near[0].shape[0] // 16
    outputs = [(rows, sum(near_widths)), (dec.shape[0] // 16, dec.shape[1]), (8, 128)]
    enc, dec, norms, total = scatter_grads(
        [*near, dec, norms], down, outputs, described, 2, SCATTER_AHEAD, SCATTER_LAG
    )
    return enc, down, dec, norms, total


def pack_norms(enc_rows, dec_rows, blocks):
    both = [rows.reshape(4, blocks, -1).transpose(1, 0, 2) for rows in (enc_rows, dec_rows)]
    joined = jnp.concatenate(both, axis=2)
    joined = jnp.pad(joined, ((0, 0), (0, 4), (0, 128 - joined.shape[2])))
    return joined.reshape(blocks * 8, 128)


def unpack_norms(packed, blocks, enc_width, dec_width):
    split = packed.reshape(blocks, 8, 128)[:, :4].transpose(1, 0, 2)
    return (
        split[:, :, :enc_width].reshape(4, -1),
        split[:, :, enc_width : enc_width + dec_width].reshape(4, -1),
    )


def key_ranges(slots):
    tiles = slots.reshape(-1, TILE)
    low, high = jnp.min(tiles, axis=1), jnp.max(tiles, axis=1)
    meet = jnp.logical_and(low[:, None] <= high[None, :], high[:, None] >= low[None, :])
    index = jnp.arange(tiles.shape[0], dtype=jnp.int32)[None, :]
    first = jnp.min(jnp.where(meet, index, tiles.shape[0]), axis=1)
    last = jnp.max(jnp.where(meet, index + 1, 0), axis=1)
    return jnp.stack([first, last], axis=1)


def renewed(weight, first_moment, second_moment, clipped, rate, fix_first, fix_second, decay):
    new_first = BETA_FIRST * first_moment + (1.0 - BETA_FIRST) * clipped
    new_second = BETA_SECOND * second_moment + (1.0 - BETA_SECOND) * clipped * clipped
    stepped = new_first / fix_first / (jnp.sqrt(new_second / fix_second) + ADAM_EPS)
    return weight - rate * (stepped + decay * weight)


def renew_kernel(order, scalars, total, near, down, dec, norms, *refs):
    enc_state, dec_state, enc_norm_state, dec_norm_state = (refs[k : k + 3] for k in (0, 3, 6, 9))
    new_enc, new_dec, new_enc_norm, new_dec_norm, enc_clip, dec_clip, enc_norm_clip, dec_norm_clip = refs[12:]
    factor = jnp.minimum(1.0, math.sqrt(PARAMS) / (jnp.sqrt(total[0:1, :]) + 1e-06))
    fixes = scalars[2], scalars[3]

    def work(blocks, state, new, clip):
        count = len(blocks)
        for k, (ref, at) in enumerate(blocks):
            rows = pl.ds(k, ref.shape[0], stride=count)
            clipped = ref[:, at : at + 128].astype(WIDE) * factor
            values = [s[rows, :] for s in state]
            clip[rows, :] = clipped
            new[rows, :] = renewed(*values, clipped, scalars[0], *fixes, WEIGHT_DECAY)

    work([((near, down)[which], at) for which, at in order], enc_state, new_enc, enc_clip)
    work([(dec, at) for at in range(0, dec.shape[1], 128)], dec_state, new_dec, dec_clip)
    column = 0
    for state, new, clip in (
        (enc_norm_state, new_enc_norm, enc_norm_clip),
        (dec_norm_state, new_dec_norm, dec_norm_clip),
    ):
        rows, width = new.shape
        clipped = norms[0:rows, column : column + width] * factor[:, :width]
        column += width
        clip[...] = clipped
        new[...] = renewed(*[s[...] for s in state], clipped, scalars[1], *fixes, 0.0)


def renew_all(scalars, total, near, down, down_at, dec, norms, enc, decoder, enc_norm, dec_norm):
    order = [(0, at) for at in range(0, near.shape[1], 128)]
    order[down_at // 128 : down_at // 128] = [(1, at) for at in range(0, down.shape[1], 128)]
    flat = [[v.reshape(-1, 128) for v in group] for group in (enc, decoder)]
    groups = [*flat, enc_norm, dec_norm]
    shapes = [jax.ShapeDtypeStruct(group[0].shape, WIDE) for group in groups] * 2
    results = pl.pallas_call(
        functools.partial(renew_kernel, order),
        in_specs=[pl.BlockSpec(memory_space=pltpu.SMEM)]
        + [pl.BlockSpec(memory_space=pltpu.VMEM)] * 17,
        out_specs=[pl.BlockSpec(memory_space=pltpu.VMEM)] * 8,
        out_shape=shapes,
        compiler_params=pltpu.CompilerParams(vmem_limit_bytes=40 * 2**20),
    )(scalars, total, near, down, dec, norms, *[v for group in groups for v in group])
    given = (enc, decoder, enc_norm, dec_norm) * 2
    return [r.reshape(group[0].shape) for r, group in zip(results, given)]


def per_device(
    act_in,
    packing,
    enc_weights,
    enc_first,
    enc_second,
    dec_weights,
    dec_first,
    dec_second,
    enc_norms,
    enc_norm_first,
    enc_norm_second,
    dec_norms,
    dec_norm_first,
    dec_norm_second,
    mask_token,
    dec_position,
    learning_rate,
    step_count,
):
    encoder_side = lax.axis_index("section") == 0
    decoder_side = jnp.logical_not(encoder_side)
    mp_rank = lax.axis_index("mp")
    mp_count = lax.axis_size("mp")
    first_half = mp_rank == 0
    slot_ids = packing[0, 0]
    patch_ids = packing[0, 1]
    local_images = IMG // mp_count
    grid_cells = local_images * GRID
    local_slot = slot_ids - mp_rank * local_images
    inside = jnp.logical_and(local_slot >= 0, local_slot < local_images)
    target = jnp.where(inside, local_slot * GRID + patch_ids, grid_cells)

    local_rows, width = act_in.shape[1], act_in.shape[2]
    real_rows = local_rows * mp_count
    rows = -(-real_rows // ROW_BLOCK) * ROW_BLOCK
    lanes = -(-rows // TILE) * TILE
    part = width // mp_count
    units = FF // mp_count
    head = width // HEADS
    dec_width = dec_position.shape[1]
    dec_part = dec_width // mp_count
    widths = (3 * part, part, units, units, dec_part)
    slots = jnp.pad(slot_ids, (0, lanes - real_rows), constant_values=IMG + 1)
    ranges = key_ranges(slots)

    def halves(own, other, axis):
        return jnp.where(
            first_half,
            jnp.concatenate([own, other], axis=axis),
            jnp.concatenate([other, own], axis=axis),
        )

    (qkv_w, out_w, up_w, down_w, projection), dec_own, norm_rows = gather_all(
        enc_weights[:, 0, :].astype(LOW),
        dec_weights[:, 0, :].astype(LOW),
        pack_norms(enc_norms, dec_norms, 1),
        widths,
    )
    enc_gains, dec_gains = (
        v.astype(LOW).astype(WIDE)
        for v in unpack_norms(
            norm_rows, norm_rows.shape[0] // 8, enc_norms.shape[1], dec_norms.shape[1]
        )
    )
    stream = halves(act_in[0], partner(act_in[0]), 0)
    stream = jnp.pad(stream, ((0, rows - real_rows), (0, 0)))
    first, turned, mixture, log_sum, mix_own = encoder_attend(
        stream, slots, ranges, enc_gains, qkv_w, out_w, head
    )
    after, second, hidden, slope, feed_own = encoder_feed(
        stream, mix_own, partner(mix_own), enc_gains, up_w, down_w, ROW_BLOCK
    )
    encoded = (after + (feed_own.astype(WIDE) + partner(feed_own).astype(WIDE))).astype(LOW)
    shown = min(real_rows, -(-IMG * MOST_VISIBLE // 16) * 16)
    packed = -(-shown // 128) * 128
    projected = mm(encoded[:shown], projection).astype(LOW)
    arrived = from_behind(projected, "section", 1)
    arrived = jnp.pad(arrived, ((0, packed - shown), (0, 0)))
    seen_target = jnp.pad(target[:shown], (0, packed - shown), constant_values=-1)
    decoded, grad_keep, grad_send, dec_grad_own, dec_grad_other, dec_gain_grad = decoder_step(
        first_half,
        arrived,
        partner(arrived),
        seen_target,
        mask_token,
        dec_position,
        dec_gains,
        dec_own,
        partner(dec_own),
        act_in[0],
        local_images,
    )
    returned = grad_keep[:shown] + partner(grad_send[:shown])
    grad_projected = from_behind(returned, "section", -1)
    grad_projected = jnp.pad(grad_projected, ((0, rows - shown), (0, 0)))
    dec_grad = dec_grad_own.astype(WIDE) + partner(dec_grad_other).astype(WIDE)
    dec_grad = dec_grad.astype(LOW)
    dec_gain_grad = dec_gain_grad + partner(dec_gain_grad)

    grad_projection = mm(encoded, grad_projected, 0, 0).astype(LOW)
    end_own = mm(grad_projected, projection, 1, 1).astype(LOW)
    end_other = partner(end_own)
    grad_up_w, grad_down_w, back_own = encoder_feed_back(
        jnp.where(encoder_side, 1, 0).astype(jnp.int32).reshape(1),
        end_own,
        end_other,
        second,
        hidden,
        slope,
        up_w,
        down_w,
    )
    grad_after, grad_low, gains_two = encoder_norm_back(
        after, back_own, partner(back_own), (end_own, end_other), enc_gains, 2, ROW_BLOCK, True
    )
    grad_qkv_w, grad_out_w, start_own = encoder_attend_back(
        slots, ranges, first, turned, mixture, log_sum, grad_low, qkv_w, out_w, head
    )
    grad_stream, gains_one = encoder_norm_back(
        stream, start_own, partner(start_own), (grad_after,), enc_gains, 0, ROW_BLOCK, False
    )
    enc_gain_grad = jnp.concatenate([gains_one[:2], gains_two[:2]], axis=0)
    norm_grads = pack_norms(
        jnp.where(encoder_side, enc_gain_grad, 0.0),
        jnp.where(decoder_side, dec_gain_grad, 0.0),
        norm_rows.shape[0] // 8,
    )
    near_shard, down_shard, dec_shard, norm_shard, square_total = scatter_all(
        (grad_qkv_w, grad_out_w, grad_up_w, grad_down_w, grad_projection),
        dec_grad,
        norm_grads,
        encoder_side,
    )
    step_value = step_count[0].astype(jnp.float32)
    scalars = jnp.stack(
        [
            learning_rate[0],
            learning_rate[1],
            1.0 - jnp.power(BETA_FIRST, step_value),
            1.0 - jnp.power(BETA_SECOND, step_value),
        ]
    )
    results = renew_all(
        scalars,
        square_total,
        near_shard,
        down_shard,
        sum(widths[:3]),
        dec_shard,
        norm_shard,
        (enc_weights, enc_first, enc_second),
        (dec_weights, dec_first, dec_second),
        (enc_norms, enc_norm_first, enc_norm_second),
        (dec_norms, dec_norm_first, dec_norm_second),
    )
    own_grad = lax.dynamic_slice_in_dim(grad_stream, mp_rank * local_rows, local_rows, axis=0)
    act_out = jnp.where(encoder_side, own_grad, decoded.reshape(local_rows, width))[None]
    return (act_out, *results, jnp.sqrt(square_total[0, 0]).reshape(1))


def solution(mesh):
    in_specs = (
        P("section", ("dp", "mp"), None),
        P("dp", None, None),
        P(("section", "dp"), "mp", None),
        P(("section", "dp"), "mp", None),
        P(("section", "dp"), "mp", None),
        P(("section", "dp"), "mp", None),
        P(("section", "dp"), "mp", None),
        P(("section", "dp"), "mp", None),
        P(None, ("section", "dp")),
        P(None, ("section", "dp")),
        P(None, ("section", "dp")),
        P(None, ("section", "dp")),
        P(None, ("section", "dp")),
        P(None, ("section", "dp")),
        P(),
        P(),
        P(),
        P(),
    )
    out_specs = (
        P("section", ("dp", "mp"), None),
        P(("section", "dp"), "mp", None),
        P(("section", "dp"), "mp", None),
        P(None, ("section", "dp")),
        P(None, ("section", "dp")),
        P(("section", "dp"), "mp", None),
        P(("section", "dp"), "mp", None),
        P(None, ("section", "dp")),
        P(None, ("section", "dp")),
        P(),
    )
    return jax.shard_map(
        per_device, mesh=mesh, in_specs=in_specs, out_specs=out_specs, check_vma=False
    )
```

```python
import functools
import itertools
import math

import jax
import jax.numpy as jnp
from jax import lax
from jax.experimental import pallas as pl
from jax.experimental.pallas import tpu as pltpu
from jax.sharding import PartitionSpec as P

FF = 4096
GRID = 196
IMG = 12
PARAMS = 16259072

BETA_FIRST = 0.9
BETA_SECOND = 0.999
ADAM_EPS = 1e-08
WEIGHT_DECAY = 0.05
ROW_BLOCK = 240
MOST_VISIBLE = 73
GATHER_ORDERS = ("hlxy", "hlyx", "hlxy", "hlyx", "yxhl")
DEC_GATHER_ORDERS = ("xhly", "xyhl")
DEC_SCATTER_ORDERS = ("ylhx", "ylhx")
GATHER_AHEAD, GATHER_LAG = 4, (1, 3)
SCATTER_AHEAD, SCATTER_LAG = 4, (2, 2, 2)
SCATTER_ORDERS = ("xylh", "yxlh", "xylh", "yxlh", "lhxy")

MESH_ID = pl.DeviceIdType.MESH
EVERY = slice(None)
BOTH = -1
DIMS = "xhly"


class Place:
    def __init__(self):
        s, depth, core = lax.axis_index("section"), lax.axis_index("dp"), lax.axis_index("mp")
        y, low, high = depth % 2, (depth // 2) % 2, depth // 4
        self.at = {"x": s, "h": high, "l": low, "y": y}
        self.s, self.core = s, core
        self.device = {
            "x": (1 - s, depth, core),
            "h": (s, depth + 4 - 8 * high, core),
            "l": (s, depth + 2 - 4 * low, core),
            "y": (s, depth + 1 - 2 * y, core),
            "c": (s, depth, 1 - core),
        }

    def greet(self):
        barrier = pltpu.get_barrier_semaphore()
        for name in self.device:
            pl.semaphore_signal(
                barrier, inc=1, device_id=self.device[name], device_id_type=MESH_ID
            )
        pl.semaphore_wait(barrier, len(self.device))


def run(condition, action):
    if condition is None:
        action()
    else:
        pl.when(condition)(action)


def gather_kernel(chunks, n_in, n_out, ahead, lag, *refs):
    ins, outs = refs[:n_in], refs[n_in : n_in + n_out]
    send, recv, local = refs[n_in + n_out :]
    here = Place()
    count = len(chunks)

    def region(chunk, gathered, sender):
        at = [
            EVERY if d in gathered else 1 - here.at[d] if d == sender else here.at[d] for d in DIMS
        ]
        return outs[chunk[1]].at[(*at, EVERY, pl.ds(chunk[3], chunk[4]))]

    def own(i):
        chunk = chunks[i]
        return pltpu.make_async_copy(
            ins[chunk[0]].at[:, pl.ds(chunk[2], chunk[4])], region(chunk, "", None), local.at[i]
        )

    def copy(i, stage, incoming):
        chunk = chunks[i]
        order = chunk[5]
        axis = order[stage]
        block = region(chunk, order[:stage], axis if incoming else None)
        source = block
        if stage == 0 and not incoming:
            source = ins[chunk[0]].at[:, pl.ds(chunk[2], chunk[4])]
        return pltpu.make_async_remote_copy(
            src_ref=source,
            dst_ref=block,
            send_sem=send.at[i, stage],
            recv_sem=recv.at[i, stage],
            device_id=here.device[axis],
            device_id_type=MESH_ID,
        )

    def roles(i, stage):
        order, owner = chunks[i][5], chunks[i][6]
        if owner == BOTH:
            return None, None
        if order[stage] == "x":
            return here.s != owner, here.s == owner
        if "x" in order[:stage]:
            return here.s == owner, here.s == owner
        return None, None

    def begin(i, stage):
        run(roles(i, stage)[0], lambda: copy(i, stage, False).start())

    def arrive(i, stage):
        run(roles(i, stage)[1], lambda: copy(i, stage, True).wait_recv())
        if stage == 0:
            own(i).wait()

    here.greet()
    for i in range(count):
        own(i).start()
    for i in range(min(ahead, count)):
        begin(i, 0)
    for step in range(count + sum(lag)):
        for stage in range(3):
            i = step - sum(lag[:stage])
            if not 0 <= i < count:
                continue
            arrive(i, stage)
            begin(i, stage + 1)
            if stage == 0 and i + ahead < count:
                begin(i + ahead, 0)
    for i in range(count):
        arrive(i, 3)
    for i in range(count):
        for stage in range(4):
            run(
                roles(i, stage)[0],
                lambda i=i, stage=stage: copy(i, stage, False).wait_send(),
            )


def gather_weights(shards, outputs, chunks, collective_id, ahead=4, lag=(1, 1)):
    count = len(chunks)
    call = pl.pallas_call(
        functools.partial(gather_kernel, chunks, len(shards), len(outputs), ahead, lag),
        out_shape=[
            jax.ShapeDtypeStruct((2, 2, 2, 2, rows, width), dtype) for rows, width, dtype in outputs
        ],
        in_specs=[pl.BlockSpec(memory_space=pltpu.VMEM)] * len(shards),
        out_specs=[pl.BlockSpec(memory_space=pltpu.HBM)] * len(outputs),
        scratch_shapes=[
            pltpu.SemaphoreType.DMA((count, 4)),
            pltpu.SemaphoreType.DMA((count, 4)),
            pltpu.SemaphoreType.DMA((count,)),
        ],
        compiler_params=pltpu.CompilerParams(
            collective_id=collective_id, has_side_effects=True, vmem_limit_bytes=40 * 2**20
        ),
    )
    results = call(*shards)
    return [
        r.reshape(16 * rows, width) for r, (rows, width, _) in zip(results, outputs, strict=True)
    ]


def spread(total, pieces, unit=128):
    units = total // unit
    widths = [units // pieces + (1 if k < units % pieces else 0) for k in range(pieces)]
    return [w * unit for w in widths if w]


def chunk_list(widths, pieces, owner, orders):
    chunks = []
    column = turn = 0
    for index, (width, count) in enumerate(zip(widths, pieces, strict=True)):
        begin = 0
        for piece in spread(width, count):
            chunks.append((index, begin, column, piece, orders[turn % len(orders)], owner))
            begin += piece
            column += piece
            turn += 1
    return chunks


def left_after(order, stage):
    return [d for d in DIMS if d not in order[: stage + 1]]


def scatter_buffers(order, owner):
    shapes = [(2,) * 3]
    for stage in range(4):
        if order[stage] == "x" and owner != BOTH:
            continue
        shapes.append((2,) * (3 - stage))
    return shapes


def squares(ref):
    def step(k, total):
        block = ref[:, pl.ds(pl.multiple_of(k * 128, 128), 128)].astype(jnp.float32)
        block = block * block
        for r in range(0, block.shape[0], 8):
            total = total + block[r : r + 8]
        return total

    return lax.fori_loop(0, ref.shape[1] // 128, step, jnp.zeros((8, 128), jnp.float32))


def scatter_kernel(chunks, n_in, n_out, ahead, lag, cores, *refs):
    ins, summed, outs = refs[:n_in], refs[n_in], refs[n_in + 1 : n_in + 1 + n_out]
    square_total = refs[n_in + 1 + n_out]
    rest = refs[n_in + n_out + 2 :]
    send, recv, local, square_send, square_recv, square_mine, square_there, last, last_there = rest[:9]
    here = Place()
    s = here.s
    count = len(chunks)
    given, ins = ins[-1], (*ins[:-1], last)
    own, got = [], []
    position = 9
    for chunk in chunks:
        order, owner = chunk[5], chunk[6]
        own.append(rest[position])
        position += 1
        mine = []
        for stage in range(4):
            if order[stage] == "x" and owner != BOTH:
                mine.append(None)
                continue
            mine.append(rest[position])
            position += 1
        got.append(mine)

    def source(i, axis, keep):
        chunk = chunks[i]
        at = [
            (here.at[d] if keep else 1 - here.at[d]) if d == axis else EVERY for d in DIMS
        ]
        return ins[chunk[0]].at[(*at, EVERY, pl.ds(chunk[2], chunk[4]))]

    def load(i):
        return pltpu.make_async_copy(source(i, chunks[i][5][0], True), own[i], local.at[i])

    def spot(i, stage, flip):
        order = chunks[i][5]
        at = []
        for d in DIMS:
            if d == order[0]:
                continue
            if d in order[:stage]:
                at.append(here.at[d])
            elif d == order[stage]:
                at.append(1 - here.at[d] if flip else here.at[d])
            else:
                at.append(EVERY)
        return tuple(at)

    def copy(i, stage, incoming):
        order = chunks[i][5]
        axis = order[stage]
        moved = got[i][stage] is None
        src = source(i, axis, False) if stage == 0 else own[i].at[spot(i, stage, True)]
        if not moved:
            there = mine = got[i][stage]
        elif stage == 0:
            there = mine = own[i]
        else:
            there, mine = own[i].at[spot(i, stage, True)], own[i].at[spot(i, stage, False)]
        return pltpu.make_async_remote_copy(
            src_ref=mine if incoming else src,
            dst_ref=mine if incoming else there,
            send_sem=send.at[i, stage],
            recv_sem=recv.at[i, stage],
            device_id=here.device[axis],
            device_id_type=MESH_ID,
        )

    def roles(i, stage):
        order, owner = chunks[i][5], chunks[i][6]
        if owner == BOTH:
            return None, None
        if order[stage] == "x":
            return s == owner, s != owner
        if "x" in order[:stage]:
            return None, None
        return s == owner, s == owner

    def begin(i, stage):
        run(roles(i, stage)[0], lambda: copy(i, stage, False).start())

    def arrive(i, stage):
        chunk, a, r = chunks[i], own[i], got[i][stage]
        order, owner = chunk[5], chunk[6]
        run(roles(i, stage)[1], lambda: copy(i, stage, True).wait_recv())
        if stage == 0:
            run(None if owner == BOTH else s == owner, lambda: load(i).wait())
        out = outs[chunk[1]].at[:, pl.ds(chunk[3], chunk[4])]
        place = spot(i, stage, False)
        if stage == 3:
            result = a[place].astype(jnp.float32)
            if r is not None:
                result = result + r[...].astype(jnp.float32)
            out[...] = result
            return
        if r is None:
            return

        def add():
            free = [k for k, p in enumerate(place) if p is EVERY]
            for combo in itertools.product(range(2), repeat=len(free)):
                at = list(place)
                for k, c in zip(free, combo):
                    at[k] = c
                at = tuple(at)
                a[at] = (a[at].astype(jnp.float32) + r[combo].astype(jnp.float32)).astype(a.dtype)

        run(roles(i, stage)[1], add)

    here.greet()
    join = pltpu.make_async_remote_copy(
        src_ref=given,
        dst_ref=last_there,
        send_sem=square_send.at[5],
        recv_sem=square_recv.at[5],
        device_id=here.device["c"],
        device_id_type=MESH_ID,
    )
    join.start()
    for i in range(count - 1):
        run(
            None if chunks[i][6] == BOTH else s == chunks[i][6],
            lambda i=i: load(i).start(),
        )
    for i in range(min(ahead, count)):
        begin(i, 0)
    join.wait()
    last[...] = given[...] + last_there[...]
    load(count - 1).start()
    for step in range(count + sum(lag)):
        for stage in range(3, -1, -1):
            i = step - sum(lag[:stage])
            if not 0 <= i < count:
                continue
            arrive(i, stage)
            if stage < 3:
                begin(i, stage + 1)
            if stage == 0 and i + ahead < count:
                begin(i + ahead, 0)
    for i in range(count):
        for stage in range(4):
            run(
                roles(i, stage)[0],
                lambda i=i, stage=stage: copy(i, stage, False).wait_send(),
            )

    value = squares(summed)
    for k, out in enumerate(outs):
        value = value + squares(out) * (1.0 / cores if k == n_out - 1 else 1.0)
    value = jnp.broadcast_to(jnp.sum(value, keepdims=True), (8, 128))
    for k, axis in enumerate("cyxlh"):
        square_mine[k] = value
        move = pltpu.make_async_remote_copy(
            src_ref=square_mine.at[k],
            dst_ref=square_there.at[k],
            send_sem=square_send.at[k],
            recv_sem=square_recv.at[k],
            device_id=here.device[axis],
            device_id_type=MESH_ID,
        )
        move.start()
        move.wait()
        value = value + square_there[k]
    square_total[...] = value


def scatter_grads(parts, summed, outputs, chunks, collective_id, ahead=4, lag=(1, 1, 1)):
    count = len(chunks)
    views = [p.reshape(2, 2, 2, 2, p.shape[0] // 16, p.shape[1]) for p in parts]
    buffers = []
    for chunk in chunks:
        view = views[chunk[0]]
        for lead in scatter_buffers(chunk[5], chunk[6]):
            buffers.append(pltpu.VMEM((*lead, view.shape[4], chunk[4]), view.dtype))
    call = pl.pallas_call(
        functools.partial(scatter_kernel, chunks, len(parts), len(outputs), ahead, lag, lax.axis_size("mp")),
        out_shape=[
            jax.ShapeDtypeStruct((rows, width), jnp.float32) for rows, width in [*outputs, (8, 128)]
        ],
        in_specs=[pl.BlockSpec(memory_space=pl.ANY)] * (len(parts) - 1)
        + [pl.BlockSpec(memory_space=pltpu.VMEM)] * 2,
        out_specs=[pl.BlockSpec(memory_space=pltpu.VMEM)] * (len(outputs) + 1),
        scratch_shapes=[
            pltpu.SemaphoreType.DMA((count, 4)),
            pltpu.SemaphoreType.DMA((count, 4)),
            pltpu.SemaphoreType.DMA((count,)),
            pltpu.SemaphoreType.DMA((6,)),
            pltpu.SemaphoreType.DMA((6,)),
            pltpu.VMEM((5, 8, 128), jnp.float32),
            pltpu.VMEM((5, 8, 128), jnp.float32),
            pltpu.VMEM(views[-1].shape, views[-1].dtype),
            pltpu.VMEM(views[-1].shape, views[-1].dtype),
            *buffers,
        ],
        compiler_params=pltpu.CompilerParams(
            collective_id=collective_id, has_side_effects=True, vmem_limit_bytes=56 * 2**20
        ),
    )
    return call(*views, summed)


HEADS = 16
TOGETHER = 8
NORM_EPS = 1e-06
MASKED = -1e30
LOW = jnp.bfloat16
WIDE = jnp.float32


def mm(left, right, left_dim=1, right_dim=0):
    return lax.dot_general(
        left, right, (((left_dim,), (right_dim,)), ((), ())), preferred_element_type=WIDE
    )


def centre(tokens):
    average = jnp.mean(tokens, axis=-1, keepdims=True)
    centred = tokens - average
    spread_ = jnp.mean(centred * centred, axis=-1, keepdims=True)
    scale = lax.rsqrt(spread_ + NORM_EPS)
    return centred * scale, scale


def centre_back(unit, scale, gain, grad):
    pulled = grad * gain
    first = jnp.mean(pulled, axis=-1, keepdims=True)
    second = jnp.mean(pulled * unit, axis=-1, keepdims=True)
    return scale * (pulled - first - unit * second)


def gelu_pair(z):
    cdf = 0.5 * (1.0 + lax.erf(z * math.sqrt(0.5)))
    return z * cdf, cdf + z * (jnp.exp(-0.5 * z * z) * (1.0 / math.sqrt(2.0 * math.pi)))


def decoder_kernel(
    length,
    flag,
    target_row,
    target_column,
    visible_own,
    visible_other,
    mask,
    position,
    gains,
    pack_own,
    pack_other,
    cotangent,
    decoded,
    grad_keep,
    grad_send,
    grad_own,
    grad_other,
    grad_gains,
    qkv_t,
    out_t,
    qkv_rows,
    shares,
    mixture,
    hidden,
    slope,
    grad_mixture,
    stream,
    first,
    after,
    grad_low,
    grad_first,
    grad_visible,
    grad_qkv,
    grad_out,
    grad_up,
    grad_down,
):
    step = pl.program_id(0)
    images, rows, width = decoded.shape
    head = width // HEADS
    units = hidden.shape[1]
    part, half = width // 2, units // 2
    up_at, down_at = 4 * part, 4 * part + half
    scaling = head ** (-0.5)
    packs = (pack_own, pack_other)
    halves = ((slice(0, half), pack_own), (slice(half, units), pack_other))

    @pl.when(step == 0)
    def _():
        for ref in (grad_visible, grad_qkv, grad_out, grad_up, grad_down, grad_gains):
            ref[...] = jnp.zeros_like(ref)
        for which in range(4):
            for k, pack in enumerate(packs):
                at = (2 * which + k) * part
                piece = jnp.transpose(pack[:, which * part : (which + 1) * part])
                if which < 3:
                    qkv_t[at : at + part, :] = piece
                else:
                    out_t[k * part : (k + 1) * part, :] = piece

    packed = target_row.shape[1]
    left = flag[0] > 0
    spans = [slice(k * rows, (k + 1) * rows) for k in range(images)]
    for k, span in enumerate(spans):
        number = step * images + k
        cell = lax.broadcasted_iota(jnp.int32, (rows, packed), 0)
        wanted = jnp.where(cell < length, cell + number * length, -7)
        chosen = (target_row[...] == wanted).astype(WIDE)
        seen = jnp.max(chosen, axis=1, keepdims=True)
        chosen = chosen.astype(LOW)
        placed_own, placed_other = mm(chosen, visible_own[...]), mm(chosen, visible_other[...])
        placed = jnp.concatenate(
            [
                jnp.where(left, placed_own, placed_other),
                jnp.where(left, placed_other, placed_own),
            ],
            axis=1,
        )
        stream[span, :] = jnp.where(seen > 0.0, placed, mask[...]) + position[...]

    unit_one, scale_one = centre(stream[...])
    first[...] = (unit_one * gains[0:1] + gains[1:2]).astype(LOW)
    key_index = lax.broadcasted_iota(jnp.int32, (rows, rows), 0)

    def lines(which, h):
        return slice(which * width + h * head, which * width + (h + 1) * head)

    for k, span in enumerate(spans):
        qkv, mixed = qkv_rows.at[k], mixture.at[k]
        qkv[...] = mm(qkv_t[...], first[span, :], 1, 1).astype(LOW)
        for begin in range(0, HEADS, TOGETHER):
            group = range(begin, begin + TOGETHER)
            scores = [mm(qkv[lines(1, h), :], qkv[lines(0, h), :], 0, 0) * scaling for h in group]
            scores = [jnp.where(key_index < length, s, MASKED) for s in scores]
            weights = [jnp.exp(s - jnp.max(s, axis=0, keepdims=True)) for s in scores]
            group_shares = [w * (1.0 / jnp.sum(w, axis=0, keepdims=True)) for w in weights]
            for h, share in zip(group, group_shares):
                shares[k, h] = share
                mixed[lines(0, h), :] = mm(qkv[lines(2, h), :], share.astype(LOW)).astype(LOW)
        after[span, :] = stream[span, :] + mm(mixed[...], out_t[...], 0, 0)

    unit_two, scale_two = centre(after[...])
    second = (unit_two * gains[2:3] + gains[3:4]).astype(LOW)
    piece = 256
    for c in range(0, units, piece):
        pack, at = packs[c // half], up_at + c % half
        z = mm(second, pack[:, at : at + piece])
        h, g = gelu_pair(z)
        hidden[:, c : c + piece] = h.astype(LOW)
        slope[:, c : c + piece] = g
    fed = [mm(hidden[:, cut], pack[:, down_at : down_at + half], 1, 1) for cut, pack in halves]
    result = after[...] + (fed[0] + fed[1])
    for k, span in enumerate(spans):
        decoded[k] = result[span]

    for k, span in enumerate(spans):
        grad_low[span, :] = cotangent[k]
    turned = jnp.transpose(grad_low[...])
    second_turned = jnp.transpose(second)
    for c in range(0, units, piece):
        cut = slice(c, c + piece)
        grad_down[:, cut] += mm(turned, hidden[:, cut])
        pack, at = packs[c // half], down_at + c % half
        grad_z = (mm(grad_low[...], pack[:, at : at + piece]) * slope[:, cut]).astype(LOW)
        hidden[:, cut] = grad_z
        grad_up[:, cut] += mm(second_turned, grad_z)
    pulled = [mm(hidden[:, cut], pack[:, up_at : up_at + half], 1, 1) for cut, pack in halves]
    grad_second = pulled[0] + pulled[1]
    grad_gains[2:3] += jnp.sum(grad_second * unit_two, axis=0, keepdims=True)
    grad_gains[3:4] += jnp.sum(grad_second, axis=0, keepdims=True)
    after[...] = grad_low[...].astype(WIDE) + centre_back(
        unit_two, scale_two, gains[2:3], grad_second
    )

    for k, span in enumerate(spans):
        qkv, mixed, grad_rows = qkv_rows.at[k], mixture.at[k], grad_mixture.at[k]
        after_low = after[span, :].astype(LOW)
        grad_out[...] += mm(mixed[...], after_low)
        grad_rows[...] = mm(out_t[...], after_low, 1, 1).astype(LOW)
        for begin in range(0, HEADS, TOGETHER):
            group = range(begin, begin + TOGETHER)
            queries = [qkv[lines(0, h), :] for h in group]
            keys = [qkv[lines(1, h), :] for h in group]
            values = [qkv[lines(2, h), :] for h in group]
            grads_in = [grad_rows[lines(0, h), :] for h in group]
            grad_shares = [mm(v, g, 0, 0) for v, g in zip(values, grads_in)]
            grad_values = [mm(g, shares[k, h].astype(LOW), 1, 1) for g, h in zip(grads_in, group)]
            grad_scores = []
            for h, g in zip(group, grad_shares):
                share = shares[k, h]
                inner = jnp.sum(share * g, axis=0, keepdims=True)
                grad_scores.append((share * (g - inner)).astype(LOW))
            for n, h in enumerate(group):
                qkv[lines(0, h), :] = (mm(keys[n], grad_scores[n]) * scaling).astype(LOW)
                qkv[lines(1, h), :] = (mm(queries[n], grad_scores[n], 1, 1) * scaling).astype(LOW)
                qkv[lines(2, h), :] = grad_values[n].astype(LOW)
        grad_qkv[...] += mm(qkv[...], first[span, :])
        grad_first[span, :] = mm(qkv[...], qkv_t[...], 0, 0)

    unit_one, scale_one = centre(stream[...])
    pulled = grad_first[...]
    grad_stream = after[...] + centre_back(unit_one, scale_one, gains[0:1], pulled)
    grad_gains[0:1] += jnp.sum(pulled * unit_one, axis=0, keepdims=True)
    grad_gains[1:2] += jnp.sum(pulled, axis=0, keepdims=True)

    for k, span in enumerate(spans):
        cell_lane = lax.broadcasted_iota(jnp.int32, (packed, rows), 1)
        wanted_lane = jnp.where(cell_lane < length, cell_lane + (step * images + k) * length, -7)
        chosen_back = (target_column[...] == wanted_lane).astype(WIDE).astype(LOW)
        grad_visible[...] += mm(chosen_back, grad_stream[span].astype(LOW))

    @pl.when(step == pl.num_programs(0) - 1)
    def _():
        gathered = grad_visible[...].astype(LOW)
        one, two = gathered[:, :part], gathered[:, part:]
        grad_keep[...] = jnp.where(left, one, two)
        grad_send[...] = jnp.where(left, two, one)
        for k, ref in enumerate((grad_own, grad_other)):
            for which in range(4):
                at = (2 * which + k) * part
                piece = grad_qkv[at : at + part, :] if which < 3 else grad_out[k * part : (k + 1) * part, :]
                ref[:, which * part : (which + 1) * part] = jnp.transpose(piece.astype(LOW))
            cut = slice(k * half, (k + 1) * half)
            ref[:, up_at:down_at] = grad_up[:, cut].astype(LOW)
            ref[:, down_at:] = grad_down[:, cut].astype(LOW)


def decoder_step(
    length, left, visible_own, visible_other, target, mask, position, gains, pack_own, pack_other, cotangent
):
    rows, width = position.shape
    packed = visible_own.shape[0]
    images, columns = cotangent.shape[0], pack_own.shape[1]
    units = columns - 2 * width

    def fixed(shape):
        return pl.BlockSpec(shape, lambda i: (0,) * len(shape), pipeline_mode=pl.Buffered(1))

    at_once = 2 if images % 2 == 0 else 1
    per_image = pl.BlockSpec((at_once, rows, width), lambda i: (i, 0, 0))
    tall = at_once * rows
    grads = [
        ((packed, width // 2), LOW),
        ((packed, width // 2), LOW),
        ((width, columns), LOW),
        ((width, columns), LOW),
        ((8, width), WIDE),
    ]
    decoded, keep, send, grad_own, grad_other, grad_gains = pl.pallas_call(
        functools.partial(decoder_kernel, length),
        grid=(images // at_once,),
        out_shape=[jax.ShapeDtypeStruct((images, rows, width), WIDE)]
        + [jax.ShapeDtypeStruct(s, d) for s, d in grads],
        in_specs=[
            pl.BlockSpec(memory_space=pltpu.SMEM),
            fixed((1, packed)),
            fixed((packed, 1)),
            fixed((packed, width // 2)),
            fixed((packed, width // 2)),
            fixed((1, width)),
            fixed((rows, width)),
            fixed((4, width)),
            fixed((width, columns)),
            fixed((width, columns)),
            per_image,
        ],
        out_specs=[per_image] + [fixed(s) for s, _ in grads],
        scratch_shapes=[
            pltpu.VMEM((3 * width, width), LOW),
            pltpu.VMEM((width, width), LOW),
            pltpu.VMEM((at_once, 3 * width, rows), LOW),
            pltpu.VMEM((at_once, HEADS, rows, rows), WIDE),
            pltpu.VMEM((at_once, width, rows), LOW),
            pltpu.VMEM((tall, units), LOW),
            pltpu.VMEM((tall, units), WIDE),
            pltpu.VMEM((at_once, width, rows), LOW),
            pltpu.VMEM((tall, width), WIDE),
            pltpu.VMEM((tall, width), LOW),
            pltpu.VMEM((tall, width), WIDE),
            pltpu.VMEM((tall, width), LOW),
            pltpu.VMEM((tall, width), WIDE),
            pltpu.VMEM((packed, width), WIDE),
            pltpu.VMEM((3 * width, width), WIDE),
            pltpu.VMEM((width, width), WIDE),
            pltpu.VMEM((width, units), WIDE),
            pltpu.VMEM((width, units), WIDE),
        ],
        compiler_params=pltpu.CompilerParams(
            dimension_semantics=("arbitrary",), vmem_limit_bytes=60 * 2**20
        ),
    )(
        left.astype(jnp.int32).reshape(1),
        target[None, :],
        target[:, None],
        visible_own,
        visible_other,
        mask[None, :],
        position,
        gains,
        pack_own,
        pack_other,
        cotangent,
    )
    return decoded, keep, send, grad_own, grad_other, grad_gains[:4]


TILE = 256
GROUP = 4


def fixed(shape):
    return pl.BlockSpec(shape, lambda i: (0,) * len(shape), pipeline_mode=pl.Buffered(1))


def down_rows(rows, width):
    return pl.BlockSpec((rows, width), lambda i: (i, 0))


def params(megabytes=60):
    return pltpu.CompilerParams(
        dimension_semantics=("arbitrary",), vmem_limit_bytes=megabytes * 2**20
    )


def attend_kernel(
    head, bounds, stream, slots_row, slots_column, gains, qkv_w, out_w, first, turned, mixture, log_sum, partial
):
    rows, width = stream.shape
    part, lanes = mixture.shape
    tiles = lanes // TILE
    scaling = head ** (-0.5)
    unit, _ = centre(stream[...].astype(WIDE))
    first[...] = (unit * gains[0:1] + gains[1:2]).astype(LOW)
    turned[:, rows:] = jnp.zeros((3 * part, lanes - rows), LOW)
    for c in range(0, 3 * part, TILE):
        weight = jnp.transpose(qkv_w[:, c : c + TILE])
        turned[c : c + TILE, :rows] = mm(weight, first[...], 1, 1).astype(LOW)

    def at(which, h, tile):
        return (
            pl.ds(pl.multiple_of(which * part + h * head, head), head),
            pl.ds(pl.multiple_of(tile * TILE, TILE), TILE),
        )

    def step(n, carry):
        group, i = n // tiles, n % tiles
        heads = [group * GROUP + g for g in range(GROUP)]
        lane_i = pl.ds(pl.multiple_of(i * TILE, TILE), TILE)
        queries = [turned[at(0, h, i)] for h in heads]
        slot_i = slots_row[:, lane_i]

        def inner(j, state):
            same = slots_column[pl.ds(pl.multiple_of(j * TILE, TILE), TILE), :] == slot_i
            scores = [mm(turned[at(1, h, j)], q, 0, 0) * scaling for h, q in zip(heads, queries)]
            scores = [jnp.where(same, s, MASKED) for s in scores]
            highs = [
                jnp.maximum(state[g][0], jnp.max(s, axis=0, keepdims=True))
                for g, s in enumerate(scores)
            ]
            weights = [jnp.exp(s - high) for s, high in zip(scores, highs)]
            fixes = [jnp.exp(state[g][0] - high) for g, high in enumerate(highs)]
            sums = [jnp.sum(w, axis=0, keepdims=True) for w in weights]
            mixes = [mm(turned[at(2, h, j)], w.astype(LOW)) for h, w in zip(heads, weights)]
            return tuple(
                (highs[g], state[g][1] * fixes[g] + sums[g], state[g][2] * fixes[g] + mixes[g])
                for g in range(GROUP)
            )

        begin = (
            jnp.full((1, TILE), MASKED, WIDE),
            jnp.zeros((1, TILE), WIDE),
            jnp.zeros((head, TILE), WIDE),
        )
        state = lax.fori_loop(bounds[i, 0], bounds[i, 1], inner, (begin,) * GROUP)
        for g, h in enumerate(heads):
            high, total, mixed = state[g]
            mixture[at(0, h, i)] = (mixed / total).astype(LOW)
            log_sum[pl.ds(h, 1), lane_i] = high + jnp.log(total)
        return carry

    lax.fori_loop(0, part // head // GROUP * tiles, step, 0)
    mixed = jnp.transpose(mixture[...])[:rows]
    for c in range(0, width, TILE):
        partial[:, c : c + TILE] = mm(mixed, out_w[c : c + TILE, :], 1, 1).astype(LOW)


def encoder_attend(stream, slots, bounds, gains, qkv_w, out_w, head):
    rows, width = stream.shape
    lanes = slots.shape[0]
    part = out_w.shape[1]
    return pl.pallas_call(
        functools.partial(attend_kernel, head),
        in_specs=[pl.BlockSpec(memory_space=pltpu.SMEM)]
        + [pl.BlockSpec(memory_space=pltpu.VMEM)] * 6,
        out_specs=[pl.BlockSpec(memory_space=pltpu.VMEM)] * 5,
        out_shape=[
            jax.ShapeDtypeStruct((rows, width), LOW),
            jax.ShapeDtypeStruct((3 * part, lanes), LOW),
            jax.ShapeDtypeStruct((part, lanes), LOW),
            jax.ShapeDtypeStruct((part // head, lanes), WIDE),
            jax.ShapeDtypeStruct((rows, width), LOW),
        ],
        compiler_params=pltpu.CompilerParams(vmem_limit_bytes=60 * 2**20),
    )(bounds, stream, slots[None, :], slots[:, None], gains, qkv_w, out_w)


def attend_back_kernel(
    head,
    bounds,
    slots_row,
    slots_column,
    first,
    turned,
    mixture,
    log_sum,
    grad_low,
    qkv_w,
    out_w,
    grad_qkv_w,
    grad_out_w,
    partial,
    grad_mixture,
    grad_turned,
    inner_sum,
    key_sum,
    value_sum,
):
    rows, width = grad_low.shape
    part, lanes = mixture.shape
    tiles = lanes // TILE
    scaling = head ** (-0.5)
    grad_mixture[:, rows:] = jnp.zeros((part, lanes - rows), LOW)
    for c in range(0, width, TILE):
        grad_out_w[c : c + TILE, :] = jnp.transpose(
            mm(mixture[:, :rows], grad_low[:, c : c + TILE]).astype(LOW)
        )
    for c in range(0, part, TILE):
        weight = jnp.transpose(out_w[:, c : c + TILE])
        grad_mixture[c : c + TILE, :rows] = mm(weight, grad_low[...], 1, 1).astype(LOW)
    for h in range(part // head):
        cut = slice(h * head, (h + 1) * head)
        inner_sum[h : h + 1, :] = jnp.sum(
            grad_mixture[cut, :].astype(WIDE) * mixture[cut, :].astype(WIDE), axis=0, keepdims=True
        )

    def at(which, h, tile):
        return (
            pl.ds(pl.multiple_of(which * part + h * head, head), head),
            pl.ds(pl.multiple_of(tile * TILE, TILE), TILE),
        )

    def over_group(group, carry):
        heads = [group * GROUP + g for g in range(GROUP)]
        key_sum[...] = jnp.zeros_like(key_sum)
        value_sum[...] = jnp.zeros_like(value_sum)

        def over_queries(i, carry):
            lane_i = pl.ds(pl.multiple_of(i * TILE, TILE), TILE)
            slot_i = slots_row[:, lane_i]
            queries = [turned[at(0, h, i)] for h in heads]
            grads = [grad_mixture[at(0, h, i)] for h in heads]
            logs = [log_sum[pl.ds(h, 1), lane_i] for h in heads]
            sums = [inner_sum[pl.ds(h, 1), lane_i] for h in heads]

            def inner(j, state):
                lane_j = pl.ds(pl.multiple_of(j * TILE, TILE), TILE)
                same = slots_column[lane_j, :] == slot_i
                cuts = [slice(g * head, (g + 1) * head) for g in range(GROUP)]
                keys = [turned[at(1, h, j)] for h in heads]
                values = [turned[at(2, h, j)] for h in heads]
                scores = [mm(k, q, 0, 0) * scaling for k, q in zip(keys, queries)]
                grad_shares = [mm(v, g, 0, 0) for v, g in zip(values, grads)]
                shares = [
                    jnp.exp(jnp.where(same, s, MASKED) - log) for s, log in zip(scores, logs)
                ]
                grad_scores = [
                    (s * (g - total)).astype(LOW) for s, g, total in zip(shares, grad_shares, sums)
                ]
                for g, cut in enumerate(cuts):
                    value_sum[cut, lane_j] += mm(grads[g], shares[g].astype(LOW), 1, 1)
                for g, cut in enumerate(cuts):
                    key_sum[cut, lane_j] += mm(queries[g], grad_scores[g], 1, 1)
                return tuple(
                    state[g] + mm(keys[g], grad_scores[g]) for g in range(GROUP)
                )

            begin = (jnp.zeros((head, TILE), WIDE),) * GROUP
            state = lax.fori_loop(bounds[i, 0], bounds[i, 1], inner, begin)
            for g, h in enumerate(heads):
                grad_turned[at(0, h, i)] = (state[g] * scaling).astype(LOW)
            return carry

        lax.fori_loop(0, tiles, over_queries, 0)
        size = GROUP * head
        key_at = pl.ds(pl.multiple_of(part + group * size, size), size)
        value_at = pl.ds(pl.multiple_of(2 * part + group * size, size), size)
        grad_turned[key_at, :] = (key_sum[...] * scaling).astype(LOW)
        grad_turned[value_at, :] = value_sum[...].astype(LOW)
        return carry

    lax.fori_loop(0, part // head // GROUP, over_group, 0)
    for c in range(0, 3 * part, TILE):
        grad_qkv_w[:, c : c + TILE] = jnp.transpose(
            mm(grad_turned[c : c + TILE, :rows], first[...]).astype(LOW)
        )
    for c in range(0, width, TILE):
        partial[:, c : c + TILE] = jnp.transpose(
            mm(qkv_w[c : c + TILE, :], grad_turned[:, :rows]).astype(LOW)
        )


def encoder_attend_back(
    slots, bounds, first, turned, mixture, log_sum, grad_low, qkv_w, out_w, head
):
    rows, width = first.shape
    part, lanes = mixture.shape
    return pl.pallas_call(
        functools.partial(attend_back_kernel, head),
        in_specs=[pl.BlockSpec(memory_space=pltpu.SMEM)]
        + [pl.BlockSpec(memory_space=pltpu.VMEM)] * 9,
        out_specs=[pl.BlockSpec(memory_space=pltpu.VMEM)] * 3,
        out_shape=[
            jax.ShapeDtypeStruct((width, 3 * part), LOW),
            jax.ShapeDtypeStruct((width, part), LOW),
            jax.ShapeDtypeStruct((rows, width), LOW),
        ],
        scratch_shapes=[
            pltpu.VMEM((part, lanes), LOW),
            pltpu.VMEM((3 * part, lanes), LOW),
            pltpu.VMEM((part // head, lanes), WIDE),
            pltpu.VMEM((GROUP * head, lanes), WIDE),
            pltpu.VMEM((GROUP * head, lanes), WIDE),
        ],
        compiler_params=pltpu.CompilerParams(vmem_limit_bytes=60 * 2**20),
    )(
        bounds,
        slots[None, :],
        slots[:, None],
        first,
        turned,
        mixture,
        log_sum,
        grad_low,
        qkv_w,
        out_w,
    )


def feed_kernel(stream, own, other, gains, up_w, down_w, after, second, hidden, slope, partial):
    summed = stream[...].astype(WIDE) + (own[...].astype(WIDE) + other[...].astype(WIDE))
    after[...] = summed
    unit, _ = centre(summed)
    second[...] = (unit * gains[2:3] + gains[3:4]).astype(LOW)
    units = up_w.shape[1]
    for c in range(0, units, TILE):
        cut = slice(c, c + TILE)
        h, g = gelu_pair(mm(second[...], up_w[:, cut]))
        hidden[:, cut] = h.astype(LOW)
        slope[:, cut] = g.astype(LOW)
    partial[...] = mm(hidden[...], down_w[...], 1, 1).astype(LOW)


def encoder_feed(stream, own, other, gains, up_w, down_w, block):
    rows, width = stream.shape
    units = up_w.shape[1]
    wide, tall = down_rows(block, width), down_rows(block, units)
    return pl.pallas_call(
        feed_kernel,
        grid=(rows // block,),
        in_specs=[wide, wide, wide, fixed((4, width)), fixed(up_w.shape), fixed(down_w.shape)],
        out_specs=[wide, wide, tall, tall, wide],
        out_shape=[
            jax.ShapeDtypeStruct((rows, width), WIDE),
            jax.ShapeDtypeStruct((rows, width), LOW),
            jax.ShapeDtypeStruct((rows, units), LOW),
            jax.ShapeDtypeStruct((rows, units), LOW),
            jax.ShapeDtypeStruct((rows, width), LOW),
        ],
        compiler_params=params(),
    )(stream, own, other, gains, up_w, down_w)


def feed_back_kernel(
    counts,
    own,
    other,
    second,
    hidden,
    slope,
    up_w,
    down_w,
    grad_up,
    grad_down,
    partial,
    grad_low,
    grad_turned,
    second_turned,
    total,
):
    @pl.when(pl.program_id(0) == 0)
    def _():
        grad_low[...] = (own[...].astype(WIDE) + other[...].astype(WIDE)).astype(LOW)
        grad_turned[...] = jnp.transpose(grad_low[...])
        second_turned[...] = jnp.transpose(second[...])
        total[...] = jnp.zeros_like(total)

    down = mm(grad_turned[...], hidden[...])
    grad_down[...] = jnp.where(counts[0] > 0, down, jnp.zeros_like(down)).astype(LOW)
    grad_z = (mm(grad_low[...], down_w[...]) * slope[...].astype(WIDE)).astype(LOW)
    grad_up[...] = mm(second_turned[...], grad_z).astype(LOW)
    total[...] += mm(grad_z, up_w[...], 1, 1)

    @pl.when(pl.program_id(0) == pl.num_programs(0) - 1)
    def _():
        partial[...] = total[...].astype(LOW)


def encoder_feed_back(counts, own, other, second, hidden, slope, up_w, down_w):
    rows, width = own.shape
    units = up_w.shape[1]
    piece = 256
    whole = fixed((rows, width))
    tall = pl.BlockSpec((rows, piece), lambda i: (0, i))
    weight = pl.BlockSpec((width, piece), lambda i: (0, i))
    return pl.pallas_call(
        feed_back_kernel,
        grid=(units // piece,),
        in_specs=[pl.BlockSpec(memory_space=pltpu.SMEM)]
        + [whole, whole, whole, tall, tall, weight, weight],
        out_specs=[weight, weight, whole],
        out_shape=[
            jax.ShapeDtypeStruct((width, units), LOW),
            jax.ShapeDtypeStruct((width, units), LOW),
            jax.ShapeDtypeStruct((rows, width), LOW),
        ],
        scratch_shapes=[
            pltpu.VMEM((rows, width), LOW),
            pltpu.VMEM((width, rows), LOW),
            pltpu.VMEM((width, rows), LOW),
            pltpu.VMEM((rows, width), WIDE),
        ],
        compiler_params=params(),
    )(counts, own, other, second, hidden, slope, up_w, down_w)


def norm_back_kernel(tokens, own, other, skip_own, skip_other, gains, grad, grad_low, grad_gains, *, at):
    @pl.when(pl.program_id(0) == 0)
    def _():
        grad_gains[...] = jnp.zeros_like(grad_gains)

    pulled = own[...].astype(WIDE) + other[...].astype(WIDE)
    unit, scale = centre(tokens[...].astype(WIDE))
    result = skip_own[...].astype(WIDE)
    if skip_other is not None:
        result = result + skip_other[...].astype(WIDE)
    result = result + centre_back(unit, scale, gains[at : at + 1], pulled)
    grad[...] = result
    if grad_low is not None:
        grad_low[...] = result.astype(LOW)
    grad_gains[0:1] += jnp.sum(pulled * unit, axis=0, keepdims=True)
    grad_gains[1:2] += jnp.sum(pulled, axis=0, keepdims=True)


def encoder_norm_back(tokens, own, other, skip, gains, at, block, low):
    rows, width = tokens.shape
    wide = down_rows(block, width)
    two = len(skip) == 2

    def kernel(*refs):
        refs = list(refs)
        if not two:
            refs.insert(4, None)
        if not low:
            refs.insert(7, None)
        norm_back_kernel(*refs, at=at)

    shapes = [jax.ShapeDtypeStruct((rows, width), WIDE)]
    if low:
        shapes.append(jax.ShapeDtypeStruct((rows, width), LOW))
    shapes.append(jax.ShapeDtypeStruct((8, width), WIDE))
    return pl.pallas_call(
        kernel,
        grid=(rows // block,),
        in_specs=[wide, wide, wide] + [wide] * len(skip) + [fixed((4, width))],
        out_specs=[wide] * (2 if low else 1) + [fixed((8, width))],
        out_shape=shapes,
        compiler_params=params(),
    )(tokens, own, other, *skip, gains)


def finish_kernel(length, flag, tokens, own, other, skip, gains, decoded, result, grad_gains):
    pulled = own[...].astype(WIDE) + other[...].astype(WIDE)
    unit, scale = centre(tokens[...].astype(WIDE))
    grad_gains[...] = jnp.zeros_like(grad_gains)
    grad_gains[0:1] = jnp.sum(pulled * unit, axis=0, keepdims=True)
    grad_gains[1:2] = jnp.sum(pulled, axis=0, keepdims=True)
    rows, width = tokens.shape
    pieces = width // 128

    @pl.when(flag[0] > 0)
    def _():
        grad = skip[...] + centre_back(unit, scale, gains[0:1], pulled)
        for k in range(pieces):
            result[pl.ds(k, rows, stride=pieces), :] = grad[:, k * 128 : (k + 1) * 128]

    @pl.when(flag[0] == 0)
    def _():
        images, _, columns = decoded.shape
        count = columns // 128
        for i in range(images):
            for k in range(count):
                result[pl.ds(i * length * count + k, length, stride=count), :] = decoded[
                    i, 0:length, k * 128 : (k + 1) * 128
                ]


def encoder_finish(encoder_side, tokens, own, other, skip, gains, decoded, length):
    rows, width = tokens.shape
    return pl.pallas_call(
        functools.partial(finish_kernel, length),
        in_specs=[pl.BlockSpec(memory_space=pltpu.SMEM)]
        + [pl.BlockSpec(memory_space=pltpu.VMEM)] * 6,
        out_specs=[pl.BlockSpec(memory_space=pltpu.VMEM)] * 2,
        out_shape=[
            jax.ShapeDtypeStruct((rows * width // 128, 128), WIDE),
            jax.ShapeDtypeStruct((8, width), WIDE),
        ],
        compiler_params=pltpu.CompilerParams(vmem_limit_bytes=60 * 2**20),
    )(encoder_side.astype(jnp.int32).reshape(1), tokens, own, other, skip, gains, decoded)


def from_behind(value, axis, by):
    length = lax.axis_size(axis)
    pairs = [(i, i + by) for i in range(length) if 0 <= i + by < length]
    return lax.ppermute(value, axis, pairs)


def partner(value):
    length = lax.axis_size("mp")
    return lax.ppermute(value, "mp", [(i, (i + 1) % length) for i in range(length)])


def is_fast():
    return lax.axis_size("section") == 2 and lax.axis_size("dp") == 8


def plan(widths, pieces, dec_width, orders, dec_orders):
    enc = chunk_list(widths, pieces, 0, orders)
    dec = [
        (len(widths), b, c, w, o, k)
        for _, b, c, w, o, k in chunk_list((dec_width,), (4,), 1, dec_orders)
    ]
    for k, chunk in enumerate(dec):
        enc.insert(3 * k + 2, chunk)
    return enc


def gather_all(low_enc, low_dec, norms, widths):
    count = len(widths)
    if not is_fast():
        both = ("section", "dp")
        enc = lax.all_gather(low_enc, both, axis=0, tiled=True)
        dec = lax.all_gather(low_dec, both, axis=0, tiled=True)
        rows = lax.all_gather(norms, both, axis=0, tiled=True)
        parts, column = [], 0
        for w in widths:
            parts.append(enc[:, column : column + w])
            column += w
        return parts, dec, rows
    columns = [sum(widths[:k]) for k in range(count + 1)]
    ahead = [low_enc[:, : columns[3]], low_enc[:, columns[4] :]]
    near = (*widths[:3], widths[4])
    chunks = plan(near, (4, 1, 4, 2), low_dec.shape[1], GATHER_ORDERS, DEC_GATHER_ORDERS)
    outputs = [(low_enc.shape[0], w, LOW) for w in near]
    outputs += [(low_dec.shape[0], low_dec.shape[1], LOW), (8, 128, WIDE)]
    described = [(k // 4, k, c, b, w, o, own) for k, b, c, w, o, own in chunks]
    described.append((2, 5, 0, 0, 128, "hlyx", BOTH))
    shards = [jnp.concatenate(ahead, axis=1), low_dec, norms]
    results = gather_weights(shards, outputs, described, 1, GATHER_AHEAD, GATHER_LAG)
    low_down, norm_rows = lax.optimization_barrier(
        (low_enc[:, columns[3] : columns[4]], results[5])
    )
    down = lax.all_gather(low_down, ("section", "dp"), axis=0, tiled=True)
    return [*results[:3], down, results[3]], results[4], norm_rows


def scatter_all(enc_parts, dec, norms, encoder_side):
    widths = [p.shape[1] for p in enc_parts]
    both = ("section", "dp")

    def scattered(v):
        return lax.psum_scatter(v, both, scatter_dimension=0, tiled=True)

    if not is_fast():
        parts = [scattered(jnp.where(encoder_side, p.astype(WIDE), 0.0)) for p in enc_parts]
        dec = scattered(jnp.where(encoder_side, 0.0, dec.astype(WIDE)))
        norms = lax.psum(scattered(norms), "mp")
        local = sum(jnp.sum(v * v) for v in (*parts, dec))
        local = local + jnp.sum(norms * norms) / lax.axis_size("mp")
        total = jnp.full((8, 128), lax.psum(local, (*both, "mp")))
        return jnp.concatenate([*parts[:3], parts[4]], axis=1), parts[3], dec, norms, total
    down = scattered(enc_parts[3])
    near = (*enc_parts[:3], enc_parts[4])
    near_widths = (*widths[:3], widths[4])
    chunks = plan(near_widths, (4, 1, 4, 2), dec.shape[1], SCATTER_ORDERS, DEC_SCATTER_ORDERS)
    described = [(k, k // 4, b, c, w, o, own) for k, b, c, w, o, own in chunks]
    described.append((5, 2, 0, 0, 128, "xylh", BOTH))
    rows = near[0].shape[0] // 16
    outputs = [(rows, sum(near_widths)), (dec.shape[0] // 16, dec.shape[1]), (8, 128)]
    enc, dec, norms, total = scatter_grads(
        [*near, dec, norms], down, outputs, described, 2, SCATTER_AHEAD, SCATTER_LAG
    )
    return enc, down, dec, norms, total


def pack_norms(enc_rows, dec_rows, blocks):
    both = [rows.reshape(4, blocks, -1).transpose(1, 0, 2) for rows in (enc_rows, dec_rows)]
    joined = jnp.concatenate(both, axis=2)
    joined = jnp.pad(joined, ((0, 0), (0, 4), (0, 128 - joined.shape[2])))
    return joined.reshape(blocks * 8, 128)


def unpack_norms(packed, blocks, enc_width, dec_width):
    split = packed.reshape(blocks, 8, 128)[:, :4].transpose(1, 0, 2)
    return (
        split[:, :, :enc_width].reshape(4, -1),
        split[:, :, enc_width : enc_width + dec_width].reshape(4, -1),
    )


def key_ranges(slots):
    tiles = slots.reshape(-1, TILE)
    low, high = jnp.min(tiles, axis=1), jnp.max(tiles, axis=1)
    meet = jnp.logical_and(low[:, None] <= high[None, :], high[:, None] >= low[None, :])
    index = jnp.arange(tiles.shape[0], dtype=jnp.int32)[None, :]
    first = jnp.min(jnp.where(meet, index, tiles.shape[0]), axis=1)
    last = jnp.max(jnp.where(meet, index + 1, 0), axis=1)
    return jnp.stack([first, last], axis=1)


def renewed(weight, first_moment, second_moment, clipped, rate, fix_first, fix_second, decay):
    new_first = BETA_FIRST * first_moment + (1.0 - BETA_FIRST) * clipped
    new_second = BETA_SECOND * second_moment + (1.0 - BETA_SECOND) * clipped * clipped
    stepped = new_first / fix_first / (jnp.sqrt(new_second / fix_second) + ADAM_EPS)
    return weight - rate * (stepped + decay * weight)


def renew_kernel(order, scalars, total, near, down, dec, norms, *refs):
    enc_state, dec_state, enc_norm_state, dec_norm_state = (refs[k : k + 3] for k in (0, 3, 6, 9))
    new_enc, new_dec, new_enc_norm, new_dec_norm, enc_clip, dec_clip, enc_norm_clip, dec_norm_clip = refs[12:]
    factor = jnp.minimum(1.0, math.sqrt(PARAMS) / (jnp.sqrt(total[0:1, :]) + 1e-06))
    fixes = scalars[2], scalars[3]

    def work(blocks, state, new, clip):
        count = len(blocks)
        for k, (ref, at) in enumerate(blocks):
            rows = pl.ds(k, ref.shape[0], stride=count)
            clipped = ref[:, at : at + 128].astype(WIDE) * factor
            values = [s[rows, :] for s in state]
            clip[rows, :] = clipped
            new[rows, :] = renewed(*values, clipped, scalars[0], *fixes, WEIGHT_DECAY)

    work([((near, down)[which], at) for which, at in order], enc_state, new_enc, enc_clip)
    work([(dec, at) for at in range(0, dec.shape[1], 128)], dec_state, new_dec, dec_clip)
    column = 0
    for state, new, clip in (
        (enc_norm_state, new_enc_norm, enc_norm_clip),
        (dec_norm_state, new_dec_norm, dec_norm_clip),
    ):
        rows, width = new.shape
        clipped = norms[0:rows, column : column + width] * factor[:, :width]
        column += width
        clip[...] = clipped
        new[...] = renewed(*[s[...] for s in state], clipped, scalars[1], *fixes, 0.0)


def renew_all(scalars, total, near, down, down_at, dec, norms, enc, decoder, enc_norm, dec_norm):
    order = [(0, at) for at in range(0, near.shape[1], 128)]
    order[down_at // 128 : down_at // 128] = [(1, at) for at in range(0, down.shape[1], 128)]
    flat = [[v.reshape(-1, 128) for v in group] for group in (enc, decoder)]
    groups = [*flat, enc_norm, dec_norm]
    shapes = [jax.ShapeDtypeStruct(group[0].shape, WIDE) for group in groups] * 2
    results = pl.pallas_call(
        functools.partial(renew_kernel, order),
        in_specs=[pl.BlockSpec(memory_space=pltpu.SMEM)]
        + [pl.BlockSpec(memory_space=pltpu.VMEM)] * 17,
        out_specs=[pl.BlockSpec(memory_space=pltpu.VMEM)] * 8,
        out_shape=shapes,
        compiler_params=pltpu.CompilerParams(vmem_limit_bytes=40 * 2**20),
    )(scalars, total, near, down, dec, norms, *[v for group in groups for v in group])
    given = (enc, decoder, enc_norm, dec_norm) * 2
    return [r.reshape(group[0].shape) for r, group in zip(results, given)]


def per_device(
    act_in,
    packing,
    enc_weights,
    enc_first,
    enc_second,
    dec_weights,
    dec_first,
    dec_second,
    enc_norms,
    enc_norm_first,
    enc_norm_second,
    dec_norms,
    dec_norm_first,
    dec_norm_second,
    mask_token,
    dec_position,
    learning_rate,
    step_count,
):
    encoder_side = lax.axis_index("section") == 0
    decoder_side = jnp.logical_not(encoder_side)
    mp_rank = lax.axis_index("mp")
    mp_count = lax.axis_size("mp")
    first_half = mp_rank == 0
    slot_ids = packing[0, 0]
    patch_ids = packing[0, 1]
    local_images = IMG // mp_count
    grid_cells = local_images * GRID
    local_slot = slot_ids - mp_rank * local_images
    inside = jnp.logical_and(local_slot >= 0, local_slot < local_images)
    target = jnp.where(inside, local_slot * GRID + patch_ids, grid_cells)

    local_rows, width = act_in.shape[1], act_in.shape[2]
    real_rows = local_rows * mp_count
    rows = -(-real_rows // ROW_BLOCK) * ROW_BLOCK
    lanes = -(-rows // TILE) * TILE
    part = width // mp_count
    units = FF // mp_count
    head = width // HEADS
    dec_width = dec_position.shape[1]
    dec_part = dec_width // mp_count
    widths = (3 * part, part, units, units, dec_part)
    slots = jnp.pad(slot_ids, (0, lanes - real_rows), constant_values=IMG + 1)
    ranges = key_ranges(slots)

    (qkv_w, out_w, up_w, down_w, projection), dec_own, norm_rows = gather_all(
        enc_weights[:, 0, :].astype(LOW),
        dec_weights[:, 0, :].astype(LOW),
        pack_norms(enc_norms, dec_norms, 1),
        widths,
    )
    enc_gains, dec_gains = (
        v.astype(LOW).astype(WIDE)
        for v in unpack_norms(
            norm_rows, norm_rows.shape[0] // 8, enc_norms.shape[1], dec_norms.shape[1]
        )
    )
    own_stream, other_stream = act_in[0], partner(act_in[0])
    stream = jnp.where(
        first_half,
        jnp.concatenate([own_stream, other_stream], axis=0),
        jnp.concatenate([other_stream, own_stream], axis=0),
    )
    stream = jnp.pad(stream, ((0, rows - real_rows), (0, 0)))
    first, turned, mixture, log_sum, mix_own = encoder_attend(
        stream, slots, ranges, enc_gains, qkv_w, out_w, head
    )
    shown = min(real_rows, -(-IMG * MOST_VISIBLE // 16) * 16)
    packed = -(-shown // 128) * 128
    cell_rows = -(-GRID // 16) * 16
    longer = (0, cell_rows - GRID)
    seen_target = jnp.pad(target[:shown], (0, packed - shown), constant_values=-1)
    cotangent = act_in[0].reshape(local_images, GRID, dec_width)
    cotangent = jnp.pad(cotangent, ((0, 0), longer, (0, 0)))
    position = jnp.pad(dec_position, (longer, (0, 0)))
    mix_other, seen_target, cotangent, position, dec_gains = lax.optimization_barrier(
        (partner(mix_own), seen_target, cotangent, position, dec_gains)
    )
    after, second, hidden, slope, feed_own = encoder_feed(
        stream, mix_own, mix_other, enc_gains, up_w, down_w, ROW_BLOCK
    )
    encoded = (after + (feed_own.astype(WIDE) + partner(feed_own).astype(WIDE))).astype(LOW)
    projected = mm(encoded[:shown], projection).astype(LOW)
    arrived = from_behind(projected, "section", 1)
    arrived = jnp.pad(arrived, ((0, packed - shown), (0, 0)))
    decoded, grad_keep, grad_send, dec_grad_own, dec_grad_other, dec_gain_grad = decoder_step(
        GRID,
        first_half,
        arrived,
        partner(arrived),
        seen_target,
        mask_token,
        position,
        dec_gains,
        dec_own,
        partner(dec_own),
        cotangent,
    )
    returned = grad_keep[:shown] + partner(grad_send[:shown])
    grad_projected = from_behind(returned, "section", -1)
    grad_projected = jnp.pad(grad_projected, ((0, rows - shown), (0, 0)))
    dec_grad = dec_grad_own.astype(WIDE) + partner(dec_grad_other).astype(WIDE)
    dec_grad = dec_grad.astype(LOW)

    grad_projection = mm(encoded, grad_projected, 0, 0).astype(LOW)
    end_own = mm(grad_projected, projection, 1, 1).astype(LOW)
    end_other = partner(end_own)
    grad_up_w, grad_down_w, back_own = encoder_feed_back(
        jnp.where(encoder_side, 1, 0).astype(jnp.int32).reshape(1),
        end_own,
        end_other,
        second,
        hidden,
        slope,
        up_w,
        down_w,
    )
    grad_after, grad_low, gains_two = encoder_norm_back(
        after, back_own, partner(back_own), (end_own, end_other), enc_gains, 2, ROW_BLOCK, True
    )
    grad_qkv_w, grad_out_w, start_own = encoder_attend_back(
        slots, ranges, first, turned, mixture, log_sum, grad_low, qkv_w, out_w, head
    )
    def choose(matrix):
        top, bottom = matrix[:local_rows], matrix[local_rows:real_rows]
        return jnp.where(first_half, top, bottom), jnp.where(first_half, bottom, top)

    start_keep, start_send = choose(start_own)
    act_out, gains_one = encoder_finish(
        encoder_side,
        own_stream,
        start_keep,
        partner(start_send),
        choose(grad_after)[0],
        enc_gains,
        decoded,
        GRID,
    )
    enc_gain_grad = jnp.concatenate(
        [gains_one[:2], jnp.where(first_half, gains_two[:2], 0.0)], axis=0
    )
    norm_grads = pack_norms(
        jnp.where(encoder_side, enc_gain_grad, 0.0),
        jnp.where(decoder_side, dec_gain_grad, 0.0),
        norm_rows.shape[0] // 8,
    )
    near_shard, down_shard, dec_shard, norm_shard, square_total = scatter_all(
        (grad_qkv_w, grad_out_w, grad_up_w, grad_down_w, grad_projection),
        dec_grad,
        norm_grads,
        encoder_side,
    )
    step_value = step_count[0].astype(jnp.float32)
    scalars = jnp.stack(
        [
            learning_rate[0],
            learning_rate[1],
            1.0 - jnp.power(BETA_FIRST, step_value),
            1.0 - jnp.power(BETA_SECOND, step_value),
        ]
    )
    results = renew_all(
        scalars,
        square_total,
        near_shard,
        down_shard,
        sum(widths[:3]),
        dec_shard,
        norm_shard,
        (enc_weights, enc_first, enc_second),
        (dec_weights, dec_first, dec_second),
        (enc_norms, enc_norm_first, enc_norm_second),
        (dec_norms, dec_norm_first, dec_norm_second),
    )
    return (act_out.reshape(act_in.shape), *results, jnp.sqrt(square_total[0, 0]).reshape(1))


def solution(mesh):
    in_specs = (
        P("section", ("dp", "mp"), None),
        P("dp", None, None),
        P(("section", "dp"), "mp", None),
        P(("section", "dp"), "mp", None),
        P(("section", "dp"), "mp", None),
        P(("section", "dp"), "mp", None),
        P(("section", "dp"), "mp", None),
        P(("section", "dp"), "mp", None),
        P(None, ("section", "dp")),
        P(None, ("section", "dp")),
        P(None, ("section", "dp")),
        P(None, ("section", "dp")),
        P(None, ("section", "dp")),
        P(None, ("section", "dp")),
        P(),
        P(),
        P(),
        P(),
    )
    out_specs = (
        P("section", ("dp", "mp"), None),
        P(("section", "dp"), "mp", None),
        P(("section", "dp"), "mp", None),
        P(None, ("section", "dp")),
        P(None, ("section", "dp")),
        P(("section", "dp"), "mp", None),
        P(("section", "dp"), "mp", None),
        P(None, ("section", "dp")),
        P(None, ("section", "dp")),
        P(),
    )
    return jax.shard_map(
        per_device, mesh=mesh, in_specs=in_specs, out_specs=out_specs, check_vma=False
    )
```

```python
import functools
import itertools
import math

import jax
import jax.numpy as jnp
from jax import lax
from jax.experimental import pallas as pl
from jax.experimental.pallas import tpu as pltpu
from jax.sharding import PartitionSpec as P

FF = 4096
GRID = 196
IMG = 12
PARAMS = 16259072

BETA_FIRST = 0.9
BETA_SECOND = 0.999
ADAM_EPS = 1e-08
WEIGHT_DECAY = 0.05
ROW_BLOCK = 240
MOST_VISIBLE = 73
GATHER_ORDERS = ("hlxy", "hlyx", "hlxy", "hlyx", "yxhl")
DEC_GATHER_ORDERS = ("xhly", "xyhl")
DEC_SCATTER_ORDERS = ("ylhx", "ylhx")
PIECES, DEC_PIECES = (6, 2, 8, 1), 4
GATHER_AHEAD, GATHER_LAG = 6, (3, 6)
SCATTER_AHEAD, SCATTER_LAG = 6, (3, 3, 3)
SCATTER_ORDERS = ("xylh", "yxlh", "xylh", "yxlh", "lhxy")

MESH_ID = pl.DeviceIdType.MESH
EVERY = slice(None)
BOTH = -1
DIMS = "xhly"


class Place:
    def __init__(self):
        s, depth, core = lax.axis_index("section"), lax.axis_index("dp"), lax.axis_index("mp")
        y, low, high = depth % 2, (depth // 2) % 2, depth // 4
        self.at = {"x": s, "h": high, "l": low, "y": y}
        self.s, self.core = s, core
        self.device = {
            "x": (1 - s, depth, core),
            "h": (s, depth + 4 - 8 * high, core),
            "l": (s, depth + 2 - 4 * low, core),
            "y": (s, depth + 1 - 2 * y, core),
            "c": (s, depth, 1 - core),
        }

    def greet(self):
        barrier = pltpu.get_barrier_semaphore()
        for name in self.device:
            pl.semaphore_signal(
                barrier, inc=1, device_id=self.device[name], device_id_type=MESH_ID
            )
        pl.semaphore_wait(barrier, len(self.device))


def run(condition, action):
    if condition is None:
        action()
    else:
        pl.when(condition)(action)


def gather_kernel(chunks, n_in, n_out, ahead, lag, *refs):
    ins, outs = refs[:n_in], refs[n_in : n_in + n_out]
    send, recv, local = refs[n_in + n_out :]
    here = Place()
    count = len(chunks)

    def region(chunk, gathered, sender):
        at = [
            EVERY if d in gathered else 1 - here.at[d] if d == sender else here.at[d] for d in DIMS
        ]
        return outs[chunk[1]].at[(*at, EVERY, pl.ds(chunk[3], chunk[4]))]

    def own(i):
        chunk = chunks[i]
        return pltpu.make_async_copy(
            ins[chunk[0]].at[:, pl.ds(chunk[2], chunk[4])], region(chunk, "", None), local.at[i]
        )

    def copy(i, stage, incoming):
        chunk = chunks[i]
        order = chunk[5]
        axis = order[stage]
        block = region(chunk, order[:stage], axis if incoming else None)
        source = block
        if stage == 0 and not incoming:
            source = ins[chunk[0]].at[:, pl.ds(chunk[2], chunk[4])]
        return pltpu.make_async_remote_copy(
            src_ref=source,
            dst_ref=block,
            send_sem=send.at[i, stage],
            recv_sem=recv.at[i, stage],
            device_id=here.device[axis],
            device_id_type=MESH_ID,
        )

    def roles(i, stage):
        order, owner = chunks[i][5], chunks[i][6]
        if owner == BOTH:
            return None, None
        if order[stage] == "x":
            return here.s != owner, here.s == owner
        if "x" in order[:stage]:
            return here.s == owner, here.s == owner
        return None, None

    def begin(i, stage):
        run(roles(i, stage)[0], lambda: copy(i, stage, False).start())

    def arrive(i, stage):
        run(roles(i, stage)[1], lambda: copy(i, stage, True).wait_recv())
        if stage == 0:
            own(i).wait()

    here.greet()
    for i in range(count):
        own(i).start()
    for i in range(min(ahead, count)):
        begin(i, 0)
    for step in range(count + sum(lag)):
        for stage in range(3):
            i = step - sum(lag[:stage])
            if not 0 <= i < count:
                continue
            arrive(i, stage)
            begin(i, stage + 1)
            if stage == 0 and i + ahead < count:
                begin(i + ahead, 0)
    for i in range(count):
        arrive(i, 3)
    for i in range(count):
        for stage in range(4):
            run(
                roles(i, stage)[0],
                lambda i=i, stage=stage: copy(i, stage, False).wait_send(),
            )


def gather_weights(shards, outputs, chunks, collective_id, ahead=4, lag=(1, 1)):
    count = len(chunks)
    call = pl.pallas_call(
        functools.partial(gather_kernel, chunks, len(shards), len(outputs), ahead, lag),
        out_shape=[
            jax.ShapeDtypeStruct((2, 2, 2, 2, rows, width), dtype) for rows, width, dtype in outputs
        ],
        in_specs=[pl.BlockSpec(memory_space=pltpu.VMEM)] * len(shards),
        out_specs=[pl.BlockSpec(memory_space=pltpu.HBM)] * len(outputs),
        scratch_shapes=[
            pltpu.SemaphoreType.DMA((count, 4)),
            pltpu.SemaphoreType.DMA((count, 4)),
            pltpu.SemaphoreType.DMA((count,)),
        ],
        compiler_params=pltpu.CompilerParams(
            collective_id=collective_id, has_side_effects=True, vmem_limit_bytes=40 * 2**20
        ),
    )
    results = call(*shards)
    return [
        r.reshape(16 * rows, width) for r, (rows, width, _) in zip(results, outputs, strict=True)
    ]


def spread(total, pieces, unit=128):
    units = total // unit
    widths = [units // pieces + (1 if k < units % pieces else 0) for k in range(pieces)]
    return [w * unit for w in widths if w]


def chunk_list(widths, pieces, owner, orders):
    chunks = []
    column = turn = 0
    for index, (width, count) in enumerate(zip(widths, pieces, strict=True)):
        begin = 0
        for piece in spread(width, count):
            chunks.append((index, begin, column, piece, orders[turn % len(orders)], owner))
            begin += piece
            column += piece
            turn += 1
    return chunks


def left_after(order, stage):
    return [d for d in DIMS if d not in order[: stage + 1]]


def scatter_buffers(order, owner):
    shapes = [(2,) * 3]
    for stage in range(4):
        if order[stage] == "x" and owner != BOTH:
            continue
        shapes.append((2,) * (3 - stage))
    return shapes


def squares(ref):
    def step(k, total):
        block = ref[:, pl.ds(pl.multiple_of(k * 128, 128), 128)].astype(jnp.float32)
        block = block * block
        for r in range(0, block.shape[0], 8):
            total = total + block[r : r + 8]
        return total

    return lax.fori_loop(0, ref.shape[1] // 128, step, jnp.zeros((8, 128), jnp.float32))


def scatter_kernel(chunks, n_in, n_out, ahead, lag, cores, *refs):
    ins, summed, outs = refs[:n_in], refs[n_in], refs[n_in + 1 : n_in + 1 + n_out]
    square_total = refs[n_in + 1 + n_out]
    rest = refs[n_in + n_out + 2 :]
    send, recv, local, square_send, square_recv, square_mine, square_there, last, last_there = rest[:9]
    here = Place()
    s = here.s
    count = len(chunks)
    given, ins = ins[-1], (*ins[:-1], last)
    own, got = [], []
    position = 9
    for chunk in chunks:
        order, owner = chunk[5], chunk[6]
        own.append(rest[position])
        position += 1
        mine = []
        for stage in range(4):
            if order[stage] == "x" and owner != BOTH:
                mine.append(None)
                continue
            mine.append(rest[position])
            position += 1
        got.append(mine)

    def source(i, axis, keep):
        chunk = chunks[i]
        at = [
            (here.at[d] if keep else 1 - here.at[d]) if d == axis else EVERY for d in DIMS
        ]
        return ins[chunk[0]].at[(*at, EVERY, pl.ds(chunk[2], chunk[4]))]

    def load(i):
        return pltpu.make_async_copy(source(i, chunks[i][5][0], True), own[i], local.at[i])

    def spot(i, stage, flip):
        order = chunks[i][5]
        at = []
        for d in DIMS:
            if d == order[0]:
                continue
            if d in order[:stage]:
                at.append(here.at[d])
            elif d == order[stage]:
                at.append(1 - here.at[d] if flip else here.at[d])
            else:
                at.append(EVERY)
        return tuple(at)

    def copy(i, stage, incoming):
        order = chunks[i][5]
        axis = order[stage]
        moved = got[i][stage] is None
        src = source(i, axis, False) if stage == 0 else own[i].at[spot(i, stage, True)]
        if not moved:
            there = mine = got[i][stage]
        elif stage == 0:
            there = mine = own[i]
        else:
            there, mine = own[i].at[spot(i, stage, True)], own[i].at[spot(i, stage, False)]
        return pltpu.make_async_remote_copy(
            src_ref=mine if incoming else src,
            dst_ref=mine if incoming else there,
            send_sem=send.at[i, stage],
            recv_sem=recv.at[i, stage],
            device_id=here.device[axis],
            device_id_type=MESH_ID,
        )

    def roles(i, stage):
        order, owner = chunks[i][5], chunks[i][6]
        if owner == BOTH:
            return None, None
        if order[stage] == "x":
            return s == owner, s != owner
        if "x" in order[:stage]:
            return None, None
        return s == owner, s == owner

    def begin(i, stage):
        run(roles(i, stage)[0], lambda: copy(i, stage, False).start())

    def arrive(i, stage):
        chunk, a, r = chunks[i], own[i], got[i][stage]
        order, owner = chunk[5], chunk[6]
        run(roles(i, stage)[1], lambda: copy(i, stage, True).wait_recv())
        if stage == 0:
            run(None if owner == BOTH else s == owner, lambda: load(i).wait())
        out = outs[chunk[1]].at[:, pl.ds(chunk[3], chunk[4])]
        place = spot(i, stage, False)
        if stage == 3:
            result = a[place].astype(jnp.float32)
            if r is not None:
                result = result + r[...].astype(jnp.float32)
            out[...] = result
            return
        if r is None:
            return

        def add():
            free = [k for k, p in enumerate(place) if p is EVERY]
            for combo in itertools.product(range(2), repeat=len(free)):
                at = list(place)
                for k, c in zip(free, combo):
                    at[k] = c
                at = tuple(at)
                a[at] = (a[at].astype(jnp.float32) + r[combo].astype(jnp.float32)).astype(a.dtype)

        run(roles(i, stage)[1], add)

    here.greet()
    join = pltpu.make_async_remote_copy(
        src_ref=given,
        dst_ref=last_there,
        send_sem=square_send.at[5],
        recv_sem=square_recv.at[5],
        device_id=here.device["c"],
        device_id_type=MESH_ID,
    )
    join.start()
    for i in range(count - 1):
        run(
            None if chunks[i][6] == BOTH else s == chunks[i][6],
            lambda i=i: load(i).start(),
        )
    for i in range(min(ahead, count)):
        begin(i, 0)
    join.wait()
    last[...] = given[...] + last_there[...]
    load(count - 1).start()
    for step in range(count + sum(lag)):
        for stage in range(3, -1, -1):
            i = step - sum(lag[:stage])
            if not 0 <= i < count:
                continue
            arrive(i, stage)
            if stage < 3:
                begin(i, stage + 1)
            if stage == 0 and i + ahead < count:
                begin(i + ahead, 0)
    for i in range(count):
        for stage in range(4):
            run(
                roles(i, stage)[0],
                lambda i=i, stage=stage: copy(i, stage, False).wait_send(),
            )

    value = squares(summed)
    for k, out in enumerate(outs):
        value = value + squares(out) * (1.0 / cores if k == n_out - 1 else 1.0)
    value = jnp.broadcast_to(jnp.sum(value, keepdims=True), (8, 128))
    for k, axis in enumerate("cyxlh"):
        square_mine[k] = value
        move = pltpu.make_async_remote_copy(
            src_ref=square_mine.at[k],
            dst_ref=square_there.at[k],
            send_sem=square_send.at[k],
            recv_sem=square_recv.at[k],
            device_id=here.device[axis],
            device_id_type=MESH_ID,
        )
        move.start()
        move.wait()
        value = value + square_there[k]
    square_total[...] = value


def scatter_grads(parts, summed, outputs, chunks, collective_id, ahead=4, lag=(1, 1, 1)):
    count = len(chunks)
    views = [p.reshape(2, 2, 2, 2, p.shape[0] // 16, p.shape[1]) for p in parts]
    buffers = []
    for chunk in chunks:
        view = views[chunk[0]]
        for lead in scatter_buffers(chunk[5], chunk[6]):
            buffers.append(pltpu.VMEM((*lead, view.shape[4], chunk[4]), view.dtype))
    call = pl.pallas_call(
        functools.partial(scatter_kernel, chunks, len(parts), len(outputs), ahead, lag, lax.axis_size("mp")),
        out_shape=[
            jax.ShapeDtypeStruct((rows, width), jnp.float32) for rows, width in [*outputs, (8, 128)]
        ],
        in_specs=[pl.BlockSpec(memory_space=pl.ANY)] * (len(parts) - 1)
        + [pl.BlockSpec(memory_space=pltpu.VMEM)] * 2,
        out_specs=[pl.BlockSpec(memory_space=pltpu.VMEM)] * (len(outputs) + 1),
        scratch_shapes=[
            pltpu.SemaphoreType.DMA((count, 4)),
            pltpu.SemaphoreType.DMA((count, 4)),
            pltpu.SemaphoreType.DMA((count,)),
            pltpu.SemaphoreType.DMA((6,)),
            pltpu.SemaphoreType.DMA((6,)),
            pltpu.VMEM((5, 8, 128), jnp.float32),
            pltpu.VMEM((5, 8, 128), jnp.float32),
            pltpu.VMEM(views[-1].shape, views[-1].dtype),
            pltpu.VMEM(views[-1].shape, views[-1].dtype),
            *buffers,
        ],
        compiler_params=pltpu.CompilerParams(
            collective_id=collective_id, has_side_effects=True, vmem_limit_bytes=56 * 2**20
        ),
    )
    return call(*views, summed)


HEADS = 16
TOGETHER = 8
NORM_EPS = 1e-06
MASKED = -1e30
LOW = jnp.bfloat16
WIDE = jnp.float32


def mm(left, right, left_dim=1, right_dim=0):
    return lax.dot_general(
        left, right, (((left_dim,), (right_dim,)), ((), ())), preferred_element_type=WIDE
    )


def centre(tokens):
    average = jnp.mean(tokens, axis=-1, keepdims=True)
    centred = tokens - average
    spread_ = jnp.mean(centred * centred, axis=-1, keepdims=True)
    scale = lax.rsqrt(spread_ + NORM_EPS)
    return centred * scale, scale


def centre_back(unit, scale, gain, grad):
    pulled = grad * gain
    first = jnp.mean(pulled, axis=-1, keepdims=True)
    second = jnp.mean(pulled * unit, axis=-1, keepdims=True)
    return scale * (pulled - first - unit * second)


def gelu_pair(z):
    cdf = 0.5 * (1.0 + lax.erf(z * math.sqrt(0.5)))
    return z * cdf, cdf + z * (jnp.exp(-0.5 * z * z) * (1.0 / math.sqrt(2.0 * math.pi)))


def decoder_kernel(
    length,
    flag,
    target_row,
    target_column,
    visible_own,
    visible_other,
    mask,
    position,
    gains,
    pack_own,
    pack_other,
    cotangent,
    decoded,
    grad_keep,
    grad_send,
    grad_own,
    grad_other,
    grad_gains,
    qkv_t,
    out_t,
    qkv_rows,
    shares,
    mixture,
    hidden,
    slope,
    grad_mixture,
    stream,
    first,
    after,
    grad_low,
    grad_first,
    grad_visible,
    grad_qkv,
    grad_out,
    grad_up,
    grad_down,
):
    step = pl.program_id(0)
    images, rows, width = decoded.shape
    head = width // HEADS
    units = hidden.shape[1]
    part, half = width // 2, units // 2
    up_at, down_at = 4 * part, 4 * part + half
    scaling = head ** (-0.5)
    packs = (pack_own, pack_other)
    halves = ((slice(0, half), pack_own), (slice(half, units), pack_other))

    @pl.when(step == 0)
    def _():
        for ref in (grad_visible, grad_qkv, grad_out, grad_up, grad_down, grad_gains):
            ref[...] = jnp.zeros_like(ref)
        for which in range(4):
            for k, pack in enumerate(packs):
                at = (2 * which + k) * part
                piece = jnp.transpose(pack[:, which * part : (which + 1) * part])
                if which < 3:
                    qkv_t[at : at + part, :] = piece
                else:
                    out_t[k * part : (k + 1) * part, :] = piece

    packed = target_row.shape[1]
    left = flag[0] > 0
    spans = [slice(k * rows, (k + 1) * rows) for k in range(images)]
    for k, span in enumerate(spans):
        number = step * images + k
        cell = lax.broadcasted_iota(jnp.int32, (rows, packed), 0)
        wanted = jnp.where(cell < length, cell + number * length, -7)
        chosen = (target_row[...] == wanted).astype(WIDE)
        seen = jnp.max(chosen, axis=1, keepdims=True)
        chosen = chosen.astype(LOW)
        placed_own, placed_other = mm(chosen, visible_own[...]), mm(chosen, visible_other[...])
        placed = jnp.concatenate(
            [
                jnp.where(left, placed_own, placed_other),
                jnp.where(left, placed_other, placed_own),
            ],
            axis=1,
        )
        stream[span, :] = jnp.where(seen > 0.0, placed, mask[...]) + position[...]

    unit_one, scale_one = centre(stream[...])
    first[...] = (unit_one * gains[0:1] + gains[1:2]).astype(LOW)
    key_index = lax.broadcasted_iota(jnp.int32, (rows, rows), 0)

    def lines(which, h):
        return slice(which * width + h * head, which * width + (h + 1) * head)

    for k, span in enumerate(spans):
        qkv, mixed = qkv_rows.at[k], mixture.at[k]
        qkv[...] = mm(qkv_t[...], first[span, :], 1, 1).astype(LOW)
        for begin in range(0, HEADS, TOGETHER):
            group = range(begin, begin + TOGETHER)
            scores = [mm(qkv[lines(1, h), :], qkv[lines(0, h), :], 0, 0) * scaling for h in group]
            scores = [jnp.where(key_index < length, s, MASKED) for s in scores]
            weights = [jnp.exp(s - jnp.max(s, axis=0, keepdims=True)) for s in scores]
            group_shares = [w * (1.0 / jnp.sum(w, axis=0, keepdims=True)) for w in weights]
            for h, share in zip(group, group_shares):
                shares[k, h] = share
                mixed[lines(0, h), :] = mm(qkv[lines(2, h), :], share.astype(LOW)).astype(LOW)
        after[span, :] = stream[span, :] + mm(mixed[...], out_t[...], 0, 0)

    unit_two, scale_two = centre(after[...])
    second = (unit_two * gains[2:3] + gains[3:4]).astype(LOW)
    piece = 256
    for c in range(0, units, piece):
        pack, at = packs[c // half], up_at + c % half
        z = mm(second, pack[:, at : at + piece])
        h, g = gelu_pair(z)
        hidden[:, c : c + piece] = h.astype(LOW)
        slope[:, c : c + piece] = g
    fed = [mm(hidden[:, cut], pack[:, down_at : down_at + half], 1, 1) for cut, pack in halves]
    result = after[...] + (fed[0] + fed[1])
    for k, span in enumerate(spans):
        decoded[k] = result[span]

    for k, span in enumerate(spans):
        grad_low[span, :] = cotangent[k]
    turned = jnp.transpose(grad_low[...])
    second_turned = jnp.transpose(second)
    for c in range(0, units, piece):
        cut = slice(c, c + piece)
        grad_down[:, cut] += mm(turned, hidden[:, cut])
        pack, at = packs[c // half], down_at + c % half
        grad_z = (mm(grad_low[...], pack[:, at : at + piece]) * slope[:, cut]).astype(LOW)
        hidden[:, cut] = grad_z
        grad_up[:, cut] += mm(second_turned, grad_z)
    pulled = [mm(hidden[:, cut], pack[:, up_at : up_at + half], 1, 1) for cut, pack in halves]
    grad_second = pulled[0] + pulled[1]
    grad_gains[2:3] += jnp.sum(grad_second * unit_two, axis=0, keepdims=True)
    grad_gains[3:4] += jnp.sum(grad_second, axis=0, keepdims=True)
    after[...] = grad_low[...].astype(WIDE) + centre_back(
        unit_two, scale_two, gains[2:3], grad_second
    )

    for k, span in enumerate(spans):
        qkv, mixed, grad_rows = qkv_rows.at[k], mixture.at[k], grad_mixture.at[k]
        after_low = after[span, :].astype(LOW)
        grad_out[...] += mm(mixed[...], after_low)
        grad_rows[...] = mm(out_t[...], after_low, 1, 1).astype(LOW)
        for begin in range(0, HEADS, TOGETHER):
            group = range(begin, begin + TOGETHER)
            queries = [qkv[lines(0, h), :] for h in group]
            keys = [qkv[lines(1, h), :] for h in group]
            values = [qkv[lines(2, h), :] for h in group]
            grads_in = [grad_rows[lines(0, h), :] for h in group]
            grad_shares = [mm(v, g, 0, 0) for v, g in zip(values, grads_in)]
            grad_values = [mm(g, shares[k, h].astype(LOW), 1, 1) for g, h in zip(grads_in, group)]
            grad_scores = []
            for h, g in zip(group, grad_shares):
                share = shares[k, h]
                inner = jnp.sum(share * g, axis=0, keepdims=True)
                grad_scores.append((share * (g - inner)).astype(LOW))
            for n, h in enumerate(group):
                qkv[lines(0, h), :] = (mm(keys[n], grad_scores[n]) * scaling).astype(LOW)
                qkv[lines(1, h), :] = (mm(queries[n], grad_scores[n], 1, 1) * scaling).astype(LOW)
                qkv[lines(2, h), :] = grad_values[n].astype(LOW)
        grad_qkv[...] += mm(qkv[...], first[span, :])
        grad_first[span, :] = mm(qkv[...], qkv_t[...], 0, 0)

    unit_one, scale_one = centre(stream[...])
    pulled = grad_first[...]
    grad_stream = after[...] + centre_back(unit_one, scale_one, gains[0:1], pulled)
    grad_gains[0:1] += jnp.sum(pulled * unit_one, axis=0, keepdims=True)
    grad_gains[1:2] += jnp.sum(pulled, axis=0, keepdims=True)

    for k, span in enumerate(spans):
        cell_lane = lax.broadcasted_iota(jnp.int32, (packed, rows), 1)
        wanted_lane = jnp.where(cell_lane < length, cell_lane + (step * images + k) * length, -7)
        chosen_back = (target_column[...] == wanted_lane).astype(WIDE).astype(LOW)
        grad_visible[...] += mm(chosen_back, grad_stream[span].astype(LOW))

    @pl.when(step == pl.num_programs(0) - 1)
    def _():
        gathered = grad_visible[...].astype(LOW)
        one, two = gathered[:, :part], gathered[:, part:]
        grad_keep[...] = jnp.where(left, one, two)
        grad_send[...] = jnp.where(left, two, one)
        for k, ref in enumerate((grad_own, grad_other)):
            for which in range(4):
                at = (2 * which + k) * part
                piece = grad_qkv[at : at + part, :] if which < 3 else grad_out[k * part : (k + 1) * part, :]
                ref[:, which * part : (which + 1) * part] = jnp.transpose(piece.astype(LOW))
            cut = slice(k * half, (k + 1) * half)
            ref[:, up_at:down_at] = grad_up[:, cut].astype(LOW)
            ref[:, down_at:] = grad_down[:, cut].astype(LOW)


def decoder_step(
    length, left, visible_own, visible_other, target, mask, position, gains, pack_own, pack_other, cotangent
):
    rows, width = position.shape
    packed = visible_own.shape[0]
    images, columns = cotangent.shape[0], pack_own.shape[1]
    units = columns - 2 * width

    def fixed(shape):
        return pl.BlockSpec(shape, lambda i: (0,) * len(shape), pipeline_mode=pl.Buffered(1))

    at_once = 2 if images % 2 == 0 else 1
    per_image = pl.BlockSpec((at_once, rows, width), lambda i: (i, 0, 0))
    tall = at_once * rows
    grads = [
        ((packed, width // 2), LOW),
        ((packed, width // 2), LOW),
        ((width, columns), LOW),
        ((width, columns), LOW),
        ((8, width), WIDE),
    ]
    decoded, keep, send, grad_own, grad_other, grad_gains = pl.pallas_call(
        functools.partial(decoder_kernel, length),
        grid=(images // at_once,),
        out_shape=[jax.ShapeDtypeStruct((images, rows, width), WIDE)]
        + [jax.ShapeDtypeStruct(s, d) for s, d in grads],
        in_specs=[
            pl.BlockSpec(memory_space=pltpu.SMEM),
            fixed((1, packed)),
            fixed((packed, 1)),
            fixed((packed, width // 2)),
            fixed((packed, width // 2)),
            fixed((1, width)),
            fixed((rows, width)),
            fixed((4, width)),
            fixed((width, columns)),
            fixed((width, columns)),
            per_image,
        ],
        out_specs=[per_image] + [fixed(s) for s, _ in grads],
        scratch_shapes=[
            pltpu.VMEM((3 * width, width), LOW),
            pltpu.VMEM((width, width), LOW),
            pltpu.VMEM((at_once, 3 * width, rows), LOW),
            pltpu.VMEM((at_once, HEADS, rows, rows), WIDE),
            pltpu.VMEM((at_once, width, rows), LOW),
            pltpu.VMEM((tall, units), LOW),
            pltpu.VMEM((tall, units), WIDE),
            pltpu.VMEM((at_once, width, rows), LOW),
            pltpu.VMEM((tall, width), WIDE),
            pltpu.VMEM((tall, width), LOW),
            pltpu.VMEM((tall, width), WIDE),
            pltpu.VMEM((tall, width), LOW),
            pltpu.VMEM((tall, width), WIDE),
            pltpu.VMEM((packed, width), WIDE),
            pltpu.VMEM((3 * width, width), WIDE),
            pltpu.VMEM((width, width), WIDE),
            pltpu.VMEM((width, units), WIDE),
            pltpu.VMEM((width, units), WIDE),
        ],
        compiler_params=pltpu.CompilerParams(
            dimension_semantics=("arbitrary",), vmem_limit_bytes=60 * 2**20
        ),
    )(
        left.astype(jnp.int32).reshape(1),
        target[None, :],
        target[:, None],
        visible_own,
        visible_other,
        mask[None, :],
        position,
        gains,
        pack_own,
        pack_other,
        cotangent,
    )
    return decoded, keep, send, grad_own, grad_other, grad_gains[:4]


TILE = 256
GROUP = 4


def fixed(shape):
    return pl.BlockSpec(shape, lambda i: (0,) * len(shape), pipeline_mode=pl.Buffered(1))


def down_rows(rows, width):
    return pl.BlockSpec((rows, width), lambda i: (i, 0))


def params(megabytes=60):
    return pltpu.CompilerParams(
        dimension_semantics=("arbitrary",), vmem_limit_bytes=megabytes * 2**20
    )


def attend_kernel(
    head, bounds, stream, slots_row, slots_column, gains, qkv_w, out_w, first, turned, mixture, log_sum, partial
):
    rows, width = stream.shape
    part, lanes = mixture.shape
    tiles = lanes // TILE
    scaling = head ** (-0.5)
    unit, _ = centre(stream[...].astype(WIDE))
    first[...] = (unit * gains[0:1] + gains[1:2]).astype(LOW)
    turned[:, rows:] = jnp.zeros((3 * part, lanes - rows), LOW)
    for c in range(0, 3 * part, TILE):
        weight = jnp.transpose(qkv_w[:, c : c + TILE])
        turned[c : c + TILE, :rows] = mm(weight, first[...], 1, 1).astype(LOW)

    def at(which, h, tile):
        return (
            pl.ds(pl.multiple_of(which * part + h * head, head), head),
            pl.ds(pl.multiple_of(tile * TILE, TILE), TILE),
        )

    def step(n, carry):
        group, i = n // tiles, n % tiles
        heads = [group * GROUP + g for g in range(GROUP)]
        lane_i = pl.ds(pl.multiple_of(i * TILE, TILE), TILE)
        queries = [turned[at(0, h, i)] for h in heads]
        slot_i = slots_row[:, lane_i]

        def inner(j, state):
            same = slots_column[pl.ds(pl.multiple_of(j * TILE, TILE), TILE), :] == slot_i
            scores = [mm(turned[at(1, h, j)], q, 0, 0) * scaling for h, q in zip(heads, queries)]
            scores = [jnp.where(same, s, MASKED) for s in scores]
            highs = [
                jnp.maximum(state[g][0], jnp.max(s, axis=0, keepdims=True))
                for g, s in enumerate(scores)
            ]
            weights = [jnp.exp(s - high) for s, high in zip(scores, highs)]
            fixes = [jnp.exp(state[g][0] - high) for g, high in enumerate(highs)]
            sums = [jnp.sum(w, axis=0, keepdims=True) for w in weights]
            mixes = [mm(turned[at(2, h, j)], w.astype(LOW)) for h, w in zip(heads, weights)]
            return tuple(
                (highs[g], state[g][1] * fixes[g] + sums[g], state[g][2] * fixes[g] + mixes[g])
                for g in range(GROUP)
            )

        begin = (
            jnp.full((1, TILE), MASKED, WIDE),
            jnp.zeros((1, TILE), WIDE),
            jnp.zeros((head, TILE), WIDE),
        )
        state = lax.fori_loop(bounds[i, 0], bounds[i, 1], inner, (begin,) * GROUP)
        for g, h in enumerate(heads):
            high, total, mixed = state[g]
            mixture[at(0, h, i)] = (mixed / total).astype(LOW)
            log_sum[pl.ds(h, 1), lane_i] = high + jnp.log(total)
        return carry

    lax.fori_loop(0, part // head // GROUP * tiles, step, 0)
    mixed = jnp.transpose(mixture[...])[:rows]
    for c in range(0, width, TILE):
        partial[:, c : c + TILE] = mm(mixed, out_w[c : c + TILE, :], 1, 1).astype(LOW)


def encoder_attend(stream, slots, bounds, gains, qkv_w, out_w, head):
    rows, width = stream.shape
    lanes = slots.shape[0]
    part = out_w.shape[1]
    return pl.pallas_call(
        functools.partial(attend_kernel, head),
        in_specs=[pl.BlockSpec(memory_space=pltpu.SMEM)]
        + [pl.BlockSpec(memory_space=pltpu.VMEM)] * 6,
        out_specs=[pl.BlockSpec(memory_space=pltpu.VMEM)] * 5,
        out_shape=[
            jax.ShapeDtypeStruct((rows, width), LOW),
            jax.ShapeDtypeStruct((3 * part, lanes), LOW),
            jax.ShapeDtypeStruct((part, lanes), LOW),
            jax.ShapeDtypeStruct((part // head, lanes), WIDE),
            jax.ShapeDtypeStruct((rows, width), LOW),
        ],
        compiler_params=pltpu.CompilerParams(vmem_limit_bytes=60 * 2**20),
    )(bounds, stream, slots[None, :], slots[:, None], gains, qkv_w, out_w)


def attend_back_kernel(
    head,
    bounds,
    slots_row,
    slots_column,
    first,
    turned,
    mixture,
    log_sum,
    grad_low,
    qkv_w,
    out_w,
    grad_qkv_w,
    grad_out_w,
    partial,
    grad_mixture,
    grad_turned,
    inner_sum,
    key_sum,
    value_sum,
):
    rows, width = grad_low.shape
    part, lanes = mixture.shape
    tiles = lanes // TILE
    scaling = head ** (-0.5)
    grad_mixture[:, rows:] = jnp.zeros((part, lanes - rows), LOW)
    for c in range(0, width, TILE):
        grad_out_w[c : c + TILE, :] = jnp.transpose(
            mm(mixture[:, :rows], grad_low[:, c : c + TILE]).astype(LOW)
        )
    for c in range(0, part, TILE):
        weight = jnp.transpose(out_w[:, c : c + TILE])
        grad_mixture[c : c + TILE, :rows] = mm(weight, grad_low[...], 1, 1).astype(LOW)
    for h in range(part // head):
        cut = slice(h * head, (h + 1) * head)
        inner_sum[h : h + 1, :] = jnp.sum(
            grad_mixture[cut, :].astype(WIDE) * mixture[cut, :].astype(WIDE), axis=0, keepdims=True
        )

    def at(which, h, tile):
        return (
            pl.ds(pl.multiple_of(which * part + h * head, head), head),
            pl.ds(pl.multiple_of(tile * TILE, TILE), TILE),
        )

    def over_group(group, carry):
        heads = [group * GROUP + g for g in range(GROUP)]
        key_sum[...] = jnp.zeros_like(key_sum)
        value_sum[...] = jnp.zeros_like(value_sum)

        def over_queries(i, carry):
            lane_i = pl.ds(pl.multiple_of(i * TILE, TILE), TILE)
            slot_i = slots_row[:, lane_i]
            queries = [turned[at(0, h, i)] for h in heads]
            grads = [grad_mixture[at(0, h, i)] for h in heads]
            logs = [log_sum[pl.ds(h, 1), lane_i] for h in heads]
            sums = [inner_sum[pl.ds(h, 1), lane_i] for h in heads]

            def inner(j, state):
                lane_j = pl.ds(pl.multiple_of(j * TILE, TILE), TILE)
                same = slots_column[lane_j, :] == slot_i
                cuts = [slice(g * head, (g + 1) * head) for g in range(GROUP)]
                keys = [turned[at(1, h, j)] for h in heads]
                values = [turned[at(2, h, j)] for h in heads]
                scores = [mm(k, q, 0, 0) * scaling for k, q in zip(keys, queries)]
                grad_shares = [mm(v, g, 0, 0) for v, g in zip(values, grads)]
                shares = [
                    jnp.exp(jnp.where(same, s, MASKED) - log) for s, log in zip(scores, logs)
                ]
                grad_scores = [
                    (s * (g - total)).astype(LOW) for s, g, total in zip(shares, grad_shares, sums)
                ]
                for g, cut in enumerate(cuts):
                    value_sum[cut, lane_j] += mm(grads[g], shares[g].astype(LOW), 1, 1)
                for g, cut in enumerate(cuts):
                    key_sum[cut, lane_j] += mm(queries[g], grad_scores[g], 1, 1)
                return tuple(
                    state[g] + mm(keys[g], grad_scores[g]) for g in range(GROUP)
                )

            begin = (jnp.zeros((head, TILE), WIDE),) * GROUP
            state = lax.fori_loop(bounds[i, 0], bounds[i, 1], inner, begin)
            for g, h in enumerate(heads):
                grad_turned[at(0, h, i)] = (state[g] * scaling).astype(LOW)
            return carry

        lax.fori_loop(0, tiles, over_queries, 0)
        size = GROUP * head
        key_at = pl.ds(pl.multiple_of(part + group * size, size), size)
        value_at = pl.ds(pl.multiple_of(2 * part + group * size, size), size)
        grad_turned[key_at, :] = (key_sum[...] * scaling).astype(LOW)
        grad_turned[value_at, :] = value_sum[...].astype(LOW)
        return carry

    lax.fori_loop(0, part // head // GROUP, over_group, 0)
    for c in range(0, 3 * part, TILE):
        grad_qkv_w[:, c : c + TILE] = jnp.transpose(
            mm(grad_turned[c : c + TILE, :rows], first[...]).astype(LOW)
        )
    for c in range(0, width, TILE):
        partial[:, c : c + TILE] = jnp.transpose(
            mm(qkv_w[c : c + TILE, :], grad_turned[:, :rows]).astype(LOW)
        )


def encoder_attend_back(
    slots, bounds, first, turned, mixture, log_sum, grad_low, qkv_w, out_w, head
):
    rows, width = first.shape
    part, lanes = mixture.shape
    return pl.pallas_call(
        functools.partial(attend_back_kernel, head),
        in_specs=[pl.BlockSpec(memory_space=pltpu.SMEM)]
        + [pl.BlockSpec(memory_space=pltpu.VMEM)] * 9,
        out_specs=[pl.BlockSpec(memory_space=pltpu.VMEM)] * 3,
        out_shape=[
            jax.ShapeDtypeStruct((width, 3 * part), LOW),
            jax.ShapeDtypeStruct((width, part), LOW),
            jax.ShapeDtypeStruct((rows, width), LOW),
        ],
        scratch_shapes=[
            pltpu.VMEM((part, lanes), LOW),
            pltpu.VMEM((3 * part, lanes), LOW),
            pltpu.VMEM((part // head, lanes), WIDE),
            pltpu.VMEM((GROUP * head, lanes), WIDE),
            pltpu.VMEM((GROUP * head, lanes), WIDE),
        ],
        compiler_params=pltpu.CompilerParams(vmem_limit_bytes=60 * 2**20),
    )(
        bounds,
        slots[None, :],
        slots[:, None],
        first,
        turned,
        mixture,
        log_sum,
        grad_low,
        qkv_w,
        out_w,
    )


def feed_kernel(stream, own, other, gains, up_w, down_w, after, second, hidden, slope, partial):
    summed = stream[...].astype(WIDE) + (own[...].astype(WIDE) + other[...].astype(WIDE))
    after[...] = summed
    unit, _ = centre(summed)
    second[...] = (unit * gains[2:3] + gains[3:4]).astype(LOW)
    units = up_w.shape[1]
    for c in range(0, units, TILE):
        cut = slice(c, c + TILE)
        h, g = gelu_pair(mm(second[...], up_w[:, cut]))
        hidden[:, cut] = h.astype(LOW)
        slope[:, cut] = g.astype(LOW)
    partial[...] = mm(hidden[...], down_w[...], 1, 1).astype(LOW)


def encoder_feed(stream, own, other, gains, up_w, down_w, block):
    rows, width = stream.shape
    units = up_w.shape[1]
    wide, tall = down_rows(block, width), down_rows(block, units)
    return pl.pallas_call(
        feed_kernel,
        grid=(rows // block,),
        in_specs=[wide, wide, wide, fixed((4, width)), fixed(up_w.shape), fixed(down_w.shape)],
        out_specs=[wide, wide, tall, tall, wide],
        out_shape=[
            jax.ShapeDtypeStruct((rows, width), WIDE),
            jax.ShapeDtypeStruct((rows, width), LOW),
            jax.ShapeDtypeStruct((rows, units), LOW),
            jax.ShapeDtypeStruct((rows, units), LOW),
            jax.ShapeDtypeStruct((rows, width), LOW),
        ],
        compiler_params=params(),
    )(stream, own, other, gains, up_w, down_w)


def feed_back_kernel(
    counts,
    own,
    other,
    second,
    hidden,
    slope,
    up_w,
    down_w,
    grad_up,
    grad_down,
    partial,
    grad_low,
    grad_turned,
    second_turned,
    total,
):
    @pl.when(pl.program_id(0) == 0)
    def _():
        grad_low[...] = (own[...].astype(WIDE) + other[...].astype(WIDE)).astype(LOW)
        grad_turned[...] = jnp.transpose(grad_low[...])
        second_turned[...] = jnp.transpose(second[...])
        total[...] = jnp.zeros_like(total)

    down = mm(grad_turned[...], hidden[...])
    grad_down[...] = jnp.where(counts[0] > 0, down, jnp.zeros_like(down)).astype(LOW)
    grad_z = (mm(grad_low[...], down_w[...]) * slope[...].astype(WIDE)).astype(LOW)
    grad_up[...] = mm(second_turned[...], grad_z).astype(LOW)
    total[...] += mm(grad_z, up_w[...], 1, 1)

    @pl.when(pl.program_id(0) == pl.num_programs(0) - 1)
    def _():
        partial[...] = total[...].astype(LOW)


def encoder_feed_back(counts, own, other, second, hidden, slope, up_w, down_w):
    rows, width = own.shape
    units = up_w.shape[1]
    piece = 256
    whole = fixed((rows, width))
    tall = pl.BlockSpec((rows, piece), lambda i: (0, i))
    weight = pl.BlockSpec((width, piece), lambda i: (0, i))
    return pl.pallas_call(
        feed_back_kernel,
        grid=(units // piece,),
        in_specs=[pl.BlockSpec(memory_space=pltpu.SMEM)]
        + [whole, whole, whole, tall, tall, weight, weight],
        out_specs=[weight, weight, whole],
        out_shape=[
            jax.ShapeDtypeStruct((width, units), LOW),
            jax.ShapeDtypeStruct((width, units), LOW),
            jax.ShapeDtypeStruct((rows, width), LOW),
        ],
        scratch_shapes=[
            pltpu.VMEM((rows, width), LOW),
            pltpu.VMEM((width, rows), LOW),
            pltpu.VMEM((width, rows), LOW),
            pltpu.VMEM((rows, width), WIDE),
        ],
        compiler_params=params(),
    )(counts, own, other, second, hidden, slope, up_w, down_w)


def norm_back_kernel(tokens, own, other, skip_own, skip_other, gains, grad, grad_low, grad_gains, *, at):
    @pl.when(pl.program_id(0) == 0)
    def _():
        grad_gains[...] = jnp.zeros_like(grad_gains)

    pulled = own[...].astype(WIDE) + other[...].astype(WIDE)
    unit, scale = centre(tokens[...].astype(WIDE))
    result = skip_own[...].astype(WIDE)
    if skip_other is not None:
        result = result + skip_other[...].astype(WIDE)
    result = result + centre_back(unit, scale, gains[at : at + 1], pulled)
    grad[...] = result
    if grad_low is not None:
        grad_low[...] = result.astype(LOW)
    grad_gains[0:1] += jnp.sum(pulled * unit, axis=0, keepdims=True)
    grad_gains[1:2] += jnp.sum(pulled, axis=0, keepdims=True)


def encoder_norm_back(tokens, own, other, skip, gains, at, block, low):
    rows, width = tokens.shape
    wide = down_rows(block, width)
    two = len(skip) == 2

    def kernel(*refs):
        refs = list(refs)
        if not two:
            refs.insert(4, None)
        if not low:
            refs.insert(7, None)
        norm_back_kernel(*refs, at=at)

    shapes = [jax.ShapeDtypeStruct((rows, width), WIDE)]
    if low:
        shapes.append(jax.ShapeDtypeStruct((rows, width), LOW))
    shapes.append(jax.ShapeDtypeStruct((8, width), WIDE))
    return pl.pallas_call(
        kernel,
        grid=(rows // block,),
        in_specs=[wide, wide, wide] + [wide] * len(skip) + [fixed((4, width))],
        out_specs=[wide] * (2 if low else 1) + [fixed((8, width))],
        out_shape=shapes,
        compiler_params=params(),
    )(tokens, own, other, *skip, gains)


def finish_kernel(length, flag, tokens, own, other, skip, gains, decoded, result, grad_gains):
    pulled = own[...].astype(WIDE) + other[...].astype(WIDE)
    unit, scale = centre(tokens[...].astype(WIDE))
    grad_gains[...] = jnp.zeros_like(grad_gains)
    grad_gains[0:1] = jnp.sum(pulled * unit, axis=0, keepdims=True)
    grad_gains[1:2] = jnp.sum(pulled, axis=0, keepdims=True)
    rows, width = tokens.shape
    pieces = width // 128

    @pl.when(flag[0] > 0)
    def _():
        grad = skip[...] + centre_back(unit, scale, gains[0:1], pulled)
        for k in range(pieces):
            result[pl.ds(k, rows, stride=pieces), :] = grad[:, k * 128 : (k + 1) * 128]

    @pl.when(flag[0] == 0)
    def _():
        images, _, columns = decoded.shape
        count = columns // 128
        for i in range(images):
            for k in range(count):
                result[pl.ds(i * length * count + k, length, stride=count), :] = decoded[
                    i, 0:length, k * 128 : (k + 1) * 128
                ]


def encoder_finish(encoder_side, tokens, own, other, skip, gains, decoded, length):
    rows, width = tokens.shape
    return pl.pallas_call(
        functools.partial(finish_kernel, length),
        in_specs=[pl.BlockSpec(memory_space=pltpu.SMEM)]
        + [pl.BlockSpec(memory_space=pltpu.VMEM)] * 6,
        out_specs=[pl.BlockSpec(memory_space=pltpu.VMEM)] * 2,
        out_shape=[
            jax.ShapeDtypeStruct((rows * width // 128, 128), WIDE),
            jax.ShapeDtypeStruct((8, width), WIDE),
        ],
        compiler_params=pltpu.CompilerParams(vmem_limit_bytes=60 * 2**20),
    )(encoder_side.astype(jnp.int32).reshape(1), tokens, own, other, skip, gains, decoded)


def from_behind(value, axis, by):
    length = lax.axis_size(axis)
    pairs = [(i, i + by) for i in range(length) if 0 <= i + by < length]
    return lax.ppermute(value, axis, pairs)


def partner(value):
    length = lax.axis_size("mp")
    return lax.ppermute(value, "mp", [(i, (i + 1) % length) for i in range(length)])


def is_fast():
    return lax.axis_size("section") == 2 and lax.axis_size("dp") == 8


def plan(widths, dec_width, orders, dec_orders, among):
    chunks = chunk_list(widths, PIECES, 0, orders)
    dec = chunk_list((dec_width,), (DEC_PIECES,), 1, dec_orders)
    for k, (_, b, c, w, o, owner) in enumerate(dec):
        chunks.insert(3 * k + 2 if among else len(chunks), (len(widths), b, c, w, o, owner))
    return chunks


def gather_all(low_enc, low_dec, norms, widths):
    count = len(widths)
    if not is_fast():
        both = ("section", "dp")
        enc = lax.all_gather(low_enc, both, axis=0, tiled=True)
        dec = lax.all_gather(low_dec, both, axis=0, tiled=True)
        rows = lax.all_gather(norms, both, axis=0, tiled=True)
        parts, column = [], 0
        for w in widths:
            parts.append(enc[:, column : column + w])
            column += w
        return parts, dec, rows
    columns = [sum(widths[:k]) for k in range(count + 1)]
    ahead = [low_enc[:, : columns[3]], low_enc[:, columns[4] :]]
    near = (*widths[:3], widths[4])
    chunks = plan(near, low_dec.shape[1], GATHER_ORDERS, DEC_GATHER_ORDERS, False)
    outputs = [(low_enc.shape[0], w, LOW) for w in near]
    outputs += [(low_dec.shape[0], low_dec.shape[1], LOW), (8, 128, WIDE)]
    described = [(k // 4, k, c, b, w, o, own) for k, b, c, w, o, own in chunks]
    described.append((2, 5, 0, 0, 128, "hlyx", BOTH))
    shards = [jnp.concatenate(ahead, axis=1), low_dec, norms]
    results = gather_weights(shards, outputs, described, 1, GATHER_AHEAD, GATHER_LAG)
    low_down, norm_rows = lax.optimization_barrier(
        (low_enc[:, columns[3] : columns[4]], results[5])
    )
    down = lax.all_gather(low_down, ("section", "dp"), axis=0, tiled=True)
    return [*results[:3], down, results[3]], results[4], norm_rows


def scatter_all(enc_parts, dec, norms, encoder_side):
    widths = [p.shape[1] for p in enc_parts]
    both = ("section", "dp")

    def scattered(v):
        return lax.psum_scatter(v, both, scatter_dimension=0, tiled=True)

    if not is_fast():
        parts = [scattered(jnp.where(encoder_side, p.astype(WIDE), 0.0)) for p in enc_parts]
        dec = scattered(jnp.where(encoder_side, 0.0, dec.astype(WIDE)))
        norms = lax.psum(scattered(norms), "mp")
        local = sum(jnp.sum(v * v) for v in (*parts, dec))
        local = local + jnp.sum(norms * norms) / lax.axis_size("mp")
        total = jnp.full((8, 128), lax.psum(local, (*both, "mp")))
        return jnp.concatenate([*parts[:3], parts[4]], axis=1), parts[3], dec, norms, total
    down = scattered(enc_parts[3])
    near = (*enc_parts[:3], enc_parts[4])
    near_widths = (*widths[:3], widths[4])
    chunks = plan(near_widths, dec.shape[1], SCATTER_ORDERS, DEC_SCATTER_ORDERS, True)
    described = [(k, k // 4, b, c, w, o, own) for k, b, c, w, o, own in chunks]
    described.append((5, 2, 0, 0, 128, "xylh", BOTH))
    rows = near[0].shape[0] // 16
    outputs = [(rows, sum(near_widths)), (dec.shape[0] // 16, dec.shape[1]), (8, 128)]
    enc, dec, norms, total = scatter_grads(
        [*near, dec, norms], down, outputs, described, 2, SCATTER_AHEAD, SCATTER_LAG
    )
    return enc, down, dec, norms, total


def pack_norms(enc_rows, dec_rows, blocks):
    both = [rows.reshape(4, blocks, -1).transpose(1, 0, 2) for rows in (enc_rows, dec_rows)]
    joined = jnp.concatenate(both, axis=2)
    joined = jnp.pad(joined, ((0, 0), (0, 4), (0, 128 - joined.shape[2])))
    return joined.reshape(blocks * 8, 128)


def unpack_norms(packed, blocks, enc_width, dec_width):
    split = packed.reshape(blocks, 8, 128)[:, :4].transpose(1, 0, 2)
    return (
        split[:, :, :enc_width].reshape(4, -1),
        split[:, :, enc_width : enc_width + dec_width].reshape(4, -1),
    )


def key_ranges(slots):
    tiles = slots.reshape(-1, TILE)
    low, high = jnp.min(tiles, axis=1), jnp.max(tiles, axis=1)
    meet = jnp.logical_and(low[:, None] <= high[None, :], high[:, None] >= low[None, :])
    index = jnp.arange(tiles.shape[0], dtype=jnp.int32)[None, :]
    first = jnp.min(jnp.where(meet, index, tiles.shape[0]), axis=1)
    last = jnp.max(jnp.where(meet, index + 1, 0), axis=1)
    return jnp.stack([first, last], axis=1)


def renewed(weight, first_moment, second_moment, clipped, rate, fix_first, fix_second, decay):
    new_first = BETA_FIRST * first_moment + (1.0 - BETA_FIRST) * clipped
    new_second = BETA_SECOND * second_moment + (1.0 - BETA_SECOND) * clipped * clipped
    stepped = new_first / fix_first / (jnp.sqrt(new_second / fix_second) + ADAM_EPS)
    return weight - rate * (stepped + decay * weight)


def renew_kernel(order, scalars, total, near, down, dec, norms, *refs):
    enc_state, dec_state, enc_norm_state, dec_norm_state = (refs[k : k + 3] for k in (0, 3, 6, 9))
    new_enc, new_dec, new_enc_norm, new_dec_norm, enc_clip, dec_clip, enc_norm_clip, dec_norm_clip = refs[12:]
    factor = jnp.minimum(1.0, math.sqrt(PARAMS) / (jnp.sqrt(total[0:1, :]) + 1e-06))
    fixes = scalars[2], scalars[3]

    def work(blocks, state, new, clip):
        count = len(blocks)
        for k, (ref, at) in enumerate(blocks):
            rows = pl.ds(k, ref.shape[0], stride=count)
            clipped = ref[:, at : at + 128].astype(WIDE) * factor
            values = [s[rows, :] for s in state]
            clip[rows, :] = clipped
            new[rows, :] = renewed(*values, clipped, scalars[0], *fixes, WEIGHT_DECAY)

    work([((near, down)[which], at) for which, at in order], enc_state, new_enc, enc_clip)
    work([(dec, at) for at in range(0, dec.shape[1], 128)], dec_state, new_dec, dec_clip)
    column = 0
    for state, new, clip in (
        (enc_norm_state, new_enc_norm, enc_norm_clip),
        (dec_norm_state, new_dec_norm, dec_norm_clip),
    ):
        rows, width = new.shape
        clipped = norms[0:rows, column : column + width] * factor[:, :width]
        column += width
        clip[...] = clipped
        new[...] = renewed(*[s[...] for s in state], clipped, scalars[1], *fixes, 0.0)


def renew_all(scalars, total, near, down, down_at, dec, norms, enc, decoder, enc_norm, dec_norm):
    order = [(0, at) for at in range(0, near.shape[1], 128)]
    order[down_at // 128 : down_at // 128] = [(1, at) for at in range(0, down.shape[1], 128)]
    flat = [[v.reshape(-1, 128) for v in group] for group in (enc, decoder)]
    groups = [*flat, enc_norm, dec_norm]
    shapes = [jax.ShapeDtypeStruct(group[0].shape, WIDE) for group in groups] * 2
    results = pl.pallas_call(
        functools.partial(renew_kernel, order),
        in_specs=[pl.BlockSpec(memory_space=pltpu.SMEM)]
        + [pl.BlockSpec(memory_space=pltpu.VMEM)] * 17,
        out_specs=[pl.BlockSpec(memory_space=pltpu.VMEM)] * 8,
        out_shape=shapes,
        compiler_params=pltpu.CompilerParams(vmem_limit_bytes=40 * 2**20),
    )(scalars, total, near, down, dec, norms, *[v for group in groups for v in group])
    given = (enc, decoder, enc_norm, dec_norm) * 2
    return [r.reshape(group[0].shape) for r, group in zip(results, given)]


def per_device(
    act_in,
    packing,
    enc_weights,
    enc_first,
    enc_second,
    dec_weights,
    dec_first,
    dec_second,
    enc_norms,
    enc_norm_first,
    enc_norm_second,
    dec_norms,
    dec_norm_first,
    dec_norm_second,
    mask_token,
    dec_position,
    learning_rate,
    step_count,
):
    encoder_side = lax.axis_index("section") == 0
    decoder_side = jnp.logical_not(encoder_side)
    mp_rank = lax.axis_index("mp")
    mp_count = lax.axis_size("mp")
    first_half = mp_rank == 0
    slot_ids = packing[0, 0]
    patch_ids = packing[0, 1]
    local_images = IMG // mp_count
    grid_cells = local_images * GRID
    local_slot = slot_ids - mp_rank * local_images
    inside = jnp.logical_and(local_slot >= 0, local_slot < local_images)
    target = jnp.where(inside, local_slot * GRID + patch_ids, grid_cells)

    local_rows, width = act_in.shape[1], act_in.shape[2]
    real_rows = local_rows * mp_count
    rows = -(-real_rows // ROW_BLOCK) * ROW_BLOCK
    lanes = -(-rows // TILE) * TILE
    part = width // mp_count
    units = FF // mp_count
    head = width // HEADS
    dec_width = dec_position.shape[1]
    dec_part = dec_width // mp_count
    widths = (3 * part, part, units, units, dec_part)
    slots = jnp.pad(slot_ids, (0, lanes - real_rows), constant_values=IMG + 1)
    ranges = key_ranges(slots)

    (qkv_w, out_w, up_w, down_w, projection), dec_own, norm_rows = gather_all(
        enc_weights[:, 0, :].astype(LOW),
        dec_weights[:, 0, :].astype(LOW),
        pack_norms(enc_norms, dec_norms, 1),
        widths,
    )
    enc_gains, dec_gains = (
        v.astype(LOW).astype(WIDE)
        for v in unpack_norms(
            norm_rows, norm_rows.shape[0] // 8, enc_norms.shape[1], dec_norms.shape[1]
        )
    )
    own_stream, other_stream = act_in[0], partner(act_in[0])
    stream = jnp.where(
        first_half,
        jnp.concatenate([own_stream, other_stream], axis=0),
        jnp.concatenate([other_stream, own_stream], axis=0),
    )
    stream = jnp.pad(stream, ((0, rows - real_rows), (0, 0)))
    first, turned, mixture, log_sum, mix_own = encoder_attend(
        stream, slots, ranges, enc_gains, qkv_w, out_w, head
    )
    shown = min(real_rows, -(-IMG * MOST_VISIBLE // 16) * 16)
    packed = -(-shown // 128) * 128
    cell_rows = -(-GRID // 16) * 16
    longer = (0, cell_rows - GRID)
    seen_target = jnp.pad(target[:shown], (0, packed - shown), constant_values=-1)
    cotangent = act_in[0].reshape(local_images, GRID, dec_width)
    cotangent = jnp.pad(cotangent, ((0, 0), longer, (0, 0)))
    position = jnp.pad(dec_position, (longer, (0, 0)))
    mix_other, seen_target, cotangent, position, dec_gains = lax.optimization_barrier(
        (partner(mix_own), seen_target, cotangent, position, dec_gains)
    )
    after, second, hidden, slope, feed_own = encoder_feed(
        stream, mix_own, mix_other, enc_gains, up_w, down_w, ROW_BLOCK
    )
    encoded = (after + (feed_own.astype(WIDE) + partner(feed_own).astype(WIDE))).astype(LOW)
    projected = mm(encoded[:shown], projection).astype(LOW)
    arrived = from_behind(projected, "section", 1)
    arrived = jnp.pad(arrived, ((0, packed - shown), (0, 0)))
    decoded, grad_keep, grad_send, dec_grad_own, dec_grad_other, dec_gain_grad = decoder_step(
        GRID,
        first_half,
        arrived,
        partner(arrived),
        seen_target,
        mask_token,
        position,
        dec_gains,
        dec_own,
        partner(dec_own),
        cotangent,
    )
    returned = grad_keep[:shown] + partner(grad_send[:shown])
    grad_projected = from_behind(returned, "section", -1)
    grad_projected = jnp.pad(grad_projected, ((0, rows - shown), (0, 0)))
    dec_grad = dec_grad_own.astype(WIDE) + partner(dec_grad_other).astype(WIDE)
    dec_grad = dec_grad.astype(LOW)

    grad_projection = mm(encoded, grad_projected, 0, 0).astype(LOW)
    end_own = mm(grad_projected, projection, 1, 1).astype(LOW)
    end_other = partner(end_own)
    grad_up_w, grad_down_w, back_own = encoder_feed_back(
        jnp.where(encoder_side, 1, 0).astype(jnp.int32).reshape(1),
        end_own,
        end_other,
        second,
        hidden,
        slope,
        up_w,
        down_w,
    )
    grad_after, grad_low, gains_two = encoder_norm_back(
        after, back_own, partner(back_own), (end_own, end_other), enc_gains, 2, ROW_BLOCK, True
    )
    grad_qkv_w, grad_out_w, start_own = encoder_attend_back(
        slots, ranges, first, turned, mixture, log_sum, grad_low, qkv_w, out_w, head
    )
    def choose(matrix):
        top, bottom = matrix[:local_rows], matrix[local_rows:real_rows]
        return jnp.where(first_half, top, bottom), jnp.where(first_half, bottom, top)

    start_keep, start_send = choose(start_own)
    act_out, gains_one = encoder_finish(
        encoder_side,
        own_stream,
        start_keep,
        partner(start_send),
        choose(grad_after)[0],
        enc_gains,
        decoded,
        GRID,
    )
    enc_gain_grad = jnp.concatenate(
        [gains_one[:2], jnp.where(first_half, gains_two[:2], 0.0)], axis=0
    )
    norm_grads = pack_norms(
        jnp.where(encoder_side, enc_gain_grad, 0.0),
        jnp.where(decoder_side, dec_gain_grad, 0.0),
        norm_rows.shape[0] // 8,
    )
    near_shard, down_shard, dec_shard, norm_shard, square_total = scatter_all(
        (grad_qkv_w, grad_out_w, grad_up_w, grad_down_w, grad_projection),
        dec_grad,
        norm_grads,
        encoder_side,
    )
    step_value = step_count[0].astype(jnp.float32)
    scalars = jnp.stack(
        [
            learning_rate[0],
            learning_rate[1],
            1.0 - jnp.power(BETA_FIRST, step_value),
            1.0 - jnp.power(BETA_SECOND, step_value),
        ]
    )
    results = renew_all(
        scalars,
        square_total,
        near_shard,
        down_shard,
        sum(widths[:3]),
        dec_shard,
        norm_shard,
        (enc_weights, enc_first, enc_second),
        (dec_weights, dec_first, dec_second),
        (enc_norms, enc_norm_first, enc_norm_second),
        (dec_norms, dec_norm_first, dec_norm_second),
    )
    return (act_out.reshape(act_in.shape), *results, jnp.sqrt(square_total[0, 0]).reshape(1))


def solution(mesh):
    in_specs = (
        P("section", ("dp", "mp"), None),
        P("dp", None, None),
        P(("section", "dp"), "mp", None),
        P(("section", "dp"), "mp", None),
        P(("section", "dp"), "mp", None),
        P(("section", "dp"), "mp", None),
        P(("section", "dp"), "mp", None),
        P(("section", "dp"), "mp", None),
        P(None, ("section", "dp")),
        P(None, ("section", "dp")),
        P(None, ("section", "dp")),
        P(None, ("section", "dp")),
        P(None, ("section", "dp")),
        P(None, ("section", "dp")),
        P(),
        P(),
        P(),
        P(),
    )
    out_specs = (
        P("section", ("dp", "mp"), None),
        P(("section", "dp"), "mp", None),
        P(("section", "dp"), "mp", None),
        P(None, ("section", "dp")),
        P(None, ("section", "dp")),
        P(("section", "dp"), "mp", None),
        P(("section", "dp"), "mp", None),
        P(None, ("section", "dp")),
        P(None, ("section", "dp")),
        P(),
    )
    return jax.shard_map(
        per_device, mesh=mesh, in_specs=in_specs, out_specs=out_specs, check_vma=False
    )
```

```python
import functools
import itertools
import math

import jax
import jax.numpy as jnp
from jax import lax
from jax.experimental import pallas as pl
from jax.experimental.pallas import tpu as pltpu
from jax.sharding import PartitionSpec as P

FF = 4096
GRID = 196
IMG = 12
PARAMS = 16259072

BETA_FIRST = 0.9
BETA_SECOND = 0.999
ADAM_EPS = 1e-08
WEIGHT_DECAY = 0.05
ROW_BLOCK = 240
MOST_VISIBLE = 73
GATHER_ORDERS = ("hlxy", "hlyx", "hlxy", "hlyx", "yxhl")
DEC_GATHER_ORDERS = ("xhly", "xyhl")
DEC_SCATTER_ORDERS = ("ylhx", "ylhx")
PIECES, DEC_PIECES = (6, 2, 8, 1), 4
GATHER_AHEAD, GATHER_LAG = 6, (3, 6)
SCATTER_AHEAD, SCATTER_LAG = 6, (3, 3, 3)
SCATTER_ORDERS = ("xylh", "yxlh", "xylh", "yxlh", "lhxy")

MESH_ID = pl.DeviceIdType.MESH
EVERY = slice(None)
BOTH = -1
DIMS = "xhly"
NEAR_WAYS = ("x", "y", "c", "xy", "xc", "yc", "xyc")
LINE_WAYS = ("h", "l", "hl")
FAR = ("c", "xy", "xc", "yc", "xyc", "hl")


class Place:
    def __init__(self):
        s, depth, core = lax.axis_index("section"), lax.axis_index("dp"), lax.axis_index("mp")
        y, low, high = depth % 2, (depth // 2) % 2, depth // 4
        self.at = {"x": s, "h": high, "l": low, "y": y}
        self.s, self.core = s, core
        self.device = {
            "x": (1 - s, depth, core),
            "h": (s, depth + 4 - 8 * high, core),
            "l": (s, depth + 2 - 4 * low, core),
            "y": (s, depth + 1 - 2 * y, core),
        }

    def across(self, flips):
        other = {d: 1 - self.at[d] if d in flips else self.at[d] for d in DIMS}
        core = 1 - self.core if "c" in flips else self.core
        return other["x"], 4 * other["h"] + 2 * other["l"] + other["y"], core

    def greet(self, more=()):
        barrier = pltpu.get_barrier_semaphore()
        for flips in more:
            pl.semaphore_signal(
                barrier, inc=1, device_id=self.across(flips), device_id_type=MESH_ID
            )
        for name in self.device:
            pl.semaphore_signal(
                barrier, inc=1, device_id=self.device[name], device_id_type=MESH_ID
            )
        pl.semaphore_wait(barrier, len(self.device) + len(more))


def run(condition, action):
    if condition is None:
        action()
    else:
        pl.when(condition)(action)


def gather_kernel(chunks, n_in, n_out, ahead, lag, *refs):
    ins, outs = refs[:n_in], refs[n_in : n_in + n_out]
    send, recv, local = refs[n_in + n_out :]
    here = Place()
    count = len(chunks)

    def region(chunk, gathered, sender):
        at = [
            EVERY if d in gathered else 1 - here.at[d] if d == sender else here.at[d] for d in DIMS
        ]
        return outs[chunk[1]].at[(*at, EVERY, pl.ds(chunk[3], chunk[4]))]

    def own(i):
        chunk = chunks[i]
        return pltpu.make_async_copy(
            ins[chunk[0]].at[:, pl.ds(chunk[2], chunk[4])], region(chunk, "", None), local.at[i]
        )

    def copy(i, stage, incoming):
        chunk = chunks[i]
        order = chunk[5]
        axis = order[stage]
        block = region(chunk, order[:stage], axis if incoming else None)
        source = block
        if stage == 0 and not incoming:
            source = ins[chunk[0]].at[:, pl.ds(chunk[2], chunk[4])]
        return pltpu.make_async_remote_copy(
            src_ref=source,
            dst_ref=block,
            send_sem=send.at[i, stage],
            recv_sem=recv.at[i, stage],
            device_id=here.device[axis],
            device_id_type=MESH_ID,
        )

    def roles(i, stage):
        order, owner = chunks[i][5], chunks[i][6]
        if owner == BOTH:
            return None, None
        if order[stage] == "x":
            return here.s != owner, here.s == owner
        if "x" in order[:stage]:
            return here.s == owner, here.s == owner
        return None, None

    def begin(i, stage):
        run(roles(i, stage)[0], lambda: copy(i, stage, False).start())

    def arrive(i, stage):
        run(roles(i, stage)[1], lambda: copy(i, stage, True).wait_recv())
        if stage == 0:
            own(i).wait()

    here.greet()
    for i in range(count):
        own(i).start()
    for i in range(min(ahead, count)):
        begin(i, 0)
    for step in range(count + sum(lag)):
        for stage in range(3):
            i = step - sum(lag[:stage])
            if not 0 <= i < count:
                continue
            arrive(i, stage)
            begin(i, stage + 1)
            if stage == 0 and i + ahead < count:
                begin(i + ahead, 0)
    for i in range(count):
        arrive(i, 3)
    for i in range(count):
        for stage in range(4):
            run(
                roles(i, stage)[0],
                lambda i=i, stage=stage: copy(i, stage, False).wait_send(),
            )


def gather_weights(shards, outputs, chunks, collective_id, ahead=4, lag=(1, 1)):
    count = len(chunks)
    call = pl.pallas_call(
        functools.partial(gather_kernel, chunks, len(shards), len(outputs), ahead, lag),
        out_shape=[
            jax.ShapeDtypeStruct((2, 2, 2, 2, rows, width), dtype) for rows, width, dtype in outputs
        ],
        in_specs=[pl.BlockSpec(memory_space=pltpu.VMEM)] * len(shards),
        out_specs=[pl.BlockSpec(memory_space=pltpu.HBM)] * len(outputs),
        scratch_shapes=[
            pltpu.SemaphoreType.DMA((count, 4)),
            pltpu.SemaphoreType.DMA((count, 4)),
            pltpu.SemaphoreType.DMA((count,)),
        ],
        compiler_params=pltpu.CompilerParams(
            collective_id=collective_id, has_side_effects=True, vmem_limit_bytes=40 * 2**20
        ),
    )
    results = call(*shards)
    return [
        r.reshape(16 * rows, width) for r, (rows, width, _) in zip(results, outputs, strict=True)
    ]


def spread(total, pieces, unit=128):
    units = total // unit
    widths = [units // pieces + (1 if k < units % pieces else 0) for k in range(pieces)]
    return [w * unit for w in widths if w]


def chunk_list(widths, pieces, owner, orders):
    chunks = []
    column = turn = 0
    for index, (width, count) in enumerate(zip(widths, pieces, strict=True)):
        begin = 0
        for piece in spread(width, count):
            chunks.append((index, begin, column, piece, orders[turn % len(orders)], owner))
            begin += piece
            column += piece
            turn += 1
    return chunks


def left_after(order, stage):
    return [d for d in DIMS if d not in order[: stage + 1]]


def scatter_buffers(order, owner):
    shapes = [(2,) * 3]
    for stage in range(4):
        if order[stage] == "x" and owner != BOTH:
            continue
        shapes.append((2,) * (3 - stage))
    return shapes


def squares(ref):
    def step(k, total):
        block = ref[:, pl.ds(pl.multiple_of(k * 128, 128), 128)].astype(jnp.float32)
        block = block * block
        for r in range(0, block.shape[0], 8):
            total = total + block[r : r + 8]
        return total

    return lax.fori_loop(0, ref.shape[1] // 128, step, jnp.zeros((8, 128), jnp.float32))


def scatter_kernel(chunks, n_in, n_out, ahead, lag, cores, *refs):
    ins, summed, outs = refs[:n_in], refs[n_in], refs[n_in + 1 : n_in + 1 + n_out]
    square_total = refs[n_in + 1 + n_out]
    rest = refs[n_in + n_out + 2 :]
    send, recv, local, square_send, square_recv, square_mine, square_there, last, last_there = rest[:9]
    here = Place()
    s = here.s
    count = len(chunks)
    given, ins = ins[-1], (*ins[:-1], last)
    own, got = [], []
    position = 9
    for chunk in chunks:
        order, owner = chunk[5], chunk[6]
        own.append(rest[position])
        position += 1
        mine = []
        for stage in range(4):
            if order[stage] == "x" and owner != BOTH:
                mine.append(None)
                continue
            mine.append(rest[position])
            position += 1
        got.append(mine)

    def source(i, axis, keep):
        chunk = chunks[i]
        at = [
            (here.at[d] if keep else 1 - here.at[d]) if d == axis else EVERY for d in DIMS
        ]
        return ins[chunk[0]].at[(*at, EVERY, pl.ds(chunk[2], chunk[4]))]

    def load(i):
        return pltpu.make_async_copy(source(i, chunks[i][5][0], True), own[i], local.at[i])

    def spot(i, stage, flip):
        order = chunks[i][5]
        at = []
        for d in DIMS:
            if d == order[0]:
                continue
            if d in order[:stage]:
                at.append(here.at[d])
            elif d == order[stage]:
                at.append(1 - here.at[d] if flip else here.at[d])
            else:
                at.append(EVERY)
        return tuple(at)

    def copy(i, stage, incoming):
        order = chunks[i][5]
        axis = order[stage]
        moved = got[i][stage] is None
        src = source(i, axis, False) if stage == 0 else own[i].at[spot(i, stage, True)]
        if not moved:
            there = mine = got[i][stage]
        elif stage == 0:
            there = mine = own[i]
        else:
            there, mine = own[i].at[spot(i, stage, True)], own[i].at[spot(i, stage, False)]
        return pltpu.make_async_remote_copy(
            src_ref=mine if incoming else src,
            dst_ref=mine if incoming else there,
            send_sem=send.at[i, stage],
            recv_sem=recv.at[i, stage],
            device_id=here.device[axis],
            device_id_type=MESH_ID,
        )

    def roles(i, stage):
        order, owner = chunks[i][5], chunks[i][6]
        if owner == BOTH:
            return None, None
        if order[stage] == "x":
            return s == owner, s != owner
        if "x" in order[:stage]:
            return None, None
        return s == owner, s == owner

    def begin(i, stage):
        run(roles(i, stage)[0], lambda: copy(i, stage, False).start())

    def arrive(i, stage):
        chunk, a, r = chunks[i], own[i], got[i][stage]
        order, owner = chunk[5], chunk[6]
        run(roles(i, stage)[1], lambda: copy(i, stage, True).wait_recv())
        if stage == 0:
            run(None if owner == BOTH else s == owner, lambda: load(i).wait())
        out = outs[chunk[1]].at[:, pl.ds(chunk[3], chunk[4])]
        place = spot(i, stage, False)
        if stage == 3:
            result = a[place].astype(jnp.float32)
            if r is not None:
                result = result + r[...].astype(jnp.float32)
            out[...] = result
            return
        if r is None:
            return

        def add():
            free = [k for k, p in enumerate(place) if p is EVERY]
            for combo in itertools.product(range(2), repeat=len(free)):
                at = list(place)
                for k, c in zip(free, combo):
                    at[k] = c
                at = tuple(at)
                a[at] = (a[at].astype(jnp.float32) + r[combo].astype(jnp.float32)).astype(a.dtype)

        run(roles(i, stage)[1], add)

    here.greet(FAR)
    join = pltpu.make_async_remote_copy(
        src_ref=given,
        dst_ref=last_there,
        send_sem=square_send.at[11],
        recv_sem=square_recv.at[11],
        device_id=here.across("c"),
        device_id_type=MESH_ID,
    )
    join.start()
    for i in range(count - 1):
        run(
            None if chunks[i][6] == BOTH else s == chunks[i][6],
            lambda i=i: load(i).start(),
        )
    for i in range(min(ahead, count)):
        begin(i, 0)
    join.wait()
    last[...] = given[...] + last_there[...]
    load(count - 1).start()
    for step in range(count + sum(lag)):
        for stage in range(3, -1, -1):
            i = step - sum(lag[:stage])
            if not 0 <= i < count:
                continue
            arrive(i, stage)
            if stage < 3:
                begin(i, stage + 1)
            if stage == 0 and i + ahead < count:
                begin(i + ahead, 0)
    for i in range(count):
        for stage in range(4):
            run(
                roles(i, stage)[0],
                lambda i=i, stage=stage: copy(i, stage, False).wait_send(),
            )

    value = squares(summed)
    for k, out in enumerate(outs):
        value = value + squares(out) * (1.0 / cores if k == n_out - 1 else 1.0)
    value = jnp.broadcast_to(jnp.sum(value, keepdims=True), (8, 128))
    begin = 0
    for bits, ways in (("xyc", NEAR_WAYS), ("hl", LINE_WAYS)):
        names = {**here.at, "c": here.core}

        def number(flips):
            total = 0
            for bit in bits:
                total = 2 * total + (1 - names[bit] if bit in flips else names[bit])
            return total

        mine = square_mine.at[0 if begin == 0 else 1]
        mine[...] = value
        moves = []
        for k, flips in enumerate(ways):
            moves.append(
                pltpu.make_async_remote_copy(
                    src_ref=mine,
                    dst_ref=square_there.at[begin + number("")],
                    send_sem=square_send.at[begin + k],
                    recv_sem=square_recv.at[begin + k],
                    device_id=here.across(flips),
                    device_id_type=MESH_ID,
                )
            )
            moves[-1].start()
        square_there[begin + number("")] = value
        for k, flips in enumerate(ways):
            moves[k].wait_send()
            slot = square_there.at[begin + number(flips)]
            pltpu.make_async_remote_copy(
                src_ref=slot,
                dst_ref=slot,
                send_sem=square_send.at[begin + k],
                recv_sem=square_recv.at[begin + k],
                device_id=here.across(flips),
                device_id_type=MESH_ID,
            ).wait_recv()
        value = square_there[begin]
        for k in range(1, len(ways) + 1):
            value = value + square_there[begin + k]
        begin += len(ways)
        if begin == 7:
            begin = 8
    square_total[...] = value


def scatter_grads(parts, summed, outputs, chunks, collective_id, ahead=4, lag=(1, 1, 1)):
    count = len(chunks)
    views = [p.reshape(2, 2, 2, 2, p.shape[0] // 16, p.shape[1]) for p in parts]
    buffers = []
    for chunk in chunks:
        view = views[chunk[0]]
        for lead in scatter_buffers(chunk[5], chunk[6]):
            buffers.append(pltpu.VMEM((*lead, view.shape[4], chunk[4]), view.dtype))
    call = pl.pallas_call(
        functools.partial(scatter_kernel, chunks, len(parts), len(outputs), ahead, lag, lax.axis_size("mp")),
        out_shape=[
            jax.ShapeDtypeStruct((rows, width), jnp.float32) for rows, width in [*outputs, (8, 128)]
        ],
        in_specs=[pl.BlockSpec(memory_space=pl.ANY)] * (len(parts) - 1)
        + [pl.BlockSpec(memory_space=pltpu.VMEM)] * 2,
        out_specs=[pl.BlockSpec(memory_space=pltpu.VMEM)] * (len(outputs) + 1),
        scratch_shapes=[
            pltpu.SemaphoreType.DMA((count, 4)),
            pltpu.SemaphoreType.DMA((count, 4)),
            pltpu.SemaphoreType.DMA((count,)),
            pltpu.SemaphoreType.DMA((12,)),
            pltpu.SemaphoreType.DMA((12,)),
            pltpu.VMEM((2, 8, 128), jnp.float32),
            pltpu.VMEM((12, 8, 128), jnp.float32),
            pltpu.VMEM(views[-1].shape, views[-1].dtype),
            pltpu.VMEM(views[-1].shape, views[-1].dtype),
            *buffers,
        ],
        compiler_params=pltpu.CompilerParams(
            collective_id=collective_id, has_side_effects=True, vmem_limit_bytes=56 * 2**20
        ),
    )
    return call(*views, summed)


HEADS = 16
TOGETHER = 8
NORM_EPS = 1e-06
MASKED = -1e30
LOW = jnp.bfloat16
WIDE = jnp.float32


def mm(left, right, left_dim=1, right_dim=0):
    return lax.dot_general(
        left, right, (((left_dim,), (right_dim,)), ((), ())), preferred_element_type=WIDE
    )


def centre(tokens):
    average = jnp.mean(tokens, axis=-1, keepdims=True)
    centred = tokens - average
    spread_ = jnp.mean(centred * centred, axis=-1, keepdims=True)
    scale = lax.rsqrt(spread_ + NORM_EPS)
    return centred * scale, scale


def centre_back(unit, scale, gain, grad):
    pulled = grad * gain
    first = jnp.mean(pulled, axis=-1, keepdims=True)
    second = jnp.mean(pulled * unit, axis=-1, keepdims=True)
    return scale * (pulled - first - unit * second)


def gelu_pair(z):
    cdf = 0.5 * (1.0 + lax.erf(z * math.sqrt(0.5)))
    return z * cdf, cdf + z * (jnp.exp(-0.5 * z * z) * (1.0 / math.sqrt(2.0 * math.pi)))


def decoder_kernel(
    length,
    flag,
    target_row,
    target_column,
    visible_own,
    visible_other,
    mask,
    position,
    gains,
    pack_own,
    pack_other,
    cotangent,
    decoded,
    grad_keep,
    grad_send,
    grad_own,
    grad_other,
    grad_gains,
    qkv_t,
    out_t,
    qkv_rows,
    shares,
    mixture,
    hidden,
    slope,
    grad_mixture,
    stream,
    first,
    after,
    grad_low,
    grad_first,
    grad_visible,
    grad_qkv,
    grad_out,
    grad_up,
    grad_down,
):
    step = pl.program_id(0)
    images, rows, width = decoded.shape
    head = width // HEADS
    units = hidden.shape[1]
    part, half = width // 2, units // 2
    up_at, down_at = 4 * part, 4 * part + half
    scaling = head ** (-0.5)
    packs = (pack_own, pack_other)
    halves = ((slice(0, half), pack_own), (slice(half, units), pack_other))

    @pl.when(step == 0)
    def _():
        for ref in (grad_visible, grad_qkv, grad_out, grad_up, grad_down, grad_gains):
            ref[...] = jnp.zeros_like(ref)
        for which in range(4):
            for k, pack in enumerate(packs):
                at = (2 * which + k) * part
                piece = jnp.transpose(pack[:, which * part : (which + 1) * part])
                if which < 3:
                    qkv_t[at : at + part, :] = piece
                else:
                    out_t[k * part : (k + 1) * part, :] = piece

    packed = target_row.shape[1]
    left = flag[0] > 0
    spans = [slice(k * rows, (k + 1) * rows) for k in range(images)]
    for k, span in enumerate(spans):
        number = step * images + k
        cell = lax.broadcasted_iota(jnp.int32, (rows, packed), 0)
        wanted = jnp.where(cell < length, cell + number * length, -7)
        chosen = (target_row[...] == wanted).astype(WIDE)
        seen = jnp.max(chosen, axis=1, keepdims=True)
        chosen = chosen.astype(LOW)
        placed_own, placed_other = mm(chosen, visible_own[...]), mm(chosen, visible_other[...])
        placed = jnp.concatenate(
            [
                jnp.where(left, placed_own, placed_other),
                jnp.where(left, placed_other, placed_own),
            ],
            axis=1,
        )
        stream[span, :] = jnp.where(seen > 0.0, placed, mask[...]) + position[...]

    unit_one, scale_one = centre(stream[...])
    first[...] = (unit_one * gains[0:1] + gains[1:2]).astype(LOW)
    key_index = lax.broadcasted_iota(jnp.int32, (rows, rows), 0)

    def lines(which, h):
        return slice(which * width + h * head, which * width + (h + 1) * head)

    for k, span in enumerate(spans):
        qkv, mixed = qkv_rows.at[k], mixture.at[k]
        qkv[...] = mm(qkv_t[...], first[span, :], 1, 1).astype(LOW)
        for begin in range(0, HEADS, TOGETHER):
            group = range(begin, begin + TOGETHER)
            scores = [mm(qkv[lines(1, h), :], qkv[lines(0, h), :], 0, 0) * scaling for h in group]
            scores = [jnp.where(key_index < length, s, MASKED) for s in scores]
            weights = [jnp.exp(s - jnp.max(s, axis=0, keepdims=True)) for s in scores]
            group_shares = [w * (1.0 / jnp.sum(w, axis=0, keepdims=True)) for w in weights]
            for h, share in zip(group, group_shares):
                shares[k, h] = share
                mixed[lines(0, h), :] = mm(qkv[lines(2, h), :], share.astype(LOW)).astype(LOW)
        after[span, :] = stream[span, :] + mm(mixed[...], out_t[...], 0, 0)

    unit_two, scale_two = centre(after[...])
    second = (unit_two * gains[2:3] + gains[3:4]).astype(LOW)
    piece = 256
    for c in range(0, units, piece):
        pack, at = packs[c // half], up_at + c % half
        z = mm(second, pack[:, at : at + piece])
        h, g = gelu_pair(z)
        hidden[:, c : c + piece] = h.astype(LOW)
        slope[:, c : c + piece] = g
    fed = [mm(hidden[:, cut], pack[:, down_at : down_at + half], 1, 1) for cut, pack in halves]
    result = after[...] + (fed[0] + fed[1])
    for k, span in enumerate(spans):
        decoded[k] = result[span]

    for k, span in enumerate(spans):
        grad_low[span, :] = cotangent[k]
    turned = jnp.transpose(grad_low[...])
    second_turned = jnp.transpose(second)
    for c in range(0, units, piece):
        cut = slice(c, c + piece)
        grad_down[:, cut] += mm(turned, hidden[:, cut])
        pack, at = packs[c // half], down_at + c % half
        grad_z = (mm(grad_low[...], pack[:, at : at + piece]) * slope[:, cut]).astype(LOW)
        hidden[:, cut] = grad_z
        grad_up[:, cut] += mm(second_turned, grad_z)
    pulled = [mm(hidden[:, cut], pack[:, up_at : up_at + half], 1, 1) for cut, pack in halves]
    grad_second = pulled[0] + pulled[1]
    grad_gains[2:3] += jnp.sum(grad_second * unit_two, axis=0, keepdims=True)
    grad_gains[3:4] += jnp.sum(grad_second, axis=0, keepdims=True)
    after[...] = grad_low[...].astype(WIDE) + centre_back(
        unit_two, scale_two, gains[2:3], grad_second
    )

    for k, span in enumerate(spans):
        qkv, mixed, grad_rows = qkv_rows.at[k], mixture.at[k], grad_mixture.at[k]
        after_low = after[span, :].astype(LOW)
        grad_out[...] += mm(mixed[...], after_low)
        grad_rows[...] = mm(out_t[...], after_low, 1, 1).astype(LOW)
        for begin in range(0, HEADS, TOGETHER):
            group = range(begin, begin + TOGETHER)
            queries = [qkv[lines(0, h), :] for h in group]
            keys = [qkv[lines(1, h), :] for h in group]
            values = [qkv[lines(2, h), :] for h in group]
            grads_in = [grad_rows[lines(0, h), :] for h in group]
            grad_shares = [mm(v, g, 0, 0) for v, g in zip(values, grads_in)]
            grad_values = [mm(g, shares[k, h].astype(LOW), 1, 1) for g, h in zip(grads_in, group)]
            grad_scores = []
            for h, g in zip(group, grad_shares):
                share = shares[k, h]
                inner = jnp.sum(share * g, axis=0, keepdims=True)
                grad_scores.append((share * (g - inner)).astype(LOW))
            for n, h in enumerate(group):
                qkv[lines(0, h), :] = (mm(keys[n], grad_scores[n]) * scaling).astype(LOW)
                qkv[lines(1, h), :] = (mm(queries[n], grad_scores[n], 1, 1) * scaling).astype(LOW)
                qkv[lines(2, h), :] = grad_values[n].astype(LOW)
        grad_qkv[...] += mm(qkv[...], first[span, :])
        grad_first[span, :] = mm(qkv[...], qkv_t[...], 0, 0)

    unit_one, scale_one = centre(stream[...])
    pulled = grad_first[...]
    grad_stream = after[...] + centre_back(unit_one, scale_one, gains[0:1], pulled)
    grad_gains[0:1] += jnp.sum(pulled * unit_one, axis=0, keepdims=True)
    grad_gains[1:2] += jnp.sum(pulled, axis=0, keepdims=True)

    for k, span in enumerate(spans):
        cell_lane = lax.broadcasted_iota(jnp.int32, (packed, rows), 1)
        wanted_lane = jnp.where(cell_lane < length, cell_lane + (step * images + k) * length, -7)
        chosen_back = (target_column[...] == wanted_lane).astype(WIDE).astype(LOW)
        grad_visible[...] += mm(chosen_back, grad_stream[span].astype(LOW))

    @pl.when(step == pl.num_programs(0) - 1)
    def _():
        gathered = grad_visible[...].astype(LOW)
        one, two = gathered[:, :part], gathered[:, part:]
        grad_keep[...] = jnp.where(left, one, two)
        grad_send[...] = jnp.where(left, two, one)
        for k, ref in enumerate((grad_own, grad_other)):
            for which in range(4):
                at = (2 * which + k) * part
                piece = grad_qkv[at : at + part, :] if which < 3 else grad_out[k * part : (k + 1) * part, :]
                ref[:, which * part : (which + 1) * part] = jnp.transpose(piece.astype(LOW))
            cut = slice(k * half, (k + 1) * half)
            ref[:, up_at:down_at] = grad_up[:, cut].astype(LOW)
            ref[:, down_at:] = grad_down[:, cut].astype(LOW)


def decoder_step(
    length, left, visible_own, visible_other, target, mask, position, gains, pack_own, pack_other, cotangent
):
    rows, width = position.shape
    packed = visible_own.shape[0]
    images, columns = cotangent.shape[0], pack_own.shape[1]
    units = columns - 2 * width

    def fixed(shape):
        return pl.BlockSpec(shape, lambda i: (0,) * len(shape), pipeline_mode=pl.Buffered(1))

    at_once = 2 if images % 2 == 0 else 1
    per_image = pl.BlockSpec((at_once, rows, width), lambda i: (i, 0, 0))
    tall = at_once * rows
    grads = [
        ((packed, width // 2), LOW),
        ((packed, width // 2), LOW),
        ((width, columns), LOW),
        ((width, columns), LOW),
        ((8, width), WIDE),
    ]
    decoded, keep, send, grad_own, grad_other, grad_gains = pl.pallas_call(
        functools.partial(decoder_kernel, length),
        grid=(images // at_once,),
        out_shape=[jax.ShapeDtypeStruct((images, rows, width), WIDE)]
        + [jax.ShapeDtypeStruct(s, d) for s, d in grads],
        in_specs=[
            pl.BlockSpec(memory_space=pltpu.SMEM),
            fixed((1, packed)),
            fixed((packed, 1)),
            fixed((packed, width // 2)),
            fixed((packed, width // 2)),
            fixed((1, width)),
            fixed((rows, width)),
            fixed((4, width)),
            fixed((width, columns)),
            fixed((width, columns)),
            per_image,
        ],
        out_specs=[per_image] + [fixed(s) for s, _ in grads],
        scratch_shapes=[
            pltpu.VMEM((3 * width, width), LOW),
            pltpu.VMEM((width, width), LOW),
            pltpu.VMEM((at_once, 3 * width, rows), LOW),
            pltpu.VMEM((at_once, HEADS, rows, rows), WIDE),
            pltpu.VMEM((at_once, width, rows), LOW),
            pltpu.VMEM((tall, units), LOW),
            pltpu.VMEM((tall, units), WIDE),
            pltpu.VMEM((at_once, width, rows), LOW),
            pltpu.VMEM((tall, width), WIDE),
            pltpu.VMEM((tall, width), LOW),
            pltpu.VMEM((tall, width), WIDE),
            pltpu.VMEM((tall, width), LOW),
            pltpu.VMEM((tall, width), WIDE),
            pltpu.VMEM((packed, width), WIDE),
            pltpu.VMEM((3 * width, width), WIDE),
            pltpu.VMEM((width, width), WIDE),
            pltpu.VMEM((width, units), WIDE),
            pltpu.VMEM((width, units), WIDE),
        ],
        compiler_params=pltpu.CompilerParams(
            dimension_semantics=("arbitrary",), vmem_limit_bytes=60 * 2**20
        ),
    )(
        left.astype(jnp.int32).reshape(1),
        target[None, :],
        target[:, None],
        visible_own,
        visible_other,
        mask[None, :],
        position,
        gains,
        pack_own,
        pack_other,
        cotangent,
    )
    return decoded, keep, send, grad_own, grad_other, grad_gains[:4]


TILE = 256
GROUP = 4


def fixed(shape):
    return pl.BlockSpec(shape, lambda i: (0,) * len(shape), pipeline_mode=pl.Buffered(1))


def down_rows(rows, width):
    return pl.BlockSpec((rows, width), lambda i: (i, 0))


def params(megabytes=60):
    return pltpu.CompilerParams(
        dimension_semantics=("arbitrary",), vmem_limit_bytes=megabytes * 2**20
    )


def attend_kernel(
    head, bounds, stream, slots_row, slots_column, gains, qkv_w, out_w, first, turned, mixture, log_sum, partial
):
    rows, width = stream.shape
    part, lanes = mixture.shape
    tiles = lanes // TILE
    scaling = head ** (-0.5)
    unit, _ = centre(stream[...].astype(WIDE))
    first[...] = (unit * gains[0:1] + gains[1:2]).astype(LOW)
    turned[:, rows:] = jnp.zeros((3 * part, lanes - rows), LOW)
    for c in range(0, 3 * part, TILE):
        weight = jnp.transpose(qkv_w[:, c : c + TILE])
        turned[c : c + TILE, :rows] = mm(weight, first[...], 1, 1).astype(LOW)

    def at(which, h, tile):
        return (
            pl.ds(pl.multiple_of(which * part + h * head, head), head),
            pl.ds(pl.multiple_of(tile * TILE, TILE), TILE),
        )

    def step(n, carry):
        group, i = n // tiles, n % tiles
        heads = [group * GROUP + g for g in range(GROUP)]
        lane_i = pl.ds(pl.multiple_of(i * TILE, TILE), TILE)
        queries = [turned[at(0, h, i)] for h in heads]
        slot_i = slots_row[:, lane_i]

        def inner(j, state):
            same = slots_column[pl.ds(pl.multiple_of(j * TILE, TILE), TILE), :] == slot_i
            scores = [mm(turned[at(1, h, j)], q, 0, 0) * scaling for h, q in zip(heads, queries)]
            scores = [jnp.where(same, s, MASKED) for s in scores]
            highs = [
                jnp.maximum(state[g][0], jnp.max(s, axis=0, keepdims=True))
                for g, s in enumerate(scores)
            ]
            weights = [jnp.exp(s - high) for s, high in zip(scores, highs)]
            fixes = [jnp.exp(state[g][0] - high) for g, high in enumerate(highs)]
            sums = [jnp.sum(w, axis=0, keepdims=True) for w in weights]
            mixes = [mm(turned[at(2, h, j)], w.astype(LOW)) for h, w in zip(heads, weights)]
            return tuple(
                (highs[g], state[g][1] * fixes[g] + sums[g], state[g][2] * fixes[g] + mixes[g])
                for g in range(GROUP)
            )

        begin = (
            jnp.full((1, TILE), MASKED, WIDE),
            jnp.zeros((1, TILE), WIDE),
            jnp.zeros((head, TILE), WIDE),
        )
        state = lax.fori_loop(bounds[i, 0], bounds[i, 1], inner, (begin,) * GROUP)
        for g, h in enumerate(heads):
            high, total, mixed = state[g]
            mixture[at(0, h, i)] = (mixed / total).astype(LOW)
            log_sum[pl.ds(h, 1), lane_i] = high + jnp.log(total)
        return carry

    lax.fori_loop(0, part // head // GROUP * tiles, step, 0)
    mixed = jnp.transpose(mixture[...])[:rows]
    for c in range(0, width, TILE):
        partial[:, c : c + TILE] = mm(mixed, out_w[c : c + TILE, :], 1, 1).astype(LOW)


def encoder_attend(stream, slots, bounds, gains, qkv_w, out_w, head):
    rows, width = stream.shape
    lanes = slots.shape[0]
    part = out_w.shape[1]
    return pl.pallas_call(
        functools.partial(attend_kernel, head),
        in_specs=[pl.BlockSpec(memory_space=pltpu.SMEM)]
        + [pl.BlockSpec(memory_space=pltpu.VMEM)] * 6,
        out_specs=[pl.BlockSpec(memory_space=pltpu.VMEM)] * 5,
        out_shape=[
            jax.ShapeDtypeStruct((rows, width), LOW),
            jax.ShapeDtypeStruct((3 * part, lanes), LOW),
            jax.ShapeDtypeStruct((part, lanes), LOW),
            jax.ShapeDtypeStruct((part // head, lanes), WIDE),
            jax.ShapeDtypeStruct((rows, width), LOW),
        ],
        compiler_params=pltpu.CompilerParams(vmem_limit_bytes=60 * 2**20),
    )(bounds, stream, slots[None, :], slots[:, None], gains, qkv_w, out_w)


def attend_back_kernel(
    head,
    bounds,
    slots_row,
    slots_column,
    first,
    turned,
    mixture,
    log_sum,
    grad_low,
    qkv_w,
    out_w,
    grad_qkv_w,
    grad_out_w,
    partial,
    grad_mixture,
    grad_turned,
    inner_sum,
    key_sum,
    value_sum,
):
    rows, width = grad_low.shape
    part, lanes = mixture.shape
    tiles = lanes // TILE
    scaling = head ** (-0.5)
    grad_mixture[:, rows:] = jnp.zeros((part, lanes - rows), LOW)
    for c in range(0, width, TILE):
        grad_out_w[c : c + TILE, :] = jnp.transpose(
            mm(mixture[:, :rows], grad_low[:, c : c + TILE]).astype(LOW)
        )
    for c in range(0, part, TILE):
        weight = jnp.transpose(out_w[:, c : c + TILE])
        grad_mixture[c : c + TILE, :rows] = mm(weight, grad_low[...], 1, 1).astype(LOW)
    for h in range(part // head):
        cut = slice(h * head, (h + 1) * head)
        inner_sum[h : h + 1, :] = jnp.sum(
            grad_mixture[cut, :].astype(WIDE) * mixture[cut, :].astype(WIDE), axis=0, keepdims=True
        )

    def at(which, h, tile):
        return (
            pl.ds(pl.multiple_of(which * part + h * head, head), head),
            pl.ds(pl.multiple_of(tile * TILE, TILE), TILE),
        )

    def over_group(group, carry):
        heads = [group * GROUP + g for g in range(GROUP)]
        key_sum[...] = jnp.zeros_like(key_sum)
        value_sum[...] = jnp.zeros_like(value_sum)

        def over_queries(i, carry):
            lane_i = pl.ds(pl.multiple_of(i * TILE, TILE), TILE)
            slot_i = slots_row[:, lane_i]
            queries = [turned[at(0, h, i)] for h in heads]
            grads = [grad_mixture[at(0, h, i)] for h in heads]
            logs = [log_sum[pl.ds(h, 1), lane_i] for h in heads]
            sums = [inner_sum[pl.ds(h, 1), lane_i] for h in heads]

            def inner(j, state):
                lane_j = pl.ds(pl.multiple_of(j * TILE, TILE), TILE)
                same = slots_column[lane_j, :] == slot_i
                cuts = [slice(g * head, (g + 1) * head) for g in range(GROUP)]
                keys = [turned[at(1, h, j)] for h in heads]
                values = [turned[at(2, h, j)] for h in heads]
                scores = [mm(k, q, 0, 0) * scaling for k, q in zip(keys, queries)]
                grad_shares = [mm(v, g, 0, 0) for v, g in zip(values, grads)]
                shares = [
                    jnp.exp(jnp.where(same, s, MASKED) - log) for s, log in zip(scores, logs)
                ]
                grad_scores = [
                    (s * (g - total)).astype(LOW) for s, g, total in zip(shares, grad_shares, sums)
                ]
                for g, cut in enumerate(cuts):
                    value_sum[cut, lane_j] += mm(grads[g], shares[g].astype(LOW), 1, 1)
                for g, cut in enumerate(cuts):
                    key_sum[cut, lane_j] += mm(queries[g], grad_scores[g], 1, 1)
                return tuple(
                    state[g] + mm(keys[g], grad_scores[g]) for g in range(GROUP)
                )

            begin = (jnp.zeros((head, TILE), WIDE),) * GROUP
            state = lax.fori_loop(bounds[i, 0], bounds[i, 1], inner, begin)
            for g, h in enumerate(heads):
                grad_turned[at(0, h, i)] = (state[g] * scaling).astype(LOW)
            return carry

        lax.fori_loop(0, tiles, over_queries, 0)
        size = GROUP * head
        key_at = pl.ds(pl.multiple_of(part + group * size, size), size)
        value_at = pl.ds(pl.multiple_of(2 * part + group * size, size), size)
        grad_turned[key_at, :] = (key_sum[...] * scaling).astype(LOW)
        grad_turned[value_at, :] = value_sum[...].astype(LOW)
        return carry

    lax.fori_loop(0, part // head // GROUP, over_group, 0)
    for c in range(0, 3 * part, TILE):
        grad_qkv_w[:, c : c + TILE] = jnp.transpose(
            mm(grad_turned[c : c + TILE, :rows], first[...]).astype(LOW)
        )
    for c in range(0, width, TILE):
        partial[:, c : c + TILE] = jnp.transpose(
            mm(qkv_w[c : c + TILE, :], grad_turned[:, :rows]).astype(LOW)
        )


def encoder_attend_back(
    slots, bounds, first, turned, mixture, log_sum, grad_low, qkv_w, out_w, head
):
    rows, width = first.shape
    part, lanes = mixture.shape
    return pl.pallas_call(
        functools.partial(attend_back_kernel, head),
        in_specs=[pl.BlockSpec(memory_space=pltpu.SMEM)]
        + [pl.BlockSpec(memory_space=pltpu.VMEM)] * 9,
        out_specs=[pl.BlockSpec(memory_space=pltpu.VMEM)] * 3,
        out_shape=[
            jax.ShapeDtypeStruct((width, 3 * part), LOW),
            jax.ShapeDtypeStruct((width, part), LOW),
            jax.ShapeDtypeStruct((rows, width), LOW),
        ],
        scratch_shapes=[
            pltpu.VMEM((part, lanes), LOW),
            pltpu.VMEM((3 * part, lanes), LOW),
            pltpu.VMEM((part // head, lanes), WIDE),
            pltpu.VMEM((GROUP * head, lanes), WIDE),
            pltpu.VMEM((GROUP * head, lanes), WIDE),
        ],
        compiler_params=pltpu.CompilerParams(vmem_limit_bytes=60 * 2**20),
    )(
        bounds,
        slots[None, :],
        slots[:, None],
        first,
        turned,
        mixture,
        log_sum,
        grad_low,
        qkv_w,
        out_w,
    )


def feed_kernel(stream, own, other, gains, up_w, down_w, after, second, hidden, slope, partial):
    summed = stream[...].astype(WIDE) + (own[...].astype(WIDE) + other[...].astype(WIDE))
    after[...] = summed
    unit, _ = centre(summed)
    second[...] = (unit * gains[2:3] + gains[3:4]).astype(LOW)
    units = up_w.shape[1]
    for c in range(0, units, TILE):
        cut = slice(c, c + TILE)
        h, g = gelu_pair(mm(second[...], up_w[:, cut]))
        hidden[:, cut] = h.astype(LOW)
        slope[:, cut] = g.astype(LOW)
    partial[...] = mm(hidden[...], down_w[...], 1, 1).astype(LOW)


def encoder_feed(stream, own, other, gains, up_w, down_w, block):
    rows, width = stream.shape
    units = up_w.shape[1]
    wide, tall = down_rows(block, width), down_rows(block, units)
    return pl.pallas_call(
        feed_kernel,
        grid=(rows // block,),
        in_specs=[wide, wide, wide, fixed((4, width)), fixed(up_w.shape), fixed(down_w.shape)],
        out_specs=[wide, wide, tall, tall, wide],
        out_shape=[
            jax.ShapeDtypeStruct((rows, width), WIDE),
            jax.ShapeDtypeStruct((rows, width), LOW),
            jax.ShapeDtypeStruct((rows, units), LOW),
            jax.ShapeDtypeStruct((rows, units), LOW),
            jax.ShapeDtypeStruct((rows, width), LOW),
        ],
        compiler_params=params(),
    )(stream, own, other, gains, up_w, down_w)


def feed_back_kernel(
    counts,
    own,
    other,
    second,
    hidden,
    slope,
    up_w,
    down_w,
    grad_up,
    grad_down,
    partial,
    grad_low,
    grad_turned,
    second_turned,
    total,
):
    @pl.when(pl.program_id(0) == 0)
    def _():
        grad_low[...] = (own[...].astype(WIDE) + other[...].astype(WIDE)).astype(LOW)
        grad_turned[...] = jnp.transpose(grad_low[...])
        second_turned[...] = jnp.transpose(second[...])
        total[...] = jnp.zeros_like(total)

    down = mm(grad_turned[...], hidden[...])
    grad_down[...] = jnp.where(counts[0] > 0, down, jnp.zeros_like(down)).astype(LOW)
    grad_z = (mm(grad_low[...], down_w[...]) * slope[...].astype(WIDE)).astype(LOW)
    grad_up[...] = mm(second_turned[...], grad_z).astype(LOW)
    total[...] += mm(grad_z, up_w[...], 1, 1)

    @pl.when(pl.program_id(0) == pl.num_programs(0) - 1)
    def _():
        partial[...] = total[...].astype(LOW)


def encoder_feed_back(counts, own, other, second, hidden, slope, up_w, down_w):
    rows, width = own.shape
    units = up_w.shape[1]
    piece = 256
    whole = fixed((rows, width))
    tall = pl.BlockSpec((rows, piece), lambda i: (0, i))
    weight = pl.BlockSpec((width, piece), lambda i: (0, i))
    return pl.pallas_call(
        feed_back_kernel,
        grid=(units // piece,),
        in_specs=[pl.BlockSpec(memory_space=pltpu.SMEM)]
        + [whole, whole, whole, tall, tall, weight, weight],
        out_specs=[weight, weight, whole],
        out_shape=[
            jax.ShapeDtypeStruct((width, units), LOW),
            jax.ShapeDtypeStruct((width, units), LOW),
            jax.ShapeDtypeStruct((rows, width), LOW),
        ],
        scratch_shapes=[
            pltpu.VMEM((rows, width), LOW),
            pltpu.VMEM((width, rows), LOW),
            pltpu.VMEM((width, rows), LOW),
            pltpu.VMEM((rows, width), WIDE),
        ],
        compiler_params=params(),
    )(counts, own, other, second, hidden, slope, up_w, down_w)


def norm_back_kernel(tokens, own, other, skip_own, skip_other, gains, grad, grad_low, grad_gains, *, at):
    @pl.when(pl.program_id(0) == 0)
    def _():
        grad_gains[...] = jnp.zeros_like(grad_gains)

    pulled = own[...].astype(WIDE) + other[...].astype(WIDE)
    unit, scale = centre(tokens[...].astype(WIDE))
    result = skip_own[...].astype(WIDE)
    if skip_other is not None:
        result = result + skip_other[...].astype(WIDE)
    result = result + centre_back(unit, scale, gains[at : at + 1], pulled)
    grad[...] = result
    if grad_low is not None:
        grad_low[...] = result.astype(LOW)
    grad_gains[0:1] += jnp.sum(pulled * unit, axis=0, keepdims=True)
    grad_gains[1:2] += jnp.sum(pulled, axis=0, keepdims=True)


def encoder_norm_back(tokens, own, other, skip, gains, at, block, low):
    rows, width = tokens.shape
    wide = down_rows(block, width)
    two = len(skip) == 2

    def kernel(*refs):
        refs = list(refs)
        if not two:
            refs.insert(4, None)
        if not low:
            refs.insert(7, None)
        norm_back_kernel(*refs, at=at)

    shapes = [jax.ShapeDtypeStruct((rows, width), WIDE)]
    if low:
        shapes.append(jax.ShapeDtypeStruct((rows, width), LOW))
    shapes.append(jax.ShapeDtypeStruct((8, width), WIDE))
    return pl.pallas_call(
        kernel,
        grid=(rows // block,),
        in_specs=[wide, wide, wide] + [wide] * len(skip) + [fixed((4, width))],
        out_specs=[wide] * (2 if low else 1) + [fixed((8, width))],
        out_shape=shapes,
        compiler_params=params(),
    )(tokens, own, other, *skip, gains)


def finish_kernel(length, flag, tokens, own, other, skip, gains, decoded, result, grad_gains):
    pulled = own[...].astype(WIDE) + other[...].astype(WIDE)
    unit, scale = centre(tokens[...].astype(WIDE))
    grad_gains[...] = jnp.zeros_like(grad_gains)
    grad_gains[0:1] = jnp.sum(pulled * unit, axis=0, keepdims=True)
    grad_gains[1:2] = jnp.sum(pulled, axis=0, keepdims=True)
    rows, width = tokens.shape
    pieces = width // 128

    @pl.when(flag[0] > 0)
    def _():
        grad = skip[...] + centre_back(unit, scale, gains[0:1], pulled)
        for k in range(pieces):
            result[pl.ds(k, rows, stride=pieces), :] = grad[:, k * 128 : (k + 1) * 128]

    @pl.when(flag[0] == 0)
    def _():
        images, _, columns = decoded.shape
        count = columns // 128
        for i in range(images):
            for k in range(count):
                result[pl.ds(i * length * count + k, length, stride=count), :] = decoded[
                    i, 0:length, k * 128 : (k + 1) * 128
                ]


def encoder_finish(encoder_side, tokens, own, other, skip, gains, decoded, length):
    rows, width = tokens.shape
    return pl.pallas_call(
        functools.partial(finish_kernel, length),
        in_specs=[pl.BlockSpec(memory_space=pltpu.SMEM)]
        + [pl.BlockSpec(memory_space=pltpu.VMEM)] * 6,
        out_specs=[pl.BlockSpec(memory_space=pltpu.VMEM)] * 2,
        out_shape=[
            jax.ShapeDtypeStruct((rows * width // 128, 128), WIDE),
            jax.ShapeDtypeStruct((8, width), WIDE),
        ],
        compiler_params=pltpu.CompilerParams(vmem_limit_bytes=60 * 2**20),
    )(encoder_side.astype(jnp.int32).reshape(1), tokens, own, other, skip, gains, decoded)


def from_behind(value, axis, by):
    length = lax.axis_size(axis)
    pairs = [(i, i + by) for i in range(length) if 0 <= i + by < length]
    return lax.ppermute(value, axis, pairs)


def partner(value):
    length = lax.axis_size("mp")
    return lax.ppermute(value, "mp", [(i, (i + 1) % length) for i in range(length)])


def is_fast():
    return lax.axis_size("section") == 2 and lax.axis_size("dp") == 8


def plan(widths, dec_width, orders, dec_orders, among):
    chunks = chunk_list(widths, PIECES, 0, orders)
    dec = chunk_list((dec_width,), (DEC_PIECES,), 1, dec_orders)
    for k, (_, b, c, w, o, owner) in enumerate(dec):
        chunks.insert(3 * k + 2 if among else len(chunks), (len(widths), b, c, w, o, owner))
    return chunks


def gather_all(low_enc, low_dec, norms, widths):
    count = len(widths)
    if not is_fast():
        both = ("section", "dp")
        enc = lax.all_gather(low_enc, both, axis=0, tiled=True)
        dec = lax.all_gather(low_dec, both, axis=0, tiled=True)
        rows = lax.all_gather(norms, both, axis=0, tiled=True)
        parts, column = [], 0
        for w in widths:
            parts.append(enc[:, column : column + w])
            column += w
        return parts, dec, rows
    columns = [sum(widths[:k]) for k in range(count + 1)]
    ahead = [low_enc[:, : columns[3]], low_enc[:, columns[4] :]]
    near = (*widths[:3], widths[4])
    chunks = plan(near, low_dec.shape[1], GATHER_ORDERS, DEC_GATHER_ORDERS, False)
    outputs = [(low_enc.shape[0], w, LOW) for w in near]
    outputs += [(low_dec.shape[0], low_dec.shape[1], LOW), (8, 128, WIDE)]
    described = [(k // 4, k, c, b, w, o, own) for k, b, c, w, o, own in chunks]
    described.append((2, 5, 0, 0, 128, "hlyx", BOTH))
    shards = [jnp.concatenate(ahead, axis=1), low_dec, norms]
    results = gather_weights(shards, outputs, described, 1, GATHER_AHEAD, GATHER_LAG)
    low_down, norm_rows = lax.optimization_barrier(
        (low_enc[:, columns[3] : columns[4]], results[5])
    )
    down = lax.all_gather(low_down, ("section", "dp"), axis=0, tiled=True)
    return [*results[:3], down, results[3]], results[4], norm_rows


def scatter_all(enc_parts, dec, norms, encoder_side):
    widths = [p.shape[1] for p in enc_parts]
    both = ("section", "dp")

    def scattered(v):
        return lax.psum_scatter(v, both, scatter_dimension=0, tiled=True)

    if not is_fast():
        parts = [scattered(jnp.where(encoder_side, p.astype(WIDE), 0.0)) for p in enc_parts]
        dec = scattered(jnp.where(encoder_side, 0.0, dec.astype(WIDE)))
        norms = lax.psum(scattered(norms), "mp")
        local = sum(jnp.sum(v * v) for v in (*parts, dec))
        local = local + jnp.sum(norms * norms) / lax.axis_size("mp")
        total = jnp.full((8, 128), lax.psum(local, (*both, "mp")))
        return jnp.concatenate([*parts[:3], parts[4]], axis=1), parts[3], dec, norms, total
    down = scattered(enc_parts[3])
    near = (*enc_parts[:3], enc_parts[4])
    near_widths = (*widths[:3], widths[4])
    chunks = plan(near_widths, dec.shape[1], SCATTER_ORDERS, DEC_SCATTER_ORDERS, True)
    described = [(k, k // 4, b, c, w, o, own) for k, b, c, w, o, own in chunks]
    described.append((5, 2, 0, 0, 128, "xylh", BOTH))
    rows = near[0].shape[0] // 16
    outputs = [(rows, sum(near_widths)), (dec.shape[0] // 16, dec.shape[1]), (8, 128)]
    enc, dec, norms, total = scatter_grads(
        [*near, dec, norms], down, outputs, described, 2, SCATTER_AHEAD, SCATTER_LAG
    )
    return enc, down, dec, norms, total


def pack_norms(enc_rows, dec_rows, blocks):
    both = [rows.reshape(4, blocks, -1).transpose(1, 0, 2) for rows in (enc_rows, dec_rows)]
    joined = jnp.concatenate(both, axis=2)
    joined = jnp.pad(joined, ((0, 0), (0, 4), (0, 128 - joined.shape[2])))
    return joined.reshape(blocks * 8, 128)


def unpack_norms(packed, blocks, enc_width, dec_width):
    split = packed.reshape(blocks, 8, 128)[:, :4].transpose(1, 0, 2)
    return (
        split[:, :, :enc_width].reshape(4, -1),
        split[:, :, enc_width : enc_width + dec_width].reshape(4, -1),
    )


def key_ranges(slots):
    tiles = slots.reshape(-1, TILE)
    low, high = jnp.min(tiles, axis=1), jnp.max(tiles, axis=1)
    meet = jnp.logical_and(low[:, None] <= high[None, :], high[:, None] >= low[None, :])
    index = jnp.arange(tiles.shape[0], dtype=jnp.int32)[None, :]
    first = jnp.min(jnp.where(meet, index, tiles.shape[0]), axis=1)
    last = jnp.max(jnp.where(meet, index + 1, 0), axis=1)
    return jnp.stack([first, last], axis=1)


def renewed(weight, first_moment, second_moment, clipped, rate, fix_first, fix_second, decay):
    new_first = BETA_FIRST * first_moment + (1.0 - BETA_FIRST) * clipped
    new_second = BETA_SECOND * second_moment + (1.0 - BETA_SECOND) * clipped * clipped
    stepped = new_first / fix_first / (jnp.sqrt(new_second / fix_second) + ADAM_EPS)
    return weight - rate * (stepped + decay * weight)


def renew_kernel(order, scalars, total, near, down, dec, norms, *refs):
    enc_state, dec_state, enc_norm_state, dec_norm_state = (refs[k : k + 3] for k in (0, 3, 6, 9))
    new_enc, new_dec, new_enc_norm, new_dec_norm, enc_clip, dec_clip, enc_norm_clip, dec_norm_clip = refs[12:]
    factor = jnp.minimum(1.0, math.sqrt(PARAMS) / (jnp.sqrt(total[0:1, :]) + 1e-06))
    fixes = scalars[2], scalars[3]

    def work(blocks, state, new, clip):
        count = len(blocks)
        for k, (ref, at) in enumerate(blocks):
            rows = pl.ds(k, ref.shape[0], stride=count)
            clipped = ref[:, at : at + 128].astype(WIDE) * factor
            values = [s[rows, :] for s in state]
            clip[rows, :] = clipped
            new[rows, :] = renewed(*values, clipped, scalars[0], *fixes, WEIGHT_DECAY)

    work([((near, down)[which], at) for which, at in order], enc_state, new_enc, enc_clip)
    work([(dec, at) for at in range(0, dec.shape[1], 128)], dec_state, new_dec, dec_clip)
    column = 0
    for state, new, clip in (
        (enc_norm_state, new_enc_norm, enc_norm_clip),
        (dec_norm_state, new_dec_norm, dec_norm_clip),
    ):
        rows, width = new.shape
        clipped = norms[0:rows, column : column + width] * factor[:, :width]
        column += width
        clip[...] = clipped
        new[...] = renewed(*[s[...] for s in state], clipped, scalars[1], *fixes, 0.0)


def renew_all(scalars, total, near, down, down_at, dec, norms, enc, decoder, enc_norm, dec_norm):
    order = [(0, at) for at in range(0, near.shape[1], 128)]
    order[down_at // 128 : down_at // 128] = [(1, at) for at in range(0, down.shape[1], 128)]
    flat = [[v.reshape(-1, 128) for v in group] for group in (enc, decoder)]
    groups = [*flat, enc_norm, dec_norm]
    shapes = [jax.ShapeDtypeStruct(group[0].shape, WIDE) for group in groups] * 2
    results = pl.pallas_call(
        functools.partial(renew_kernel, order),
        in_specs=[pl.BlockSpec(memory_space=pltpu.SMEM)]
        + [pl.BlockSpec(memory_space=pltpu.VMEM)] * 17,
        out_specs=[pl.BlockSpec(memory_space=pltpu.VMEM)] * 8,
        out_shape=shapes,
        compiler_params=pltpu.CompilerParams(vmem_limit_bytes=40 * 2**20),
    )(scalars, total, near, down, dec, norms, *[v for group in groups for v in group])
    given = (enc, decoder, enc_norm, dec_norm) * 2
    return [r.reshape(group[0].shape) for r, group in zip(results, given)]


def per_device(
    act_in,
    packing,
    enc_weights,
    enc_first,
    enc_second,
    dec_weights,
    dec_first,
    dec_second,
    enc_norms,
    enc_norm_first,
    enc_norm_second,
    dec_norms,
    dec_norm_first,
    dec_norm_second,
    mask_token,
    dec_position,
    learning_rate,
    step_count,
):
    encoder_side = lax.axis_index("section") == 0
    decoder_side = jnp.logical_not(encoder_side)
    mp_rank = lax.axis_index("mp")
    mp_count = lax.axis_size("mp")
    first_half = mp_rank == 0
    slot_ids = packing[0, 0]
    patch_ids = packing[0, 1]
    local_images = IMG // mp_count
    grid_cells = local_images * GRID
    local_slot = slot_ids - mp_rank * local_images
    inside = jnp.logical_and(local_slot >= 0, local_slot < local_images)
    target = jnp.where(inside, local_slot * GRID + patch_ids, grid_cells)

    local_rows, width = act_in.shape[1], act_in.shape[2]
    real_rows = local_rows * mp_count
    rows = -(-real_rows // ROW_BLOCK) * ROW_BLOCK
    lanes = -(-rows // TILE) * TILE
    part = width // mp_count
    units = FF // mp_count
    head = width // HEADS
    dec_width = dec_position.shape[1]
    dec_part = dec_width // mp_count
    widths = (3 * part, part, units, units, dec_part)
    slots = jnp.pad(slot_ids, (0, lanes - real_rows), constant_values=IMG + 1)
    ranges = key_ranges(slots)

    (qkv_w, out_w, up_w, down_w, projection), dec_own, norm_rows = gather_all(
        enc_weights[:, 0, :].astype(LOW),
        dec_weights[:, 0, :].astype(LOW),
        pack_norms(enc_norms, dec_norms, 1),
        widths,
    )
    enc_gains, dec_gains = (
        v.astype(LOW).astype(WIDE)
        for v in unpack_norms(
            norm_rows, norm_rows.shape[0] // 8, enc_norms.shape[1], dec_norms.shape[1]
        )
    )
    own_stream, other_stream = act_in[0], partner(act_in[0])
    stream = jnp.where(
        first_half,
        jnp.concatenate([own_stream, other_stream], axis=0),
        jnp.concatenate([other_stream, own_stream], axis=0),
    )
    stream = jnp.pad(stream, ((0, rows - real_rows), (0, 0)))
    first, turned, mixture, log_sum, mix_own = encoder_attend(
        stream, slots, ranges, enc_gains, qkv_w, out_w, head
    )
    shown = min(real_rows, -(-IMG * MOST_VISIBLE // 16) * 16)
    packed = -(-shown // 128) * 128
    cell_rows = -(-GRID // 16) * 16
    longer = (0, cell_rows - GRID)
    seen_target = jnp.pad(target[:shown], (0, packed - shown), constant_values=-1)
    cotangent = act_in[0].reshape(local_images, GRID, dec_width)
    cotangent = jnp.pad(cotangent, ((0, 0), longer, (0, 0)))
    position = jnp.pad(dec_position, (longer, (0, 0)))
    mix_other, seen_target, cotangent, position, dec_gains = lax.optimization_barrier(
        (partner(mix_own), seen_target, cotangent, position, dec_gains)
    )
    after, second, hidden, slope, feed_own = encoder_feed(
        stream, mix_own, mix_other, enc_gains, up_w, down_w, ROW_BLOCK
    )
    encoded = (after + (feed_own.astype(WIDE) + partner(feed_own).astype(WIDE))).astype(LOW)
    projected = mm(encoded[:shown], projection).astype(LOW)
    arrived = from_behind(projected, "section", 1)
    arrived = jnp.pad(arrived, ((0, packed - shown), (0, 0)))
    decoded, grad_keep, grad_send, dec_grad_own, dec_grad_other, dec_gain_grad = decoder_step(
        GRID,
        first_half,
        arrived,
        partner(arrived),
        seen_target,
        mask_token,
        position,
        dec_gains,
        dec_own,
        partner(dec_own),
        cotangent,
    )
    returned = grad_keep[:shown] + partner(grad_send[:shown])
    grad_projected = from_behind(returned, "section", -1)
    grad_projected = jnp.pad(grad_projected, ((0, rows - shown), (0, 0)))
    dec_grad = dec_grad_own.astype(WIDE) + partner(dec_grad_other).astype(WIDE)
    dec_grad = dec_grad.astype(LOW)

    grad_projection = mm(encoded, grad_projected, 0, 0).astype(LOW)
    end_own = mm(grad_projected, projection, 1, 1).astype(LOW)
    end_other = partner(end_own)
    grad_up_w, grad_down_w, back_own = encoder_feed_back(
        jnp.where(encoder_side, 1, 0).astype(jnp.int32).reshape(1),
        end_own,
        end_other,
        second,
        hidden,
        slope,
        up_w,
        down_w,
    )
    grad_after, grad_low, gains_two = encoder_norm_back(
        after, back_own, partner(back_own), (end_own, end_other), enc_gains, 2, ROW_BLOCK, True
    )
    grad_qkv_w, grad_out_w, start_own = encoder_attend_back(
        slots, ranges, first, turned, mixture, log_sum, grad_low, qkv_w, out_w, head
    )
    def choose(matrix):
        top, bottom = matrix[:local_rows], matrix[local_rows:real_rows]
        return jnp.where(first_half, top, bottom), jnp.where(first_half, bottom, top)

    start_keep, start_send = choose(start_own)
    act_out, gains_one = encoder_finish(
        encoder_side,
        own_stream,
        start_keep,
        partner(start_send),
        choose(grad_after)[0],
        enc_gains,
        decoded,
        GRID,
    )
    enc_gain_grad = jnp.concatenate(
        [gains_one[:2], jnp.where(first_half, gains_two[:2], 0.0)], axis=0
    )
    norm_grads = pack_norms(
        jnp.where(encoder_side, enc_gain_grad, 0.0),
        jnp.where(decoder_side, dec_gain_grad, 0.0),
        norm_rows.shape[0] // 8,
    )
    near_shard, down_shard, dec_shard, norm_shard, square_total = scatter_all(
        (grad_qkv_w, grad_out_w, grad_up_w, grad_down_w, grad_projection),
        dec_grad,
        norm_grads,
        encoder_side,
    )
    step_value = step_count[0].astype(jnp.float32)
    scalars = jnp.stack(
        [
            learning_rate[0],
            learning_rate[1],
            1.0 - jnp.power(BETA_FIRST, step_value),
            1.0 - jnp.power(BETA_SECOND, step_value),
        ]
    )
    results = renew_all(
        scalars,
        square_total,
        near_shard,
        down_shard,
        sum(widths[:3]),
        dec_shard,
        norm_shard,
        (enc_weights, enc_first, enc_second),
        (dec_weights, dec_first, dec_second),
        (enc_norms, enc_norm_first, enc_norm_second),
        (dec_norms, dec_norm_first, dec_norm_second),
    )
    return (act_out.reshape(act_in.shape), *results, jnp.sqrt(square_total[0, 0]).reshape(1))


def solution(mesh):
    in_specs = (
        P("section", ("dp", "mp"), None),
        P("dp", None, None),
        P(("section", "dp"), "mp", None),
        P(("section", "dp"), "mp", None),
        P(("section", "dp"), "mp", None),
        P(("section", "dp"), "mp", None),
        P(("section", "dp"), "mp", None),
        P(("section", "dp"), "mp", None),
        P(None, ("section", "dp")),
        P(None, ("section", "dp")),
        P(None, ("section", "dp")),
        P(None, ("section", "dp")),
        P(None, ("section", "dp")),
        P(None, ("section", "dp")),
        P(),
        P(),
        P(),
        P(),
    )
    out_specs = (
        P("section", ("dp", "mp"), None),
        P(("section", "dp"), "mp", None),
        P(("section", "dp"), "mp", None),
        P(None, ("section", "dp")),
        P(None, ("section", "dp")),
        P(("section", "dp"), "mp", None),
        P(("section", "dp"), "mp", None),
        P(None, ("section", "dp")),
        P(None, ("section", "dp")),
        P(),
    )
    return jax.shard_map(
        per_device, mesh=mesh, in_specs=in_specs, out_specs=out_specs, check_vma=False
    )
```

```python
import functools
import itertools
import math

import jax
import jax.numpy as jnp
from jax import lax
from jax.experimental import pallas as pl
from jax.experimental.pallas import tpu as pltpu
from jax.sharding import PartitionSpec as P

FF = 4096
GRID = 196
IMG = 12
PARAMS = 16259072

BETA_FIRST = 0.9
BETA_SECOND = 0.999
ADAM_EPS = 1e-08
WEIGHT_DECAY = 0.05
ROW_BLOCK = 240
MOST_VISIBLE = 73
GATHER_ORDERS = ("hlxy", "hlyx", "hlxy", "hlyx", "yxhl")
DEC_GATHER_ORDERS = ("xhly", "xyhl")
DEC_SCATTER_ORDERS = ("ylhx", "ylhx")
PIECES, DEC_PIECES = (6, 2, 8, 1), 4
GATHER_AHEAD, GATHER_LAG = 6, (3, 6)
SCATTER_AHEAD, SCATTER_LAG = 6, (3, 3, 3)
SCATTER_ORDERS = ("xylh", "yxlh", "xylh", "yxlh", "lhxy")

MESH_ID = pl.DeviceIdType.MESH
EVERY = slice(None)
BOTH = -1
DIMS = "xhly"
NEAR_WAYS = ("x", "y", "c", "xy", "xc", "yc", "xyc")
LINE_WAYS = ("h", "l", "hl")
FAR = ("c", "xy", "xc", "yc", "xyc", "hl")


class Place:
    def __init__(self):
        s, depth, core = lax.axis_index("section"), lax.axis_index("dp"), lax.axis_index("mp")
        y, low, high = depth % 2, (depth // 2) % 2, depth // 4
        self.at = {"x": s, "h": high, "l": low, "y": y}
        self.s, self.core = s, core
        self.device = {
            "x": (1 - s, depth, core),
            "h": (s, depth + 4 - 8 * high, core),
            "l": (s, depth + 2 - 4 * low, core),
            "y": (s, depth + 1 - 2 * y, core),
        }

    def across(self, flips):
        other = {d: 1 - self.at[d] if d in flips else self.at[d] for d in DIMS}
        core = 1 - self.core if "c" in flips else self.core
        return other["x"], 4 * other["h"] + 2 * other["l"] + other["y"], core

    def greet(self, more=()):
        barrier = pltpu.get_barrier_semaphore()
        for flips in more:
            pl.semaphore_signal(
                barrier, inc=1, device_id=self.across(flips), device_id_type=MESH_ID
            )
        for name in self.device:
            pl.semaphore_signal(
                barrier, inc=1, device_id=self.device[name], device_id_type=MESH_ID
            )
        pl.semaphore_wait(barrier, len(self.device) + len(more))


def run(condition, action):
    if condition is None:
        action()
    else:
        pl.when(condition)(action)


def gather_kernel(chunks, n_in, n_out, ahead, lag, *refs):
    ins, outs = refs[:n_in], refs[n_in : n_in + n_out]
    send, recv, local = refs[n_in + n_out :]
    here = Place()
    count = len(chunks)

    def region(chunk, gathered, sender):
        at = [
            EVERY if d in gathered else 1 - here.at[d] if d == sender else here.at[d] for d in DIMS
        ]
        return outs[chunk[1]].at[(*at, EVERY, pl.ds(chunk[3], chunk[4]))]

    def own(i):
        chunk = chunks[i]
        return pltpu.make_async_copy(
            ins[chunk[0]].at[:, pl.ds(chunk[2], chunk[4])], region(chunk, "", None), local.at[i]
        )

    def copy(i, stage, incoming):
        chunk = chunks[i]
        order = chunk[5]
        axis = order[stage]
        block = region(chunk, order[:stage], axis if incoming else None)
        source = block
        if stage == 0 and not incoming:
            source = ins[chunk[0]].at[:, pl.ds(chunk[2], chunk[4])]
        return pltpu.make_async_remote_copy(
            src_ref=source,
            dst_ref=block,
            send_sem=send.at[i, stage],
            recv_sem=recv.at[i, stage],
            device_id=here.device[axis],
            device_id_type=MESH_ID,
        )

    def roles(i, stage):
        order, owner = chunks[i][5], chunks[i][6]
        if owner == BOTH:
            return None, None
        if order[stage] == "x":
            return here.s != owner, here.s == owner
        if "x" in order[:stage]:
            return here.s == owner, here.s == owner
        return None, None

    def begin(i, stage):
        run(roles(i, stage)[0], lambda: copy(i, stage, False).start())

    def arrive(i, stage):
        run(roles(i, stage)[1], lambda: copy(i, stage, True).wait_recv())
        if stage == 0:
            own(i).wait()

    here.greet()
    for i in range(count):
        own(i).start()
    for i in range(min(ahead, count)):
        begin(i, 0)
    for step in range(count + sum(lag)):
        for stage in range(3):
            i = step - sum(lag[:stage])
            if not 0 <= i < count:
                continue
            arrive(i, stage)
            begin(i, stage + 1)
            if stage == 0 and i + ahead < count:
                begin(i + ahead, 0)
    for i in range(count):
        arrive(i, 3)
    for i in range(count):
        for stage in range(4):
            run(
                roles(i, stage)[0],
                lambda i=i, stage=stage: copy(i, stage, False).wait_send(),
            )


def gather_weights(shards, outputs, chunks, collective_id, ahead=4, lag=(1, 1)):
    count = len(chunks)
    call = pl.pallas_call(
        functools.partial(gather_kernel, chunks, len(shards), len(outputs), ahead, lag),
        out_shape=[
            jax.ShapeDtypeStruct((2, 2, 2, 2, rows, width), dtype) for rows, width, dtype in outputs
        ],
        in_specs=[pl.BlockSpec(memory_space=pltpu.VMEM)] * len(shards),
        out_specs=[pl.BlockSpec(memory_space=pltpu.HBM)] * len(outputs),
        scratch_shapes=[
            pltpu.SemaphoreType.DMA((count, 4)),
            pltpu.SemaphoreType.DMA((count, 4)),
            pltpu.SemaphoreType.DMA((count,)),
        ],
        compiler_params=pltpu.CompilerParams(
            collective_id=collective_id, has_side_effects=True, vmem_limit_bytes=40 * 2**20
        ),
    )
    results = call(*shards)
    return [
        r.reshape(16 * rows, width) for r, (rows, width, _) in zip(results, outputs, strict=True)
    ]


def spread(total, pieces, unit=128):
    units = total // unit
    widths = [units // pieces + (1 if k < units % pieces else 0) for k in range(pieces)]
    return [w * unit for w in widths if w]


def chunk_list(widths, pieces, owner, orders):
    chunks = []
    column = turn = 0
    for index, (width, count) in enumerate(zip(widths, pieces, strict=True)):
        begin = 0
        for piece in spread(width, count):
            chunks.append((index, begin, column, piece, orders[turn % len(orders)], owner))
            begin += piece
            column += piece
            turn += 1
    return chunks


def left_after(order, stage):
    return [d for d in DIMS if d not in order[: stage + 1]]


def scatter_buffers(order, owner):
    shapes = [(2,) * 3]
    for stage in range(4):
        if order[stage] == "x" and owner != BOTH:
            continue
        shapes.append((2,) * (3 - stage))
    return shapes


def squares(ref):
    def step(k, total):
        block = ref[:, pl.ds(pl.multiple_of(k * 128, 128), 128)].astype(jnp.float32)
        block = block * block
        for r in range(0, block.shape[0], 8):
            total = total + block[r : r + 8]
        return total

    return lax.fori_loop(0, ref.shape[1] // 128, step, jnp.zeros((8, 128), jnp.float32))


def scatter_kernel(chunks, n_in, n_out, ahead, lag, cores, *refs):
    ins, summed, outs = refs[:n_in], refs[n_in], refs[n_in + 1 : n_in + 1 + n_out]
    square_total = refs[n_in + 1 + n_out]
    rest = refs[n_in + n_out + 2 :]
    send, recv, local, square_send, square_recv, square_mine, square_there, last, last_there = rest[:9]
    here = Place()
    s = here.s
    count = len(chunks)
    given, ins = ins[-1], (*ins[:-1], last)
    own, got = [], []
    position = 9
    for chunk in chunks:
        order, owner = chunk[5], chunk[6]
        own.append(rest[position])
        position += 1
        mine = []
        for stage in range(4):
            if order[stage] == "x" and owner != BOTH:
                mine.append(None)
                continue
            mine.append(rest[position])
            position += 1
        got.append(mine)

    def source(i, axis, keep):
        chunk = chunks[i]
        at = [
            (here.at[d] if keep else 1 - here.at[d]) if d == axis else EVERY for d in DIMS
        ]
        return ins[chunk[0]].at[(*at, EVERY, pl.ds(chunk[2], chunk[4]))]

    def load(i):
        return pltpu.make_async_copy(source(i, chunks[i][5][0], True), own[i], local.at[i])

    def spot(i, stage, flip):
        order = chunks[i][5]
        at = []
        for d in DIMS:
            if d == order[0]:
                continue
            if d in order[:stage]:
                at.append(here.at[d])
            elif d == order[stage]:
                at.append(1 - here.at[d] if flip else here.at[d])
            else:
                at.append(EVERY)
        return tuple(at)

    def copy(i, stage, incoming):
        order = chunks[i][5]
        axis = order[stage]
        moved = got[i][stage] is None
        src = source(i, axis, False) if stage == 0 else own[i].at[spot(i, stage, True)]
        if not moved:
            there = mine = got[i][stage]
        elif stage == 0:
            there = mine = own[i]
        else:
            there, mine = own[i].at[spot(i, stage, True)], own[i].at[spot(i, stage, False)]
        return pltpu.make_async_remote_copy(
            src_ref=mine if incoming else src,
            dst_ref=mine if incoming else there,
            send_sem=send.at[i, stage],
            recv_sem=recv.at[i, stage],
            device_id=here.device[axis],
            device_id_type=MESH_ID,
        )

    def roles(i, stage):
        order, owner = chunks[i][5], chunks[i][6]
        if owner == BOTH:
            return None, None
        if order[stage] == "x":
            return s == owner, s != owner
        if "x" in order[:stage]:
            return None, None
        return s == owner, s == owner

    def begin(i, stage):
        run(roles(i, stage)[0], lambda: copy(i, stage, False).start())

    def arrive(i, stage):
        chunk, a, r = chunks[i], own[i], got[i][stage]
        order, owner = chunk[5], chunk[6]
        run(roles(i, stage)[1], lambda: copy(i, stage, True).wait_recv())
        if stage == 0:
            run(None if owner == BOTH else s == owner, lambda: load(i).wait())
        out = outs[chunk[1]].at[:, pl.ds(chunk[3], chunk[4])]
        place = spot(i, stage, False)
        if stage == 3:
            result = a[place].astype(jnp.float32)
            if r is not None:
                result = result + r[...].astype(jnp.float32)
            out[...] = result
            return
        if r is None:
            return

        def add():
            free = [k for k, p in enumerate(place) if p is EVERY]
            for combo in itertools.product(range(2), repeat=len(free)):
                at = list(place)
                for k, c in zip(free, combo):
                    at[k] = c
                at = tuple(at)
                a[at] = (a[at].astype(jnp.float32) + r[combo].astype(jnp.float32)).astype(a.dtype)

        run(roles(i, stage)[1], add)

    here.greet(FAR)
    join = pltpu.make_async_remote_copy(
        src_ref=given,
        dst_ref=last_there,
        send_sem=square_send.at[11],
        recv_sem=square_recv.at[11],
        device_id=here.across("c"),
        device_id_type=MESH_ID,
    )
    join.start()
    for i in range(count - 1):
        run(
            None if chunks[i][6] == BOTH else s == chunks[i][6],
            lambda i=i: load(i).start(),
        )
    for i in range(min(ahead, count)):
        begin(i, 0)
    join.wait()
    last[...] = given[...] + last_there[...]
    load(count - 1).start()
    for step in range(count + sum(lag)):
        for stage in range(3, -1, -1):
            i = step - sum(lag[:stage])
            if not 0 <= i < count:
                continue
            arrive(i, stage)
            if stage < 3:
                begin(i, stage + 1)
            if stage == 0 and i + ahead < count:
                begin(i + ahead, 0)
    for i in range(count):
        for stage in range(4):
            run(
                roles(i, stage)[0],
                lambda i=i, stage=stage: copy(i, stage, False).wait_send(),
            )

    value = squares(summed)
    for k, out in enumerate(outs):
        value = value + squares(out) * (1.0 / cores if k == n_out - 1 else 1.0)
    value = jnp.broadcast_to(jnp.sum(value, keepdims=True), (8, 128))
    begin = 0
    for bits, ways in (("xyc", NEAR_WAYS), ("hl", LINE_WAYS)):
        names = {**here.at, "c": here.core}

        def number(flips):
            total = 0
            for bit in bits:
                total = 2 * total + (1 - names[bit] if bit in flips else names[bit])
            return total

        mine = square_mine.at[0 if begin == 0 else 1]
        mine[...] = value
        moves = []
        for k, flips in enumerate(ways):
            moves.append(
                pltpu.make_async_remote_copy(
                    src_ref=mine,
                    dst_ref=square_there.at[begin + number("")],
                    send_sem=square_send.at[begin + k],
                    recv_sem=square_recv.at[begin + k],
                    device_id=here.across(flips),
                    device_id_type=MESH_ID,
                )
            )
            moves[-1].start()
        square_there[begin + number("")] = value
        for k, flips in enumerate(ways):
            moves[k].wait_send()
            slot = square_there.at[begin + number(flips)]
            pltpu.make_async_remote_copy(
                src_ref=slot,
                dst_ref=slot,
                send_sem=square_send.at[begin + k],
                recv_sem=square_recv.at[begin + k],
                device_id=here.across(flips),
                device_id_type=MESH_ID,
            ).wait_recv()
        value = square_there[begin]
        for k in range(1, len(ways) + 1):
            value = value + square_there[begin + k]
        begin += len(ways)
        if begin == 7:
            begin = 8
    square_total[...] = value


def scatter_grads(parts, summed, outputs, chunks, collective_id, ahead=4, lag=(1, 1, 1)):
    count = len(chunks)
    views = [p.reshape(2, 2, 2, 2, p.shape[0] // 16, p.shape[1]) for p in parts]
    buffers = []
    for chunk in chunks:
        view = views[chunk[0]]
        for lead in scatter_buffers(chunk[5], chunk[6]):
            buffers.append(pltpu.VMEM((*lead, view.shape[4], chunk[4]), view.dtype))
    call = pl.pallas_call(
        functools.partial(scatter_kernel, chunks, len(parts), len(outputs), ahead, lag, lax.axis_size("mp")),
        out_shape=[
            jax.ShapeDtypeStruct((rows, width), jnp.float32) for rows, width in [*outputs, (8, 128)]
        ],
        in_specs=[pl.BlockSpec(memory_space=pl.ANY)] * (len(parts) - 1)
        + [pl.BlockSpec(memory_space=pltpu.VMEM)] * 2,
        out_specs=[pl.BlockSpec(memory_space=pltpu.VMEM)] * (len(outputs) + 1),
        scratch_shapes=[
            pltpu.SemaphoreType.DMA((count, 4)),
            pltpu.SemaphoreType.DMA((count, 4)),
            pltpu.SemaphoreType.DMA((count,)),
            pltpu.SemaphoreType.DMA((12,)),
            pltpu.SemaphoreType.DMA((12,)),
            pltpu.VMEM((2, 8, 128), jnp.float32),
            pltpu.VMEM((12, 8, 128), jnp.float32),
            pltpu.VMEM(views[-1].shape, views[-1].dtype),
            pltpu.VMEM(views[-1].shape, views[-1].dtype),
            *buffers,
        ],
        compiler_params=pltpu.CompilerParams(
            collective_id=collective_id, has_side_effects=True, vmem_limit_bytes=56 * 2**20
        ),
    )
    return call(*views, summed)


HEADS = 16
TOGETHER = 8
NORM_EPS = 1e-06
MASKED = -1e30
LOW = jnp.bfloat16
WIDE = jnp.float32


def mm(left, right, left_dim=1, right_dim=0):
    return lax.dot_general(
        left, right, (((left_dim,), (right_dim,)), ((), ())), preferred_element_type=WIDE
    )


def centre(tokens):
    average = jnp.mean(tokens, axis=-1, keepdims=True)
    centred = tokens - average
    spread_ = jnp.mean(centred * centred, axis=-1, keepdims=True)
    scale = lax.rsqrt(spread_ + NORM_EPS)
    return centred * scale, scale


def centre_back(unit, scale, gain, grad):
    pulled = grad * gain
    first = jnp.mean(pulled, axis=-1, keepdims=True)
    second = jnp.mean(pulled * unit, axis=-1, keepdims=True)
    return scale * (pulled - first - unit * second)


def gelu_pair(z):
    cdf = 0.5 * (1.0 + lax.erf(z * math.sqrt(0.5)))
    return z * cdf, cdf + z * (jnp.exp(-0.5 * z * z) * (1.0 / math.sqrt(2.0 * math.pi)))


def decoder_kernel(
    length,
    flag,
    target_row,
    target_column,
    visible_own,
    visible_other,
    mask,
    position,
    gains,
    pack_own,
    pack_other,
    cotangent,
    decoded,
    grad_keep,
    grad_send,
    grad_own,
    grad_other,
    grad_gains,
    qkv_t,
    out_t,
    qkv_rows,
    shares,
    mixture,
    hidden,
    slope,
    grad_mixture,
    stream,
    first,
    after,
    grad_low,
    grad_first,
    grad_visible,
    grad_qkv,
    grad_out,
    grad_up,
    grad_down,
):
    step = pl.program_id(0)
    images, rows, width = decoded.shape
    head = width // HEADS
    units = hidden.shape[1]
    part, half = width // 2, units // 2
    up_at, down_at = 4 * part, 4 * part + half
    scaling = head ** (-0.5)
    packs = (pack_own, pack_other)
    halves = ((slice(0, half), pack_own), (slice(half, units), pack_other))

    @pl.when(step == 0)
    def _():
        for ref in (grad_visible, grad_qkv, grad_out, grad_up, grad_down, grad_gains):
            ref[...] = jnp.zeros_like(ref)
        for which in range(4):
            for k, pack in enumerate(packs):
                at = (2 * which + k) * part
                piece = jnp.transpose(pack[:, which * part : (which + 1) * part])
                if which < 3:
                    qkv_t[at : at + part, :] = piece
                else:
                    out_t[k * part : (k + 1) * part, :] = piece

    packed = target_row.shape[1]
    left = flag[0] > 0
    spans = [slice(k * rows, (k + 1) * rows) for k in range(images)]
    for k, span in enumerate(spans):
        number = step * images + k
        cell = lax.broadcasted_iota(jnp.int32, (rows, packed), 0)
        wanted = jnp.where(cell < length, cell + number * length, -7)
        chosen = (target_row[...] == wanted).astype(WIDE)
        seen = jnp.max(chosen, axis=1, keepdims=True)
        chosen = chosen.astype(LOW)
        placed_own, placed_other = mm(chosen, visible_own[...]), mm(chosen, visible_other[...])
        placed = jnp.concatenate(
            [
                jnp.where(left, placed_own, placed_other),
                jnp.where(left, placed_other, placed_own),
            ],
            axis=1,
        )
        stream[span, :] = jnp.where(seen > 0.0, placed, mask[...]) + position[...]

    unit_one, scale_one = centre(stream[...])
    first[...] = (unit_one * gains[0:1] + gains[1:2]).astype(LOW)
    key_index = lax.broadcasted_iota(jnp.int32, (rows, rows), 0)

    def lines(which, h):
        return slice(which * width + h * head, which * width + (h + 1) * head)

    for k, span in enumerate(spans):
        qkv, mixed = qkv_rows.at[k], mixture.at[k]
        qkv[...] = mm(qkv_t[...], first[span, :], 1, 1).astype(LOW)
        for begin in range(0, HEADS, TOGETHER):
            group = range(begin, begin + TOGETHER)
            scores = [mm(qkv[lines(1, h), :], qkv[lines(0, h), :], 0, 0) * scaling for h in group]
            scores = [jnp.where(key_index < length, s, MASKED) for s in scores]
            weights = [jnp.exp(s - jnp.max(s, axis=0, keepdims=True)) for s in scores]
            group_shares = [w * (1.0 / jnp.sum(w, axis=0, keepdims=True)) for w in weights]
            for h, share in zip(group, group_shares):
                shares[k, h] = share
                mixed[lines(0, h), :] = mm(qkv[lines(2, h), :], share.astype(LOW)).astype(LOW)
        after[span, :] = stream[span, :] + mm(mixed[...], out_t[...], 0, 0)

    unit_two, scale_two = centre(after[...])
    second = (unit_two * gains[2:3] + gains[3:4]).astype(LOW)
    piece = 256
    for c in range(0, units, piece):
        pack, at = packs[c // half], up_at + c % half
        z = mm(second, pack[:, at : at + piece])
        h, g = gelu_pair(z)
        hidden[:, c : c + piece] = h.astype(LOW)
        slope[:, c : c + piece] = g
    fed = [mm(hidden[:, cut], pack[:, down_at : down_at + half], 1, 1) for cut, pack in halves]
    result = after[...] + (fed[0] + fed[1])
    for k, span in enumerate(spans):
        decoded[k] = result[span]

    for k, span in enumerate(spans):
        grad_low[span, :] = cotangent[k]
    turned = jnp.transpose(grad_low[...])
    second_turned = jnp.transpose(second)
    for c in range(0, units, piece):
        cut = slice(c, c + piece)
        grad_down[:, cut] += mm(turned, hidden[:, cut])
        pack, at = packs[c // half], down_at + c % half
        grad_z = (mm(grad_low[...], pack[:, at : at + piece]) * slope[:, cut]).astype(LOW)
        hidden[:, cut] = grad_z
        grad_up[:, cut] += mm(second_turned, grad_z)
    pulled = [mm(hidden[:, cut], pack[:, up_at : up_at + half], 1, 1) for cut, pack in halves]
    grad_second = pulled[0] + pulled[1]
    grad_gains[2:3] += jnp.sum(grad_second * unit_two, axis=0, keepdims=True)
    grad_gains[3:4] += jnp.sum(grad_second, axis=0, keepdims=True)
    after[...] = grad_low[...].astype(WIDE) + centre_back(
        unit_two, scale_two, gains[2:3], grad_second
    )

    for k, span in enumerate(spans):
        qkv, mixed, grad_rows = qkv_rows.at[k], mixture.at[k], grad_mixture.at[k]
        after_low = after[span, :].astype(LOW)
        grad_out[...] += mm(mixed[...], after_low)
        grad_rows[...] = mm(out_t[...], after_low, 1, 1).astype(LOW)
        for begin in range(0, HEADS, TOGETHER):
            group = range(begin, begin + TOGETHER)
            queries = [qkv[lines(0, h), :] for h in group]
            keys = [qkv[lines(1, h), :] for h in group]
            values = [qkv[lines(2, h), :] for h in group]
            grads_in = [grad_rows[lines(0, h), :] for h in group]
            grad_shares = [mm(v, g, 0, 0) for v, g in zip(values, grads_in)]
            grad_values = [mm(g, shares[k, h].astype(LOW), 1, 1) for g, h in zip(grads_in, group)]
            grad_scores = []
            for h, g in zip(group, grad_shares):
                share = shares[k, h]
                inner = jnp.sum(share * g, axis=0, keepdims=True)
                grad_scores.append((share * (g - inner)).astype(LOW))
            for n, h in enumerate(group):
                qkv[lines(0, h), :] = (mm(keys[n], grad_scores[n]) * scaling).astype(LOW)
                qkv[lines(1, h), :] = (mm(queries[n], grad_scores[n], 1, 1) * scaling).astype(LOW)
                qkv[lines(2, h), :] = grad_values[n].astype(LOW)
        grad_qkv[...] += mm(qkv[...], first[span, :])
        grad_first[span, :] = mm(qkv[...], qkv_t[...], 0, 0)

    unit_one, scale_one = centre(stream[...])
    pulled = grad_first[...]
    grad_stream = after[...] + centre_back(unit_one, scale_one, gains[0:1], pulled)
    grad_gains[0:1] += jnp.sum(pulled * unit_one, axis=0, keepdims=True)
    grad_gains[1:2] += jnp.sum(pulled, axis=0, keepdims=True)

    for k, span in enumerate(spans):
        cell_lane = lax.broadcasted_iota(jnp.int32, (packed, rows), 1)
        wanted_lane = jnp.where(cell_lane < length, cell_lane + (step * images + k) * length, -7)
        chosen_back = (target_column[...] == wanted_lane).astype(WIDE).astype(LOW)
        grad_visible[...] += mm(chosen_back, grad_stream[span].astype(LOW))

    @pl.when(step == pl.num_programs(0) - 1)
    def _():
        gathered = grad_visible[...].astype(LOW)
        one, two = gathered[:, :part], gathered[:, part:]
        grad_keep[...] = jnp.where(left, one, two)
        grad_send[...] = jnp.where(left, two, one)
        for k, ref in enumerate((grad_own, grad_other)):
            for which in range(4):
                at = (2 * which + k) * part
                piece = grad_qkv[at : at + part, :] if which < 3 else grad_out[k * part : (k + 1) * part, :]
                ref[:, which * part : (which + 1) * part] = jnp.transpose(piece.astype(LOW))
            cut = slice(k * half, (k + 1) * half)
            ref[:, up_at:down_at] = grad_up[:, cut].astype(LOW)
            ref[:, down_at:] = grad_down[:, cut].astype(LOW)


def decoder_step(
    length, left, visible_own, visible_other, target, mask, position, gains, pack_own, pack_other, cotangent
):
    rows, width = position.shape
    packed = visible_own.shape[0]
    images, columns = cotangent.shape[0], pack_own.shape[1]
    units = columns - 2 * width

    def fixed(shape):
        return pl.BlockSpec(shape, lambda i: (0,) * len(shape), pipeline_mode=pl.Buffered(1))

    at_once = 2 if images % 2 == 0 else 1
    per_image = pl.BlockSpec((at_once, rows, width), lambda i: (i, 0, 0))
    tall = at_once * rows
    grads = [
        ((packed, width // 2), LOW),
        ((packed, width // 2), LOW),
        ((width, columns), LOW),
        ((width, columns), LOW),
        ((8, width), WIDE),
    ]
    decoded, keep, send, grad_own, grad_other, grad_gains = pl.pallas_call(
        functools.partial(decoder_kernel, length),
        grid=(images // at_once,),
        out_shape=[jax.ShapeDtypeStruct((images, rows, width), WIDE)]
        + [jax.ShapeDtypeStruct(s, d) for s, d in grads],
        in_specs=[
            pl.BlockSpec(memory_space=pltpu.SMEM),
            fixed((1, packed)),
            fixed((packed, 1)),
            fixed((packed, width // 2)),
            fixed((packed, width // 2)),
            fixed((1, width)),
            fixed((rows, width)),
            fixed((4, width)),
            fixed((width, columns)),
            fixed((width, columns)),
            per_image,
        ],
        out_specs=[per_image] + [fixed(s) for s, _ in grads],
        scratch_shapes=[
            pltpu.VMEM((3 * width, width), LOW),
            pltpu.VMEM((width, width), LOW),
            pltpu.VMEM((at_once, 3 * width, rows), LOW),
            pltpu.VMEM((at_once, HEADS, rows, rows), WIDE),
            pltpu.VMEM((at_once, width, rows), LOW),
            pltpu.VMEM((tall, units), LOW),
            pltpu.VMEM((tall, units), WIDE),
            pltpu.VMEM((at_once, width, rows), LOW),
            pltpu.VMEM((tall, width), WIDE),
            pltpu.VMEM((tall, width), LOW),
            pltpu.VMEM((tall, width), WIDE),
            pltpu.VMEM((tall, width), LOW),
            pltpu.VMEM((tall, width), WIDE),
            pltpu.VMEM((packed, width), WIDE),
            pltpu.VMEM((3 * width, width), WIDE),
            pltpu.VMEM((width, width), WIDE),
            pltpu.VMEM((width, units), WIDE),
            pltpu.VMEM((width, units), WIDE),
        ],
        compiler_params=pltpu.CompilerParams(
            dimension_semantics=("arbitrary",), vmem_limit_bytes=60 * 2**20
        ),
    )(
        left.astype(jnp.int32).reshape(1),
        target[None, :],
        target[:, None],
        visible_own,
        visible_other,
        mask[None, :],
        position,
        gains,
        pack_own,
        pack_other,
        cotangent,
    )
    return decoded, keep, send, grad_own, grad_other, grad_gains[:4]


TILE = 256
GROUP = 4


def fixed(shape):
    return pl.BlockSpec(shape, lambda i: (0,) * len(shape), pipeline_mode=pl.Buffered(1))


def down_rows(rows, width):
    return pl.BlockSpec((rows, width), lambda i: (i, 0))


def params(megabytes=60):
    return pltpu.CompilerParams(
        dimension_semantics=("arbitrary",), vmem_limit_bytes=megabytes * 2**20
    )


def attend_kernel(
    head, bounds, stream, slots_row, slots_column, gains, qkv_w, out_w, first, turned, mixture, log_sum, partial
):
    rows, width = stream.shape
    part, lanes = mixture.shape
    tiles = lanes // TILE
    scaling = head ** (-0.5)
    unit, _ = centre(stream[...].astype(WIDE))
    first[...] = (unit * gains[0:1] + gains[1:2]).astype(LOW)
    turned[:, rows:] = jnp.zeros((3 * part, lanes - rows), LOW)
    for c in range(0, 3 * part, TILE):
        weight = jnp.transpose(qkv_w[:, c : c + TILE])
        turned[c : c + TILE, :rows] = mm(weight, first[...], 1, 1).astype(LOW)

    def at(which, h, tile):
        return (
            pl.ds(pl.multiple_of(which * part + h * head, head), head),
            pl.ds(pl.multiple_of(tile * TILE, TILE), TILE),
        )

    def step(n, carry):
        group, i = n // tiles, n % tiles
        heads = [group * GROUP + g for g in range(GROUP)]
        lane_i = pl.ds(pl.multiple_of(i * TILE, TILE), TILE)
        queries = [turned[at(0, h, i)] for h in heads]
        slot_i = slots_row[:, lane_i]

        def inner(j, state):
            same = slots_column[pl.ds(pl.multiple_of(j * TILE, TILE), TILE), :] == slot_i
            scores = [mm(turned[at(1, h, j)], q, 0, 0) * scaling for h, q in zip(heads, queries)]
            scores = [jnp.where(same, s, MASKED) for s in scores]
            highs = [
                jnp.maximum(state[g][0], jnp.max(s, axis=0, keepdims=True))
                for g, s in enumerate(scores)
            ]
            weights = [jnp.exp(s - high) for s, high in zip(scores, highs)]
            fixes = [jnp.exp(state[g][0] - high) for g, high in enumerate(highs)]
            sums = [jnp.sum(w, axis=0, keepdims=True) for w in weights]
            mixes = [mm(turned[at(2, h, j)], w.astype(LOW)) for h, w in zip(heads, weights)]
            return tuple(
                (highs[g], state[g][1] * fixes[g] + sums[g], state[g][2] * fixes[g] + mixes[g])
                for g in range(GROUP)
            )

        begin = (
            jnp.full((1, TILE), MASKED, WIDE),
            jnp.zeros((1, TILE), WIDE),
            jnp.zeros((head, TILE), WIDE),
        )
        state = lax.fori_loop(bounds[i, 0], bounds[i, 1], inner, (begin,) * GROUP)
        for g, h in enumerate(heads):
            high, total, mixed = state[g]
            mixture[at(0, h, i)] = (mixed / total).astype(LOW)
            log_sum[pl.ds(h, 1), lane_i] = high + jnp.log(total)
        return carry

    lax.fori_loop(0, part // head // GROUP * tiles, step, 0)
    mixed = jnp.transpose(mixture[...])[:rows]
    for c in range(0, width, TILE):
        partial[:, c : c + TILE] = mm(mixed, out_w[c : c + TILE, :], 1, 1).astype(LOW)


def encoder_attend(stream, slots, bounds, gains, qkv_w, out_w, head):
    rows, width = stream.shape
    lanes = slots.shape[0]
    part = out_w.shape[1]
    return pl.pallas_call(
        functools.partial(attend_kernel, head),
        in_specs=[pl.BlockSpec(memory_space=pltpu.SMEM)]
        + [pl.BlockSpec(memory_space=pltpu.VMEM)] * 6,
        out_specs=[pl.BlockSpec(memory_space=pltpu.VMEM)] * 5,
        out_shape=[
            jax.ShapeDtypeStruct((rows, width), LOW),
            jax.ShapeDtypeStruct((3 * part, lanes), LOW),
            jax.ShapeDtypeStruct((part, lanes), LOW),
            jax.ShapeDtypeStruct((part // head, lanes), WIDE),
            jax.ShapeDtypeStruct((rows, width), LOW),
        ],
        compiler_params=pltpu.CompilerParams(vmem_limit_bytes=60 * 2**20),
    )(bounds, stream, slots[None, :], slots[:, None], gains, qkv_w, out_w)


def attend_back_kernel(
    head,
    bounds,
    slots_row,
    slots_column,
    first,
    turned,
    mixture,
    log_sum,
    grad_low,
    qkv_w,
    out_w,
    grad_qkv_w,
    grad_out_w,
    partial,
    grad_mixture,
    grad_turned,
    inner_sum,
    key_sum,
    value_sum,
):
    rows, width = grad_low.shape
    part, lanes = mixture.shape
    tiles = lanes // TILE
    scaling = head ** (-0.5)
    grad_mixture[:, rows:] = jnp.zeros((part, lanes - rows), LOW)
    for c in range(0, width, TILE):
        grad_out_w[c : c + TILE, :] = jnp.transpose(
            mm(mixture[:, :rows], grad_low[:, c : c + TILE]).astype(LOW)
        )
    for c in range(0, part, TILE):
        weight = jnp.transpose(out_w[:, c : c + TILE])
        grad_mixture[c : c + TILE, :rows] = mm(weight, grad_low[...], 1, 1).astype(LOW)
    for h in range(part // head):
        cut = slice(h * head, (h + 1) * head)
        inner_sum[h : h + 1, :] = jnp.sum(
            grad_mixture[cut, :].astype(WIDE) * mixture[cut, :].astype(WIDE), axis=0, keepdims=True
        )

    def at(which, h, tile):
        return (
            pl.ds(pl.multiple_of(which * part + h * head, head), head),
            pl.ds(pl.multiple_of(tile * TILE, TILE), TILE),
        )

    def over_group(group, carry):
        heads = [group * GROUP + g for g in range(GROUP)]
        key_sum[...] = jnp.zeros_like(key_sum)
        value_sum[...] = jnp.zeros_like(value_sum)

        def over_queries(i, carry):
            lane_i = pl.ds(pl.multiple_of(i * TILE, TILE), TILE)
            slot_i = slots_row[:, lane_i]
            queries = [turned[at(0, h, i)] for h in heads]
            grads = [grad_mixture[at(0, h, i)] for h in heads]
            logs = [log_sum[pl.ds(h, 1), lane_i] for h in heads]
            sums = [inner_sum[pl.ds(h, 1), lane_i] for h in heads]

            def inner(j, state):
                lane_j = pl.ds(pl.multiple_of(j * TILE, TILE), TILE)
                same = slots_column[lane_j, :] == slot_i
                cuts = [slice(g * head, (g + 1) * head) for g in range(GROUP)]
                keys = [turned[at(1, h, j)] for h in heads]
                values = [turned[at(2, h, j)] for h in heads]
                scores = [mm(k, q, 0, 0) * scaling for k, q in zip(keys, queries)]
                grad_shares = [mm(v, g, 0, 0) for v, g in zip(values, grads)]
                shares = [
                    jnp.exp(jnp.where(same, s, MASKED) - log) for s, log in zip(scores, logs)
                ]
                grad_scores = [
                    (s * (g - total)).astype(LOW) for s, g, total in zip(shares, grad_shares, sums)
                ]
                for g, cut in enumerate(cuts):
                    value_sum[cut, lane_j] += mm(grads[g], shares[g].astype(LOW), 1, 1)
                for g, cut in enumerate(cuts):
                    key_sum[cut, lane_j] += mm(queries[g], grad_scores[g], 1, 1)
                return tuple(
                    state[g] + mm(keys[g], grad_scores[g]) for g in range(GROUP)
                )

            begin = (jnp.zeros((head, TILE), WIDE),) * GROUP
            state = lax.fori_loop(bounds[i, 0], bounds[i, 1], inner, begin)
            for g, h in enumerate(heads):
                grad_turned[at(0, h, i)] = (state[g] * scaling).astype(LOW)
            return carry

        lax.fori_loop(0, tiles, over_queries, 0)
        size = GROUP * head
        key_at = pl.ds(pl.multiple_of(part + group * size, size), size)
        value_at = pl.ds(pl.multiple_of(2 * part + group * size, size), size)
        grad_turned[key_at, :] = (key_sum[...] * scaling).astype(LOW)
        grad_turned[value_at, :] = value_sum[...].astype(LOW)
        return carry

    lax.fori_loop(0, part // head // GROUP, over_group, 0)
    for c in range(0, 3 * part, TILE):
        grad_qkv_w[:, c : c + TILE] = jnp.transpose(
            mm(grad_turned[c : c + TILE, :rows], first[...]).astype(LOW)
        )
    for c in range(0, width, TILE):
        partial[:, c : c + TILE] = jnp.transpose(
            mm(qkv_w[c : c + TILE, :], grad_turned[:, :rows]).astype(LOW)
        )


def encoder_attend_back(
    slots, bounds, first, turned, mixture, log_sum, grad_low, qkv_w, out_w, head
):
    rows, width = first.shape
    part, lanes = mixture.shape
    return pl.pallas_call(
        functools.partial(attend_back_kernel, head),
        in_specs=[pl.BlockSpec(memory_space=pltpu.SMEM)]
        + [pl.BlockSpec(memory_space=pltpu.VMEM)] * 9,
        out_specs=[pl.BlockSpec(memory_space=pltpu.VMEM)] * 3,
        out_shape=[
            jax.ShapeDtypeStruct((width, 3 * part), LOW),
            jax.ShapeDtypeStruct((width, part), LOW),
            jax.ShapeDtypeStruct((rows, width), LOW),
        ],
        scratch_shapes=[
            pltpu.VMEM((part, lanes), LOW),
            pltpu.VMEM((3 * part, lanes), LOW),
            pltpu.VMEM((part // head, lanes), WIDE),
            pltpu.VMEM((GROUP * head, lanes), WIDE),
            pltpu.VMEM((GROUP * head, lanes), WIDE),
        ],
        compiler_params=pltpu.CompilerParams(vmem_limit_bytes=60 * 2**20),
    )(
        bounds,
        slots[None, :],
        slots[:, None],
        first,
        turned,
        mixture,
        log_sum,
        grad_low,
        qkv_w,
        out_w,
    )


def feed_kernel(stream, own, other, gains, up_w, down_one, down_two, after, second, hidden, slope, partial):
    summed = stream[...].astype(WIDE) + (own[...].astype(WIDE) + other[...].astype(WIDE))
    after[...] = summed
    unit, _ = centre(summed)
    second[...] = (unit * gains[2:3] + gains[3:4]).astype(LOW)
    units = up_w.shape[1]
    for c in range(0, units, TILE):
        cut = slice(c, c + TILE)
        h, g = gelu_pair(mm(second[...], up_w[:, cut]))
        hidden[:, cut] = h.astype(LOW)
        slope[:, cut] = g.astype(LOW)
    cut = down_one.shape[1]
    fed = mm(hidden[:, :cut], down_one[...], 1, 1) + mm(hidden[:, cut:], down_two[...], 1, 1)
    partial[...] = fed.astype(LOW)


def encoder_feed(stream, own, other, gains, up_w, down_one, down_two, block):
    rows, width = stream.shape
    units = up_w.shape[1]
    wide, tall = down_rows(block, width), down_rows(block, units)
    return pl.pallas_call(
        feed_kernel,
        grid=(rows // block,),
        in_specs=[wide, wide, wide, fixed((4, width))]
        + [fixed(w.shape) for w in (up_w, down_one, down_two)],
        out_specs=[wide, wide, tall, tall, wide],
        out_shape=[
            jax.ShapeDtypeStruct((rows, width), WIDE),
            jax.ShapeDtypeStruct((rows, width), LOW),
            jax.ShapeDtypeStruct((rows, units), LOW),
            jax.ShapeDtypeStruct((rows, units), LOW),
            jax.ShapeDtypeStruct((rows, width), LOW),
        ],
        compiler_params=params(),
    )(stream, own, other, gains, up_w, down_one, down_two)


def feed_back_kernel(
    early,
    counts,
    own,
    other,
    second,
    hidden,
    slope,
    up_w,
    down_one,
    down_two,
    grad_up,
    grad_down,
    partial,
    grad_low,
    grad_turned,
    second_turned,
    total,
):
    @pl.when(pl.program_id(0) == 0)
    def _():
        grad_low[...] = (own[...].astype(WIDE) + other[...].astype(WIDE)).astype(LOW)
        grad_turned[...] = jnp.transpose(grad_low[...])
        second_turned[...] = jnp.transpose(second[...])
        total[...] = jnp.zeros_like(total)

    down = mm(grad_turned[...], hidden[...])
    grad_down[...] = jnp.where(counts[0] > 0, down, jnp.zeros_like(down)).astype(LOW)
    down_w = jnp.where(pl.program_id(0) < early, down_one[...], down_two[...])
    grad_z = (mm(grad_low[...], down_w) * slope[...].astype(WIDE)).astype(LOW)
    grad_up[...] = mm(second_turned[...], grad_z).astype(LOW)
    total[...] += mm(grad_z, up_w[...], 1, 1)

    @pl.when(pl.program_id(0) == pl.num_programs(0) - 1)
    def _():
        partial[...] = total[...].astype(LOW)


def encoder_feed_back(counts, own, other, second, hidden, slope, up_w, down_one, down_two):
    rows, width = own.shape
    units = up_w.shape[1]
    piece = 256
    whole = fixed((rows, width))
    tall = pl.BlockSpec((rows, piece), lambda i: (0, i))
    weight = pl.BlockSpec((width, piece), lambda i: (0, i))
    early = down_one.shape[1] // piece
    one = pl.BlockSpec((width, piece), lambda i: (0, jnp.minimum(i, early - 1)))
    two = pl.BlockSpec((width, piece), lambda i: (0, jnp.maximum(i - early, 0)))
    return pl.pallas_call(
        functools.partial(feed_back_kernel, early),
        grid=(units // piece,),
        in_specs=[pl.BlockSpec(memory_space=pltpu.SMEM)]
        + [whole, whole, whole, tall, tall, weight, one, two],
        out_specs=[weight, weight, whole],
        out_shape=[
            jax.ShapeDtypeStruct((width, units), LOW),
            jax.ShapeDtypeStruct((width, units), LOW),
            jax.ShapeDtypeStruct((rows, width), LOW),
        ],
        scratch_shapes=[
            pltpu.VMEM((rows, width), LOW),
            pltpu.VMEM((width, rows), LOW),
            pltpu.VMEM((width, rows), LOW),
            pltpu.VMEM((rows, width), WIDE),
        ],
        compiler_params=params(),
    )(counts, own, other, second, hidden, slope, up_w, down_one, down_two)


def norm_back_kernel(tokens, own, other, skip_own, skip_other, gains, grad, grad_low, grad_gains, *, at):
    @pl.when(pl.program_id(0) == 0)
    def _():
        grad_gains[...] = jnp.zeros_like(grad_gains)

    pulled = own[...].astype(WIDE) + other[...].astype(WIDE)
    unit, scale = centre(tokens[...].astype(WIDE))
    result = skip_own[...].astype(WIDE)
    if skip_other is not None:
        result = result + skip_other[...].astype(WIDE)
    result = result + centre_back(unit, scale, gains[at : at + 1], pulled)
    grad[...] = result
    if grad_low is not None:
        grad_low[...] = result.astype(LOW)
    grad_gains[0:1] += jnp.sum(pulled * unit, axis=0, keepdims=True)
    grad_gains[1:2] += jnp.sum(pulled, axis=0, keepdims=True)


def encoder_norm_back(tokens, own, other, skip, gains, at, block, low):
    rows, width = tokens.shape
    wide = down_rows(block, width)
    two = len(skip) == 2

    def kernel(*refs):
        refs = list(refs)
        if not two:
            refs.insert(4, None)
        if not low:
            refs.insert(7, None)
        norm_back_kernel(*refs, at=at)

    shapes = [jax.ShapeDtypeStruct((rows, width), WIDE)]
    if low:
        shapes.append(jax.ShapeDtypeStruct((rows, width), LOW))
    shapes.append(jax.ShapeDtypeStruct((8, width), WIDE))
    return pl.pallas_call(
        kernel,
        grid=(rows // block,),
        in_specs=[wide, wide, wide] + [wide] * len(skip) + [fixed((4, width))],
        out_specs=[wide] * (2 if low else 1) + [fixed((8, width))],
        out_shape=shapes,
        compiler_params=params(),
    )(tokens, own, other, *skip, gains)


def finish_kernel(length, flag, tokens, own, other, skip, gains, decoded, result, grad_gains):
    pulled = own[...].astype(WIDE) + other[...].astype(WIDE)
    unit, scale = centre(tokens[...].astype(WIDE))
    grad_gains[...] = jnp.zeros_like(grad_gains)
    grad_gains[0:1] = jnp.sum(pulled * unit, axis=0, keepdims=True)
    grad_gains[1:2] = jnp.sum(pulled, axis=0, keepdims=True)
    rows, width = tokens.shape
    pieces = width // 128

    @pl.when(flag[0] > 0)
    def _():
        grad = skip[...] + centre_back(unit, scale, gains[0:1], pulled)
        for k in range(pieces):
            result[pl.ds(k, rows, stride=pieces), :] = grad[:, k * 128 : (k + 1) * 128]

    @pl.when(flag[0] == 0)
    def _():
        images, _, columns = decoded.shape
        count = columns // 128
        for i in range(images):
            for k in range(count):
                result[pl.ds(i * length * count + k, length, stride=count), :] = decoded[
                    i, 0:length, k * 128 : (k + 1) * 128
                ]


def encoder_finish(encoder_side, tokens, own, other, skip, gains, decoded, length):
    rows, width = tokens.shape
    return pl.pallas_call(
        functools.partial(finish_kernel, length),
        in_specs=[pl.BlockSpec(memory_space=pltpu.SMEM)]
        + [pl.BlockSpec(memory_space=pltpu.VMEM)] * 6,
        out_specs=[pl.BlockSpec(memory_space=pltpu.VMEM)] * 2,
        out_shape=[
            jax.ShapeDtypeStruct((rows * width // 128, 128), WIDE),
            jax.ShapeDtypeStruct((8, width), WIDE),
        ],
        compiler_params=pltpu.CompilerParams(vmem_limit_bytes=60 * 2**20),
    )(encoder_side.astype(jnp.int32).reshape(1), tokens, own, other, skip, gains, decoded)


def from_behind(value, axis, by):
    length = lax.axis_size(axis)
    pairs = [(i, i + by) for i in range(length) if 0 <= i + by < length]
    return lax.ppermute(value, axis, pairs)


def partner(value):
    length = lax.axis_size("mp")
    return lax.ppermute(value, "mp", [(i, (i + 1) % length) for i in range(length)])


def is_fast():
    return lax.axis_size("section") == 2 and lax.axis_size("dp") == 8


def plan(widths, pieces, dec_width, orders, dec_orders, among):
    chunks = chunk_list(widths, pieces, 0, orders)
    dec = chunk_list((dec_width,), (DEC_PIECES,), 1, dec_orders)
    for k, (_, b, c, w, o, owner) in enumerate(dec):
        chunks.insert(3 * k + 2 if among else len(chunks), (len(widths), b, c, w, o, owner))
    return chunks


def gather_all(low_enc, low_dec, norms, widths):
    count = len(widths)
    cut = widths[3] // 4
    if not is_fast():
        both = ("section", "dp")
        enc = lax.all_gather(low_enc, both, axis=0, tiled=True)
        dec = lax.all_gather(low_dec, both, axis=0, tiled=True)
        rows = lax.all_gather(norms, both, axis=0, tiled=True)
        parts, column = [], 0
        for w in widths:
            parts.append(enc[:, column : column + w])
            column += w
        parts[3] = (parts[3][:, :cut], parts[3][:, cut:])
        return parts, dec, rows
    columns = [sum(widths[:k]) for k in range(count + 1)]
    ahead = [low_enc[:, : columns[3] + cut], low_enc[:, columns[4] :]]
    near = (*widths[:3], cut, widths[4])
    pieces = (*PIECES[:3], 2, PIECES[3])
    chunks = plan(near, pieces, low_dec.shape[1], GATHER_ORDERS, DEC_GATHER_ORDERS, False)
    outputs = [(low_enc.shape[0], w, LOW) for w in near]
    outputs += [(low_dec.shape[0], low_dec.shape[1], LOW), (8, 128, WIDE)]
    described = [(k // 5, k, c, b, w, o, own) for k, b, c, w, o, own in chunks]
    described.append((2, 6, 0, 0, 128, "hlyx", BOTH))
    shards = [jnp.concatenate(ahead, axis=1), low_dec, norms]
    results = gather_weights(shards, outputs, described, 1, GATHER_AHEAD, GATHER_LAG)
    low_down, norm_rows = lax.optimization_barrier(
        (low_enc[:, columns[3] + cut : columns[4]], results[6])
    )
    down = lax.all_gather(low_down, ("section", "dp"), axis=0, tiled=True)
    return [*results[:3], (results[3], down), results[4]], results[5], norm_rows


def scatter_all(enc_parts, dec, norms, encoder_side):
    widths = [p.shape[1] for p in enc_parts]
    both = ("section", "dp")

    def scattered(v):
        return lax.psum_scatter(v, both, scatter_dimension=0, tiled=True)

    if not is_fast():
        parts = [scattered(jnp.where(encoder_side, p.astype(WIDE), 0.0)) for p in enc_parts]
        dec = scattered(jnp.where(encoder_side, 0.0, dec.astype(WIDE)))
        norms = lax.psum(scattered(norms), "mp")
        local = sum(jnp.sum(v * v) for v in (*parts, dec))
        local = local + jnp.sum(norms * norms) / lax.axis_size("mp")
        total = jnp.full((8, 128), lax.psum(local, (*both, "mp")))
        return jnp.concatenate([*parts[:3], parts[4]], axis=1), parts[3], dec, norms, total
    down = scattered(enc_parts[3])
    near = (*enc_parts[:3], enc_parts[4])
    near_widths = (*widths[:3], widths[4])
    chunks = plan(near_widths, PIECES, dec.shape[1], SCATTER_ORDERS, DEC_SCATTER_ORDERS, True)
    described = [(k, k // 4, b, c, w, o, own) for k, b, c, w, o, own in chunks]
    described.append((5, 2, 0, 0, 128, "xylh", BOTH))
    rows = near[0].shape[0] // 16
    outputs = [(rows, sum(near_widths)), (dec.shape[0] // 16, dec.shape[1]), (8, 128)]
    enc, dec, norms, total = scatter_grads(
        [*near, dec, norms], down, outputs, described, 2, SCATTER_AHEAD, SCATTER_LAG
    )
    return enc, down, dec, norms, total


def pack_norms(enc_rows, dec_rows, blocks):
    both = [rows.reshape(4, blocks, -1).transpose(1, 0, 2) for rows in (enc_rows, dec_rows)]
    joined = jnp.concatenate(both, axis=2)
    joined = jnp.pad(joined, ((0, 0), (0, 4), (0, 128 - joined.shape[2])))
    return joined.reshape(blocks * 8, 128)


def unpack_norms(packed, blocks, enc_width, dec_width):
    split = packed.reshape(blocks, 8, 128)[:, :4].transpose(1, 0, 2)
    return (
        split[:, :, :enc_width].reshape(4, -1),
        split[:, :, enc_width : enc_width + dec_width].reshape(4, -1),
    )


def key_ranges(slots):
    tiles = slots.reshape(-1, TILE)
    low, high = jnp.min(tiles, axis=1), jnp.max(tiles, axis=1)
    meet = jnp.logical_and(low[:, None] <= high[None, :], high[:, None] >= low[None, :])
    index = jnp.arange(tiles.shape[0], dtype=jnp.int32)[None, :]
    first = jnp.min(jnp.where(meet, index, tiles.shape[0]), axis=1)
    last = jnp.max(jnp.where(meet, index + 1, 0), axis=1)
    return jnp.stack([first, last], axis=1)


def renewed(weight, first_moment, second_moment, clipped, rate, fix_first, fix_second, decay):
    new_first = BETA_FIRST * first_moment + (1.0 - BETA_FIRST) * clipped
    new_second = BETA_SECOND * second_moment + (1.0 - BETA_SECOND) * clipped * clipped
    stepped = new_first / fix_first / (jnp.sqrt(new_second / fix_second) + ADAM_EPS)
    return weight - rate * (stepped + decay * weight)


def renew_kernel(order, scalars, total, near, down, dec, norms, *refs):
    enc_state, dec_state, enc_norm_state, dec_norm_state = (refs[k : k + 3] for k in (0, 3, 6, 9))
    new_enc, new_dec, new_enc_norm, new_dec_norm, enc_clip, dec_clip, enc_norm_clip, dec_norm_clip = refs[12:]
    factor = jnp.minimum(1.0, math.sqrt(PARAMS) / (jnp.sqrt(total[0:1, :]) + 1e-06))
    fixes = scalars[2], scalars[3]

    def work(blocks, state, new, clip):
        count = len(blocks)
        for k, (ref, at) in enumerate(blocks):
            rows = pl.ds(k, ref.shape[0], stride=count)
            clipped = ref[:, at : at + 128].astype(WIDE) * factor
            values = [s[rows, :] for s in state]
            clip[rows, :] = clipped
            new[rows, :] = renewed(*values, clipped, scalars[0], *fixes, WEIGHT_DECAY)

    work([((near, down)[which], at) for which, at in order], enc_state, new_enc, enc_clip)
    work([(dec, at) for at in range(0, dec.shape[1], 128)], dec_state, new_dec, dec_clip)
    column = 0
    for state, new, clip in (
        (enc_norm_state, new_enc_norm, enc_norm_clip),
        (dec_norm_state, new_dec_norm, dec_norm_clip),
    ):
        rows, width = new.shape
        clipped = norms[0:rows, column : column + width] * factor[:, :width]
        column += width
        clip[...] = clipped
        new[...] = renewed(*[s[...] for s in state], clipped, scalars[1], *fixes, 0.0)


def renew_all(scalars, total, near, down, down_at, dec, norms, enc, decoder, enc_norm, dec_norm):
    order = [(0, at) for at in range(0, near.shape[1], 128)]
    order[down_at // 128 : down_at // 128] = [(1, at) for at in range(0, down.shape[1], 128)]
    flat = [[v.reshape(-1, 128) for v in group] for group in (enc, decoder)]
    groups = [*flat, enc_norm, dec_norm]
    shapes = [jax.ShapeDtypeStruct(group[0].shape, WIDE) for group in groups] * 2
    results = pl.pallas_call(
        functools.partial(renew_kernel, order),
        in_specs=[pl.BlockSpec(memory_space=pltpu.SMEM)]
        + [pl.BlockSpec(memory_space=pltpu.VMEM)] * 17,
        out_specs=[pl.BlockSpec(memory_space=pltpu.VMEM)] * 8,
        out_shape=shapes,
        compiler_params=pltpu.CompilerParams(vmem_limit_bytes=40 * 2**20),
    )(scalars, total, near, down, dec, norms, *[v for group in groups for v in group])
    given = (enc, decoder, enc_norm, dec_norm) * 2
    return [r.reshape(group[0].shape) for r, group in zip(results, given)]


def per_device(
    act_in,
    packing,
    enc_weights,
    enc_first,
    enc_second,
    dec_weights,
    dec_first,
    dec_second,
    enc_norms,
    enc_norm_first,
    enc_norm_second,
    dec_norms,
    dec_norm_first,
    dec_norm_second,
    mask_token,
    dec_position,
    learning_rate,
    step_count,
):
    encoder_side = lax.axis_index("section") == 0
    decoder_side = jnp.logical_not(encoder_side)
    mp_rank = lax.axis_index("mp")
    mp_count = lax.axis_size("mp")
    first_half = mp_rank == 0
    slot_ids = packing[0, 0]
    patch_ids = packing[0, 1]
    local_images = IMG // mp_count
    grid_cells = local_images * GRID
    local_slot = slot_ids - mp_rank * local_images
    inside = jnp.logical_and(local_slot >= 0, local_slot < local_images)
    target = jnp.where(inside, local_slot * GRID + patch_ids, grid_cells)

    local_rows, width = act_in.shape[1], act_in.shape[2]
    real_rows = local_rows * mp_count
    rows = -(-real_rows // ROW_BLOCK) * ROW_BLOCK
    lanes = -(-rows // TILE) * TILE
    part = width // mp_count
    units = FF // mp_count
    head = width // HEADS
    dec_width = dec_position.shape[1]
    dec_part = dec_width // mp_count
    widths = (3 * part, part, units, units, dec_part)
    slots = jnp.pad(slot_ids, (0, lanes - real_rows), constant_values=IMG + 1)
    ranges = key_ranges(slots)

    (qkv_w, out_w, up_w, down_w, projection), dec_own, norm_rows = gather_all(
        enc_weights[:, 0, :].astype(LOW),
        dec_weights[:, 0, :].astype(LOW),
        pack_norms(enc_norms, dec_norms, 1),
        widths,
    )
    enc_gains, dec_gains = (
        v.astype(LOW).astype(WIDE)
        for v in unpack_norms(
            norm_rows, norm_rows.shape[0] // 8, enc_norms.shape[1], dec_norms.shape[1]
        )
    )
    own_stream, other_stream = act_in[0], partner(act_in[0])
    stream = jnp.where(
        first_half,
        jnp.concatenate([own_stream, other_stream], axis=0),
        jnp.concatenate([other_stream, own_stream], axis=0),
    )
    stream = jnp.pad(stream, ((0, rows - real_rows), (0, 0)))
    first, turned, mixture, log_sum, mix_own = encoder_attend(
        stream, slots, ranges, enc_gains, qkv_w, out_w, head
    )
    shown = min(real_rows, -(-IMG * MOST_VISIBLE // 16) * 16)
    packed = -(-shown // 128) * 128
    cell_rows = -(-GRID // 16) * 16
    longer = (0, cell_rows - GRID)
    seen_target = jnp.pad(target[:shown], (0, packed - shown), constant_values=-1)
    cotangent = act_in[0].reshape(local_images, GRID, dec_width)
    cotangent = jnp.pad(cotangent, ((0, 0), longer, (0, 0)))
    position = jnp.pad(dec_position, (longer, (0, 0)))
    mix_other, seen_target, cotangent, position, dec_gains = lax.optimization_barrier(
        (partner(mix_own), seen_target, cotangent, position, dec_gains)
    )
    after, second, hidden, slope, feed_own = encoder_feed(
        stream, mix_own, mix_other, enc_gains, up_w, *down_w, ROW_BLOCK
    )
    encoded = (after + (feed_own.astype(WIDE) + partner(feed_own).astype(WIDE))).astype(LOW)
    projected = mm(encoded[:shown], projection).astype(LOW)
    arrived = from_behind(projected, "section", 1)
    arrived = jnp.pad(arrived, ((0, packed - shown), (0, 0)))
    decoded, grad_keep, grad_send, dec_grad_own, dec_grad_other, dec_gain_grad = decoder_step(
        GRID,
        first_half,
        arrived,
        partner(arrived),
        seen_target,
        mask_token,
        position,
        dec_gains,
        dec_own,
        partner(dec_own),
        cotangent,
    )
    returned = grad_keep[:shown] + partner(grad_send[:shown])
    grad_projected = from_behind(returned, "section", -1)
    grad_projected = jnp.pad(grad_projected, ((0, rows - shown), (0, 0)))
    dec_grad = dec_grad_own.astype(WIDE) + partner(dec_grad_other).astype(WIDE)
    dec_grad = dec_grad.astype(LOW)

    grad_projection = mm(encoded, grad_projected, 0, 0).astype(LOW)
    end_own = mm(grad_projected, projection, 1, 1).astype(LOW)
    end_other = partner(end_own)
    grad_up_w, grad_down_w, back_own = encoder_feed_back(
        jnp.where(encoder_side, 1, 0).astype(jnp.int32).reshape(1),
        end_own,
        end_other,
        second,
        hidden,
        slope,
        up_w,
        *down_w,
    )
    grad_after, grad_low, gains_two = encoder_norm_back(
        after, back_own, partner(back_own), (end_own, end_other), enc_gains, 2, ROW_BLOCK, True
    )
    grad_qkv_w, grad_out_w, start_own = encoder_attend_back(
        slots, ranges, first, turned, mixture, log_sum, grad_low, qkv_w, out_w, head
    )
    def choose(matrix):
        top, bottom = matrix[:local_rows], matrix[local_rows:real_rows]
        return jnp.where(first_half, top, bottom), jnp.where(first_half, bottom, top)

    start_keep, start_send = choose(start_own)
    act_out, gains_one = encoder_finish(
        encoder_side,
        own_stream,
        start_keep,
        partner(start_send),
        choose(grad_after)[0],
        enc_gains,
        decoded,
        GRID,
    )
    enc_gain_grad = jnp.concatenate(
        [gains_one[:2], jnp.where(first_half, gains_two[:2], 0.0)], axis=0
    )
    norm_grads = pack_norms(
        jnp.where(encoder_side, enc_gain_grad, 0.0),
        jnp.where(decoder_side, dec_gain_grad, 0.0),
        norm_rows.shape[0] // 8,
    )
    near_shard, down_shard, dec_shard, norm_shard, square_total = scatter_all(
        (grad_qkv_w, grad_out_w, grad_up_w, grad_down_w, grad_projection),
        dec_grad,
        norm_grads,
        encoder_side,
    )
    step_value = step_count[0].astype(jnp.float32)
    scalars = jnp.stack(
        [
            learning_rate[0],
            learning_rate[1],
            1.0 - jnp.power(BETA_FIRST, step_value),
            1.0 - jnp.power(BETA_SECOND, step_value),
        ]
    )
    results = renew_all(
        scalars,
        square_total,
        near_shard,
        down_shard,
        sum(widths[:3]),
        dec_shard,
        norm_shard,
        (enc_weights, enc_first, enc_second),
        (dec_weights, dec_first, dec_second),
        (enc_norms, enc_norm_first, enc_norm_second),
        (dec_norms, dec_norm_first, dec_norm_second),
    )
    return (act_out.reshape(act_in.shape), *results, jnp.sqrt(square_total[0, 0]).reshape(1))


def solution(mesh):
    in_specs = (
        P("section", ("dp", "mp"), None),
        P("dp", None, None),
        P(("section", "dp"), "mp", None),
        P(("section", "dp"), "mp", None),
        P(("section", "dp"), "mp", None),
        P(("section", "dp"), "mp", None),
        P(("section", "dp"), "mp", None),
        P(("section", "dp"), "mp", None),
        P(None, ("section", "dp")),
        P(None, ("section", "dp")),
        P(None, ("section", "dp")),
        P(None, ("section", "dp")),
        P(None, ("section", "dp")),
        P(None, ("section", "dp")),
        P(),
        P(),
        P(),
        P(),
    )
    out_specs = (
        P("section", ("dp", "mp"), None),
        P(("section", "dp"), "mp", None),
        P(("section", "dp"), "mp", None),
        P(None, ("section", "dp")),
        P(None, ("section", "dp")),
        P(("section", "dp"), "mp", None),
        P(("section", "dp"), "mp", None),
        P(None, ("section", "dp")),
        P(None, ("section", "dp")),
        P(),
    )
    return jax.shard_map(
        per_device, mesh=mesh, in_specs=in_specs, out_specs=out_specs, check_vma=False
    )
```
